32 devices in a mesh: row: 8 (over z, x), col: 4 (over y, core).
Axes of the slice: x: 2, y: 2, z: 4, core: 2. Of those that a mesh axis runs over, the one named last changes fastest.
Arguments:
- block_input: bfloat16 [1, 64, 128, 512], P(None, 'row', 'col'), may hold values from -6 to 6
- kernel_three: float32 [7, 7, 512], replicated, may hold values from -0.875 to 0.875
- gain_three: float32 [512], replicated, may hold values from 0.1 to 1.9
- expand_weight: bfloat16 [512, 2048], replicated, may hold values from -0.25 to 0.25
- project_weight: bfloat16 [2048, 512], replicated, may hold values from -0.125 to 0.125
- layer_scale: float32 [512], replicated, may hold values from 0.1 to 1
- merge_gain: float32 [512], replicated, may hold values from 0.1 to 1.9
- patch_weight: bfloat16 [2048, 1024], replicated, may hold values from -0.125 to 0.125
- kernel_four: float32 [7, 7, 1024], replicated, may hold values from -0.875 to 0.875
- gain_four: float32 [1024], replicated, may hold values from 0.1 to 1.9
- normed_cotangent: bfloat16 [1, 32, 64, 1024], P(None, 'row', 'col'), may hold values from -6 to 6
- residual_cotangent: bfloat16 [1, 32, 64, 1024], P(None, 'row', 'col'), may hold values from -6 to 6
Outputs:
- input_grad: bfloat16 [1, 64, 128, 512], P(None, 'row', 'col')
- kernel_three_grad: float32 [7, 7, 512], replicated
- gain_three_grad: float32 [512], replicated
- expand_grad: float32 [512, 2048], P('row')
- project_grad: float32 [2048, 512], P('row')
- scale_grad: float32 [512], replicated
- merge_gain_grad: float32 [512], replicated
- patch_grad: float32 [2048, 1024], P('row')
- kernel_four_grad: float32 [7, 7, 1024], replicated
- gain_four_grad: float32 [1024], replicated
The draws below stay inside these ranges and needn't reach their ends.
All inputs are finite; a program needn't handle non-finite values.
Results may differ from the reference program's by a relative error of at most 0.03.
Values may be sent and summed in bfloat16 or wider, within the bound.
No kernel may reach another device: no remote copies, remote signals or barrier semaphores. Data moves between devices by JAX's collectives and lax.ppermute only.
A program may use at most 128 MiB of HBM per device.

```python
import math
import jax
import jax.numpy as jnp
from jax import lax

D3 = 512
FF3 = 2048
D4 = 1024
BATCH = 1
R3 = 8
H3 = 64
W3 = 128
H4 = 32
W4 = 64


def block_scale(key, shape, shards, low, top_value):
    factor_of = 1.0
    for dim, blocks in shards:
        heights = jax.random.uniform(jax.random.fold_in(jax.random.fold_in(key, 6), dim), (blocks,), jnp.float32, low / len(shards), top_value / len(shards))
        factor_of = factor_of * jnp.repeat(jnp.exp(heights), shape[dim] // blocks).reshape((-1,) + (1,) * (len(shape) - 1 - dim))
    return factor_of


def centred(rng, dims, scale, reach, split=(), dtype=jnp.bfloat16):
    result = scale * jax.random.normal(rng, dims, jnp.float32)
    if split:
        result = result * block_scale(rng, dims, split, -0.22, 0.18)
    return jnp.clip(result, -reach, reach).astype(dtype)


def setup_inputs(seed: int = 0) -> dict:
    seeds = jax.random.split(jax.random.key(seed), 13)
    return {
        "block_input": centred(seeds[0], (BATCH, H3, W3, D3), 1.0, 6.0, ((1, 8), (2, 4))),
        "kernel_three": centred(seeds[1], (7, 7, D3), 49 ** -0.5, 0.875, (), jnp.float32),
        "gain_three": jnp.clip(1.0 + 0.18 * jax.random.normal(seeds[2], (D3,), jnp.float32), 0.1, 1.9),
        "expand_weight": centred(seeds[3], (D3, FF3), D3 ** -0.5, 0.25),
        "project_weight": centred(seeds[4], (FF3, D3), FF3 ** -0.5, 0.125),
        "layer_scale": jnp.clip(jnp.exp(jax.random.uniform(seeds[5], (D3,), jnp.float32, math.log(0.1), math.log(1.0))), 0.1, 1.0),
        "merge_gain": jnp.clip(1.0 + 0.18 * jax.random.normal(seeds[6], (D3,), jnp.float32), 0.1, 1.9),
        "patch_weight": centred(seeds[7], (4 * D3, D4), (4 * D3) ** -0.5, 0.125),
        "kernel_four": centred(seeds[8], (7, 7, D4), 49 ** -0.5, 0.875, (), jnp.float32),
        "gain_four": jnp.clip(1.0 + 0.18 * jax.random.normal(seeds[9], (D4,), jnp.float32), 0.1, 1.9),
        "normed_cotangent": centred(seeds[10], (BATCH, H4, W4, D4), 1.0, 6.0, ((1, 8), (2, 4))),
        "residual_cotangent": centred(seeds[11], (BATCH, H4, W4, D4), 1.0, 6.0, ((1, 8), (2, 4))),
    }


EPSILON = 1e-06

def conv_forward(values, kernel):
    extent = values.shape
    padded = jnp.pad(values, ((0, 0), (3, 3), (3, 3), (0, 0)))
    running = jnp.zeros(extent, jnp.float32)
    for vertical in range(7):
        for lateral in range(7):
            window = padded[:, vertical:vertical + extent[1], lateral:lateral + extent[2], :]
            running = running + window.astype(jnp.float32) * kernel[vertical, lateral]
    return running

def conv_transpose(values, kernel):
    extent = values.shape
    padded = jnp.pad(values, ((0, 0), (3, 3), (3, 3), (0, 0)))
    running = jnp.zeros(extent, jnp.float32)
    for vertical in range(7):
        for lateral in range(7):
            window = padded[:, 6 - vertical:6 - vertical + extent[1], 6 - lateral:6 - lateral + extent[2], :]
            running = running + window.astype(jnp.float32) * kernel[vertical, lateral]
    return running

def conv_weight_grad(values, grads):
    extent = values.shape
    padded = jnp.pad(values, ((0, 0), (3, 3), (3, 3), (0, 0)))
    grads_wide = grads.astype(jnp.float32)
    pieces = []
    for vertical in range(7):
        for lateral in range(7):
            window = padded[:, vertical:vertical + extent[1], lateral:lateral + extent[2], :]
            pieces.append(lax.optimization_barrier(jnp.sum(window.astype(jnp.float32) * grads_wide, axis=(0, 1, 2))))
    return jnp.stack(pieces).reshape(7, 7, extent[3])

def normalize(values):
    mean_value = lax.optimization_barrier(jnp.mean(values, axis=-1, keepdims=True))
    square = lax.optimization_barrier(jnp.mean(values * values, axis=-1, keepdims=True))
    inverse = lax.rsqrt(square - mean_value * mean_value + EPSILON)
    return ((values - mean_value) * inverse, inverse)

def normalize_back(grads, unit_values, inverse):
    return (grads - lax.optimization_barrier(jnp.mean(grads, axis=-1, keepdims=True)) - unit_values * lax.optimization_barrier(jnp.mean(grads * unit_values, axis=-1, keepdims=True))) * inverse

def gelu_slope(values):
    cumulative = 0.5 * (1.0 + jax.scipy.special.erf(values * (1.0 / math.sqrt(2.0))))
    return cumulative + values * jnp.exp(-0.5 * values * values) * (1.0 / math.sqrt(2.0 * math.pi))

def reference(block_input, kernel_three, gain_three, expand_weight, project_weight, layer_scale, merge_gain, patch_weight, kernel_four, gain_four, normed_cotangent, residual_cotangent):
    crop_count, height, breadth, channels = block_input.shape
    hidden_width = expand_weight.shape[1]
    wide_channels = patch_weight.shape[1]
    half_height = height // 2
    half_breadth = breadth // 2
    scale_three = 1.0 / math.sqrt(crop_count * height * breadth)
    scale_four = 1.0 / math.sqrt(crop_count * half_height * half_breadth)
    mixed = conv_forward(block_input, kernel_three)
    groups = crop_count * height // R3
    mixed_blocks = mixed.reshape(groups, R3 * breadth, channels)
    input_blocks = block_input.reshape(groups, R3 * breadth, channels)

    def forward_block(mixed_block):
        unit_mixed, inverse_mixed = normalize(mixed_block)
        normed = (unit_mixed * gain_three).astype(jnp.bfloat16)
        upward = jnp.dot(normed, expand_weight, preferred_element_type=jnp.float32)
        hidden = jax.nn.gelu(upward, approximate=False).astype(jnp.bfloat16)
        branch = jnp.dot(hidden, project_weight, preferred_element_type=jnp.float32)
        return (unit_mixed, inverse_mixed, normed, upward, hidden, branch)

    def branch_only(mixed_block):
        return forward_block(mixed_block)[5]
    branches = lax.map(branch_only, mixed_blocks)
    summed = (input_blocks.astype(jnp.float32) + layer_scale * branches).reshape(crop_count, height, breadth, channels)
    unit_summed, inverse_summed = normalize(summed)
    merged = (unit_summed * merge_gain).astype(jnp.bfloat16)
    patches = merged.reshape(crop_count, half_height, 2, half_breadth, 2, channels)
    patches = patches.transpose(0, 1, 3, 2, 4, 5).reshape(crop_count * half_height * half_breadth, 4 * channels)
    section_in = jnp.dot(patches, patch_weight, preferred_element_type=jnp.float32).astype(jnp.bfloat16)
    section_in = section_in.reshape(crop_count, half_height, half_breadth, wide_channels)
    mixed_four = conv_forward(section_in, kernel_four)
    unit_four, inverse_four = normalize(mixed_four)
    cot_four = normed_cotangent.astype(jnp.float32)
    gain_four_grad = scale_four * lax.optimization_barrier(jnp.sum(cot_four * unit_four, axis=(0, 1, 2)))
    grad_four = normalize_back(cot_four * gain_four, unit_four, inverse_four)
    kernel_four_grad = scale_four * conv_weight_grad(section_in, grad_four)
    section_grad = (residual_cotangent.astype(jnp.float32) + conv_transpose(grad_four, kernel_four)).astype(jnp.bfloat16)
    flat_grad = section_grad.reshape(-1, wide_channels)
    patch_grad = scale_four * lax.dot_general(patches, flat_grad, (((0,), (0,)), ((), ())), preferred_element_type=jnp.float32)
    grad_patches = lax.dot_general(flat_grad, patch_weight, (((1,), (1,)), ((), ())), preferred_element_type=jnp.float32)
    grad_merged = grad_patches.reshape(crop_count, half_height, half_breadth, 2, 2, channels)
    grad_merged = grad_merged.transpose(0, 1, 3, 2, 4, 5).reshape(crop_count, height, breadth, channels)
    merge_gain_grad = scale_three * lax.optimization_barrier(jnp.sum(grad_merged * unit_summed, axis=(0, 1, 2)))
    grad_summed = normalize_back(grad_merged * merge_gain, unit_summed, inverse_summed)
    summed_blocks = grad_summed.reshape(groups, R3 * breadth, channels)

    def backward_block(running, inputs):
        mixed_block, grad_block = inputs
        unit_mixed, inverse_mixed, normed, upward, hidden, branch = forward_block(mixed_block)
        expand_acc, project_acc, scale_acc, gain_acc = running
        scale_acc = scale_acc + lax.optimization_barrier(jnp.sum(grad_block * branch, axis=0))
        grad_branch = (layer_scale * grad_block).astype(jnp.bfloat16)
        project_acc = project_acc + lax.dot_general(hidden, grad_branch, (((0,), (0,)), ((), ())), preferred_element_type=jnp.float32)
        grad_hidden = lax.dot_general(grad_branch, project_weight, (((1,), (1,)), ((), ())), preferred_element_type=jnp.float32)
        grad_upward = (grad_hidden * gelu_slope(upward)).astype(jnp.bfloat16)
        expand_acc = expand_acc + lax.dot_general(normed, grad_upward, (((0,), (0,)), ((), ())), preferred_element_type=jnp.float32)
        grad_normed = lax.dot_general(grad_upward, expand_weight, (((1,), (1,)), ((), ())), preferred_element_type=jnp.float32)
        gain_acc = gain_acc + lax.optimization_barrier(jnp.sum(grad_normed * unit_mixed, axis=0))
        grad_mixed_block = normalize_back(grad_normed * gain_three, unit_mixed, inverse_mixed).astype(jnp.bfloat16)
        return ((expand_acc, project_acc, scale_acc, gain_acc), grad_mixed_block)
    initial = (jnp.zeros((channels, hidden_width), jnp.float32), jnp.zeros((hidden_width, channels), jnp.float32), jnp.zeros((channels,), jnp.float32), jnp.zeros((channels,), jnp.float32))
    totals, grad_blocks = lax.scan(backward_block, initial, (mixed_blocks, summed_blocks))
    grad_mixed = grad_blocks.reshape(crop_count, height, breadth, channels)
    kernel_three_grad = scale_three * conv_weight_grad(block_input, grad_mixed)
    input_grad = (grad_summed + conv_transpose(grad_mixed, kernel_three)).astype(jnp.bfloat16)
    return (input_grad, kernel_three_grad, scale_three * totals[3], scale_three * totals[0], scale_three * totals[1], scale_three * totals[2], merge_gain_grad, patch_grad, kernel_four_grad, gain_four_grad)
```

```python
import math

import jax
import jax.numpy as jnp
from jax import lax
from jax.sharding import PartitionSpec as P

EPSILON = 1e-06
BF = jnp.bfloat16
F32 = jnp.float32


def with_halo(block, sides, width):
    for axis, dim in sides:
        count = lax.axis_size(axis)
        forward = [(i, i + 1) for i in range(count - 1)]
        backward = [(target, source) for source, target in forward]
        low = lax.ppermute(
            lax.slice_in_dim(block, block.shape[dim] - width, None, axis=dim), axis, forward
        )
        high = lax.ppermute(lax.slice_in_dim(block, 0, width, axis=dim), axis, backward)
        block = jnp.concatenate([low, block, high], axis=dim)
    return block


def swap(values, axis, bit):
    return lax.ppermute(values, axis, [(i, i ^ bit) for i in range(lax.axis_size(axis))])


def axis_bits(axis):
    return [1 << k for k in range((lax.axis_size(axis) - 1).bit_length())]


def own_bit(axis, bit):
    return (lax.axis_index(axis) // bit) % 2


def pick(values, which, dim):
    return lax.dynamic_index_in_dim(values, which, dim, keepdims=False)


def halve(values, axis, bit, dim):
    mine = own_bit(axis, bit)
    return pick(values, mine, dim) + swap(pick(values, 1 - mine, dim), axis, bit)


def scatter_rows(part):
    for bit in axis_bits("row"):
        slices, rows, columns = part.shape
        part = halve(part.reshape(slices // 2, 2, rows, columns), "row", bit, 1)
    return part[0]


def double(values, axis, bit, dim):
    other = swap(values, axis, bit)
    mine = own_bit(axis, bit)
    low = jnp.where(mine == 0, values, other)
    high = jnp.where(mine == 0, other, values)
    return jnp.concatenate([low, high], axis=dim)


def sum_columns_first(part):
    bits = axis_bits("col")[1:]
    for bit in bits:
        slices, rows, columns = part.shape
        part = halve(part.reshape(slices, rows, 2, columns // 2), "col", bit, 2)
    part = scatter_rows(part)
    for bit in reversed(bits):
        part = double(part, "col", bit, 1)
    return part


def sum_rows_first(part):
    part = scatter_rows(part)
    for bit in axis_bits("col")[1:]:
        part = part + swap(part, "col", bit)
    return part


def conv_forward(padded, kernel, height, breadth):
    running = jnp.zeros((padded.shape[0], height, breadth, padded.shape[3]), F32)
    for vertical in range(7):
        for lateral in range(7):
            window = padded[:, vertical : vertical + height, lateral : lateral + breadth, :]
            running = running + window.astype(F32) * kernel[vertical, lateral]
    return running


def conv_transpose(padded, kernel, height, breadth):
    return conv_forward(padded, kernel[::-1, ::-1], height, breadth)


def conv_weight_grad(padded, grads, height, breadth):
    grads_wide = grads.astype(F32)
    pieces = []
    for vertical in range(7):
        for lateral in range(7):
            window = padded[:, vertical : vertical + height, lateral : lateral + breadth, :]
            pieces.append(jnp.sum(window.astype(F32) * grads_wide, axis=(0, 1, 2)))
    return jnp.stack(pieces)


def normalize(values):
    mean_value = jnp.mean(values, axis=-1, keepdims=True)
    square = jnp.mean(values * values, axis=-1, keepdims=True)
    inverse = lax.rsqrt(square - mean_value * mean_value + EPSILON)
    return ((values - mean_value) * inverse, inverse)


def normalize_back(grads, unit_values, inverse):
    return (
        grads
        - jnp.mean(grads, axis=-1, keepdims=True)
        - unit_values * jnp.mean(grads * unit_values, axis=-1, keepdims=True)
    ) * inverse


def column_product(left, right):
    return lax.dot_general(left, right, (((0,), (0,)), ((), ())), preferred_element_type=F32)


def body(
    block_input,
    kernel_three,
    gain_three,
    expand_weight,
    project_weight,
    layer_scale,
    merge_gain,
    patch_weight,
    kernel_four,
    gain_four,
    normed_cotangent,
    residual_cotangent,
):
    crops, height, breadth, channels = block_input.shape
    wide = patch_weight.shape[1]
    half_height = height // 2
    half_breadth = breadth // 2
    row_count = lax.axis_size("row")
    col_count = lax.axis_size("col")
    scale_three = 1.0 / math.sqrt(crops * height * breadth * row_count * col_count)
    scale_four = 1.0 / math.sqrt(crops * half_height * half_breadth * row_count * col_count)
    sides = (("row", 1), ("col", 2))
    core = own_bit("col", 1)

    def pair_product(left, left_other, right, factor):
        halves = right.reshape(right.shape[0], 2, -1)
        kept = pick(halves, core, 1)
        other = swap(pick(halves, 1 - core, 1), "col", 1)
        product = column_product(left, kept) + column_product(left_other, other)
        return (factor * product).astype(BF).reshape(row_count, -1, kept.shape[1])

    framed = with_halo(block_input, sides, 3)
    mixed = conv_forward(framed, kernel_three, height, breadth).reshape(-1, channels)
    unit_mixed, inverse_mixed = normalize(mixed)
    normed = (unit_mixed * gain_three).astype(BF)
    upward = jnp.dot(normed, expand_weight, preferred_element_type=F32)
    cumulative = 0.5 * (1.0 + lax.erf(upward * (1.0 / math.sqrt(2.0))))
    slope = cumulative + upward * jnp.exp(-0.5 * upward * upward) * (1.0 / math.sqrt(2.0 * math.pi))
    hidden = (upward * cumulative).astype(BF)
    branch = jnp.dot(hidden, project_weight, preferred_element_type=F32)
    summed = block_input.reshape(-1, channels).astype(F32) + layer_scale * branch
    unit_summed, inverse_summed = normalize(summed)
    merged = (unit_summed * merge_gain).astype(BF)
    patches = merged.reshape(crops, half_height, 2, half_breadth, 2, channels)
    patches = patches.transpose(0, 1, 3, 2, 4, 5).reshape(-1, 4 * channels)
    section_in = jnp.dot(patches, patch_weight, preferred_element_type=F32).astype(BF)
    section_in = section_in.reshape(crops, half_height, half_breadth, wide)

    framed_four = with_halo(section_in, sides, 3)
    patches_other = swap(patches, "col", 1)
    hidden_other = swap(hidden, "col", 1)
    normed_other = swap(normed, "col", 1)
    mixed_four = conv_forward(framed_four, kernel_four, half_height, half_breadth)
    unit_four, inverse_four = normalize(mixed_four)
    cot_four = normed_cotangent.astype(F32)
    gain_four_part = jnp.sum(cot_four * unit_four, axis=(0, 1, 2))
    grad_four = normalize_back(cot_four * gain_four, unit_four, inverse_four)
    framed_grad = with_halo(grad_four.astype(BF), sides, 3)
    kernel_four_part = conv_weight_grad(framed_four, grad_four, half_height, half_breadth)
    section_grad = (
        residual_cotangent.astype(F32)
        + conv_transpose(framed_grad, kernel_four, half_height, half_breadth)
    ).astype(BF)
    flat_grad = section_grad.reshape(-1, wide)
    patch_sum = sum_columns_first(pair_product(patches, patches_other, flat_grad, scale_four))

    grad_patches = lax.dot_general(
        flat_grad, patch_weight, (((1,), (1,)), ((), ())), preferred_element_type=F32
    )
    grad_merged = grad_patches.reshape(crops, half_height, half_breadth, 2, 2, channels)
    grad_merged = grad_merged.transpose(0, 1, 3, 2, 4, 5).reshape(-1, channels)
    merge_part = jnp.sum(grad_merged * unit_summed, axis=0)
    grad_summed = normalize_back(grad_merged * merge_gain, unit_summed, inverse_summed)
    scale_part = jnp.sum(grad_summed * branch, axis=0)
    grad_branch = (layer_scale * grad_summed).astype(BF)
    project_sum = sum_rows_first(pair_product(hidden, hidden_other, grad_branch, scale_three))
    grad_hidden = lax.dot_general(
        grad_branch, project_weight, (((1,), (1,)), ((), ())), preferred_element_type=F32
    )
    grad_upward = (grad_hidden * slope).astype(BF)
    expand_sum = sum_columns_first(pair_product(normed, normed_other, grad_upward, scale_three))
    grad_normed = lax.dot_general(
        grad_upward, expand_weight, (((1,), (1,)), ((), ())), preferred_element_type=F32
    )
    gain_part = jnp.sum(grad_normed * unit_mixed, axis=0)
    grad_mixed = normalize_back(grad_normed * gain_three, unit_mixed, inverse_mixed).astype(BF)
    grad_mixed = grad_mixed.reshape(crops, height, breadth, channels)
    framed_grad_three = with_halo(grad_mixed, sides, 3)
    kernel_part = conv_weight_grad(framed, grad_mixed, height, breadth)
    input_grad = (
        grad_summed.reshape(crops, height, breadth, channels)
        + conv_transpose(framed_grad_three, kernel_three, height, breadth)
    ).astype(BF)

    small = jnp.concatenate(
        [
            scale_three * kernel_part.reshape(-1, 128),
            scale_three * gain_part.reshape(-1, 128),
            scale_three * scale_part.reshape(-1, 128),
            scale_three * merge_part.reshape(-1, 128),
            scale_four * kernel_four_part.reshape(-1, 128),
            scale_four * gain_four_part.reshape(-1, 128),
        ]
    )
    count = small.shape[0]
    total = row_count * col_count
    per = -(-count // (total * 8)) * 8
    small = jnp.pad(small, ((0, per * total - count), (0, 0)))
    small = small.reshape(col_count, row_count * per, 128)
    for bit in axis_bits("col"):
        small = halve(small.reshape(-1, 2, row_count * per, 128), "col", bit, 1)
    small = scatter_rows(small.reshape(row_count, per, 128))
    for bit in reversed(axis_bits("row")):
        pass
    small = small[None]
    for bit in reversed(axis_bits("row")):
        small = double(small[:, None], "row", bit, 1).reshape(-1, per, 128)
    small = small.reshape(1, row_count * per, 128)
    for bit in reversed(axis_bits("col")):
        small = double(small[:, None], "col", bit, 1).reshape(-1, row_count * per, 128)
    small = small.reshape(-1, 128)

    outs = []
    at = 0
    for shape in ((7, 7, channels), (channels,), (channels,), (channels,), (7, 7, wide), (wide,)):
        rows = math.prod(shape) // 128
        outs.append(small[at : at + rows].reshape(shape))
        at += rows
    expand_grad, project_grad, patch_grad = (
        double(piece, "col", 1, 1).astype(F32) for piece in (expand_sum, project_sum, patch_sum)
    )
    return (
        input_grad,
        outs[0],
        outs[1],
        expand_grad,
        project_grad,
        outs[2],
        outs[3],
        patch_grad,
        outs[4],
        outs[5],
    )


def solution(mesh):
    pixels = P(None, "row", "col", None)
    return jax.shard_map(
        body,
        mesh=mesh,
        in_specs=(pixels,) + (P(),) * 9 + (pixels, pixels),
        out_specs=(pixels, P(), P(), P("row", None), P("row", None), P(), P(), P("row", None), P(), P()),
        check_vma=False,
    )
```

```python
import functools
import math

import jax
import jax.numpy as jnp
from jax import lax
from jax.experimental import pallas as pl
from jax.experimental.pallas import tpu as pltpu
from jax.sharding import PartitionSpec as P

EPSILON = 1e-06
BF = jnp.bfloat16
F32 = jnp.float32
MIB = 1 << 20
PAD = 8
CHUNK = 256


def shape_of(*dims, dtype=F32):
    return jax.ShapeDtypeStruct(dims, dtype)


def run(kernel, name, args, outs, scratch=(), remote=(), limit=24, flops=10**7):
    inside = pl.BlockSpec(memory_space=pltpu.VMEM)
    outside = pl.BlockSpec(memory_space=pl.ANY)
    moved = sum(a.size * a.dtype.itemsize for a in args)
    moved += sum(math.prod(o.shape) * o.dtype.itemsize for o in outs)
    return pl.pallas_call(
        kernel,
        name=name,
        out_shape=outs,
        in_specs=[outside if i in remote else inside for i in range(len(args))],
        out_specs=[inside] * len(outs),
        scratch_shapes=list(scratch),
        compiler_params=pltpu.CompilerParams(vmem_limit_bytes=limit * MIB),
        cost_estimate=pl.CostEstimate(flops=flops, bytes_accessed=moved, transcendentals=0),
    )(*args)


def swap(values, axis, bit):
    return lax.ppermute(values, axis, [(i, i ^ bit) for i in range(lax.axis_size(axis))])


def axis_bits(axis):
    return [1 << k for k in range((lax.axis_size(axis) - 1).bit_length())]


def own_bit(axis, bit):
    return (lax.axis_index(axis) // bit) % 2


def pick(values, which, dim):
    return lax.dynamic_index_in_dim(values, which, dim, keepdims=False)


def scatter(values, axis, bits):
    for bit in bits:
        mine = own_bit(axis, bit)
        values = values.reshape(values.shape[0] // 2, 2, *values.shape[1:])
        values = pick(values, mine, 1) + swap(pick(values, 1 - mine, 1), axis, bit)
    return values[0]


def gather(values, axis, bits):
    values = values[None]
    for bit in reversed(bits):
        other = swap(values, axis, bit)
        mine = own_bit(axis, bit)
        low = jnp.where(mine == 0, values, other)
        high = jnp.where(mine == 0, other, values)
        values = jnp.stack([low, high], axis=1).reshape(-1, *values.shape[1:])
    return values


def neighbours(first, last, axis):
    count = lax.axis_size(axis)
    forward = [(i, i + 1) for i in range(count - 1)]
    backward = [(i + 1, i) for i in range(count - 1)]
    return lax.ppermute(last, axis, forward), lax.ppermute(first, axis, backward)


def strip_kernel(center, top, bottom, first, last):
    height, breadth = center.shape[:2]
    for source, start in ((top, 0), (center, 3), (bottom, 3 + height)):
        values = source[...].astype(F32)
        rows = slice(start, start + source.shape[0])
        first[rows] = values[:, :PAD].astype(BF)
        last[rows] = values[:, breadth - PAD :].astype(BF)


def halo(center, first_rows, last_rows, name):
    height, _, channels = center.shape
    top, bottom = neighbours(first_rows, last_rows, "row")
    strip = shape_of(height + 6, PAD, channels, dtype=BF)
    first, last = run(strip_kernel, name, (center, top, bottom), (strip, strip), limit=8)
    left, right = neighbours(first, last, "col")
    return center, top, bottom, left, right


def fill_frame(frame, parts):
    center, top, bottom, left, right = parts
    height, breadth = center.shape[:2]
    middle = slice(PAD, PAD + breadth)
    frame[0:3, middle] = top[...].astype(F32)
    frame[3 : 3 + height, middle] = center[...].astype(F32)
    frame[3 + height :, middle] = bottom[...].astype(F32)
    frame[:, :PAD] = left[...].astype(F32)
    frame[:, PAD + breadth :] = right[...].astype(F32)


def frame_scratch(center):
    height, breadth, channels = center.shape
    return pltpu.VMEM((height + 6, breadth + 2 * PAD, channels), F32)


def lane_tiles(channels):
    def over(step):
        def wrapped(index, carry):
            step(pl.ds(pl.multiple_of(index * 128, 128), 128))
            return carry

        lax.fori_loop(0, channels // 128, wrapped, 0)

    return over


def convolve(frame, taps, flip, out):
    height, breadth, channels = out.shape

    @lane_tiles(channels)
    def _(lanes):
        for column in range(0, breadth, 8):
            total = jnp.zeros((height, 8, 128), F32)
            for q in range(7):
                rows = frame[:, pl.ds(column + PAD - 3 + q, 8), lanes]
                for p in range(7):
                    a, b = (6 - p, 6 - q) if flip else (p, q)
                    total = total + rows[p : p + height] * taps[a, pl.ds(b, 1), lanes]
            out[:, pl.ds(column, 8), lanes] = total


def weight_sums(frame, grads, scale, out):
    height, breadth, channels = grads.shape

    @lane_tiles(channels)
    def _(lanes):
        for q in range(7):
            totals = [jnp.zeros((8, 128), F32)] * 7
            for column in range(0, breadth, 8):
                rows = frame[:, pl.ds(column + PAD - 3 + q, 8), lanes]
                grad = grads[:, pl.ds(column, 8), lanes]
                for p in range(7):
                    totals[p] = totals[p] + jnp.sum(rows[p : p + height] * grad, axis=0)
            for p in range(7):
                out[pl.ds(7 * p + q, 1), lanes] = scale * jnp.sum(totals[p], axis=0, keepdims=True)


def mean(values):
    return jnp.mean(values, axis=-1, keepdims=True)


def normalize(values):
    level = mean(values)
    inverse = lax.rsqrt(mean(values * values) - level * level + EPSILON)
    return (values - level) * inverse, inverse


def normalize_back(grads, unit_values, inverse):
    return (grads - mean(grads) - unit_values * mean(grads * unit_values)) * inverse


def dot(left, right):
    return jnp.dot(left, right, preferred_element_type=F32)


def dot_last(left, right):
    return lax.dot_general(left, right, (((1,), (1,)), ((), ())), preferred_element_type=F32)


def dot_first(left, right):
    return lax.dot_general(left, right, (((0,), (0,)), ((), ())), preferred_element_type=F32)


def over_rows(count, size):
    def over(step):
        def wrapped(index, carry):
            step(index, pl.ds(pl.multiple_of(index * size, size), size))
            return carry

        lax.fori_loop(0, count, wrapped, 0)

    return over


def fetch(sources, targets, semaphores):
    copies = [
        pltpu.make_async_copy(source, target, semaphores.at[i])
        for i, (source, target) in enumerate(zip(sources, targets))
    ]
    for copy in copies:
        copy.start()
    return copies


def front_kernel(
    center, top, bottom, left, right, taps, gain, expand, project, layer_scale, merge_gain, patch,
    early, unit_mixed, inverse_mixed, slope, branch, unit_summed, inverse_summed, section, first, last,
    frame, image, pairs, expand_here, project_here, patch_here, upward, semaphores,
):
    height, breadth, channels = center.shape
    hidden_width = expand.shape[1]
    pixels = height * breadth
    copies = fetch(
        (expand, project, patch), (expand_here, project_here, patch_here), semaphores
    )
    fill_frame(frame, (center, top, bottom, left, right))
    convolve(frame, taps, False, image)
    at_normed = slice(hidden_width, hidden_width + channels)
    at_patches = slice(hidden_width + channels, hidden_width + 2 * channels)

    @over_rows(height, breadth)
    def _(y, rows):
        unit, inverse = normalize(image[y])
        unit_mixed[rows] = unit
        inverse_mixed[rows] = inverse
        early[rows, at_normed] = (unit * gain[...]).astype(BF)

    copies[0].wait()

    def chunk(index, carry):
        lanes = pl.ds(pl.multiple_of(index * CHUNK, CHUNK), CHUNK)
        upward[...] = dot(early[:, at_normed], expand_here[:, lanes])
        for start in range(0, pixels, 64):
            rows = slice(start, start + 64)
            value = upward[rows]
            cumulative = 0.5 + 0.5 * lax.erf(value * (1.0 / math.sqrt(2.0)))
            density = jnp.exp(-0.5 * value * value) * (1.0 / math.sqrt(2.0 * math.pi))
            early[rows, lanes] = (value * cumulative).astype(BF)
            slope[rows, lanes] = (cumulative + value * density).astype(BF)
        return carry

    lax.fori_loop(0, hidden_width // CHUNK, chunk, 0)
    copies[1].wait()
    branch[...] = dot(early[:, :hidden_width], project_here[...])

    @over_rows(height, breadth)
    def _(y, rows):
        summed = center[y].astype(F32) + layer_scale[...] * branch[rows]
        unit, inverse = normalize(summed)
        unit_summed[rows] = unit
        inverse_summed[rows] = inverse
        merged = unit * merge_gain[...]
        for k in range(channels // 128):
            pairs[k, y] = merged[:, k * 128 : (k + 1) * 128]

    quarter = pixels // 4
    for dy in range(2):
        for dx in range(2):
            j = 2 * dy + dx
            for y in range(height // 2):
                start = j * quarter + y * (breadth // 2)
                for k in range(channels // 128):
                    piece = pairs[k, 2 * y + dy, pl.ds(dx, breadth // 2, stride=2), :]
                    lane = hidden_width + channels + k * 128
                    early[start : start + breadth // 2, lane : lane + 128] = piece.astype(BF)
    copies[2].wait()
    total = dot(early[:quarter, at_patches], patch_here[:channels])
    for j in range(1, 4):
        total = total + dot(
            early[j * quarter : (j + 1) * quarter, at_patches],
            patch_here[j * channels : (j + 1) * channels],
        )
    total = total.reshape(section.shape)
    section[...] = total.astype(BF)
    first[...] = total[:3].astype(BF)
    last[...] = total[height // 2 - 3 :].astype(BF)


def mixer_kernel(
    center, top, bottom, left, right, taps, gain, cotangent,
    grad, grad_half, first, last, gain_part,
    frame, image,
):
    height, breadth, channels = center.shape
    fill_frame(frame, (center, top, bottom, left, right))
    convolve(frame, taps, False, image)
    part = jnp.zeros((1, channels), F32)
    for y in range(height):
        unit, inverse = normalize(image[y])
        cot = cotangent[y].astype(F32)
        part = part + jnp.sum(cot * unit, axis=0, keepdims=True)
        value = normalize_back(cot * gain[...], unit, inverse)
        grad[y] = value
        narrow = value.astype(BF)
        grad_half[y] = narrow
        if y < 3:
            first[y] = narrow
        if y >= height - 3:
            last[y - (height - 3)] = narrow
    gain_part[...] = part


def weight_kernel(scale, center, top, bottom, left, right, grads, out, frame):
    fill_frame(frame, (center, top, bottom, left, right))
    weight_sums(frame, grads, scale, out)


def weight_pack_kernel(
    scale, scale_wide, center, top, bottom, left, right, grads,
    gain_part, layer_part, merge_part, wide_part, wide_gain,
    keep, send, frame, wide_grads, packed,
):
    channels = center.shape[2]
    half = channels // 2
    fill_frame(frame, (center, top, bottom, left, right))
    wide_grads[...] = grads[...].astype(F32)
    packed[...] = jnp.zeros(packed.shape, F32)
    weight_sums(frame, wide_grads, scale, packed)
    for i, part in enumerate((gain_part, layer_part, merge_part)):
        packed[49 + i : 50 + i] = scale * part[...]
    for i in range(2):
        columns = slice(i * channels, (i + 1) * channels)
        packed[52 + 49 * i : 101 + 49 * i] = wide_part[:, columns]
        packed[150 + i : 151 + i] = scale_wide * wide_gain[:, columns]
    values = packed[...].astype(BF)
    core = lax.axis_index("col") % 2
    for i in range(2):

        @pl.when(core == i)
        def _():
            keep[...] = values[:, i * half : (i + 1) * half]
            send[...] = values[:, (1 - i) * half : (2 - i) * half]


def section_kernel(
    center, top, bottom, left, right, taps, residual,
    flat, keep, send,
    frame, image,
):
    height, breadth, channels = center.shape
    fill_frame(frame, (center, top, bottom, left, right))
    convolve(frame, taps, True, image)
    value = (image[...] + residual[...].astype(F32)).reshape(flat.shape).astype(BF)
    flat[...] = value
    blocks, _, width = keep.shape
    core = lax.axis_index("col") % 2
    for i in range(2):

        @pl.when(core == i)
        def _():
            for m in range(blocks):
                mine, other = (2 * m + i) * width, (2 * m + 1 - i) * width
                keep[m] = value[:, mine : mine + width]
                send[m] = value[:, other : other + width]


def merge_kernel(
    flat, patch, unit_summed, inverse_summed, merge_gain, branch, layer_scale,
    grad_summed, grad_branch, keep, send, merge_part, layer_part,
    patch_here, pairs, semaphores,
):
    tiles, height, breadth, _ = pairs.shape
    channels = 128 * tiles
    (copy,) = fetch((patch,), (patch_here,), semaphores)
    value = flat[...]
    copy.wait()
    for dy in range(2):
        for dx in range(2):
            j = 2 * dy + dx
            part = dot_last(value, patch_here[j * channels : (j + 1) * channels])
            part = part.reshape(height // 2, breadth // 2, channels)
            for y in range(height // 2):
                for k in range(channels // 128):
                    piece = part[y, :, k * 128 : (k + 1) * 128]
                    pairs[k, 2 * y + dy, pl.ds(dx, breadth // 2, stride=2), :] = piece
    merge_part[...] = jnp.zeros(merge_part.shape, F32)
    layer_part[...] = jnp.zeros(layer_part.shape, F32)
    core = lax.axis_index("col") % 2
    half = channels // 2

    @over_rows(height, breadth)
    def _(y, rows):
        merged = jnp.concatenate([pairs[k, y] for k in range(tiles)], axis=1)
        unit = unit_summed[rows]
        merge_part[...] += jnp.sum(merged * unit, axis=0, keepdims=True)
        grad = normalize_back(merged * merge_gain[...], unit, inverse_summed[rows])
        grad_summed[rows] = grad
        layer_part[...] += jnp.sum(grad * branch[rows], axis=0, keepdims=True)
        narrow = (layer_scale[...] * grad).astype(BF)
        grad_branch[rows] = narrow
        for i in range(2):

            @pl.when(core == i)
            def _():
                keep[rows] = narrow[:, i * half : (i + 1) * half]
                send[rows] = narrow[:, (1 - i) * half : (2 - i) * half]


def back_kernel(
    grad_branch, project, slope, expand, unit_mixed, inverse_mixed, gain,
    keep, send, grad_mixed, first, last, gain_part,
    project_here, expand_here, hidden, upward, normed, semaphores,
):
    height, breadth, channels = grad_mixed.shape
    pixels, hidden_width = slope.shape
    copies = fetch((project, expand), (project_here, expand_here), semaphores)
    copies[0].wait()

    def chunk(index, carry):
        span = pl.ds(pl.multiple_of(index * CHUNK, CHUNK), CHUNK)
        hidden[...] = dot_last(grad_branch[...], project_here[span])
        for start in range(0, pixels, 64):
            rows = slice(start, start + 64)
            upward[rows, span] = (hidden[rows] * slope[rows, span].astype(F32)).astype(BF)
        return carry

    lax.fori_loop(0, hidden_width // CHUNK, chunk, 0)
    copies[1].wait()
    normed[...] = dot_last(upward[...], expand_here[...])
    half = hidden_width // 2
    core = lax.axis_index("col") % 2
    for i in range(2):

        @pl.when(core == i)
        def _():
            keep[...] = upward[:, i * half : (i + 1) * half]
            send[...] = upward[:, (1 - i) * half : (2 - i) * half]

    part = jnp.zeros((1, channels), F32)
    for y in range(height):
        rows = slice(y * breadth, (y + 1) * breadth)
        value = normed[rows]
        unit = unit_mixed[rows]
        part = part + jnp.sum(value * unit, axis=0, keepdims=True)
        narrow = normalize_back(value * gain[...], unit, inverse_mixed[rows]).astype(BF)
        grad_mixed[y] = narrow
        if y < 3:
            first[y] = narrow
        if y >= height - 3:
            last[y - (height - 3)] = narrow
    gain_part[...] = part


def patch_product_kernel(factor, early, early_other, own, other, keep, send):
    _, rows, width = keep.shape
    blocks = own.shape[0]
    channels = rows // 4
    quarter = own.shape[1]
    at_patches = early.shape[1] - channels
    bit = (lax.axis_index("col") // 2) % 2
    for j in range(4):
        span = slice(j * quarter, (j + 1) * quarter)
        left = jnp.concatenate([early[span, at_patches:], early_other[span, at_patches:]], axis=0)
        for m in range(blocks):
            right = jnp.concatenate([own[m], other[m]], axis=0)
            value = (factor * dot_first(left, right)).astype(BF)
            target = slice(j * channels, (j + 1) * channels)
            for i in range(2):

                @pl.when(bit == i)
                def _():
                    if m % 2 == i:
                        keep[m // 2, target] = value
                    else:
                        send[m // 2, target] = value


def share_product_kernel(
    factor, early, early_other, branch_own, branch_other, upward_own, upward_other,
    small_own, small_other, keep, send,
):
    slices = 2 * keep.shape[0]
    width = keep.shape[2]
    channels = 2 * width
    hidden_width = early.shape[1] - 2 * channels
    deep, shallow = hidden_width // slices, channels // slices
    blocks = upward_own.shape[1] // width
    per = small_own.shape[0] // slices
    bit = lax.axis_index("row") % 2

    def store(value, start, rows):
        begin, offset = start
        for i in range(2):

            @pl.when(bit == i)
            def _():
                for k in range(value.shape[0] // rows):
                    r = begin + k
                    target = keep if r % 2 == i else send
                    target[r // 2, offset : offset + rows] = value[k * rows : (k + 1) * rows]

    right = jnp.concatenate([branch_own[...], branch_other[...]], axis=0)
    step = max(CHUNK, deep)
    for start in range(0, hidden_width, step):
        columns = slice(start, start + step)
        left = jnp.concatenate([early[:, columns], early_other[:, columns]], axis=0)
        store((factor * dot_first(left, right)).astype(BF), (start // deep, 0), deep)
    columns = slice(hidden_width, hidden_width + channels)
    left = jnp.concatenate([early[:, columns], early_other[:, columns]], axis=0)
    for k in range(blocks):
        columns = slice(k * width, (k + 1) * width)
        right = jnp.concatenate([upward_own[:, columns], upward_other[:, columns]], axis=0)
        store((factor * dot_first(left, right)).astype(BF), (0, deep + k * shallow), shallow)
    small = (small_own[...].astype(F32) + small_other[...].astype(F32)).astype(BF)
    store(small, (0, deep + blocks * shallow), per)


def input_kernel(center, top, bottom, left, right, taps, grad_summed, out, frame, image):
    fill_frame(frame, (center, top, bottom, left, right))
    convolve(frame, taps, True, image)
    out[...] = (image[...] + grad_summed[...].reshape(image.shape)).astype(BF)


def body(
    block_input,
    kernel_three,
    gain_three,
    expand_weight,
    project_weight,
    layer_scale,
    merge_gain,
    patch_weight,
    kernel_four,
    gain_four,
    normed_cotangent,
    residual_cotangent,
):
    _, height, breadth, channels = block_input.shape
    hidden_width = expand_weight.shape[1]
    wide = patch_weight.shape[1]
    pixels = height * breadth
    quarter = pixels // 4
    rows4, cols4 = height // 2, breadth // 2
    row_count = lax.axis_size("row")
    col_count = lax.axis_size("col")
    scale_three = 1.0 / math.sqrt(pixels * row_count * col_count)
    scale_four = 1.0 / math.sqrt(quarter * row_count * col_count)
    center = block_input[0]
    cotangent = normed_cotangent[0]
    residual = residual_cotangent[0]
    gain_three, layer_scale, merge_gain, gain_four = (
        v[None] for v in (gain_three, layer_scale, merge_gain, gain_four)
    )
    dma = pltpu.SemaphoreType.DMA
    half = channels // 2

    framed = halo(center, center[:3], center[height - 3 :], "strips_input")
    (
        early, unit_mixed, inverse_mixed, slope, branch, unit_summed, inverse_summed,
        section, first, last,
    ) = run(
        front_kernel,
        "front",
        (*framed, kernel_three, gain_three, expand_weight, project_weight, layer_scale, merge_gain, patch_weight),
        (
            shape_of(pixels, hidden_width + 2 * channels, dtype=BF),
            shape_of(pixels, channels),
            shape_of(pixels, 1),
            shape_of(pixels, hidden_width, dtype=BF),
            shape_of(pixels, channels),
            shape_of(pixels, channels),
            shape_of(pixels, 1),
            shape_of(rows4, cols4, wide, dtype=BF),
            shape_of(3, cols4, wide, dtype=BF),
            shape_of(3, cols4, wide, dtype=BF),
        ),
        scratch=(
            frame_scratch(center),
            pltpu.VMEM((height, breadth, channels), F32),
            pltpu.VMEM((channels // 128, height, breadth, 128), F32),
            pltpu.VMEM(expand_weight.shape, BF),
            pltpu.VMEM(project_weight.shape, BF),
            pltpu.VMEM(patch_weight.shape, BF),
            pltpu.VMEM((pixels, CHUNK), F32),
            dma((3,)),
        ),
        remote=(7, 8, 11),
        limit=28,
        flops=2 * 10**9,
    )

    framed_four = halo(section, first, last, "strips_section")
    early_other = swap(early, "col", 1)
    mixer_image = pltpu.VMEM((rows4, cols4, wide), F32)
    grad_four, grad_four_half, first, last, gain_four_part = run(
        mixer_kernel,
        "mixer",
        (*framed_four, kernel_four, gain_four, cotangent),
        (
            shape_of(rows4, cols4, wide),
            shape_of(rows4, cols4, wide, dtype=BF),
            shape_of(3, cols4, wide, dtype=BF),
            shape_of(3, cols4, wide, dtype=BF),
            shape_of(1, wide),
        ),
        scratch=(frame_scratch(section), mixer_image),
        limit=12,
    )
    framed_grad = halo(grad_four_half, first, last, "strips_mixer")
    (kernel_four_part,) = run(
        functools.partial(weight_kernel, scale_four),
        "mixer_weights",
        (*framed_four, grad_four),
        (shape_of(49, wide),),
        scratch=(frame_scratch(section),),
        limit=12,
    )
    block_count = col_count // 2
    block = wide // col_count
    blocked = shape_of(block_count, quarter, block, dtype=BF)
    flat, flat_keep, flat_send = run(
        section_kernel,
        "section_grad",
        (*framed_grad, kernel_four, residual),
        (shape_of(quarter, wide, dtype=BF), blocked, blocked),
        scratch=(frame_scratch(section), mixer_image),
        limit=12,
    )

    flat_other = swap(flat_send, "col", 1)
    grad_summed, grad_branch, branch_keep, branch_send, merge_part, layer_part = run(
        merge_kernel,
        "merge_back",
        (flat, patch_weight, unit_summed, inverse_summed, merge_gain, branch, layer_scale),
        (
            shape_of(pixels, channels),
            shape_of(pixels, channels, dtype=BF),
            shape_of(pixels, half, dtype=BF),
            shape_of(pixels, half, dtype=BF),
            shape_of(1, channels),
            shape_of(1, channels),
        ),
        scratch=(
            pltpu.VMEM(patch_weight.shape, BF),
            pltpu.VMEM((channels // 128, height, breadth, 128), F32),
            dma((1,)),
        ),
        remote=(1,),
        limit=16,
        flops=5 * 10**8,
    )
    patch_half = shape_of(block_count // 2, 4 * channels, block, dtype=BF)
    patch_keep, patch_send = run(
        functools.partial(patch_product_kernel, scale_four),
        "patch_product",
        (early, early_other, flat_keep, flat_other),
        (patch_half, patch_half),
        limit=16,
        flops=5 * 10**8,
    )
    branch_other = swap(branch_send, "col", 1)
    upward_keep, upward_send, grad_mixed, first, last, gain_part = run(
        back_kernel,
        "mlp_back",
        (grad_branch, project_weight, slope, expand_weight, unit_mixed, inverse_mixed, gain_three),
        (
            shape_of(pixels, hidden_width // 2, dtype=BF),
            shape_of(pixels, hidden_width // 2, dtype=BF),
            shape_of(height, breadth, channels, dtype=BF),
            shape_of(3, breadth, channels, dtype=BF),
            shape_of(3, breadth, channels, dtype=BF),
            shape_of(1, channels),
        ),
        scratch=(
            pltpu.VMEM(project_weight.shape, BF),
            pltpu.VMEM(expand_weight.shape, BF),
            pltpu.VMEM((pixels, CHUNK), F32),
            pltpu.VMEM((pixels, hidden_width), BF),
            pltpu.VMEM((pixels, channels), F32),
            dma((2,)),
        ),
        remote=(1, 3),
        limit=16,
        flops=2 * 10**9,
    )
    upward_other = swap(upward_send, "col", 1)
    framed_back = halo(grad_mixed, first, last, "strips_back")
    per = -(-152 // (16 * row_count)) * 16
    small_half = shape_of(row_count * per, half, dtype=BF)
    small_keep, small_send = run(
        functools.partial(weight_pack_kernel, scale_three, scale_four),
        "block_weights",
        (*framed, grad_mixed, gain_part, layer_part, merge_part, kernel_four_part, gain_four_part),
        (small_half, small_half),
        scratch=(
            frame_scratch(center),
            pltpu.VMEM((height, breadth, channels), F32),
            pltpu.VMEM((row_count * per, channels), F32),
        ),
        limit=12,
    )
    small_other = swap(small_send, "col", 1)
    deep, shallow = hidden_width // row_count, channels // row_count
    groups = hidden_width // channels
    share_half = shape_of(row_count // 2, deep + groups * shallow + per, half, dtype=BF)
    share_keep, share_send = run(
        functools.partial(share_product_kernel, scale_three),
        "share_product",
        (early, early_other, branch_keep, branch_other, upward_keep, upward_other, small_keep, small_other),
        (share_half, share_half),
        limit=16,
        flops=2 * 10**9,
    )
    (input_grad,) = run(
        input_kernel,
        "input_grad",
        (*framed_back, kernel_three, grad_summed),
        (shape_of(height, breadth, channels, dtype=BF),),
        scratch=(frame_scratch(center), pltpu.VMEM((height, breadth, channels), F32)),
        limit=12,
    )

    row_bits, col_bits = axis_bits("row"), axis_bits("col")
    patch_sum = patch_keep + swap(patch_send, "col", 2)
    patch_sum = scatter(patch_sum, "col", col_bits[2:])
    patch_sum = scatter(patch_sum.reshape(row_count, -1, block), "row", row_bits)
    share = share_keep + swap(share_send, "row", 1)
    share = scatter(share, "row", row_bits[1:])
    for bit in col_bits[1:]:
        share = share + swap(share, "col", bit)

    patch_sum = gather(patch_sum, "col", col_bits)
    patch_grad = patch_sum.transpose(1, 0, 2).reshape(-1, wide).astype(F32)
    share = gather(share, "col", col_bits[:1])
    project_grad = share[:, :deep].transpose(1, 0, 2).reshape(deep, channels).astype(F32)
    expand_grad = share[:, deep : deep + groups * shallow].reshape(2 * groups, shallow, half)
    expand_grad = expand_grad.transpose(1, 0, 2).reshape(shallow, hidden_width).astype(F32)
    small = share[:, deep + groups * shallow :].transpose(1, 0, 2).reshape(per, channels)
    small = gather(small, "row", row_bits).reshape(row_count * per, channels).astype(F32)
    wide_rows = small[52:150].reshape(2, 49, channels).transpose(1, 0, 2).reshape(7, 7, wide)
    return (
        input_grad[None],
        small[:49].reshape(7, 7, channels),
        small[49],
        expand_grad,
        project_grad,
        small[50],
        small[51],
        patch_grad,
        wide_rows,
        small[150:152].reshape(wide),
    )


def solution(mesh):
    pixels = P(None, "row", "col", None)
    return jax.shard_map(
        body,
        mesh=mesh,
        in_specs=(pixels,) + (P(),) * 9 + (pixels, pixels),
        out_specs=(pixels, P(), P(), P("row", None), P("row", None), P(), P(), P("row", None), P(), P()),
        check_vma=False,
    )
```

```python
import functools
import math

import jax
import jax.numpy as jnp
from jax import lax
from jax.experimental import pallas as pl
from jax.experimental.pallas import tpu as pltpu
from jax.sharding import PartitionSpec as P

EPSILON = 1e-06
BF = jnp.bfloat16
F32 = jnp.float32
MIB = 1 << 20
PAD = 8
CHUNK = 256


def shape_of(*dims, dtype=F32):
    return jax.ShapeDtypeStruct(dims, dtype)


def run(kernel, name, args, outs, scratch=(), spaces=None, after=(), aliases=None, limit=24, us=1.0):
    spaces = spaces or {}
    count, extra = len(args), len(after)
    moved = sum(a.size * a.dtype.itemsize for a in args)
    moved += sum(math.prod(o.shape) * o.dtype.itemsize for o in outs)

    def spec(place):
        return pl.BlockSpec(memory_space=spaces.get(place, pltpu.VMEM))

    def inner(*refs):
        kernel(*refs[:count], *refs[count + extra :])

    return pl.pallas_call(
        inner,
        name=name,
        out_shape=outs,
        in_specs=[spec(i) for i in range(count)] + [pl.BlockSpec(memory_space=pl.ANY)] * extra,
        out_specs=[spec(("out", i)) for i in range(len(outs))],
        scratch_shapes=list(scratch),
        input_output_aliases=aliases or {},
        compiler_params=pltpu.CompilerParams(vmem_limit_bytes=limit * MIB),
        cost_estimate=pl.CostEstimate(flops=int(us * 1.1e9), bytes_accessed=moved, transcendentals=0),
    )(*args, *after)


def swap(values, axis, bit):
    return lax.ppermute(values, axis, [(i, i ^ bit) for i in range(lax.axis_size(axis))])


def axis_bits(axis):
    return [1 << k for k in range((lax.axis_size(axis) - 1).bit_length())]


def own_bit(axis, bit):
    return (lax.axis_index(axis) // bit) % 2


def chain(keep, send, order, count, rows, extra=()):
    for place, (axis, bit, _) in enumerate(order):
        received = swap(send, axis, bit)
        if place + 1 == len(order):
            return keep + received
        axis, bit, position = order[place + 1]
        grown = extra if place == 0 else ()
        count //= 2
        tail = keep.shape[0] - count * rows + (grown[0].shape[0] if grown else 0)
        out = shape_of(count // 2 * rows + tail, keep.shape[1], dtype=BF)
        keep, send = run(
            functools.partial(step_kernel, axis, bit, position, count, rows),
            "sum_step",
            (keep, received, *grown),
            (out, out),
            limit=8,
        )


def step_kernel(axis, bit, position, count, rows, keep, received, *refs):
    *grown, next_keep, next_send = refs
    mine = (lax.axis_index(axis) // bit) % 2
    low = (1 << position) - 1
    for i in range(2):

        @pl.when(mine == i)
        def _():
            for s in range(count):
                span = slice(s * rows, (s + 1) * rows)
                at = ((s >> (position + 1)) << position | (s & low)) * rows
                target = next_keep if (s >> position) & 1 == i else next_send
                target[at : at + rows] = (keep[span].astype(F32) + received[span].astype(F32)).astype(BF)

    tails = []
    if keep.shape[0] > count * rows:
        tails.append(keep[count * rows :].astype(F32) + received[count * rows :].astype(F32))
    if grown:
        tails.append(sum(g[...].astype(F32) for g in grown))
    at = count // 2 * rows
    for tail in tails:
        for target in (next_keep, next_send):
            target[at : at + tail.shape[0]] = tail.astype(BF)
        at += tail.shape[0]


def gather(values, axis, bits):
    values = values[None]
    for bit in reversed(bits):
        other = swap(values, axis, bit)
        mine = own_bit(axis, bit)
        low = jnp.where(mine == 0, values, other)
        high = jnp.where(mine == 0, other, values)
        values = jnp.stack([low, high], axis=1).reshape(-1, *values.shape[1:])
    return values


def neighbours(first, last, axis):
    count = lax.axis_size(axis)
    forward = [(i, i + 1) for i in range(count - 1)]
    backward = [(i + 1, i) for i in range(count - 1)]
    return lax.ppermute(last, axis, forward), lax.ppermute(first, axis, backward)


def strip_kernel(center, top, bottom, first, last):
    height, breadth = center.shape[:2]
    for source, start in ((top, 0), (center, 3), (bottom, 3 + height)):
        values = source[...].astype(F32)
        rows = slice(start, start + source.shape[0])
        first[rows] = values[:, :PAD].astype(BF)
        last[rows] = values[:, breadth - PAD :].astype(BF)


def halo(center, rows, name, after=()):
    height, _, channels = center.shape
    top, bottom = rows
    strip = shape_of(height + 6, PAD, channels, dtype=BF)
    first, last = run(strip_kernel, name, (center, top, bottom), (strip, strip), after=after, limit=8)
    left, right = neighbours(first, last, "col")
    return center, top, bottom, left, right


def fill_frame(frame, parts):
    center, top, bottom, left, right = parts
    height, breadth = center.shape[:2]
    middle = slice(PAD, PAD + breadth)
    frame[0:3, middle] = top[...].astype(F32)
    frame[3 : 3 + height, middle] = center[...].astype(F32)
    frame[3 + height :, middle] = bottom[...].astype(F32)
    frame[:, :PAD] = left[...].astype(F32)
    frame[:, PAD + breadth :] = right[...].astype(F32)


def frame_scratch(center):
    height, breadth, channels = center.shape
    return pltpu.VMEM((height + 6, breadth + 2 * PAD, channels), F32)


def lane_tiles(channels):
    def over(step):
        def wrapped(index, carry):
            step(pl.ds(pl.multiple_of(index * 128, 128), 128))
            return carry

        lax.fori_loop(0, channels // 128, wrapped, 0)

    return over


def convolve(frame, taps, flip, out):
    height, breadth, channels = out.shape

    @lane_tiles(channels)
    def _(lanes):
        for column in range(0, breadth, 8):
            total = jnp.zeros((height, 8, 128), F32)
            for q in range(7):
                rows = frame[:, pl.ds(column + PAD - 3 + q, 8), lanes]
                for p in range(7):
                    a, b = (6 - p, 6 - q) if flip else (p, q)
                    total = total + rows[p : p + height] * taps[a, pl.ds(b, 1), lanes]
            out[:, pl.ds(column, 8), lanes] = total


def weight_sums(frame, grads, scale, out):
    height, breadth, channels = grads.shape

    @lane_tiles(channels)
    def _(lanes):
        for q in range(7):
            totals = [jnp.zeros((8, 128), F32)] * 7
            for column in range(0, breadth, 8):
                rows = frame[:, pl.ds(column + PAD - 3 + q, 8), lanes]
                grad = grads[:, pl.ds(column, 8), lanes]
                for p in range(7):
                    totals[p] = totals[p] + jnp.sum(rows[p : p + height] * grad, axis=0)
            for p in range(7):
                out[pl.ds(7 * p + q, 1), lanes] = scale * jnp.sum(totals[p], axis=0, keepdims=True)


def mean(values):
    return jnp.mean(values, axis=-1, keepdims=True)


def normalize(values):
    level = mean(values)
    inverse = lax.rsqrt(mean(values * values) - level * level + EPSILON)
    return (values - level) * inverse, inverse


def normalize_back(grads, unit_values, inverse):
    return (grads - mean(grads) - unit_values * mean(grads * unit_values)) * inverse


def dot(left, right):
    return jnp.dot(left, right, preferred_element_type=F32)


def dot_last(left, right):
    return lax.dot_general(left, right, (((1,), (1,)), ((), ())), preferred_element_type=F32)


def dot_first(left, right):
    return lax.dot_general(left, right, (((0,), (0,)), ((), ())), preferred_element_type=F32)


def over_rows(count, size):
    def over(step):
        def wrapped(index, carry):
            step(index, pl.ds(pl.multiple_of(index * size, size), size))
            return carry

        lax.fori_loop(0, count, wrapped, 0)

    return over


def fetch(sources, targets, semaphores):
    copies = [
        pltpu.make_async_copy(source, target, semaphores.at[i])
        for i, (source, target) in enumerate(zip(sources, targets))
    ]
    for copy in copies:
        copy.start()
    return copies


def load_kernel(center, taps, gain, layer, merge, *refs):
    *outs, semaphores = refs
    height = center.shape[0]
    sources = (center.at[pl.ds(0, 3)], center.at[pl.ds(height - 3, 3)], center, taps, gain, layer, merge)
    for copy in fetch(sources, outs, semaphores):
        copy.wait()


def front_kernel(
    center, top, bottom, left, right, taps, gain, layer_scale, merge_gain,
    expand, project, patch, wide_taps, wide_gain, cotangent, residual,
    early, unit_mixed, inverse_mixed, slope, branch, unit_summed, inverse_summed, section, first, last,
    expand_here, project_here, patch_here, wide_taps_here, wide_gain_here, cotangent_here, residual_here,
    frame, image, pairs, upward, semaphores,
):
    height, breadth, channels = center.shape
    hidden_width = expand.shape[1]
    pixels = height * breadth
    copies = fetch(
        (expand, project, patch, wide_taps, wide_gain, cotangent, residual),
        (expand_here, project_here, patch_here, wide_taps_here, wide_gain_here, cotangent_here, residual_here),
        semaphores,
    )
    fill_frame(frame, (center, top, bottom, left, right))
    convolve(frame, taps, False, image)
    at_normed = slice(hidden_width, hidden_width + channels)
    at_patches = slice(hidden_width + channels, hidden_width + 2 * channels)

    @over_rows(height, breadth)
    def _(y, rows):
        unit, inverse = normalize(image[y])
        unit_mixed[rows] = unit
        inverse_mixed[rows] = inverse
        early[rows, at_normed] = (unit * gain[...]).astype(BF)

    copies[0].wait()

    def chunk(index, carry):
        lanes = pl.ds(pl.multiple_of(index * CHUNK, CHUNK), CHUNK)
        upward[...] = dot(early[:, at_normed], expand_here[:, lanes])
        for start in range(0, pixels, 64):
            rows = slice(start, start + 64)
            value = upward[rows]
            cumulative = 0.5 + 0.5 * lax.erf(value * (1.0 / math.sqrt(2.0)))
            density = jnp.exp(-0.5 * value * value) * (1.0 / math.sqrt(2.0 * math.pi))
            early[rows, lanes] = (value * cumulative).astype(BF)
            slope[rows, lanes] = (cumulative + value * density).astype(BF)
        return carry

    lax.fori_loop(0, hidden_width // CHUNK, chunk, 0)
    copies[1].wait()
    branch[...] = dot(early[:, :hidden_width], project_here[...])

    @over_rows(height, breadth)
    def _(y, rows):
        summed = center[y].astype(F32) + layer_scale[...] * branch[rows]
        unit, inverse = normalize(summed)
        unit_summed[rows] = unit
        inverse_summed[rows] = inverse
        merged = unit * merge_gain[...]
        for k in range(channels // 128):
            pairs[k, y] = merged[:, k * 128 : (k + 1) * 128]

    quarter = pixels // 4
    for dy in range(2):
        for dx in range(2):
            j = 2 * dy + dx
            for y in range(height // 2):
                start = j * quarter + y * (breadth // 2)
                for k in range(channels // 128):
                    piece = pairs[k, 2 * y + dy, pl.ds(dx, breadth // 2, stride=2), :]
                    lane = hidden_width + channels + k * 128
                    early[start : start + breadth // 2, lane : lane + 128] = piece.astype(BF)
    copies[2].wait()
    total = dot(early[:quarter, at_patches], patch_here[:channels])
    for j in range(1, 4):
        total = total + dot(
            early[j * quarter : (j + 1) * quarter, at_patches],
            patch_here[j * channels : (j + 1) * channels],
        )
    total = total.reshape(section.shape)
    section[...] = total.astype(BF)
    first[...] = total[:3].astype(BF)
    last[...] = total[height // 2 - 3 :].astype(BF)
    for copy in copies[3:]:
        copy.wait()


def mixer_kernel(
    center, top, bottom, left, right, taps, gain, cotangent,
    grad, grad_half, first, last, gain_part,
    frame, image,
):
    height, breadth, channels = center.shape
    fill_frame(frame, (center, top, bottom, left, right))
    convolve(frame, taps, False, image)
    part = jnp.zeros((1, channels), F32)
    for y in range(height):
        unit, inverse = normalize(image[y])
        cot = cotangent[y].astype(F32)
        part = part + jnp.sum(cot * unit, axis=0, keepdims=True)
        value = normalize_back(cot * gain[...], unit, inverse)
        grad[y] = value
        narrow = value.astype(BF)
        grad_half[y] = narrow
        if y < 3:
            first[y] = narrow
        if y >= height - 3:
            last[y - (height - 3)] = narrow
    gain_part[...] = part


def weight_kernel(scale, center, top, bottom, left, right, grads, _, out, __, frame):
    fill_frame(frame, (center, top, bottom, left, right))
    weight_sums(frame, grads, scale, out)


def split_halves(values, start, keep, send):
    half = values.shape[1] // 2
    rows = slice(start, start + values.shape[0])
    core = lax.axis_index("col") % 2
    for i in range(2):

        @pl.when(core == i)
        def _():
            keep[rows] = values[:, i * half : (i + 1) * half]
            send[rows] = values[:, (1 - i) * half : (2 - i) * half]


def weight_pack_kernel(
    scale, center, top, bottom, left, right, grads, gain_part,
    keep, send, frame, wide_grads, packed,
):
    fill_frame(frame, (center, top, bottom, left, right))
    wide_grads[...] = grads[...].astype(F32)
    packed[...] = jnp.zeros(packed.shape, F32)
    weight_sums(frame, wide_grads, scale, packed)
    packed[49:50] = scale * gain_part[...]
    split_halves(packed[...].astype(BF), 0, keep, send)


def section_kernel(
    center, top, bottom, left, right, taps, residual,
    flat, keep, send,
    frame, image,
):
    height, breadth, channels = center.shape
    fill_frame(frame, (center, top, bottom, left, right))
    convolve(frame, taps, True, image)
    value = (image[...] + residual[...].astype(F32)).reshape(flat.shape).astype(BF)
    flat[...] = value
    blocks, _, width = keep.shape
    core = lax.axis_index("col") % 2
    for i in range(2):

        @pl.when(core == i)
        def _():
            for m in range(blocks):
                mine, other = (2 * m + i) * width, (2 * m + 1 - i) * width
                keep[m] = value[:, mine : mine + width]
                send[m] = value[:, other : other + width]


def merge_kernel(
    scale, scale_wide,
    flat, patch, unit_summed, inverse_summed, merge_gain, branch, layer_scale, wide_part, wide_gain,
    grad_summed, grad_branch, keep, send,
    pairs, packed, sums,
):
    tiles, height, breadth, _ = pairs.shape
    channels = 128 * tiles
    value = flat[...]
    for dy in range(2):
        for dx in range(2):
            j = 2 * dy + dx
            part = dot_last(value, patch[j * channels : (j + 1) * channels])
            part = part.reshape(height // 2, breadth // 2, channels)
            for y in range(height // 2):
                for k in range(tiles):
                    piece = part[y, :, k * 128 : (k + 1) * 128]
                    pairs[k, 2 * y + dy, pl.ds(dx, breadth // 2, stride=2), :] = piece
    sums[...] = jnp.zeros(sums.shape, F32)

    @over_rows(height, breadth)
    def _(y, rows):
        merged = jnp.concatenate([pairs[k, y] for k in range(tiles)], axis=1)
        unit = unit_summed[rows]
        sums[0:1] += jnp.sum(merged * unit, axis=0, keepdims=True)
        grad = normalize_back(merged * merge_gain[...], unit, inverse_summed[rows])
        grad_summed[rows] = grad
        sums[1:2] += jnp.sum(grad * branch[rows], axis=0, keepdims=True)
        grad_branch[rows] = (layer_scale[...] * grad).astype(BF)

    split_halves(grad_branch[...], 0, keep, send)
    packed[...] = jnp.zeros(packed.shape, F32)
    for i in range(2):
        columns = slice(i * channels, (i + 1) * channels)
        packed[49 * i : 49 + 49 * i] = wide_part[:, columns]
        packed[98 + i : 99 + i] = scale_wide * wide_gain[:, columns]
        packed[100 + i : 101 + i] = scale * sums[i : i + 1]
    split_halves(packed[...].astype(BF), grad_branch.shape[0], keep, send)


def back_kernel(
    grad_branch, project, slope, expand, unit_mixed, inverse_mixed, gain,
    keep, send, grad_mixed, first, last, gain_part,
    hidden, upward, normed,
):
    height, breadth, channels = grad_mixed.shape
    pixels, hidden_width = slope.shape

    def chunk(index, carry):
        span = pl.ds(pl.multiple_of(index * CHUNK, CHUNK), CHUNK)
        hidden[...] = dot_last(grad_branch[...], project[span])
        for start in range(0, pixels, 64):
            rows = slice(start, start + 64)
            upward[rows, span] = (hidden[rows] * slope[rows, span].astype(F32)).astype(BF)
        return carry

    lax.fori_loop(0, hidden_width // CHUNK, chunk, 0)
    normed[...] = dot_last(upward[...], expand[...])
    split_halves(upward[...], 0, keep, send)
    part = jnp.zeros((1, channels), F32)
    for y in range(height):
        rows = slice(y * breadth, (y + 1) * breadth)
        value = normed[rows]
        unit = unit_mixed[rows]
        part = part + jnp.sum(value * unit, axis=0, keepdims=True)
        narrow = normalize_back(value * gain[...], unit, inverse_mixed[rows]).astype(BF)
        grad_mixed[y] = narrow
        if y < 3:
            first[y] = narrow
        if y >= height - 3:
            last[y - (height - 3)] = narrow
    gain_part[...] = part


def patch_product_kernel(factor, early, early_other, own, other, keep, send):
    blocks, quarter, _ = own.shape
    rows = keep.shape[0] // max(blocks // 2, 1)
    channels = rows // 4
    at_patches = early.shape[1] - channels
    bit = (lax.axis_index("col") // 2) % 2
    for j in range(4):
        span = slice(j * quarter, (j + 1) * quarter)
        left = jnp.concatenate([early[span, at_patches:], early_other[span, at_patches:]], axis=0)
        for m in range(blocks):
            right = jnp.concatenate([own[m], other[m]], axis=0)
            value = (factor * dot_first(left, right)).astype(BF)
            at = m // 2 * rows + j * channels
            for i in range(2):

                @pl.when(bit == i)
                def _():
                    target = keep if m % 2 == i else send
                    target[at : at + channels] = value


def store_slices(value, begin, offset, rows, pitch, keep, send):
    bit = lax.axis_index("row") % 2
    for i in range(2):

        @pl.when(bit == i)
        def _():
            for k in range(value.shape[0] // rows):
                r = begin + k
                target = keep if r % 2 == i else send
                at = r // 2 * pitch + offset
                target[at : at + rows] = value[k * rows : (k + 1) * rows]


def project_product_kernel(factor, slices, early, early_other, own, other, keep, send):
    width = keep.shape[1]
    hidden_width = early.shape[1] - 4 * width
    pixels = early.shape[0]
    deep = hidden_width // slices
    right = jnp.concatenate([own[:pixels], other[:pixels]], axis=0)
    step = max(CHUNK, deep)
    for start in range(0, hidden_width, step):
        columns = slice(start, start + step)
        left = jnp.concatenate([early[:, columns], early_other[:, columns]], axis=0)
        value = (factor * dot_first(left, right)).astype(BF)
        store_slices(value, start // deep, 0, deep, deep, keep, send)
    tail = (own[pixels:].astype(F32) + other[pixels:].astype(F32)).astype(BF)
    at = slices // 2 * deep
    keep[at:] = tail
    send[at:] = tail


def expand_product_kernel(factor, slices, early, early_other, own, other, keep, send):
    width = keep.shape[1]
    channels = 2 * width
    hidden_width = early.shape[1] - 2 * channels
    shallow = channels // slices
    blocks = own.shape[1] // width
    columns = slice(hidden_width, hidden_width + channels)
    left = jnp.concatenate([early[:, columns], early_other[:, columns]], axis=0)
    for k in range(blocks):
        columns = slice(k * width, (k + 1) * width)
        right = jnp.concatenate([own[:, columns], other[:, columns]], axis=0)
        value = (factor * dot_first(left, right)).astype(BF)
        store_slices(value, 0, k * shallow, shallow, blocks * shallow, keep, send)


def finish_patch_kernel(own, other, out):
    blocks, _, width = own.shape
    core = lax.axis_index("col") % 2
    for i in range(2):

        @pl.when(core == i)
        def _():
            for m in range(blocks):
                a, b = (2 * m + i) * width, (2 * m + 1 - i) * width
                out[:, a : a + width] = own[m].astype(F32)
                out[:, b : b + width] = other[m].astype(F32)


def join_halves(own, other, start, out):
    half = own.shape[1]
    rows = slice(start, start + out.shape[0])
    core = lax.axis_index("col") % 2
    for i in range(2):

        @pl.when(core == i)
        def _():
            out[:, i * half : (i + 1) * half] = own[rows].astype(F32)
            out[:, (1 - i) * half : (2 - i) * half] = other[rows].astype(F32)


def finish_project_kernel(own, other, project, wide_taps, wide_gain, merge, layer, small):
    deep, channels = project.shape
    join_halves(own, other, 0, project)
    join_halves(own, other, deep, small)
    for i in range(2):
        columns = slice(i * channels, (i + 1) * channels)
        for p in range(7):
            start = 49 * i + 7 * p
            wide_taps[p, :, columns] = small[start : start + 7]
        wide_gain[:, columns] = small[98 + i : 99 + i]
    merge[...] = small[100:101]
    layer[...] = small[101:102]


def finish_expand_kernel(own, other, expand, taps, gain, small):
    shallow, hidden_width = expand.shape
    width = own.shape[1]
    blocks = hidden_width // (2 * width)
    core = lax.axis_index("col") % 2
    for i in range(2):

        @pl.when(core == i)
        def _():
            for k in range(blocks):
                rows = slice(k * shallow, (k + 1) * shallow)
                a, b = (i * blocks + k) * width, ((1 - i) * blocks + k) * width
                expand[:, a : a + width] = own[rows].astype(F32)
                expand[:, b : b + width] = other[rows].astype(F32)

    join_halves(own, other, blocks * shallow, small)
    for p in range(7):
        taps[p] = small[7 * p : 7 * p + 7]
    gain[...] = small[49:50]


def input_kernel(center, top, bottom, left, right, taps, grad_summed, out, frame, image):
    fill_frame(frame, (center, top, bottom, left, right))
    convolve(frame, taps, True, image)
    out[...] = (image[...] + grad_summed[...].reshape(image.shape)).astype(BF)


def body(
    block_input,
    kernel_three,
    gain_three,
    expand_weight,
    project_weight,
    layer_scale,
    merge_gain,
    patch_weight,
    kernel_four,
    gain_four,
    normed_cotangent,
    residual_cotangent,
):
    _, height, breadth, channels = block_input.shape
    hidden_width = expand_weight.shape[1]
    wide = patch_weight.shape[1]
    pixels = height * breadth
    quarter = pixels // 4
    rows4, cols4 = height // 2, breadth // 2
    row_count = lax.axis_size("row")
    col_count = lax.axis_size("col")
    scale_three = 1.0 / math.sqrt(pixels * row_count * col_count)
    scale_four = 1.0 / math.sqrt(quarter * row_count * col_count)
    center = block_input[0]
    gain_three, layer_scale, merge_gain, gain_four = (
        v[None] for v in (gain_three, layer_scale, merge_gain, gain_four)
    )
    dma = pltpu.SemaphoreType.DMA
    half = channels // 2
    hbm = pltpu.HBM

    def like(array):
        return shape_of(*array.shape, dtype=array.dtype)

    edge = shape_of(3, breadth, channels, dtype=BF)
    inputs = (center, kernel_three, gain_three, layer_scale, merge_gain)
    first, last, *inputs = run(
        load_kernel,
        "load",
        inputs,
        (edge, edge, *map(like, inputs)),
        scratch=(dma((7,)),),
        spaces=dict.fromkeys(range(5), hbm),
        limit=4,
        us=2,
    )
    center, taps_three, gain_three, layer_scale, merge_gain = inputs
    framed = halo(center, neighbours(first, last, "row"), "strips_input")
    inputs = (
        expand_weight, project_weight, patch_weight, kernel_four, gain_four,
        normed_cotangent[0], residual_cotangent[0],
    )
    edge_four = shape_of(3, cols4, wide, dtype=BF)
    (
        early, unit_mixed, inverse_mixed, slope, branch, unit_summed, inverse_summed,
        section, first, last,
        expand_weight, project_weight, patch_weight, taps_four, gain_four, cotangent, residual,
    ) = run(
        front_kernel,
        "front",
        (*framed, taps_three, gain_three, layer_scale, merge_gain, *inputs),
        (
            shape_of(pixels, hidden_width + 2 * channels, dtype=BF),
            shape_of(pixels, channels),
            shape_of(pixels, 1),
            shape_of(pixels, hidden_width, dtype=BF),
            shape_of(pixels, channels),
            shape_of(pixels, channels),
            shape_of(pixels, 1),
            shape_of(rows4, cols4, wide, dtype=BF),
            edge_four,
            edge_four,
            *map(like, inputs),
        ),
        scratch=(
            frame_scratch(center),
            pltpu.VMEM((height, breadth, channels), F32),
            pltpu.VMEM((channels // 128, height, breadth, 128), F32),
            pltpu.VMEM((pixels, CHUNK), F32),
            dma((7,)),
        ),
        spaces=dict.fromkeys(range(9, 16), hbm),
        limit=28,
        us=12,
    )

    framed_four = halo(section, neighbours(first, last, "row"), "strips_section")
    mixer_image = pltpu.VMEM((rows4, cols4, wide), F32)
    grad_four, grad_four_half, first, last, gain_four_part = run(
        mixer_kernel,
        "mixer",
        (*framed_four, taps_four, gain_four, cotangent),
        (
            shape_of(rows4, cols4, wide),
            shape_of(rows4, cols4, wide, dtype=BF),
            edge_four,
            edge_four,
            shape_of(1, wide),
        ),
        scratch=(frame_scratch(section), mixer_image),
        limit=12,
        us=3,
    )
    rows_grad = neighbours(first, last, "row")
    kernel_four_part, early = run(
        functools.partial(weight_kernel, scale_four),
        "mixer_weights",
        (*framed_four, grad_four, early),
        (shape_of(49, wide), like(early)),
        scratch=(frame_scratch(section),),
        spaces={6: pl.ANY, ("out", 1): pl.ANY},
        aliases={6: 1},
        limit=12,
        us=3,
    )
    framed_grad = halo(grad_four_half, rows_grad, "strips_mixer", after=(kernel_four_part,))
    early_other = swap(early, "col", 1)
    block_count = col_count // 2
    block = wide // col_count
    blocked = shape_of(block_count, quarter, block, dtype=BF)
    flat, flat_keep, flat_send = run(
        section_kernel,
        "section_grad",
        (*framed_grad, taps_four, residual),
        (shape_of(quarter, wide, dtype=BF), blocked, blocked),
        scratch=(frame_scratch(section), mixer_image),
        limit=12,
        us=3,
    )

    flat_other = swap(flat_send, "col", 1)
    split = shape_of(pixels + 112, half, dtype=BF)
    grad_summed, grad_branch, branch_keep, branch_send = run(
        functools.partial(merge_kernel, scale_three, scale_four),
        "merge_back",
        (
            flat, patch_weight, unit_summed, inverse_summed, merge_gain, branch, layer_scale,
            kernel_four_part, gain_four_part,
        ),
        (shape_of(pixels, channels), shape_of(pixels, channels, dtype=BF), split, split),
        scratch=(
            pltpu.VMEM((channels // 128, height, breadth, 128), F32),
            pltpu.VMEM((112, channels), F32),
            pltpu.VMEM((8, channels), F32),
        ),
        limit=16,
        us=3,
    )
    branch_other = swap(branch_send, "col", 1)
    patch_half = shape_of(block_count // 2 * 4 * channels, block, dtype=BF)
    patch_keep, patch_send = run(
        functools.partial(patch_product_kernel, scale_four),
        "patch_product",
        (early, early_other, flat_keep, flat_other),
        (patch_half, patch_half),
        limit=16,
        us=3,
    )
    deep, shallow = hidden_width // row_count, channels // row_count
    groups = hidden_width // channels
    project_half = shape_of(row_count // 2 * deep + 112, half, dtype=BF)
    project_keep, project_send = run(
        functools.partial(project_product_kernel, scale_three, row_count),
        "project_product",
        (early, early_other, branch_keep, branch_other),
        (project_half, project_half),
        after=(patch_send,),
        limit=16,
        us=3,
    )
    upward_half = shape_of(pixels, hidden_width // 2, dtype=BF)
    upward_keep, upward_send, grad_mixed, first, last, gain_part = run(
        back_kernel,
        "mlp_back",
        (grad_branch, project_weight, slope, expand_weight, unit_mixed, inverse_mixed, gain_three),
        (
            upward_half,
            upward_half,
            shape_of(height, breadth, channels, dtype=BF),
            edge,
            edge,
            shape_of(1, channels),
        ),
        scratch=(
            pltpu.VMEM((pixels, CHUNK), F32),
            pltpu.VMEM((pixels, hidden_width), BF),
            pltpu.VMEM((pixels, channels), F32),
        ),
        after=(project_send,),
        limit=16,
        us=4,
    )
    rows_back = neighbours(first, last, "row")
    upward_other = swap(upward_send, "col", 1)
    expand_half = shape_of(row_count // 2 * groups * shallow, half, dtype=BF)
    expand_keep, expand_send = run(
        functools.partial(expand_product_kernel, scale_three, row_count),
        "expand_product",
        (early, early_other, upward_keep, upward_other),
        (expand_half, expand_half),
        limit=16,
        us=3,
    )
    framed_back = halo(grad_mixed, rows_back, "strips_back", after=(expand_send,))
    small_half = shape_of(64, half, dtype=BF)
    small_keep, small_send = run(
        functools.partial(weight_pack_kernel, scale_three),
        "block_weights",
        (*framed, grad_mixed, gain_part),
        (small_half, small_half),
        scratch=(
            frame_scratch(center),
            pltpu.VMEM((height, breadth, channels), F32),
            pltpu.VMEM((64, channels), F32),
        ),
        after=framed_back[1:3],
        limit=12,
        us=5,
    )
    (input_grad,) = run(
        input_kernel,
        "input_grad",
        (*framed_back, taps_three, grad_summed),
        (shape_of(height, breadth, channels, dtype=BF),),
        scratch=(frame_scratch(center), pltpu.VMEM((height, breadth, channels), F32)),
        after=(small_keep,),
        limit=12,
        us=5,
    )

    row_bits, col_bits = axis_bits("row"), axis_bits("col")
    outer = len(row_bits)
    low_first = [("row", bit, 0) for bit in row_bits]
    patch_order = [("col", bit, outer) for bit in col_bits[1:]]
    patch_order += [("row", bit, 1) for bit in row_bits[1:]] + [("row", 1, 0)]
    patch_sum = chain(patch_keep, patch_send, patch_order, block_count * row_count, 4 * channels // row_count)
    patch_sum = gather(patch_sum, "col", col_bits[1:])
    (patch_grad,) = run(
        finish_patch_kernel,
        "finish_patch",
        (patch_sum, swap(patch_sum, "col", 1)),
        (shape_of(4 * channels // row_count, wide),),
        limit=8,
    )

    def share(keep, send, rows, extra=()):
        total = chain(keep, send, low_first, row_count, rows, extra)
        for bit in col_bits[1:]:
            total = total + swap(total, "col", bit)
        return total, swap(total, "col", 1)

    vector, wide_vector = shape_of(1, channels), shape_of(1, wide)
    project_grad, wide_taps, wide_gain, merge_sum, layer_sum = run(
        finish_project_kernel,
        "finish_project",
        share(project_keep, project_send, deep),
        (shape_of(deep, channels), shape_of(7, 7, wide), wide_vector, vector, vector),
        scratch=(pltpu.VMEM((112, channels), F32),),
        limit=8,
    )
    small = small_keep + swap(small_send, "col", 1)
    expand_grad, taps_sum, gain_sum = run(
        finish_expand_kernel,
        "finish_expand",
        share(expand_keep, expand_send, groups * shallow, (small, swap(small, "row", 1))),
        (shape_of(shallow, hidden_width), shape_of(7, 7, channels), vector),
        scratch=(pltpu.VMEM((64, channels), F32),),
        limit=8,
    )
    return (
        input_grad[None],
        taps_sum,
        gain_sum[0],
        expand_grad,
        project_grad,
        layer_sum[0],
        merge_sum[0],
        patch_grad,
        wide_taps,
        wide_gain[0],
    )


def solution(mesh):
    pixels = P(None, "row", "col", None)
    return jax.shard_map(
        body,
        mesh=mesh,
        in_specs=(pixels,) + (P(),) * 9 + (pixels, pixels),
        out_specs=(pixels, P(), P(), P("row", None), P("row", None), P(), P(), P("row", None), P(), P()),
        check_vma=False,
    )
```

```python
import functools
import math

import jax
import jax.numpy as jnp
from jax import lax
from jax.experimental import pallas as pl
from jax.experimental.pallas import tpu as pltpu
from jax.sharding import PartitionSpec as P

EPSILON = 1e-06
BF = jnp.bfloat16
F32 = jnp.float32
MIB = 1 << 20
PAD = 8
CHUNK = 256


def shape_of(*dims, dtype=F32):
    return jax.ShapeDtypeStruct(dims, dtype)


def run(kernel, name, args, outs, scratch=(), spaces=None, after=(), aliases=None, limit=24, us=1.0):
    spaces = spaces or {}
    count, extra = len(args), len(after)
    moved = sum(a.size * a.dtype.itemsize for a in args)
    moved += sum(math.prod(o.shape) * o.dtype.itemsize for o in outs)

    def spec(place):
        return pl.BlockSpec(memory_space=spaces.get(place, pltpu.VMEM))

    def inner(*refs):
        kernel(*refs[:count], *refs[count + extra :])

    return pl.pallas_call(
        inner,
        name=name,
        out_shape=outs,
        in_specs=[spec(i) for i in range(count)] + [pl.BlockSpec(memory_space=pl.ANY)] * extra,
        out_specs=[spec(("out", i)) for i in range(len(outs))],
        scratch_shapes=list(scratch),
        input_output_aliases=aliases or {},
        compiler_params=pltpu.CompilerParams(vmem_limit_bytes=limit * MIB),
        cost_estimate=pl.CostEstimate(flops=int(us * 1.1e9), bytes_accessed=moved, transcendentals=0),
    )(*args, *after)


def swap(values, axis, bit):
    return lax.ppermute(values, axis, [(i, i ^ bit) for i in range(lax.axis_size(axis))])


def axis_bits(axis):
    return [1 << k for k in range((lax.axis_size(axis) - 1).bit_length())]


def own_bit(axis, bit):
    return (lax.axis_index(axis) // bit) % 2


def chain(keep, send, order, count, rows, extra=(), after=()):
    for place, (axis, bit, _) in enumerate(order):
        received = swap(send, axis, bit)
        if place + 1 == len(order):
            return keep + received
        axis, bit, position = order[place + 1]
        grown = extra if place == 0 else ()
        count //= 2
        tail = keep.shape[0] - count * rows + (grown[0].shape[0] if grown else 0)
        out = shape_of(count // 2 * rows + tail, keep.shape[1], dtype=BF)
        keep, send = run(
            functools.partial(step_kernel, axis, bit, position, count, rows),
            "sum_step",
            (keep, received, *grown),
            (out, out),
            after=after if place == 0 else (),
            limit=8,
        )


def step_kernel(axis, bit, position, count, rows, keep, received, *refs):
    *grown, next_keep, next_send = refs
    mine = (lax.axis_index(axis) // bit) % 2
    low = (1 << position) - 1
    for i in range(2):

        @pl.when(mine == i)
        def _():
            for s in range(count):
                span = slice(s * rows, (s + 1) * rows)
                at = ((s >> (position + 1)) << position | (s & low)) * rows
                target = next_keep if (s >> position) & 1 == i else next_send
                target[at : at + rows] = (keep[span].astype(F32) + received[span].astype(F32)).astype(BF)

    tails = []
    if keep.shape[0] > count * rows:
        tails.append(keep[count * rows :].astype(F32) + received[count * rows :].astype(F32))
    if grown:
        tails.append(sum(g[...].astype(F32) for g in grown))
    at = count // 2 * rows
    for tail in tails:
        for target in (next_keep, next_send):
            target[at : at + tail.shape[0]] = tail.astype(BF)
        at += tail.shape[0]


def gather(values, axis, bits):
    values = values[None]
    for bit in reversed(bits):
        other = swap(values, axis, bit)
        mine = own_bit(axis, bit)
        low = jnp.where(mine == 0, values, other)
        high = jnp.where(mine == 0, other, values)
        values = jnp.stack([low, high], axis=1).reshape(-1, *values.shape[1:])
    return values


def neighbours(first, last, axis):
    count = lax.axis_size(axis)
    forward = [(i, i + 1) for i in range(count - 1)]
    backward = [(i + 1, i) for i in range(count - 1)]
    return lax.ppermute(last, axis, forward), lax.ppermute(first, axis, backward)


def strip_kernel(center, top, bottom, first, last):
    height, breadth = center.shape[:2]
    for source, start in ((top, 0), (center, 3), (bottom, 3 + height)):
        values = source[...].astype(F32)
        rows = slice(start, start + source.shape[0])
        first[rows] = values[:, :PAD].astype(BF)
        last[rows] = values[:, breadth - PAD :].astype(BF)


def halo(center, rows, name, after=()):
    height, _, channels = center.shape
    top, bottom = rows
    strip = shape_of(height + 6, PAD, channels, dtype=BF)
    first, last = run(strip_kernel, name, (center, top, bottom), (strip, strip), after=after, limit=8)
    left, right = neighbours(first, last, "col")
    return center, top, bottom, left, right


def hold(kernel, name, args, outs, carried, **options):
    count = len(args)

    def inner(*refs):
        kernel(*refs[:count], *refs[count + 1 : count + 1 + len(outs)], *refs[count + 2 + len(outs) :])

    return run(
        inner,
        name,
        (*args, carried),
        (*outs, shape_of(*carried.shape, dtype=carried.dtype)),
        spaces={count: pl.ANY, ("out", len(outs)): pl.ANY},
        aliases={count: len(outs)},
        **options,
    )


def fill_frame(frame, parts):
    center, top, bottom, left, right = parts
    height, breadth = center.shape[:2]
    middle = slice(PAD, PAD + breadth)
    frame[0:3, middle] = top[...].astype(F32)
    frame[3 : 3 + height, middle] = center[...].astype(F32)
    frame[3 + height :, middle] = bottom[...].astype(F32)
    frame[:, :PAD] = left[...].astype(F32)
    frame[:, PAD + breadth :] = right[...].astype(F32)


def frame_scratch(center):
    height, breadth, channels = center.shape
    return pltpu.VMEM((height + 6, breadth + 2 * PAD, channels), F32)


def lane_tiles(channels):
    def over(step):
        def wrapped(index, carry):
            step(pl.ds(pl.multiple_of(index * 128, 128), 128))
            return carry

        lax.fori_loop(0, channels // 128, wrapped, 0)

    return over


def convolve(frame, taps, flip, out):
    height, breadth, channels = out.shape

    @lane_tiles(channels)
    def _(lanes):
        for column in range(0, breadth, 8):
            total = jnp.zeros((height, 8, 128), F32)
            for q in range(7):
                rows = frame[:, pl.ds(column + PAD - 3 + q, 8), lanes]
                for p in range(7):
                    a, b = (6 - p, 6 - q) if flip else (p, q)
                    total = total + rows[p : p + height] * taps[a, pl.ds(b, 1), lanes]
            out[:, pl.ds(column, 8), lanes] = total


def weight_sums(frame, grads, scale, out):
    height, breadth, channels = grads.shape

    @lane_tiles(channels)
    def _(lanes):
        for q in range(7):
            totals = [jnp.zeros((8, 128), F32)] * 7
            for column in range(0, breadth, 8):
                rows = frame[:, pl.ds(column + PAD - 3 + q, 8), lanes]
                grad = grads[:, pl.ds(column, 8), lanes]
                for p in range(7):
                    totals[p] = totals[p] + jnp.sum(rows[p : p + height] * grad, axis=0)
            for p in range(7):
                out[pl.ds(7 * p + q, 1), lanes] = scale * jnp.sum(totals[p], axis=0, keepdims=True)


def mean(values):
    return jnp.mean(values, axis=-1, keepdims=True)


def normalize(values):
    level = mean(values)
    inverse = lax.rsqrt(mean(values * values) - level * level + EPSILON)
    return (values - level) * inverse, inverse


def normalize_back(grads, unit_values, inverse):
    return (grads - mean(grads) - unit_values * mean(grads * unit_values)) * inverse


def dot(left, right):
    return jnp.dot(left, right, preferred_element_type=F32)


def dot_last(left, right):
    return lax.dot_general(left, right, (((1,), (1,)), ((), ())), preferred_element_type=F32)


def dot_first(left, right):
    return lax.dot_general(left, right, (((0,), (0,)), ((), ())), preferred_element_type=F32)


def over_rows(count, size):
    def over(step):
        def wrapped(index, carry):
            step(index, pl.ds(pl.multiple_of(index * size, size), size))
            return carry

        lax.fori_loop(0, count, wrapped, 0)

    return over


def fetch(sources, targets, semaphores):
    copies = [
        pltpu.make_async_copy(source, target, semaphores.at[i])
        for i, (source, target) in enumerate(zip(sources, targets))
    ]
    for copy in copies:
        copy.start()
    return copies


def load_kernel(*refs):
    *arrays, semaphores = refs
    count = len(arrays) // 2
    for copy in fetch(arrays[:count], arrays[count:], semaphores):
        copy.wait()


def front_kernel(
    center, top, bottom, left, right, taps, gain, layer_scale, merge_gain,
    expand, project, patch, wide_taps, wide_gain, cotangent, residual,
    early, unit_mixed, inverse_mixed, slope, branch, unit_summed, inverse_summed, section, first, last,
    expand_here, project_here, patch_here, wide_taps_here, wide_gain_here, cotangent_here, residual_here,
    frame, image, pairs, upward, semaphores,
):
    height, breadth, channels = center.shape
    hidden_width = expand.shape[1]
    pixels = height * breadth
    copies = fetch(
        (expand, project, patch, wide_taps, wide_gain, cotangent, residual),
        (expand_here, project_here, patch_here, wide_taps_here, wide_gain_here, cotangent_here, residual_here),
        semaphores,
    )
    fill_frame(frame, (center, top, bottom, left, right))
    convolve(frame, taps, False, image)
    at_normed = slice(hidden_width, hidden_width + channels)
    at_patches = slice(hidden_width + channels, hidden_width + 2 * channels)

    @over_rows(height, breadth)
    def _(y, rows):
        unit, inverse = normalize(image[y])
        unit_mixed[rows] = unit
        inverse_mixed[rows] = inverse
        early[rows, at_normed] = (unit * gain[...]).astype(BF)

    copies[0].wait()

    def chunk(index, carry):
        lanes = pl.ds(pl.multiple_of(index * CHUNK, CHUNK), CHUNK)
        upward[...] = dot(early[:, at_normed], expand_here[:, lanes])
        for start in range(0, pixels, 64):
            rows = slice(start, start + 64)
            value = upward[rows]
            cumulative = 0.5 + 0.5 * lax.erf(value * (1.0 / math.sqrt(2.0)))
            density = jnp.exp(-0.5 * value * value) * (1.0 / math.sqrt(2.0 * math.pi))
            early[rows, lanes] = (value * cumulative).astype(BF)
            slope[rows, lanes] = (cumulative + value * density).astype(BF)
        return carry

    lax.fori_loop(0, hidden_width // CHUNK, chunk, 0)
    copies[1].wait()
    branch[...] = dot(early[:, :hidden_width], project_here[...])

    @over_rows(height, breadth)
    def _(y, rows):
        summed = center[y].astype(F32) + layer_scale[...] * branch[rows]
        unit, inverse = normalize(summed)
        unit_summed[rows] = unit
        inverse_summed[rows] = inverse
        merged = unit * merge_gain[...]
        for k in range(channels // 128):
            pairs[k, y] = merged[:, k * 128 : (k + 1) * 128]

    quarter = pixels // 4
    for dy in range(2):
        for dx in range(2):
            j = 2 * dy + dx
            for y in range(height // 2):
                start = j * quarter + y * (breadth // 2)
                for k in range(channels // 128):
                    piece = pairs[k, 2 * y + dy, pl.ds(dx, breadth // 2, stride=2), :]
                    lane = hidden_width + channels + k * 128
                    early[start : start + breadth // 2, lane : lane + 128] = piece.astype(BF)
    copies[2].wait()
    total = dot(early[:quarter, at_patches], patch_here[:channels])
    for j in range(1, 4):
        total = total + dot(
            early[j * quarter : (j + 1) * quarter, at_patches],
            patch_here[j * channels : (j + 1) * channels],
        )
    total = total.reshape(section.shape)
    section[...] = total.astype(BF)
    first[...] = total[:3].astype(BF)
    last[...] = total[height // 2 - 3 :].astype(BF)
    for copy in copies[3:]:
        copy.wait()


def mixer_kernel(
    center, top, bottom, left, right, taps, gain, cotangent,
    grad, grad_half, first, last, gain_part,
    frame, image,
):
    height, breadth, channels = center.shape
    fill_frame(frame, (center, top, bottom, left, right))
    convolve(frame, taps, False, image)
    part = jnp.zeros((1, channels), F32)
    for y in range(height):
        unit, inverse = normalize(image[y])
        cot = cotangent[y].astype(F32)
        part = part + jnp.sum(cot * unit, axis=0, keepdims=True)
        value = normalize_back(cot * gain[...], unit, inverse)
        grad[y] = value
        narrow = value.astype(BF)
        grad_half[y] = narrow
        if y < 3:
            first[y] = narrow
        if y >= height - 3:
            last[y - (height - 3)] = narrow
    gain_part[...] = part


def weight_kernel(scale, center, top, bottom, left, right, grads, out, frame):
    fill_frame(frame, (center, top, bottom, left, right))
    weight_sums(frame, grads, scale, out)


def split_halves(values, start, keep, send):
    half = values.shape[1] // 2
    rows = slice(start, start + values.shape[0])
    core = lax.axis_index("col") % 2
    for i in range(2):

        @pl.when(core == i)
        def _():
            keep[rows] = values[:, i * half : (i + 1) * half]
            send[rows] = values[:, (1 - i) * half : (2 - i) * half]


def weight_pack_kernel(
    scale, center, top, bottom, left, right, grads, gain_part,
    keep, send, frame, wide_grads, packed,
):
    fill_frame(frame, (center, top, bottom, left, right))
    wide_grads[...] = grads[...].astype(F32)
    packed[...] = jnp.zeros(packed.shape, F32)
    weight_sums(frame, wide_grads, scale, packed)
    packed[49:50] = scale * gain_part[...]
    split_halves(packed[...].astype(BF), 0, keep, send)


def section_kernel(
    center, top, bottom, left, right, taps, residual,
    flat, keep, send,
    frame, image,
):
    height, breadth, channels = center.shape
    fill_frame(frame, (center, top, bottom, left, right))
    convolve(frame, taps, True, image)
    value = (image[...] + residual[...].astype(F32)).reshape(flat.shape).astype(BF)
    flat[...] = value
    blocks, _, width = keep.shape
    core = lax.axis_index("col") % 2
    for i in range(2):

        @pl.when(core == i)
        def _():
            for m in range(blocks):
                mine, other = (2 * m + i) * width, (2 * m + 1 - i) * width
                keep[m] = value[:, mine : mine + width]
                send[m] = value[:, other : other + width]


def merge_kernel(
    scale, scale_wide,
    flat, patch, unit_summed, inverse_summed, merge_gain, branch, layer_scale, wide_part, wide_gain,
    grad_summed, grad_branch, keep, send,
    pairs, packed, sums,
):
    tiles, height, breadth, _ = pairs.shape
    channels = 128 * tiles
    value = flat[...]
    for dy in range(2):
        for dx in range(2):
            j = 2 * dy + dx
            part = dot_last(value, patch[j * channels : (j + 1) * channels])
            part = part.reshape(height // 2, breadth // 2, channels)
            for y in range(height // 2):
                for k in range(tiles):
                    piece = part[y, :, k * 128 : (k + 1) * 128]
                    pairs[k, 2 * y + dy, pl.ds(dx, breadth // 2, stride=2), :] = piece
    sums[...] = jnp.zeros(sums.shape, F32)

    @over_rows(height, breadth)
    def _(y, rows):
        merged = jnp.concatenate([pairs[k, y] for k in range(tiles)], axis=1)
        unit = unit_summed[rows]
        sums[0:1] += jnp.sum(merged * unit, axis=0, keepdims=True)
        grad = normalize_back(merged * merge_gain[...], unit, inverse_summed[rows])
        grad_summed[rows] = grad
        sums[1:2] += jnp.sum(grad * branch[rows], axis=0, keepdims=True)
        grad_branch[rows] = (layer_scale[...] * grad).astype(BF)

    split_halves(grad_branch[...], 0, keep, send)
    packed[...] = jnp.zeros(packed.shape, F32)
    for i in range(2):
        columns = slice(i * channels, (i + 1) * channels)
        packed[49 * i : 49 + 49 * i] = wide_part[:, columns]
        packed[98 + i : 99 + i] = scale_wide * wide_gain[:, columns]
        packed[100 + i : 101 + i] = scale * sums[i : i + 1]
    split_halves(packed[...].astype(BF), grad_branch.shape[0], keep, send)


def back_kernel(
    grad_branch, project, slope, expand, unit_mixed, inverse_mixed, gain,
    keep, send, grad_mixed, first, last, gain_part,
    hidden, upward, normed,
):
    height, breadth, channels = grad_mixed.shape
    pixels, hidden_width = slope.shape

    def chunk(index, carry):
        span = pl.ds(pl.multiple_of(index * CHUNK, CHUNK), CHUNK)
        hidden[...] = dot_last(grad_branch[...], project[span])
        for start in range(0, pixels, 64):
            rows = slice(start, start + 64)
            upward[rows, span] = (hidden[rows] * slope[rows, span].astype(F32)).astype(BF)
        return carry

    lax.fori_loop(0, hidden_width // CHUNK, chunk, 0)
    normed[...] = dot_last(upward[...], expand[...])
    split_halves(upward[...], 0, keep, send)
    part = jnp.zeros((1, channels), F32)
    for y in range(height):
        rows = slice(y * breadth, (y + 1) * breadth)
        value = normed[rows]
        unit = unit_mixed[rows]
        part = part + jnp.sum(value * unit, axis=0, keepdims=True)
        narrow = normalize_back(value * gain[...], unit, inverse_mixed[rows]).astype(BF)
        grad_mixed[y] = narrow
        if y < 3:
            first[y] = narrow
        if y >= height - 3:
            last[y - (height - 3)] = narrow
    gain_part[...] = part


def patch_product_kernel(factor, early, early_other, own, other, keep, send):
    blocks, quarter, _ = own.shape
    rows = keep.shape[0] // max(blocks // 2, 1)
    channels = rows // 4
    at_patches = early.shape[1] - channels
    bit = (lax.axis_index("col") // 2) % 2
    for j in range(4):
        span = slice(j * quarter, (j + 1) * quarter)
        left = jnp.concatenate([early[span, at_patches:], early_other[span, at_patches:]], axis=0)
        for m in range(blocks):
            right = jnp.concatenate([own[m], other[m]], axis=0)
            value = (factor * dot_first(left, right)).astype(BF)
            at = m // 2 * rows + j * channels
            for i in range(2):

                @pl.when(bit == i)
                def _():
                    target = keep if m % 2 == i else send
                    target[at : at + channels] = value


def store_slices(value, begin, offset, rows, pitch, keep, send):
    bit = lax.axis_index("row") % 2
    for i in range(2):

        @pl.when(bit == i)
        def _():
            for k in range(value.shape[0] // rows):
                r = begin + k
                target = keep if r % 2 == i else send
                at = r // 2 * pitch + offset
                target[at : at + rows] = value[k * rows : (k + 1) * rows]


def project_product_kernel(factor, slices, early, early_other, own, other, keep, send):
    width = keep.shape[1]
    hidden_width = early.shape[1] - 4 * width
    pixels = early.shape[0]
    deep = hidden_width // slices
    right = jnp.concatenate([own[:pixels], other[:pixels]], axis=0)
    step = max(CHUNK, deep)
    for start in range(0, hidden_width, step):
        columns = slice(start, start + step)
        left = jnp.concatenate([early[:, columns], early_other[:, columns]], axis=0)
        value = (factor * dot_first(left, right)).astype(BF)
        store_slices(value, start // deep, 0, deep, deep, keep, send)
    tail = (own[pixels:].astype(F32) + other[pixels:].astype(F32)).astype(BF)
    at = slices // 2 * deep
    keep[at:] = tail
    send[at:] = tail


def expand_product_kernel(factor, slices, early, early_other, own, other, keep, send):
    width = keep.shape[1]
    channels = 2 * width
    hidden_width = early.shape[1] - 2 * channels
    shallow = channels // slices
    blocks = own.shape[1] // width
    columns = slice(hidden_width, hidden_width + channels)
    left = jnp.concatenate([early[:, columns], early_other[:, columns]], axis=0)
    for k in range(blocks):
        columns = slice(k * width, (k + 1) * width)
        right = jnp.concatenate([own[:, columns], other[:, columns]], axis=0)
        value = (factor * dot_first(left, right)).astype(BF)
        store_slices(value, 0, k * shallow, shallow, blocks * shallow, keep, send)


def finish_patch_kernel(own, other, out):
    blocks, _, width = own.shape
    core = lax.axis_index("col") % 2
    for i in range(2):

        @pl.when(core == i)
        def _():
            for m in range(blocks):
                a, b = (2 * m + i) * width, (2 * m + 1 - i) * width
                out[:, a : a + width] = own[m].astype(F32)
                out[:, b : b + width] = other[m].astype(F32)


def join_halves(own, other, start, out):
    half = own.shape[1]
    rows = slice(start, start + out.shape[0])
    core = lax.axis_index("col") % 2
    for i in range(2):

        @pl.when(core == i)
        def _():
            out[:, i * half : (i + 1) * half] = own[rows].astype(F32)
            out[:, (1 - i) * half : (2 - i) * half] = other[rows].astype(F32)


def finish_project_kernel(own, other, project, wide_taps, wide_gain, merge, layer, small):
    deep, channels = project.shape
    join_halves(own, other, 0, project)
    join_halves(own, other, deep, small)
    for i in range(2):
        columns = slice(i * channels, (i + 1) * channels)
        for p in range(7):
            start = 49 * i + 7 * p
            wide_taps[p, :, columns] = small[start : start + 7]
        wide_gain[:, columns] = small[98 + i : 99 + i]
    merge[...] = small[100:101]
    layer[...] = small[101:102]


def finish_expand_kernel(own, other, expand, taps, gain, small):
    shallow, hidden_width = expand.shape
    width = own.shape[1]
    blocks = hidden_width // (2 * width)
    core = lax.axis_index("col") % 2
    for i in range(2):

        @pl.when(core == i)
        def _():
            for k in range(blocks):
                rows = slice(k * shallow, (k + 1) * shallow)
                a, b = (i * blocks + k) * width, ((1 - i) * blocks + k) * width
                expand[:, a : a + width] = own[rows].astype(F32)
                expand[:, b : b + width] = other[rows].astype(F32)

    join_halves(own, other, blocks * shallow, small)
    for p in range(7):
        taps[p] = small[7 * p : 7 * p + 7]
    gain[...] = small[49:50]


def input_kernel(center, top, bottom, left, right, taps, grad_summed, out, frame, image):
    fill_frame(frame, (center, top, bottom, left, right))
    convolve(frame, taps, True, image)
    out[...] = (image[...] + grad_summed[...].reshape(image.shape)).astype(BF)


def body(
    block_input,
    kernel_three,
    gain_three,
    expand_weight,
    project_weight,
    layer_scale,
    merge_gain,
    patch_weight,
    kernel_four,
    gain_four,
    normed_cotangent,
    residual_cotangent,
):
    _, height, breadth, channels = block_input.shape
    hidden_width = expand_weight.shape[1]
    wide = patch_weight.shape[1]
    pixels = height * breadth
    quarter = pixels // 4
    rows4, cols4 = height // 2, breadth // 2
    row_count = lax.axis_size("row")
    col_count = lax.axis_size("col")
    scale_three = 1.0 / math.sqrt(pixels * row_count * col_count)
    scale_four = 1.0 / math.sqrt(quarter * row_count * col_count)
    center = block_input[0]
    gain_three, layer_scale, merge_gain, gain_four = (
        v[None] for v in (gain_three, layer_scale, merge_gain, gain_four)
    )
    dma = pltpu.SemaphoreType.DMA
    half = channels // 2
    hbm = pltpu.HBM

    def like(array):
        return shape_of(*array.shape, dtype=array.dtype)

    edge = shape_of(3, breadth, channels, dtype=BF)
    rows_input = neighbours(center[:3], center[height - 3 :], "row")
    inputs = (center, kernel_three, gain_three, layer_scale, merge_gain)
    center, taps_three, gain_three, layer_scale, merge_gain = run(
        load_kernel,
        "load",
        inputs,
        tuple(map(like, inputs)),
        scratch=(dma((5,)),),
        spaces=dict.fromkeys(range(5), hbm),
        after=rows_input[:1],
        limit=4,
        us=2,
    )
    framed = halo(center, rows_input, "strips_input")
    inputs = (
        expand_weight, project_weight, patch_weight, kernel_four, gain_four,
        normed_cotangent[0], residual_cotangent[0],
    )
    edge_four = shape_of(3, cols4, wide, dtype=BF)
    (
        early, unit_mixed, inverse_mixed, slope, branch, unit_summed, inverse_summed,
        section, first, last,
        expand_weight, project_weight, patch_weight, taps_four, gain_four, cotangent, residual,
    ) = run(
        front_kernel,
        "front",
        (*framed, taps_three, gain_three, layer_scale, merge_gain, *inputs),
        (
            shape_of(pixels, hidden_width + 2 * channels, dtype=BF),
            shape_of(pixels, channels),
            shape_of(pixels, 1),
            shape_of(pixels, hidden_width, dtype=BF),
            shape_of(pixels, channels),
            shape_of(pixels, channels),
            shape_of(pixels, 1),
            shape_of(rows4, cols4, wide, dtype=BF),
            edge_four,
            edge_four,
            *map(like, inputs),
        ),
        scratch=(
            frame_scratch(center),
            pltpu.VMEM((height, breadth, channels), F32),
            pltpu.VMEM((channels // 128, height, breadth, 128), F32),
            pltpu.VMEM((pixels, CHUNK), F32),
            dma((7,)),
        ),
        spaces=dict.fromkeys(range(9, 16), hbm),
        limit=28,
        us=12,
    )

    framed_four = halo(section, neighbours(first, last, "row"), "strips_section")
    mixer_image = pltpu.VMEM((rows4, cols4, wide), F32)
    grad_four, grad_four_half, first, last, gain_four_part = run(
        mixer_kernel,
        "mixer",
        (*framed_four, taps_four, gain_four, cotangent),
        (
            shape_of(rows4, cols4, wide),
            shape_of(rows4, cols4, wide, dtype=BF),
            edge_four,
            edge_four,
            shape_of(1, wide),
        ),
        scratch=(frame_scratch(section), mixer_image),
        limit=12,
        us=3,
    )
    rows_grad = neighbours(first, last, "row")
    (kernel_four_part,) = run(
        functools.partial(weight_kernel, scale_four),
        "mixer_weights",
        (*framed_four, grad_four),
        (shape_of(49, wide),),
        scratch=(frame_scratch(section),),
        after=rows_grad[:1],
        limit=12,
        us=3,
    )
    framed_grad = halo(grad_four_half, rows_grad, "strips_mixer", after=(kernel_four_part,))
    block_count = col_count // 2
    block = wide // col_count
    blocked = shape_of(block_count, quarter, block, dtype=BF)
    flat, flat_keep, flat_send, early = hold(
        section_kernel,
        "section_grad",
        (*framed_grad, taps_four, residual),
        (shape_of(quarter, wide, dtype=BF), blocked, blocked),
        early,
        scratch=(frame_scratch(section), mixer_image),
        limit=12,
        us=3,
    )

    flat_other = swap(flat_send, "col", 1)
    early_other = swap(early, "col", 1)
    split = shape_of(pixels + 112, half, dtype=BF)
    grad_summed, grad_branch, branch_keep, branch_send = run(
        functools.partial(merge_kernel, scale_three, scale_four),
        "merge_back",
        (
            flat, patch_weight, unit_summed, inverse_summed, merge_gain, branch, layer_scale,
            kernel_four_part, gain_four_part,
        ),
        (shape_of(pixels, channels), shape_of(pixels, channels, dtype=BF), split, split),
        scratch=(
            pltpu.VMEM((channels // 128, height, breadth, 128), F32),
            pltpu.VMEM((112, channels), F32),
            pltpu.VMEM((8, channels), F32),
        ),
        limit=16,
        us=3,
    )
    branch_other = swap(branch_send, "col", 1)
    patch_half = shape_of(block_count // 2 * 4 * channels, block, dtype=BF)
    patch_keep, patch_send = run(
        functools.partial(patch_product_kernel, scale_four),
        "patch_product",
        (early, early_other, flat_keep, flat_other),
        (patch_half, patch_half),
        limit=16,
        us=3,
    )
    deep, shallow = hidden_width // row_count, channels // row_count
    groups = hidden_width // channels
    project_half = shape_of(row_count // 2 * deep + 112, half, dtype=BF)
    project_keep, project_send = run(
        functools.partial(project_product_kernel, scale_three, row_count),
        "project_product",
        (early, early_other, branch_keep, branch_other),
        (project_half, project_half),
        after=(patch_send,),
        limit=16,
        us=3,
    )
    upward_half = shape_of(pixels, hidden_width // 2, dtype=BF)
    upward_keep, upward_send, grad_mixed, first, last, gain_part = run(
        back_kernel,
        "mlp_back",
        (grad_branch, project_weight, slope, expand_weight, unit_mixed, inverse_mixed, gain_three),
        (
            upward_half,
            upward_half,
            shape_of(height, breadth, channels, dtype=BF),
            edge,
            edge,
            shape_of(1, channels),
        ),
        scratch=(
            pltpu.VMEM((pixels, CHUNK), F32),
            pltpu.VMEM((pixels, hidden_width), BF),
            pltpu.VMEM((pixels, channels), F32),
        ),
        after=(project_send,),
        limit=16,
        us=4,
    )
    rows_back = neighbours(first, last, "row")
    upward_other = swap(upward_send, "col", 1)
    expand_half = shape_of(row_count // 2 * groups * shallow, half, dtype=BF)
    expand_keep, expand_send = run(
        functools.partial(expand_product_kernel, scale_three, row_count),
        "expand_product",
        (early, early_other, upward_keep, upward_other),
        (expand_half, expand_half),
        limit=16,
        us=3,
    )
    framed_back = halo(grad_mixed, rows_back, "strips_back", after=(expand_send,))
    small_half = shape_of(64, half, dtype=BF)
    small_keep, small_send = run(
        functools.partial(weight_pack_kernel, scale_three),
        "block_weights",
        (*framed, grad_mixed, gain_part),
        (small_half, small_half),
        scratch=(
            frame_scratch(center),
            pltpu.VMEM((height, breadth, channels), F32),
            pltpu.VMEM((64, channels), F32),
        ),
        after=framed_back[1:3],
        limit=12,
        us=5,
    )
    (input_grad,) = run(
        input_kernel,
        "input_grad",
        (*framed_back, taps_three, grad_summed),
        (shape_of(height, breadth, channels, dtype=BF),),
        scratch=(frame_scratch(center), pltpu.VMEM((height, breadth, channels), F32)),
        after=(small_keep,),
        limit=12,
        us=5,
    )

    row_bits, col_bits = axis_bits("row"), axis_bits("col")
    outer = len(row_bits)
    low_first = [("row", bit, 0) for bit in row_bits]
    patch_order = [("col", bit, outer) for bit in col_bits[1:]] + low_first
    patch_sum = chain(
        patch_keep, patch_send, patch_order, block_count * row_count, 4 * channels // row_count,
        after=(small_keep,),
    )
    patch_sum = gather(patch_sum, "col", col_bits[1:])
    (patch_grad,) = run(
        finish_patch_kernel,
        "finish_patch",
        (patch_sum, swap(patch_sum, "col", 1)),
        (shape_of(4 * channels // row_count, wide),),
        limit=8,
    )

    def share(keep, send, rows, extra=(), after=()):
        total = chain(keep, send, low_first, row_count, rows, extra, after)
        for bit in col_bits[1:]:
            total = total + swap(total, "col", bit)
        return total, swap(total, "col", 1)

    vector, wide_vector = shape_of(1, channels), shape_of(1, wide)
    project_grad, wide_taps, wide_gain, merge_sum, layer_sum = run(
        finish_project_kernel,
        "finish_project",
        share(project_keep, project_send, deep),
        (shape_of(deep, channels), shape_of(7, 7, wide), wide_vector, vector, vector),
        scratch=(pltpu.VMEM((112, channels), F32),),
        limit=8,
    )
    small = small_keep + swap(small_send, "col", 1)
    expand_grad, taps_sum, gain_sum = run(
        finish_expand_kernel,
        "finish_expand",
        share(expand_keep, expand_send, groups * shallow, (small, swap(small, "row", 1)), (input_grad,)),
        (shape_of(shallow, hidden_width), shape_of(7, 7, channels), vector),
        scratch=(pltpu.VMEM((64, channels), F32),),
        limit=8,
    )
    return (
        input_grad[None],
        taps_sum,
        gain_sum[0],
        expand_grad,
        project_grad,
        layer_sum[0],
        merge_sum[0],
        patch_grad,
        wide_taps,
        wide_gain[0],
    )


def solution(mesh):
    pixels = P(None, "row", "col", None)
    return jax.shard_map(
        body,
        mesh=mesh,
        in_specs=(pixels,) + (P(),) * 9 + (pixels, pixels),
        out_specs=(pixels, P(), P(), P("row", None), P("row", None), P(), P(), P("row", None), P(), P()),
        check_vma=False,
    )
```

```python
import functools
import math

import jax
import jax.numpy as jnp
from jax import lax
from jax.experimental import pallas as pl
from jax.experimental.pallas import tpu as pltpu
from jax.sharding import PartitionSpec as P

EPSILON = 1e-06
BF = jnp.bfloat16
F32 = jnp.float32
MIB = 1 << 20
PAD = 8
CHUNK = 256


def shape_of(*dims, dtype=F32):
    return jax.ShapeDtypeStruct(dims, dtype)


def run(kernel, name, args, outs, scratch=(), spaces=None, after=(), aliases=None, limit=24, us=0.0):
    spaces = spaces or {}
    count, extra = len(args), len(after)

    def spec(place):
        return pl.BlockSpec(memory_space=spaces.get(place, pltpu.VMEM))

    def inner(*refs):
        kernel(*refs[:count], *refs[count + extra :])

    return pl.pallas_call(
        inner,
        name=name,
        out_shape=outs,
        in_specs=[spec(i) for i in range(count)] + [pl.BlockSpec(memory_space=pl.ANY)] * extra,
        out_specs=[spec(("out", i)) for i in range(len(outs))],
        scratch_shapes=list(scratch),
        input_output_aliases=aliases or {},
        compiler_params=pltpu.CompilerParams(vmem_limit_bytes=limit * MIB),
        cost_estimate=pl.CostEstimate(flops=int(us * 1.1e9) + 1000, bytes_accessed=1000, transcendentals=0),
    )(*args, *after)


def swap(values, axis, bit):
    return lax.ppermute(values, axis, [(i, i ^ bit) for i in range(lax.axis_size(axis))])


def axis_bits(axis):
    return [1 << k for k in range((lax.axis_size(axis) - 1).bit_length())]


def own_bit(axis, bit):
    return (lax.axis_index(axis) // bit) % 2


def chain(keep, send, order, count, rows, extra=(), after=()):
    for place, (axis, bit, _) in enumerate(order):
        received = swap(send, axis, bit)
        if place + 1 == len(order):
            return keep + received
        axis, bit, position = order[place + 1]
        grown = extra if place == 0 else ()
        count //= 2
        tail = keep.shape[0] - count * rows + (grown[0].shape[0] if grown else 0)
        out = shape_of(count // 2 * rows + tail, keep.shape[1], dtype=BF)
        keep, send = run(
            functools.partial(step_kernel, axis, bit, position, count, rows),
            "sum_step",
            (keep, received, *grown),
            (out, out),
            after=after if place == 0 else (),
            limit=8,
        )


def step_kernel(axis, bit, position, count, rows, keep, received, *refs):
    *grown, next_keep, next_send = refs
    mine = (lax.axis_index(axis) // bit) % 2
    low = (1 << position) - 1
    for i in range(2):

        @pl.when(mine == i)
        def _():
            for s in range(count):
                span = slice(s * rows, (s + 1) * rows)
                at = ((s >> (position + 1)) << position | (s & low)) * rows
                target = next_keep if (s >> position) & 1 == i else next_send
                target[at : at + rows] = (keep[span].astype(F32) + received[span].astype(F32)).astype(BF)

    tails = []
    if keep.shape[0] > count * rows:
        tails.append(keep[count * rows :].astype(F32) + received[count * rows :].astype(F32))
    if grown:
        tails.append(sum(g[...].astype(F32) for g in grown))
    at = count // 2 * rows
    for tail in tails:
        for target in (next_keep, next_send):
            target[at : at + tail.shape[0]] = tail.astype(BF)
        at += tail.shape[0]


def gather(values, axis, bits):
    values = values[None]
    for bit in reversed(bits):
        other = swap(values, axis, bit)
        mine = own_bit(axis, bit)
        low = jnp.where(mine == 0, values, other)
        high = jnp.where(mine == 0, other, values)
        values = jnp.stack([low, high], axis=1).reshape(-1, *values.shape[1:])
    return values


def neighbours(first, last, axis):
    count = lax.axis_size(axis)
    forward = [(i, i + 1) for i in range(count - 1)]
    backward = [(i + 1, i) for i in range(count - 1)]
    return lax.ppermute(last, axis, forward), lax.ppermute(first, axis, backward)


def strip_kernel(center, top, bottom, first, last):
    height, breadth = center.shape[:2]
    for source, start in ((top, 0), (center, 3), (bottom, 3 + height)):
        values = source[...].astype(F32)
        rows = slice(start, start + source.shape[0])
        first[rows] = values[:, :PAD].astype(BF)
        last[rows] = values[:, breadth - PAD :].astype(BF)


def halo(center, rows, name, after=()):
    height, _, channels = center.shape
    top, bottom = rows
    strip = shape_of(height + 6, PAD, channels, dtype=BF)
    first, last = run(strip_kernel, name, (center, top, bottom), (strip, strip), after=after, limit=8)
    left, right = neighbours(first, last, "col")
    return center, top, bottom, left, right


def hold(kernel, name, args, outs, carried, **options):
    count = len(args)

    def inner(*refs):
        kernel(*refs[:count], *refs[count + 1 : count + 1 + len(outs)], *refs[count + 2 + len(outs) :])

    return run(
        inner,
        name,
        (*args, carried),
        (*outs, shape_of(*carried.shape, dtype=carried.dtype)),
        spaces={count: pl.ANY, ("out", len(outs)): pl.ANY},
        aliases={count: len(outs)},
        **options,
    )


def fill_frame(frame, parts):
    center, top, bottom, left, right = parts
    height, breadth = center.shape[:2]
    middle = slice(PAD, PAD + breadth)
    frame[0:3, middle] = top[...].astype(F32)
    frame[3 : 3 + height, middle] = center[...].astype(F32)
    frame[3 + height :, middle] = bottom[...].astype(F32)
    frame[:, :PAD] = left[...].astype(F32)
    frame[:, PAD + breadth :] = right[...].astype(F32)


def frame_scratch(center):
    height, breadth, channels = center.shape
    return pltpu.VMEM((height + 6, breadth + 2 * PAD, channels), F32)


def lane_tiles(channels):
    def over(step):
        def wrapped(index, carry):
            step(pl.ds(pl.multiple_of(index * 128, 128), 128))
            return carry

        lax.fori_loop(0, channels // 128, wrapped, 0)

    return over


def convolve(frame, taps, flip, out):
    height, breadth, channels = out.shape

    @lane_tiles(channels)
    def _(lanes):
        for column in range(0, breadth, 8):
            total = jnp.zeros((height, 8, 128), F32)
            for q in range(7):
                rows = frame[:, pl.ds(column + PAD - 3 + q, 8), lanes]
                for p in range(7):
                    a, b = (6 - p, 6 - q) if flip else (p, q)
                    total = total + rows[p : p + height] * taps[a, pl.ds(b, 1), lanes]
            out[:, pl.ds(column, 8), lanes] = total


def weight_sums(frame, grads, scale, out):
    height, breadth, channels = grads.shape

    @lane_tiles(channels)
    def _(lanes):
        for q in range(7):
            totals = [jnp.zeros((8, 128), F32)] * 7
            for column in range(0, breadth, 8):
                rows = frame[:, pl.ds(column + PAD - 3 + q, 8), lanes]
                grad = grads[:, pl.ds(column, 8), lanes]
                for p in range(7):
                    totals[p] = totals[p] + jnp.sum(rows[p : p + height] * grad, axis=0)
            for p in range(7):
                out[pl.ds(7 * p + q, 1), lanes] = scale * jnp.sum(totals[p], axis=0, keepdims=True)


def mean(values):
    return jnp.mean(values, axis=-1, keepdims=True)


def normalize(values):
    level = mean(values)
    inverse = lax.rsqrt(mean(values * values) - level * level + EPSILON)
    return (values - level) * inverse, inverse


def normalize_back(grads, unit_values, inverse):
    return (grads - mean(grads) - unit_values * mean(grads * unit_values)) * inverse


def dot(left, right):
    return jnp.dot(left, right, preferred_element_type=F32)


def dot_last(left, right):
    return lax.dot_general(left, right, (((1,), (1,)), ((), ())), preferred_element_type=F32)


def dot_first(left, right):
    return lax.dot_general(left, right, (((0,), (0,)), ((), ())), preferred_element_type=F32)


def over_rows(count, size):
    def over(step):
        def wrapped(index, carry):
            step(index, pl.ds(pl.multiple_of(index * size, size), size))
            return carry

        lax.fori_loop(0, count, wrapped, 0)

    return over


def fetch(sources, targets, semaphores):
    copies = [
        pltpu.make_async_copy(source, target, semaphores.at[i])
        for i, (source, target) in enumerate(zip(sources, targets))
    ]
    for copy in copies:
        copy.start()
    return copies


def load_kernel(*refs):
    *arrays, semaphores = refs
    count = len(arrays) // 2
    for copy in fetch(arrays[:count], arrays[count:], semaphores):
        copy.wait()


def front_kernel(
    center, top, bottom, left, right, taps, gain, layer_scale, merge_gain,
    expand, project, patch, wide_taps, wide_gain, cotangent, residual,
    early, unit_mixed, inverse_mixed, slope, branch, unit_summed, inverse_summed, section, first, last,
    expand_here, project_here, patch_here, wide_taps_here, wide_gain_here, cotangent_here, residual_here,
    frame, image, pairs, upward, semaphores,
):
    height, breadth, channels = center.shape
    hidden_width = expand.shape[1]
    pixels = height * breadth
    copies = fetch(
        (expand, project, patch, wide_taps, wide_gain, cotangent, residual),
        (expand_here, project_here, patch_here, wide_taps_here, wide_gain_here, cotangent_here, residual_here),
        semaphores,
    )
    fill_frame(frame, (center, top, bottom, left, right))
    convolve(frame, taps, False, image)
    at_normed = slice(hidden_width, hidden_width + channels)
    at_patches = slice(hidden_width + channels, hidden_width + 2 * channels)

    @over_rows(height, breadth)
    def _(y, rows):
        unit, inverse = normalize(image[y])
        unit_mixed[rows] = unit
        inverse_mixed[rows] = inverse
        early[rows, at_normed] = (unit * gain[...]).astype(BF)

    copies[0].wait()

    def chunk(index, carry):
        lanes = pl.ds(pl.multiple_of(index * CHUNK, CHUNK), CHUNK)
        upward[...] = dot(early[:, at_normed], expand_here[:, lanes])
        for start in range(0, pixels, 64):
            rows = slice(start, start + 64)
            value = upward[rows]
            cumulative = 0.5 + 0.5 * lax.erf(value * (1.0 / math.sqrt(2.0)))
            density = jnp.exp(-0.5 * value * value) * (1.0 / math.sqrt(2.0 * math.pi))
            early[rows, lanes] = (value * cumulative).astype(BF)
            slope[rows, lanes] = (cumulative + value * density).astype(BF)
        return carry

    lax.fori_loop(0, hidden_width // CHUNK, chunk, 0)
    copies[1].wait()
    branch[...] = dot(early[:, :hidden_width], project_here[...])

    @over_rows(height, breadth)
    def _(y, rows):
        summed = center[y].astype(F32) + layer_scale[...] * branch[rows]
        unit, inverse = normalize(summed)
        unit_summed[rows] = unit
        inverse_summed[rows] = inverse
        merged = unit * merge_gain[...]
        for k in range(channels // 128):
            pairs[k, y] = merged[:, k * 128 : (k + 1) * 128]

    quarter = pixels // 4
    for dy in range(2):
        for dx in range(2):
            j = 2 * dy + dx
            for y in range(height // 2):
                start = j * quarter + y * (breadth // 2)
                for k in range(channels // 128):
                    piece = pairs[k, 2 * y + dy, pl.ds(dx, breadth // 2, stride=2), :]
                    lane = hidden_width + channels + k * 128
                    early[start : start + breadth // 2, lane : lane + 128] = piece.astype(BF)
    copies[2].wait()
    total = dot(early[:quarter, at_patches], patch_here[:channels])
    for j in range(1, 4):
        total = total + dot(
            early[j * quarter : (j + 1) * quarter, at_patches],
            patch_here[j * channels : (j + 1) * channels],
        )
    total = total.reshape(section.shape)
    section[...] = total.astype(BF)
    first[...] = total[:3].astype(BF)
    last[...] = total[height // 2 - 3 :].astype(BF)
    for copy in copies[3:]:
        copy.wait()


def mixer_kernel(
    center, top, bottom, left, right, taps, gain, cotangent,
    grad, grad_half, first, last, gain_part,
    frame, image,
):
    height, breadth, channels = center.shape
    fill_frame(frame, (center, top, bottom, left, right))
    convolve(frame, taps, False, image)
    part = jnp.zeros((1, channels), F32)
    for y in range(height):
        unit, inverse = normalize(image[y])
        cot = cotangent[y].astype(F32)
        part = part + jnp.sum(cot * unit, axis=0, keepdims=True)
        value = normalize_back(cot * gain[...], unit, inverse)
        grad[y] = value
        narrow = value.astype(BF)
        grad_half[y] = narrow
        if y < 3:
            first[y] = narrow
        if y >= height - 3:
            last[y - (height - 3)] = narrow
    gain_part[...] = part


def weight_kernel(scale, center, top, bottom, left, right, grads, out, frame):
    fill_frame(frame, (center, top, bottom, left, right))
    weight_sums(frame, grads, scale, out)


def split_halves(values, start, keep, send):
    half = values.shape[1] // 2
    rows = slice(start, start + values.shape[0])
    core = lax.axis_index("col") % 2
    for i in range(2):

        @pl.when(core == i)
        def _():
            keep[rows] = values[:, i * half : (i + 1) * half]
            send[rows] = values[:, (1 - i) * half : (2 - i) * half]


def weight_pack_kernel(
    scale, center, top, bottom, left, right, grads, gain_part,
    keep, send, frame, wide_grads, packed,
):
    fill_frame(frame, (center, top, bottom, left, right))
    wide_grads[...] = grads[...].astype(F32)
    packed[...] = jnp.zeros(packed.shape, F32)
    weight_sums(frame, wide_grads, scale, packed)
    packed[49:50] = scale * gain_part[...]
    split_halves(packed[...].astype(BF), 0, keep, send)


def section_kernel(
    center, top, bottom, left, right, taps, residual,
    flat, keep, send,
    frame, image,
):
    height, breadth, channels = center.shape
    fill_frame(frame, (center, top, bottom, left, right))
    convolve(frame, taps, True, image)
    value = (image[...] + residual[...].astype(F32)).reshape(flat.shape).astype(BF)
    flat[...] = value
    blocks, _, width = keep.shape
    core = lax.axis_index("col") % 2
    for i in range(2):

        @pl.when(core == i)
        def _():
            for m in range(blocks):
                mine, other = (2 * m + i) * width, (2 * m + 1 - i) * width
                keep[m] = value[:, mine : mine + width]
                send[m] = value[:, other : other + width]


def merge_kernel(
    scale, scale_wide,
    flat, patch, unit_summed, inverse_summed, merge_gain, branch, layer_scale, wide_part, wide_gain,
    grad_summed, grad_branch, keep, send,
    pairs, packed, sums,
):
    tiles, height, breadth, _ = pairs.shape
    channels = 128 * tiles
    value = flat[...]
    for dy in range(2):
        for dx in range(2):
            j = 2 * dy + dx
            part = dot_last(value, patch[j * channels : (j + 1) * channels])
            part = part.reshape(height // 2, breadth // 2, channels)
            for y in range(height // 2):
                for k in range(tiles):
                    piece = part[y, :, k * 128 : (k + 1) * 128]
                    pairs[k, 2 * y + dy, pl.ds(dx, breadth // 2, stride=2), :] = piece
    sums[...] = jnp.zeros(sums.shape, F32)

    @over_rows(height, breadth)
    def _(y, rows):
        merged = jnp.concatenate([pairs[k, y] for k in range(tiles)], axis=1)
        unit = unit_summed[rows]
        sums[0:1] += jnp.sum(merged * unit, axis=0, keepdims=True)
        grad = normalize_back(merged * merge_gain[...], unit, inverse_summed[rows])
        grad_summed[rows] = grad
        sums[1:2] += jnp.sum(grad * branch[rows], axis=0, keepdims=True)
        grad_branch[rows] = (layer_scale[...] * grad).astype(BF)

    split_halves(grad_branch[...], 0, keep, send)
    packed[...] = jnp.zeros(packed.shape, F32)
    for i in range(2):
        columns = slice(i * channels, (i + 1) * channels)
        packed[49 * i : 49 + 49 * i] = wide_part[:, columns]
        packed[98 + i : 99 + i] = scale_wide * wide_gain[:, columns]
        packed[100 + i : 101 + i] = scale * sums[i : i + 1]
    split_halves(packed[...].astype(BF), grad_branch.shape[0], keep, send)


def back_kernel(
    grad_branch, project, slope, expand, unit_mixed, inverse_mixed, gain,
    keep, send, grad_mixed, first, last, gain_part,
    hidden, upward, normed,
):
    height, breadth, channels = grad_mixed.shape
    pixels, hidden_width = slope.shape

    def chunk(index, carry):
        span = pl.ds(pl.multiple_of(index * CHUNK, CHUNK), CHUNK)
        hidden[...] = dot_last(grad_branch[...], project[span])
        for start in range(0, pixels, 64):
            rows = slice(start, start + 64)
            upward[rows, span] = (hidden[rows] * slope[rows, span].astype(F32)).astype(BF)
        return carry

    lax.fori_loop(0, hidden_width // CHUNK, chunk, 0)
    normed[...] = dot_last(upward[...], expand[...])
    split_halves(upward[...], 0, keep, send)
    part = jnp.zeros((1, channels), F32)
    for y in range(height):
        rows = slice(y * breadth, (y + 1) * breadth)
        value = normed[rows]
        unit = unit_mixed[rows]
        part = part + jnp.sum(value * unit, axis=0, keepdims=True)
        narrow = normalize_back(value * gain[...], unit, inverse_mixed[rows]).astype(BF)
        grad_mixed[y] = narrow
        if y < 3:
            first[y] = narrow
        if y >= height - 3:
            last[y - (height - 3)] = narrow
    gain_part[...] = part


def patch_product_kernel(factor, early, early_other, own, other, keep, send):
    blocks, quarter, _ = own.shape
    rows = keep.shape[0] // max(blocks // 2, 1)
    channels = rows // 4
    at_patches = early.shape[1] - channels
    bit = (lax.axis_index("col") // 2) % 2
    for j in range(4):
        span = slice(j * quarter, (j + 1) * quarter)
        left = jnp.concatenate([early[span, at_patches:], early_other[span, at_patches:]], axis=0)
        for m in range(blocks):
            right = jnp.concatenate([own[m], other[m]], axis=0)
            value = (factor * dot_first(left, right)).astype(BF)
            at = m // 2 * rows + j * channels
            for i in range(2):

                @pl.when(bit == i)
                def _():
                    target = keep if m % 2 == i else send
                    target[at : at + channels] = value


def store_slices(position, value, begin, offset, rows, pitch, keep, send):
    bit = (lax.axis_index("row") >> position) % 2
    low = (1 << position) - 1
    for i in range(2):

        @pl.when(bit == i)
        def _():
            for k in range(value.shape[0] // rows):
                r = begin + k
                target = keep if (r >> position) & 1 == i else send
                at = ((r >> (position + 1)) << position | (r & low)) * pitch + offset
                target[at : at + rows] = value[k * rows : (k + 1) * rows]


def project_product_kernel(factor, slices, early, early_other, own, other, keep, send):
    width = keep.shape[1]
    hidden_width = early.shape[1] - 4 * width
    pixels = early.shape[0]
    deep = hidden_width // slices
    right = jnp.concatenate([own[:pixels], other[:pixels]], axis=0)
    step = max(CHUNK, deep)
    for start in range(0, hidden_width, step):
        columns = slice(start, start + step)
        left = jnp.concatenate([early[:, columns], early_other[:, columns]], axis=0)
        value = (factor * dot_first(left, right)).astype(BF)
        store_slices(1, value, start // deep, 0, deep, deep, keep, send)
    tail = (own[pixels:].astype(F32) + other[pixels:].astype(F32)).astype(BF)
    at = slices // 2 * deep
    keep[at:] = tail
    send[at:] = tail


def expand_product_kernel(factor, slices, early, early_other, own, other, keep, send):
    width = keep.shape[1]
    channels = 2 * width
    hidden_width = early.shape[1] - 2 * channels
    shallow = channels // slices
    blocks = own.shape[1] // width
    columns = slice(hidden_width, hidden_width + channels)
    left = jnp.concatenate([early[:, columns], early_other[:, columns]], axis=0)
    for k in range(blocks):
        columns = slice(k * width, (k + 1) * width)
        right = jnp.concatenate([own[:, columns], other[:, columns]], axis=0)
        value = (factor * dot_first(left, right)).astype(BF)
        store_slices(0, value, 0, k * shallow, shallow, blocks * shallow, keep, send)


def finish_patch_kernel(own, other, out):
    blocks, _, width = own.shape
    core = lax.axis_index("col") % 2
    for i in range(2):

        @pl.when(core == i)
        def _():
            for m in range(blocks):
                a, b = (2 * m + i) * width, (2 * m + 1 - i) * width
                out[:, a : a + width] = own[m].astype(F32)
                out[:, b : b + width] = other[m].astype(F32)


def join_halves(own, other, start, out):
    half = own.shape[1]
    rows = slice(start, start + out.shape[0])
    core = lax.axis_index("col") % 2
    for i in range(2):

        @pl.when(core == i)
        def _():
            out[:, i * half : (i + 1) * half] = own[rows].astype(F32)
            out[:, (1 - i) * half : (2 - i) * half] = other[rows].astype(F32)


def finish_project_kernel(own, other, project, wide_taps, wide_gain, merge, layer, small):
    deep, channels = project.shape
    join_halves(own, other, 0, project)
    join_halves(own, other, deep, small)
    for i in range(2):
        columns = slice(i * channels, (i + 1) * channels)
        for p in range(7):
            start = 49 * i + 7 * p
            wide_taps[p, :, columns] = small[start : start + 7]
        wide_gain[:, columns] = small[98 + i : 99 + i]
    merge[...] = small[100:101]
    layer[...] = small[101:102]


def finish_expand_kernel(own, other, expand, taps, gain, small):
    shallow, hidden_width = expand.shape
    width = own.shape[1]
    blocks = hidden_width // (2 * width)
    core = lax.axis_index("col") % 2
    for i in range(2):

        @pl.when(core == i)
        def _():
            for k in range(blocks):
                rows = slice(k * shallow, (k + 1) * shallow)
                a, b = (i * blocks + k) * width, ((1 - i) * blocks + k) * width
                expand[:, a : a + width] = own[rows].astype(F32)
                expand[:, b : b + width] = other[rows].astype(F32)

    join_halves(own, other, blocks * shallow, small)
    for p in range(7):
        taps[p] = small[7 * p : 7 * p + 7]
    gain[...] = small[49:50]


def input_kernel(center, top, bottom, left, right, taps, grad_summed, out, frame, image):
    fill_frame(frame, (center, top, bottom, left, right))
    convolve(frame, taps, True, image)
    out[...] = (image[...] + grad_summed[...].reshape(image.shape)).astype(BF)


def body(
    block_input,
    kernel_three,
    gain_three,
    expand_weight,
    project_weight,
    layer_scale,
    merge_gain,
    patch_weight,
    kernel_four,
    gain_four,
    normed_cotangent,
    residual_cotangent,
):
    _, height, breadth, channels = block_input.shape
    hidden_width = expand_weight.shape[1]
    wide = patch_weight.shape[1]
    pixels = height * breadth
    quarter = pixels // 4
    rows4, cols4 = height // 2, breadth // 2
    row_count = lax.axis_size("row")
    col_count = lax.axis_size("col")
    scale_three = 1.0 / math.sqrt(pixels * row_count * col_count)
    scale_four = 1.0 / math.sqrt(quarter * row_count * col_count)
    center = block_input[0]
    gain_three, layer_scale, merge_gain, gain_four = (
        v[None] for v in (gain_three, layer_scale, merge_gain, gain_four)
    )
    dma = pltpu.SemaphoreType.DMA
    half = channels // 2
    hbm = pltpu.HBM

    def like(array):
        return shape_of(*array.shape, dtype=array.dtype)

    edge = shape_of(3, breadth, channels, dtype=BF)
    rows_input = neighbours(center[:3], center[height - 3 :], "row")
    inputs = (center, kernel_three, gain_three, layer_scale, merge_gain)
    center, taps_three, gain_three, layer_scale, merge_gain = run(
        load_kernel,
        "load",
        inputs,
        tuple(map(like, inputs)),
        scratch=(dma((5,)),),
        spaces=dict.fromkeys(range(5), hbm),
        after=rows_input[:1],
        limit=4,
        us=2,
    )
    framed = halo(center, rows_input, "strips_input")
    inputs = (
        expand_weight, project_weight, patch_weight, kernel_four, gain_four,
        normed_cotangent[0], residual_cotangent[0],
    )
    edge_four = shape_of(3, cols4, wide, dtype=BF)
    (
        early, unit_mixed, inverse_mixed, slope, branch, unit_summed, inverse_summed,
        section, first, last,
        expand_weight, project_weight, patch_weight, taps_four, gain_four, cotangent, residual,
    ) = run(
        front_kernel,
        "front",
        (*framed, taps_three, gain_three, layer_scale, merge_gain, *inputs),
        (
            shape_of(pixels, hidden_width + 2 * channels, dtype=BF),
            shape_of(pixels, channels),
            shape_of(pixels, 1),
            shape_of(pixels, hidden_width, dtype=BF),
            shape_of(pixels, channels),
            shape_of(pixels, channels),
            shape_of(pixels, 1),
            shape_of(rows4, cols4, wide, dtype=BF),
            edge_four,
            edge_four,
            *map(like, inputs),
        ),
        scratch=(
            frame_scratch(center),
            pltpu.VMEM((height, breadth, channels), F32),
            pltpu.VMEM((channels // 128, height, breadth, 128), F32),
            pltpu.VMEM((pixels, CHUNK), F32),
            dma((7,)),
        ),
        spaces=dict.fromkeys(range(9, 16), hbm),
        limit=28,
        us=12,
    )

    framed_four = halo(section, neighbours(first, last, "row"), "strips_section")
    mixer_image = pltpu.VMEM((rows4, cols4, wide), F32)
    grad_four, grad_four_half, first, last, gain_four_part = run(
        mixer_kernel,
        "mixer",
        (*framed_four, taps_four, gain_four, cotangent),
        (
            shape_of(rows4, cols4, wide),
            shape_of(rows4, cols4, wide, dtype=BF),
            edge_four,
            edge_four,
            shape_of(1, wide),
        ),
        scratch=(frame_scratch(section), mixer_image),
        limit=12,
        us=3,
    )
    rows_grad = neighbours(first, last, "row")
    (kernel_four_part,) = run(
        functools.partial(weight_kernel, scale_four),
        "mixer_weights",
        (*framed_four, grad_four),
        (shape_of(49, wide),),
        scratch=(frame_scratch(section),),
        after=rows_grad[:1],
        limit=12,
        us=3,
    )
    framed_grad = halo(grad_four_half, rows_grad, "strips_mixer", after=(kernel_four_part,))
    block_count = col_count // 2
    block = wide // col_count
    blocked = shape_of(block_count, quarter, block, dtype=BF)
    flat, flat_keep, flat_send, early = hold(
        section_kernel,
        "section_grad",
        (*framed_grad, taps_four, residual),
        (shape_of(quarter, wide, dtype=BF), blocked, blocked),
        early,
        scratch=(frame_scratch(section), mixer_image),
        limit=12,
        us=3,
    )

    flat_other = swap(flat_send, "col", 1)
    early_other = swap(early, "col", 1)
    split = shape_of(pixels + 112, half, dtype=BF)
    grad_summed, grad_branch, branch_keep, branch_send = run(
        functools.partial(merge_kernel, scale_three, scale_four),
        "merge_back",
        (
            flat, patch_weight, unit_summed, inverse_summed, merge_gain, branch, layer_scale,
            kernel_four_part, gain_four_part,
        ),
        (shape_of(pixels, channels), shape_of(pixels, channels, dtype=BF), split, split),
        scratch=(
            pltpu.VMEM((channels // 128, height, breadth, 128), F32),
            pltpu.VMEM((112, channels), F32),
            pltpu.VMEM((8, channels), F32),
        ),
        limit=16,
    )
    branch_other = swap(branch_send, "col", 1)
    patch_half = shape_of(block_count // 2 * 4 * channels, block, dtype=BF)
    patch_keep, patch_send = run(
        functools.partial(patch_product_kernel, scale_four),
        "patch_product",
        (early, early_other, flat_keep, flat_other),
        (patch_half, patch_half),
        limit=16,
    )
    deep, shallow = hidden_width // row_count, channels // row_count
    groups = hidden_width // channels
    project_half = shape_of(row_count // 2 * deep + 112, half, dtype=BF)
    upward_half = shape_of(pixels, hidden_width // 2, dtype=BF)
    upward_keep, upward_send, grad_mixed, first, last, gain_part = run(
        back_kernel,
        "mlp_back",
        (grad_branch, project_weight, slope, expand_weight, unit_mixed, inverse_mixed, gain_three),
        (
            upward_half,
            upward_half,
            shape_of(height, breadth, channels, dtype=BF),
            edge,
            edge,
            shape_of(1, channels),
        ),
        scratch=(
            pltpu.VMEM((pixels, CHUNK), F32),
            pltpu.VMEM((pixels, hidden_width), BF),
            pltpu.VMEM((pixels, channels), F32),
        ),
        after=(patch_send,),
        limit=16,
    )
    rows_back = neighbours(first, last, "row")
    upward_other = swap(upward_send, "col", 1)
    project_keep, project_send = run(
        functools.partial(project_product_kernel, scale_three, row_count),
        "project_product",
        (early, early_other, branch_keep, branch_other),
        (project_half, project_half),
        after=(upward_send,),
        limit=16,
    )
    expand_half = shape_of(row_count // 2 * groups * shallow, half, dtype=BF)
    expand_keep, expand_send = run(
        functools.partial(expand_product_kernel, scale_three, row_count),
        "expand_product",
        (early, early_other, upward_keep, upward_other),
        (expand_half, expand_half),
        after=(project_send,),
        limit=16,
    )
    framed_back = halo(grad_mixed, rows_back, "strips_back", after=(expand_send,))
    small_half = shape_of(64, half, dtype=BF)
    small_keep, small_send = run(
        functools.partial(weight_pack_kernel, scale_three),
        "block_weights",
        (*framed, grad_mixed, gain_part),
        (small_half, small_half),
        scratch=(
            frame_scratch(center),
            pltpu.VMEM((height, breadth, channels), F32),
            pltpu.VMEM((64, channels), F32),
        ),
        after=(*framed_back[1:3], expand_send),
        limit=12,
    )
    (input_grad,) = run(
        input_kernel,
        "input_grad",
        (*framed_back, taps_three, grad_summed),
        (shape_of(height, breadth, channels, dtype=BF),),
        scratch=(frame_scratch(center), pltpu.VMEM((height, breadth, channels), F32)),
        after=(small_keep,),
        limit=12,
    )

    row_bits, col_bits = axis_bits("row"), axis_bits("col")
    outer = len(row_bits)
    low_first = [("row", bit, 0) for bit in row_bits]
    patch_order = [("col", bit, outer) for bit in col_bits[1:]] + low_first
    patch_sum = chain(
        patch_keep, patch_send, patch_order, block_count * row_count, 4 * channels // row_count,
        after=(small_keep,),
    )
    patch_sum = gather(patch_sum, "col", col_bits[1:])
    (patch_grad,) = run(
        finish_patch_kernel,
        "finish_patch",
        (patch_sum, swap(patch_sum, "col", 1)),
        (shape_of(4 * channels // row_count, wide),),
        limit=8,
    )

    def share(keep, send, order, rows, extra=(), after=()):
        total = chain(keep, send, order, row_count, rows, extra, after)
        for bit in col_bits[1:]:
            total = total + swap(total, "col", bit)
        return total, swap(total, "col", 1)

    vector, wide_vector = shape_of(1, channels), shape_of(1, wide)
    project_grad, wide_taps, wide_gain, merge_sum, layer_sum = run(
        finish_project_kernel,
        "finish_project",
        share(project_keep, project_send, [("row", row_bits[1], 1), low_first[0], *low_first[2:]], deep),
        (shape_of(deep, channels), shape_of(7, 7, wide), wide_vector, vector, vector),
        scratch=(pltpu.VMEM((112, channels), F32),),
        limit=8,
    )
    small = small_keep + swap(small_send, "col", 1)
    expand_grad, taps_sum, gain_sum = run(
        finish_expand_kernel,
        "finish_expand",
        share(expand_keep, expand_send, low_first, groups * shallow, (small, swap(small, "row", 1)), (input_grad,)),
        (shape_of(shallow, hidden_width), shape_of(7, 7, channels), vector),
        scratch=(pltpu.VMEM((64, channels), F32),),
        limit=8,
    )
    return (
        input_grad[None],
        taps_sum,
        gain_sum[0],
        expand_grad,
        project_grad,
        layer_sum[0],
        merge_sum[0],
        patch_grad,
        wide_taps,
        wide_gain[0],
    )


def solution(mesh):
    pixels = P(None, "row", "col", None)
    return jax.shard_map(
        body,
        mesh=mesh,
        in_specs=(pixels,) + (P(),) * 9 + (pixels, pixels),
        out_specs=(pixels, P(), P(), P("row", None), P("row", None), P(), P(), P("row", None), P(), P()),
        check_vma=False,
    )
```

```python
import functools
import math

import jax
import jax.numpy as jnp
from jax import lax
from jax.experimental import pallas as pl
from jax.experimental.pallas import tpu as pltpu
from jax.sharding import PartitionSpec as P

EPSILON = 1e-06
BF = jnp.bfloat16
F32 = jnp.float32
MIB = 1 << 20
PAD = 8
CHUNK = 256


def shape_of(*dims, dtype=F32):
    return jax.ShapeDtypeStruct(dims, dtype)


def run(kernel, name, args, outs, scratch=(), spaces=None, after=(), aliases=None, limit=24, us=0.0):
    spaces = spaces or {}
    count, extra = len(args), len(after)

    def spec(place):
        return pl.BlockSpec(memory_space=spaces.get(place, pltpu.VMEM))

    def inner(*refs):
        kernel(*refs[:count], *refs[count + extra :])

    return pl.pallas_call(
        inner,
        name=name,
        out_shape=outs,
        in_specs=[spec(i) for i in range(count)] + [pl.BlockSpec(memory_space=pl.ANY)] * extra,
        out_specs=[spec(("out", i)) for i in range(len(outs))],
        scratch_shapes=list(scratch),
        input_output_aliases=aliases or {},
        compiler_params=pltpu.CompilerParams(vmem_limit_bytes=limit * MIB),
        cost_estimate=pl.CostEstimate(flops=int(us * 1.1e9) + 1000, bytes_accessed=1000, transcendentals=0),
    )(*args, *after)


def swap(values, axis, bit):
    return lax.ppermute(values, axis, [(i, i ^ bit) for i in range(lax.axis_size(axis))])


def axis_bits(axis):
    return [1 << k for k in range((lax.axis_size(axis) - 1).bit_length())]


def own_bit(axis, bit):
    return (lax.axis_index(axis) // bit) % 2


def chain(keep, send, order, count, rows, extra=(), between=None):
    for place, (axis, bit, _) in enumerate(order):
        received = swap(send, axis, bit)
        if place + 1 == len(order):
            return keep + received
        axis, bit, position = order[place + 1]
        grown = extra if place == 0 else ()
        count //= 2
        tail = keep.shape[0] - count * rows + (grown[0].shape[0] if grown else 0)
        out = shape_of(count // 2 * rows + tail, keep.shape[1], dtype=BF)
        keep, send = run(
            functools.partial(step_kernel, axis, bit, position, count, rows),
            "sum_step",
            (keep, received, *grown),
            (out, out),
            after=between(send) if between and place == 1 else (),
            limit=8,
            us=0.2,
        )


def step_kernel(axis, bit, position, count, rows, keep, received, *refs):
    *grown, next_keep, next_send = refs
    mine = (lax.axis_index(axis) // bit) % 2
    low = (1 << position) - 1
    for i in range(2):

        @pl.when(mine == i)
        def _():
            for s in range(count):
                span = slice(s * rows, (s + 1) * rows)
                at = ((s >> (position + 1)) << position | (s & low)) * rows
                target = next_keep if (s >> position) & 1 == i else next_send
                target[at : at + rows] = (keep[span].astype(F32) + received[span].astype(F32)).astype(BF)

    tails = []
    if keep.shape[0] > count * rows:
        tails.append(keep[count * rows :].astype(F32) + received[count * rows :].astype(F32))
    if grown:
        tails.append(sum(g[...].astype(F32) for g in grown))
    at = count // 2 * rows
    for tail in tails:
        for target in (next_keep, next_send):
            target[at : at + tail.shape[0]] = tail.astype(BF)
        at += tail.shape[0]


def gather(values, axis, bits):
    values = values[None]
    for bit in reversed(bits):
        other = swap(values, axis, bit)
        mine = own_bit(axis, bit)
        low = jnp.where(mine == 0, values, other)
        high = jnp.where(mine == 0, other, values)
        values = jnp.stack([low, high], axis=1).reshape(-1, *values.shape[1:])
    return values


def neighbours(first, last, axis):
    count = lax.axis_size(axis)
    forward = [(i, i + 1) for i in range(count - 1)]
    backward = [(i + 1, i) for i in range(count - 1)]
    return lax.ppermute(last, axis, forward), lax.ppermute(first, axis, backward)


def strip_kernel(center, top, bottom, first, last):
    height, breadth = center.shape[:2]
    for source, start in ((top, 0), (center, 3), (bottom, 3 + height)):
        values = source[...].astype(F32)
        rows = slice(start, start + source.shape[0])
        first[rows] = values[:, :PAD].astype(BF)
        last[rows] = values[:, breadth - PAD :].astype(BF)


def halo(center, rows, name, after=()):
    height, _, channels = center.shape
    top, bottom = rows
    strip = shape_of(height + 6, PAD, channels, dtype=BF)
    first, last = run(strip_kernel, name, (center, top, bottom), (strip, strip), after=after, limit=8)
    left, right = neighbours(first, last, "col")
    return center, top, bottom, left, right


def hold(kernel, name, args, outs, carried, **options):
    count = len(args)

    def inner(*refs):
        kernel(*refs[:count], *refs[count + 1 : count + 1 + len(outs)], *refs[count + 2 + len(outs) :])

    return run(
        inner,
        name,
        (*args, carried),
        (*outs, shape_of(*carried.shape, dtype=carried.dtype)),
        spaces={count: pl.ANY, ("out", len(outs)): pl.ANY},
        aliases={count: len(outs)},
        **options,
    )


def fill_frame(frame, parts):
    center, top, bottom, left, right = parts
    height, breadth = center.shape[:2]
    middle = slice(PAD, PAD + breadth)
    frame[0:3, middle] = top[...].astype(F32)
    frame[3 : 3 + height, middle] = center[...].astype(F32)
    frame[3 + height :, middle] = bottom[...].astype(F32)
    frame[:, :PAD] = left[...].astype(F32)
    frame[:, PAD + breadth :] = right[...].astype(F32)


def frame_scratch(center):
    height, breadth, channels = center.shape
    return pltpu.VMEM((height + 6, breadth + 2 * PAD, channels), F32)


def lane_tiles(channels):
    def over(step):
        def wrapped(index, carry):
            step(pl.ds(pl.multiple_of(index * 128, 128), 128))
            return carry

        lax.fori_loop(0, channels // 128, wrapped, 0)

    return over


def convolve(frame, taps, flip, out):
    height, breadth, channels = out.shape

    @lane_tiles(channels)
    def _(lanes):
        for column in range(0, breadth, 8):
            total = jnp.zeros((height, 8, 128), F32)
            for q in range(7):
                rows = frame[:, pl.ds(column + PAD - 3 + q, 8), lanes]
                for p in range(7):
                    a, b = (6 - p, 6 - q) if flip else (p, q)
                    total = total + rows[p : p + height] * taps[a, pl.ds(b, 1), lanes]
            out[:, pl.ds(column, 8), lanes] = total


def weight_sums(frame, grads, scale, out):
    height, breadth, channels = grads.shape

    @lane_tiles(channels)
    def _(lanes):
        for q in range(7):
            totals = [jnp.zeros((8, 128), F32)] * 7
            for column in range(0, breadth, 8):
                rows = frame[:, pl.ds(column + PAD - 3 + q, 8), lanes]
                grad = grads[:, pl.ds(column, 8), lanes]
                for p in range(7):
                    totals[p] = totals[p] + jnp.sum(rows[p : p + height] * grad, axis=0)
            for p in range(7):
                out[pl.ds(7 * p + q, 1), lanes] = scale * jnp.sum(totals[p], axis=0, keepdims=True)


def mean(values):
    return jnp.mean(values, axis=-1, keepdims=True)


def normalize(values):
    level = mean(values)
    inverse = lax.rsqrt(mean(values * values) - level * level + EPSILON)
    return (values - level) * inverse, inverse


def normalize_back(grads, unit_values, inverse):
    return (grads - mean(grads) - unit_values * mean(grads * unit_values)) * inverse


def dot(left, right):
    return jnp.dot(left, right, preferred_element_type=F32)


def dot_last(left, right):
    return lax.dot_general(left, right, (((1,), (1,)), ((), ())), preferred_element_type=F32)


def dot_first(left, right):
    return lax.dot_general(left, right, (((0,), (0,)), ((), ())), preferred_element_type=F32)


def over_rows(count, size):
    def over(step):
        def wrapped(index, carry):
            step(index, pl.ds(pl.multiple_of(index * size, size), size))
            return carry

        lax.fori_loop(0, count, wrapped, 0)

    return over


def fetch(sources, targets, semaphores):
    copies = [
        pltpu.make_async_copy(source, target, semaphores.at[i])
        for i, (source, target) in enumerate(zip(sources, targets))
    ]
    for copy in copies:
        copy.start()
    return copies


def load_kernel(*refs):
    *arrays, semaphores = refs
    count = len(arrays) // 2
    for copy in fetch(arrays[:count], arrays[count:], semaphores):
        copy.wait()


def front_kernel(
    center, top, bottom, left, right, taps, gain, layer_scale, merge_gain,
    expand, project, patch, wide_taps, wide_gain, cotangent, residual,
    early, unit_mixed, inverse_mixed, slope, branch, unit_summed, inverse_summed, section, first, last,
    expand_here, project_here, patch_here, wide_taps_here, wide_gain_here, cotangent_here, residual_here,
    frame, image, pairs, upward, semaphores,
):
    height, breadth, channels = center.shape
    hidden_width = expand.shape[1]
    pixels = height * breadth
    copies = fetch(
        (expand, project, patch, wide_taps, wide_gain, cotangent, residual),
        (expand_here, project_here, patch_here, wide_taps_here, wide_gain_here, cotangent_here, residual_here),
        semaphores,
    )
    fill_frame(frame, (center, top, bottom, left, right))
    convolve(frame, taps, False, image)
    at_normed = slice(hidden_width, hidden_width + channels)
    at_patches = slice(hidden_width + channels, hidden_width + 2 * channels)

    @over_rows(height, breadth)
    def _(y, rows):
        unit, inverse = normalize(image[y])
        unit_mixed[rows] = unit
        inverse_mixed[rows] = inverse
        early[rows, at_normed] = (unit * gain[...]).astype(BF)

    copies[0].wait()

    def chunk(index, carry):
        lanes = pl.ds(pl.multiple_of(index * CHUNK, CHUNK), CHUNK)
        upward[...] = dot(early[:, at_normed], expand_here[:, lanes])
        for start in range(0, pixels, 64):
            rows = slice(start, start + 64)
            value = upward[rows]
            cumulative = 0.5 + 0.5 * lax.erf(value * (1.0 / math.sqrt(2.0)))
            density = jnp.exp(-0.5 * value * value) * (1.0 / math.sqrt(2.0 * math.pi))
            early[rows, lanes] = (value * cumulative).astype(BF)
            slope[rows, lanes] = (cumulative + value * density).astype(BF)
        return carry

    lax.fori_loop(0, hidden_width // CHUNK, chunk, 0)
    copies[1].wait()
    branch[...] = dot(early[:, :hidden_width], project_here[...])

    @over_rows(height, breadth)
    def _(y, rows):
        summed = center[y].astype(F32) + layer_scale[...] * branch[rows]
        unit, inverse = normalize(summed)
        unit_summed[rows] = unit
        inverse_summed[rows] = inverse
        merged = unit * merge_gain[...]
        for k in range(channels // 128):
            pairs[k, y] = merged[:, k * 128 : (k + 1) * 128]

    quarter = pixels // 4
    for dy in range(2):
        for dx in range(2):
            j = 2 * dy + dx
            for y in range(height // 2):
                start = j * quarter + y * (breadth // 2)
                for k in range(channels // 128):
                    piece = pairs[k, 2 * y + dy, pl.ds(dx, breadth // 2, stride=2), :]
                    lane = hidden_width + channels + k * 128
                    early[start : start + breadth // 2, lane : lane + 128] = piece.astype(BF)
    copies[2].wait()
    total = dot(early[:quarter, at_patches], patch_here[:channels])
    for j in range(1, 4):
        total = total + dot(
            early[j * quarter : (j + 1) * quarter, at_patches],
            patch_here[j * channels : (j + 1) * channels],
        )
    total = total.reshape(section.shape)
    section[...] = total.astype(BF)
    first[...] = total[:3].astype(BF)
    last[...] = total[height // 2 - 3 :].astype(BF)
    for copy in copies[3:]:
        copy.wait()


def mixer_kernel(
    center, top, bottom, left, right, taps, gain, cotangent,
    grad, grad_half, first, last, gain_part,
    frame, image,
):
    height, breadth, channels = center.shape
    fill_frame(frame, (center, top, bottom, left, right))
    convolve(frame, taps, False, image)
    part = jnp.zeros((1, channels), F32)
    for y in range(height):
        unit, inverse = normalize(image[y])
        cot = cotangent[y].astype(F32)
        part = part + jnp.sum(cot * unit, axis=0, keepdims=True)
        value = normalize_back(cot * gain[...], unit, inverse)
        grad[y] = value
        narrow = value.astype(BF)
        grad_half[y] = narrow
        if y < 3:
            first[y] = narrow
        if y >= height - 3:
            last[y - (height - 3)] = narrow
    gain_part[...] = part


def weight_kernel(scale, center, top, bottom, left, right, grads, out, frame):
    fill_frame(frame, (center, top, bottom, left, right))
    weight_sums(frame, grads, scale, out)


def split_halves(values, start, keep, send):
    half = values.shape[1] // 2
    rows = slice(start, start + values.shape[0])
    core = lax.axis_index("col") % 2
    for i in range(2):

        @pl.when(core == i)
        def _():
            keep[rows] = values[:, i * half : (i + 1) * half]
            send[rows] = values[:, (1 - i) * half : (2 - i) * half]


def weight_pack_kernel(
    scale, center, top, bottom, left, right, grads, gain_part,
    keep, send, frame, wide_grads, packed,
):
    fill_frame(frame, (center, top, bottom, left, right))
    wide_grads[...] = grads[...].astype(F32)
    packed[...] = jnp.zeros(packed.shape, F32)
    weight_sums(frame, wide_grads, scale, packed)
    packed[49:50] = scale * gain_part[...]
    split_halves(packed[...].astype(BF), 0, keep, send)


def section_kernel(
    center, top, bottom, left, right, taps, residual,
    flat, keep, send,
    frame, image,
):
    height, breadth, channels = center.shape
    fill_frame(frame, (center, top, bottom, left, right))
    convolve(frame, taps, True, image)
    value = (image[...] + residual[...].astype(F32)).reshape(flat.shape).astype(BF)
    flat[...] = value
    blocks, _, width = keep.shape
    core = lax.axis_index("col") % 2
    for i in range(2):

        @pl.when(core == i)
        def _():
            for m in range(blocks):
                mine, other = (2 * m + i) * width, (2 * m + 1 - i) * width
                keep[m] = value[:, mine : mine + width]
                send[m] = value[:, other : other + width]


def merge_kernel(
    scale, scale_wide,
    flat, patch, unit_summed, inverse_summed, merge_gain, branch, layer_scale, wide_part, wide_gain,
    grad_summed, grad_branch, keep, send,
    pairs, packed, sums,
):
    tiles, height, breadth, _ = pairs.shape
    channels = 128 * tiles
    value = flat[...]
    for dy in range(2):
        for dx in range(2):
            j = 2 * dy + dx
            part = dot_last(value, patch[j * channels : (j + 1) * channels])
            part = part.reshape(height // 2, breadth // 2, channels)
            for y in range(height // 2):
                for k in range(tiles):
                    piece = part[y, :, k * 128 : (k + 1) * 128]
                    pairs[k, 2 * y + dy, pl.ds(dx, breadth // 2, stride=2), :] = piece
    sums[...] = jnp.zeros(sums.shape, F32)

    @over_rows(height, breadth)
    def _(y, rows):
        merged = jnp.concatenate([pairs[k, y] for k in range(tiles)], axis=1)
        unit = unit_summed[rows]
        sums[0:1] += jnp.sum(merged * unit, axis=0, keepdims=True)
        grad = normalize_back(merged * merge_gain[...], unit, inverse_summed[rows])
        grad_summed[rows] = grad
        sums[1:2] += jnp.sum(grad * branch[rows], axis=0, keepdims=True)
        grad_branch[rows] = (layer_scale[...] * grad).astype(BF)

    split_halves(grad_branch[...], 0, keep, send)
    packed[...] = jnp.zeros(packed.shape, F32)
    for i in range(2):
        columns = slice(i * channels, (i + 1) * channels)
        packed[49 * i : 49 + 49 * i] = wide_part[:, columns]
        packed[98 + i : 99 + i] = scale_wide * wide_gain[:, columns]
        packed[100 + i : 101 + i] = scale * sums[i : i + 1]
    split_halves(packed[...].astype(BF), grad_branch.shape[0], keep, send)


def back_kernel(
    grad_branch, project, slope, expand, unit_mixed, inverse_mixed, gain,
    keep, send, grad_mixed, first, last, gain_part,
    hidden, upward, normed,
):
    height, breadth, channels = grad_mixed.shape
    pixels, hidden_width = slope.shape

    def chunk(index, carry):
        span = pl.ds(pl.multiple_of(index * CHUNK, CHUNK), CHUNK)
        hidden[...] = dot_last(grad_branch[...], project[span])
        for start in range(0, pixels, 64):
            rows = slice(start, start + 64)
            upward[rows, span] = (hidden[rows] * slope[rows, span].astype(F32)).astype(BF)
        return carry

    lax.fori_loop(0, hidden_width // CHUNK, chunk, 0)
    normed[...] = dot_last(upward[...], expand[...])
    split_halves(upward[...], 0, keep, send)
    part = jnp.zeros((1, channels), F32)
    for y in range(height):
        rows = slice(y * breadth, (y + 1) * breadth)
        value = normed[rows]
        unit = unit_mixed[rows]
        part = part + jnp.sum(value * unit, axis=0, keepdims=True)
        narrow = normalize_back(value * gain[...], unit, inverse_mixed[rows]).astype(BF)
        grad_mixed[y] = narrow
        if y < 3:
            first[y] = narrow
        if y >= height - 3:
            last[y - (height - 3)] = narrow
    gain_part[...] = part


def patch_product_kernel(factor, slices, channels, early, early_other, own, other, *outs):
    upper_keep, upper_send, lower_keep, lower_send = outs
    blocks, quarter, _ = own.shape
    part = 4 * channels // slices // 2
    at_patches = early.shape[1] - channels
    lateral = (lax.axis_index("col") // 2) % 2
    vertical = lax.axis_index("row") % 2
    per = channels // (2 * part)
    for j in range(4):
        span = slice(j * quarter, (j + 1) * quarter)
        left = jnp.concatenate([early[span, at_patches:], early_other[span, at_patches:]], axis=0)
        for m in range(blocks):
            right = jnp.concatenate([own[m], other[m]], axis=0)
            value = (factor * dot_first(left, right)).astype(BF)
            for i in range(2):

                @pl.when(lateral == i)
                def _():
                    target = upper_keep if m % 2 == i else upper_send
                    for k in range(per):
                        at = (m // 2 * slices + j * per + k) * part
                        target[at : at + part] = value[2 * k * part : (2 * k + 1) * part]

                @pl.when(vertical == i)
                def _():
                    for k in range(per):
                        r = j * per + k
                        target = lower_keep if r % 2 == i else lower_send
                        at = (m * (slices // 2) + r // 2) * part
                        target[at : at + part] = value[(2 * k + 1) * part : (2 * k + 2) * part]


def store_slices(position, value, begin, offset, rows, pitch, keep, send):
    bit = (lax.axis_index("row") >> position) % 2
    low = (1 << position) - 1
    for i in range(2):

        @pl.when(bit == i)
        def _():
            for k in range(value.shape[0] // rows):
                r = begin + k
                target = keep if (r >> position) & 1 == i else send
                at = ((r >> (position + 1)) << position | (r & low)) * pitch + offset
                target[at : at + rows] = value[k * rows : (k + 1) * rows]


def project_product_kernel(factor, slices, early, early_other, own, other, keep, send):
    width = keep.shape[1]
    hidden_width = early.shape[1] - 4 * width
    pixels = early.shape[0]
    deep = hidden_width // slices
    right = jnp.concatenate([own[:pixels], other[:pixels]], axis=0)
    step = max(CHUNK, deep)
    for start in range(0, hidden_width, step):
        columns = slice(start, start + step)
        left = jnp.concatenate([early[:, columns], early_other[:, columns]], axis=0)
        value = (factor * dot_first(left, right)).astype(BF)
        store_slices(1, value, start // deep, 0, deep, deep, keep, send)
    tail = (own[pixels:].astype(F32) + other[pixels:].astype(F32)).astype(BF)
    at = slices // 2 * deep
    keep[at:] = tail
    send[at:] = tail


def expand_product_kernel(factor, slices, early, early_other, own, other, keep, send):
    width = keep.shape[1]
    channels = 2 * width
    hidden_width = early.shape[1] - 2 * channels
    shallow = channels // slices
    blocks = own.shape[1] // width
    columns = slice(hidden_width, hidden_width + channels)
    left = jnp.concatenate([early[:, columns], early_other[:, columns]], axis=0)
    for k in range(blocks):
        columns = slice(k * width, (k + 1) * width)
        right = jnp.concatenate([own[:, columns], other[:, columns]], axis=0)
        value = (factor * dot_first(left, right)).astype(BF)
        store_slices(0, value, 0, k * shallow, shallow, blocks * shallow, keep, send)


def finish_patch_kernel(own, other, out):
    blocks, _, width = own.shape
    core = lax.axis_index("col") % 2
    for i in range(2):

        @pl.when(core == i)
        def _():
            for m in range(blocks):
                a, b = (2 * m + i) * width, (2 * m + 1 - i) * width
                out[:, a : a + width] = own[m].astype(F32)
                out[:, b : b + width] = other[m].astype(F32)


def join_halves(own, other, start, out):
    half = own.shape[1]
    rows = slice(start, start + out.shape[0])
    core = lax.axis_index("col") % 2
    for i in range(2):

        @pl.when(core == i)
        def _():
            out[:, i * half : (i + 1) * half] = own[rows].astype(F32)
            out[:, (1 - i) * half : (2 - i) * half] = other[rows].astype(F32)


def finish_project_kernel(own, other, project, wide_taps, wide_gain, merge, layer, small):
    deep, channels = project.shape
    join_halves(own, other, 0, project)
    join_halves(own, other, deep, small)
    for i in range(2):
        columns = slice(i * channels, (i + 1) * channels)
        for p in range(7):
            start = 49 * i + 7 * p
            wide_taps[p, :, columns] = small[start : start + 7]
        wide_gain[:, columns] = small[98 + i : 99 + i]
    merge[...] = small[100:101]
    layer[...] = small[101:102]


def finish_expand_kernel(own, other, expand, taps, gain, small):
    shallow, hidden_width = expand.shape
    width = own.shape[1]
    blocks = hidden_width // (2 * width)
    core = lax.axis_index("col") % 2
    for i in range(2):

        @pl.when(core == i)
        def _():
            for k in range(blocks):
                rows = slice(k * shallow, (k + 1) * shallow)
                a, b = (i * blocks + k) * width, ((1 - i) * blocks + k) * width
                expand[:, a : a + width] = own[rows].astype(F32)
                expand[:, b : b + width] = other[rows].astype(F32)

    join_halves(own, other, blocks * shallow, small)
    for p in range(7):
        taps[p] = small[7 * p : 7 * p + 7]
    gain[...] = small[49:50]


def input_kernel(center, top, bottom, left, right, taps, grad_summed, out, frame, image):
    fill_frame(frame, (center, top, bottom, left, right))
    convolve(frame, taps, True, image)
    out[...] = (image[...] + grad_summed[...].reshape(image.shape)).astype(BF)


def body(
    block_input,
    kernel_three,
    gain_three,
    expand_weight,
    project_weight,
    layer_scale,
    merge_gain,
    patch_weight,
    kernel_four,
    gain_four,
    normed_cotangent,
    residual_cotangent,
):
    _, height, breadth, channels = block_input.shape
    hidden_width = expand_weight.shape[1]
    wide = patch_weight.shape[1]
    pixels = height * breadth
    quarter = pixels // 4
    rows4, cols4 = height // 2, breadth // 2
    row_count = lax.axis_size("row")
    col_count = lax.axis_size("col")
    scale_three = 1.0 / math.sqrt(pixels * row_count * col_count)
    scale_four = 1.0 / math.sqrt(quarter * row_count * col_count)
    center = block_input[0]
    gain_three, layer_scale, merge_gain, gain_four = (
        v[None] for v in (gain_three, layer_scale, merge_gain, gain_four)
    )
    dma = pltpu.SemaphoreType.DMA
    half = channels // 2
    hbm = pltpu.HBM

    def like(array):
        return shape_of(*array.shape, dtype=array.dtype)

    edge = shape_of(3, breadth, channels, dtype=BF)
    rows_input = neighbours(center[:3], center[height - 3 :], "row")
    inputs = (center, kernel_three, gain_three, layer_scale, merge_gain)
    center, taps_three, gain_three, layer_scale, merge_gain = run(
        load_kernel,
        "load",
        inputs,
        tuple(map(like, inputs)),
        scratch=(dma((5,)),),
        spaces=dict.fromkeys(range(5), hbm),
        after=rows_input[:1],
        limit=4,
        us=2,
    )
    framed = halo(center, rows_input, "strips_input")
    inputs = (
        expand_weight, project_weight, patch_weight, kernel_four, gain_four,
        normed_cotangent[0], residual_cotangent[0],
    )
    edge_four = shape_of(3, cols4, wide, dtype=BF)
    (
        early, unit_mixed, inverse_mixed, slope, branch, unit_summed, inverse_summed,
        section, first, last,
        expand_weight, project_weight, patch_weight, taps_four, gain_four, cotangent, residual,
    ) = run(
        front_kernel,
        "front",
        (*framed, taps_three, gain_three, layer_scale, merge_gain, *inputs),
        (
            shape_of(pixels, hidden_width + 2 * channels, dtype=BF),
            shape_of(pixels, channels),
            shape_of(pixels, 1),
            shape_of(pixels, hidden_width, dtype=BF),
            shape_of(pixels, channels),
            shape_of(pixels, channels),
            shape_of(pixels, 1),
            shape_of(rows4, cols4, wide, dtype=BF),
            edge_four,
            edge_four,
            *map(like, inputs),
        ),
        scratch=(
            frame_scratch(center),
            pltpu.VMEM((height, breadth, channels), F32),
            pltpu.VMEM((channels // 128, height, breadth, 128), F32),
            pltpu.VMEM((pixels, CHUNK), F32),
            dma((7,)),
        ),
        spaces=dict.fromkeys(range(9, 16), hbm),
        limit=28,
        us=12,
    )

    framed_four = halo(section, neighbours(first, last, "row"), "strips_section")
    mixer_image = pltpu.VMEM((rows4, cols4, wide), F32)
    grad_four, grad_four_half, first, last, gain_four_part = run(
        mixer_kernel,
        "mixer",
        (*framed_four, taps_four, gain_four, cotangent),
        (
            shape_of(rows4, cols4, wide),
            shape_of(rows4, cols4, wide, dtype=BF),
            edge_four,
            edge_four,
            shape_of(1, wide),
        ),
        scratch=(frame_scratch(section), mixer_image),
        limit=12,
        us=3,
    )
    rows_grad = neighbours(first, last, "row")
    (kernel_four_part,) = run(
        functools.partial(weight_kernel, scale_four),
        "mixer_weights",
        (*framed_four, grad_four),
        (shape_of(49, wide),),
        scratch=(frame_scratch(section),),
        after=rows_grad[:1],
        limit=12,
        us=3,
    )
    framed_grad = halo(grad_four_half, rows_grad, "strips_mixer", after=(kernel_four_part,))
    block_count = col_count // 2
    block = wide // col_count
    blocked = shape_of(block_count, quarter, block, dtype=BF)
    flat, flat_keep, flat_send, early = hold(
        section_kernel,
        "section_grad",
        (*framed_grad, taps_four, residual),
        (shape_of(quarter, wide, dtype=BF), blocked, blocked),
        early,
        scratch=(frame_scratch(section), mixer_image),
        limit=12,
        us=3,
    )

    flat_other = swap(flat_send, "col", 1)
    early_other = swap(early, "col", 1)
    split = shape_of(pixels + 112, half, dtype=BF)
    grad_summed, grad_branch, branch_keep, branch_send = run(
        functools.partial(merge_kernel, scale_three, scale_four),
        "merge_back",
        (
            flat, patch_weight, unit_summed, inverse_summed, merge_gain, branch, layer_scale,
            kernel_four_part, gain_four_part,
        ),
        (shape_of(pixels, channels), shape_of(pixels, channels, dtype=BF), split, split),
        scratch=(
            pltpu.VMEM((channels // 128, height, breadth, 128), F32),
            pltpu.VMEM((112, channels), F32),
            pltpu.VMEM((8, channels), F32),
        ),
        limit=16,
        us=0.8,
    )
    branch_other = swap(branch_send, "col", 1)
    patch_part = shape_of(block_count // 2 * 2 * channels, block, dtype=BF)
    upper_keep, upper_send, lower_keep, lower_send = run(
        functools.partial(patch_product_kernel, scale_four, row_count, channels),
        "patch_product",
        (early, early_other, flat_keep, flat_other),
        (patch_part,) * 4,
        limit=16,
        us=1,
    )
    deep, shallow = hidden_width // row_count, channels // row_count
    groups = hidden_width // channels
    project_half = shape_of(row_count // 2 * deep + 112, half, dtype=BF)
    upward_half = shape_of(pixels, hidden_width // 2, dtype=BF)
    upward_keep, upward_send, grad_mixed, first, last, gain_part = run(
        back_kernel,
        "mlp_back",
        (grad_branch, project_weight, slope, expand_weight, unit_mixed, inverse_mixed, gain_three),
        (
            upward_half,
            upward_half,
            shape_of(height, breadth, channels, dtype=BF),
            edge,
            edge,
            shape_of(1, channels),
        ),
        scratch=(
            pltpu.VMEM((pixels, CHUNK), F32),
            pltpu.VMEM((pixels, hidden_width), BF),
            pltpu.VMEM((pixels, channels), F32),
        ),
        after=(upper_send,),
        limit=16,
        us=1.2,
    )
    rows_back = neighbours(first, last, "row")
    upward_other = swap(upward_send, "col", 1)
    project_keep, project_send = run(
        functools.partial(project_product_kernel, scale_three, row_count),
        "project_product",
        (early, early_other, branch_keep, branch_other),
        (project_half, project_half),
        after=(upward_send,),
        limit=16,
        us=0.9,
    )
    expand_half = shape_of(row_count // 2 * groups * shallow, half, dtype=BF)
    expand_keep, expand_send = run(
        functools.partial(expand_product_kernel, scale_three, row_count),
        "expand_product",
        (early, early_other, upward_keep, upward_other),
        (expand_half, expand_half),
        after=(project_send,),
        limit=16,
        us=0.6,
    )
    framed_back = halo(grad_mixed, rows_back, "strips_back", after=(expand_send,))
    small_half = shape_of(64, half, dtype=BF)
    small_keep, small_send = run(
        functools.partial(weight_pack_kernel, scale_three),
        "block_weights",
        (*framed, grad_mixed, gain_part),
        (small_half, small_half),
        scratch=(
            frame_scratch(center),
            pltpu.VMEM((height, breadth, channels), F32),
            pltpu.VMEM((64, channels), F32),
        ),
        after=(*framed_back[1:3], expand_send),
        limit=12,
        us=1.8,
    )
    def finish_input(sent):
        return run(
            input_kernel,
            "input_grad",
            (*framed_back, taps_three, grad_summed),
            (shape_of(height, breadth, channels, dtype=BF),),
            scratch=(frame_scratch(center), pltpu.VMEM((height, breadth, channels), F32)),
            after=(small_keep, sent),
            limit=12,
            us=2,
        )

    row_bits, col_bits = axis_bits("row"), axis_bits("col")
    outer = len(row_bits)
    low_first = [("row", bit, 0) for bit in row_bits]
    lateral = [("col", bit, outer) for bit in col_bits[1:]]
    upper_order = lateral + low_first
    lower_order = low_first[:1] + [("col", bit, outer - 1) for bit in col_bits[1:]] + low_first[1:]
    part_rows = 2 * channels // row_count
    patch_sum = jnp.concatenate(
        [
            chain(upper_keep, upper_send, upper_order, block_count * row_count, part_rows),
            chain(lower_keep, lower_send, lower_order, block_count * row_count, part_rows),
        ]
    )
    patch_sum = gather(patch_sum, "col", col_bits[1:])
    (patch_grad,) = run(
        finish_patch_kernel,
        "finish_patch",
        (patch_sum, swap(patch_sum, "col", 1)),
        (shape_of(4 * channels // row_count, wide),),
        limit=8,
    )

    def share(total):
        for bit in col_bits[1:]:
            total = total + swap(total, "col", bit)
        return total, swap(total, "col", 1)

    project_order = [("row", row_bits[1], 1), low_first[0], *low_first[2:]]
    vector, wide_vector = shape_of(1, channels), shape_of(1, wide)
    project_grad, wide_taps, wide_gain, merge_sum, layer_sum = run(
        finish_project_kernel,
        "finish_project",
        share(chain(project_keep, project_send, project_order, row_count, deep)),
        (shape_of(deep, channels), shape_of(7, 7, wide), wide_vector, vector, vector),
        scratch=(pltpu.VMEM((112, channels), F32),),
        limit=8,
    )
    small = small_keep + swap(small_send, "col", 1)
    pair = (small, swap(small, "row", 1))
    input_grad = []

    def between(sent):
        input_grad.extend(finish_input(sent))
        return input_grad

    expand_sum = chain(expand_keep, expand_send, low_first, row_count, groups * shallow, pair, between)
    expand_grad, taps_sum, gain_sum = run(
        finish_expand_kernel,
        "finish_expand",
        share(expand_sum),
        (shape_of(shallow, hidden_width), shape_of(7, 7, channels), vector),
        scratch=(pltpu.VMEM((64, channels), F32),),
        limit=8,
    )
    return (
        input_grad[0][None],
        taps_sum,
        gain_sum[0],
        expand_grad,
        project_grad,
        layer_sum[0],
        merge_sum[0],
        patch_grad,
        wide_taps,
        wide_gain[0],
    )


def solution(mesh):
    pixels = P(None, "row", "col", None)
    return jax.shard_map(
        body,
        mesh=mesh,
        in_specs=(pixels,) + (P(),) * 9 + (pixels, pixels),
        out_specs=(pixels, P(), P(), P("row", None), P("row", None), P(), P(), P("row", None), P(), P()),
        check_vma=False,
    )
```

```python
import functools
import math

import jax
import jax.numpy as jnp
from jax import lax
from jax.experimental import pallas as pl
from jax.experimental.pallas import tpu as pltpu
from jax.sharding import PartitionSpec as P

EPSILON = 1e-06
BF = jnp.bfloat16
F32 = jnp.float32
MIB = 1 << 20
PAD = 8
CHUNK = 256


def shape_of(*dims, dtype=F32):
    return jax.ShapeDtypeStruct(dims, dtype)


def run(kernel, name, args, outs, scratch=(), spaces=None, after=(), aliases=None, limit=24, us=0.0):
    spaces = spaces or {}
    count, extra = len(args), len(after)

    def spec(place):
        return pl.BlockSpec(memory_space=spaces.get(place, pltpu.VMEM))

    def inner(*refs):
        kernel(*refs[:count], *refs[count + extra :])

    return pl.pallas_call(
        inner,
        name=name,
        out_shape=outs,
        in_specs=[spec(i) for i in range(count)] + [pl.BlockSpec(memory_space=pl.ANY)] * extra,
        out_specs=[spec(("out", i)) for i in range(len(outs))],
        scratch_shapes=list(scratch),
        input_output_aliases=aliases or {},
        compiler_params=pltpu.CompilerParams(vmem_limit_bytes=limit * MIB),
        cost_estimate=pl.CostEstimate(flops=int(us * 1.1e9) + 1000, bytes_accessed=1000, transcendentals=0),
    )(*args, *after)


def swap(values, axis, bit):
    return lax.ppermute(values, axis, [(i, i ^ bit) for i in range(lax.axis_size(axis))])


def axis_bits(axis):
    return [1 << k for k in range((lax.axis_size(axis) - 1).bit_length())]


def own_bit(axis, bit):
    return (lax.axis_index(axis) // bit) % 2


def chain(keep, send, order, count, rows, extra=(), between=None):
    for place, (axis, bit, _) in enumerate(order):
        received = swap(send, axis, bit)
        if place + 1 == len(order):
            return keep + received
        axis, bit, position = order[place + 1]
        grown = extra if place == 0 else ()
        count //= 2
        tail = keep.shape[0] - count * rows + (grown[0].shape[0] if grown else 0)
        out = shape_of(count // 2 * rows + tail, keep.shape[1], dtype=BF)
        keep, send = run(
            functools.partial(step_kernel, axis, bit, position, count, rows),
            "sum_step",
            (keep, received, *grown),
            (out, out),
            after=between(send) if between and place == 1 else (),
            limit=8,
            us=0.2,
        )


def step_kernel(axis, bit, position, count, rows, keep, received, *refs):
    *grown, next_keep, next_send = refs
    mine = (lax.axis_index(axis) // bit) % 2
    low = (1 << position) - 1
    for i in range(2):

        @pl.when(mine == i)
        def _():
            for s in range(count):
                span = slice(s * rows, (s + 1) * rows)
                at = ((s >> (position + 1)) << position | (s & low)) * rows
                target = next_keep if (s >> position) & 1 == i else next_send
                target[at : at + rows] = (keep[span].astype(F32) + received[span].astype(F32)).astype(BF)

    tails = []
    if keep.shape[0] > count * rows:
        tails.append(keep[count * rows :].astype(F32) + received[count * rows :].astype(F32))
    if grown:
        tails.append(sum(g[...].astype(F32) for g in grown))
    at = count // 2 * rows
    for tail in tails:
        for target in (next_keep, next_send):
            target[at : at + tail.shape[0]] = tail.astype(BF)
        at += tail.shape[0]


def gather(values, axis, bits):
    values = values[None]
    for bit in reversed(bits):
        other = swap(values, axis, bit)
        mine = own_bit(axis, bit)
        low = jnp.where(mine == 0, values, other)
        high = jnp.where(mine == 0, other, values)
        values = jnp.stack([low, high], axis=1).reshape(-1, *values.shape[1:])
    return values


def neighbours(first, last, axis):
    count = lax.axis_size(axis)
    forward = [(i, i + 1) for i in range(count - 1)]
    backward = [(i + 1, i) for i in range(count - 1)]
    return lax.ppermute(last, axis, forward), lax.ppermute(first, axis, backward)


def strip_kernel(center, top, bottom, first, last):
    height, breadth = center.shape[:2]
    for source, start in ((top, 0), (center, 3), (bottom, 3 + height)):
        values = source[...].astype(F32)
        rows = slice(start, start + source.shape[0])
        first[rows] = values[:, :PAD].astype(BF)
        last[rows] = values[:, breadth - PAD :].astype(BF)


def halo(center, rows, name, after=()):
    height, _, channels = center.shape
    top, bottom = rows
    strip = shape_of(height + 6, PAD, channels, dtype=BF)
    first, last = run(strip_kernel, name, (center, top, bottom), (strip, strip), after=after, limit=8)
    left, right = neighbours(first, last, "col")
    return center, top, bottom, left, right


def hold(kernel, name, args, outs, carried, **options):
    count = len(args)

    def inner(*refs):
        kernel(*refs[:count], *refs[count + 1 : count + 1 + len(outs)], *refs[count + 2 + len(outs) :])

    return run(
        inner,
        name,
        (*args, carried),
        (*outs, shape_of(*carried.shape, dtype=carried.dtype)),
        spaces={count: pl.ANY, ("out", len(outs)): pl.ANY},
        aliases={count: len(outs)},
        **options,
    )


def fill_frame(frame, parts):
    center, top, bottom, left, right = parts
    height, breadth = center.shape[:2]
    middle = slice(PAD, PAD + breadth)
    frame[0:3, middle] = top[...].astype(F32)
    frame[3 : 3 + height, middle] = center[...].astype(F32)
    frame[3 + height :, middle] = bottom[...].astype(F32)
    frame[:, :PAD] = left[...].astype(F32)
    frame[:, PAD + breadth :] = right[...].astype(F32)


def frame_scratch(center):
    height, breadth, channels = center.shape
    return pltpu.VMEM((height + 6, breadth + 2 * PAD, channels), F32)


def lane_tiles(channels):
    def over(step):
        def wrapped(index, carry):
            step(pl.ds(pl.multiple_of(index * 128, 128), 128))
            return carry

        lax.fori_loop(0, channels // 128, wrapped, 0)

    return over


def convolve(frame, taps, flip, out):
    height, breadth, channels = out.shape

    @lane_tiles(channels)
    def _(lanes):
        for column in range(0, breadth, 8):
            total = jnp.zeros((height, 8, 128), F32)
            for q in range(7):
                rows = frame[:, pl.ds(column + PAD - 3 + q, 8), lanes]
                for p in range(7):
                    a, b = (6 - p, 6 - q) if flip else (p, q)
                    total = total + rows[p : p + height] * taps[a, pl.ds(b, 1), lanes]
            out[:, pl.ds(column, 8), lanes] = total


def weight_sums(frame, grads, scale, out):
    height, breadth, channels = grads.shape

    @lane_tiles(channels)
    def _(lanes):
        for q in range(7):
            totals = [jnp.zeros((8, 128), F32)] * 7
            for column in range(0, breadth, 8):
                rows = frame[:, pl.ds(column + PAD - 3 + q, 8), lanes]
                grad = grads[:, pl.ds(column, 8), lanes]
                for p in range(7):
                    totals[p] = totals[p] + jnp.sum(rows[p : p + height] * grad, axis=0)
            for p in range(7):
                out[pl.ds(7 * p + q, 1), lanes] = scale * jnp.sum(totals[p], axis=0, keepdims=True)


def mean(values):
    return jnp.mean(values, axis=-1, keepdims=True)


def normalize(values):
    level = mean(values)
    inverse = lax.rsqrt(mean(values * values) - level * level + EPSILON)
    return (values - level) * inverse, inverse


def normalize_back(grads, unit_values, inverse):
    return (grads - mean(grads) - unit_values * mean(grads * unit_values)) * inverse


def dot(left, right):
    return jnp.dot(left, right, preferred_element_type=F32)


def dot_last(left, right):
    return lax.dot_general(left, right, (((1,), (1,)), ((), ())), preferred_element_type=F32)


def dot_first(left, right):
    return lax.dot_general(left, right, (((0,), (0,)), ((), ())), preferred_element_type=F32)


def over_rows(count, size):
    def over(step):
        def wrapped(index, carry):
            step(index, pl.ds(pl.multiple_of(index * size, size), size))
            return carry

        lax.fori_loop(0, count, wrapped, 0)

    return over


def fetch(sources, targets, semaphores):
    copies = [
        pltpu.make_async_copy(source, target, semaphores.at[i])
        for i, (source, target) in enumerate(zip(sources, targets))
    ]
    for copy in copies:
        copy.start()
    return copies


def load_kernel(*refs):
    *arrays, semaphores = refs
    count = len(arrays) // 2
    for copy in fetch(arrays[:count], arrays[count:], semaphores):
        copy.wait()


def front_kernel(
    center, top, bottom, left, right, taps, gain, layer_scale, merge_gain,
    expand, project, patch, wide_taps, wide_gain, cotangent, residual,
    early, unit_mixed, inverse_mixed, slope, branch, unit_summed, inverse_summed, section, first, last,
    expand_here, project_here, patch_here, wide_taps_here, wide_gain_here, cotangent_here, residual_here,
    frame, image, pairs, upward, semaphores,
):
    height, breadth, channels = center.shape
    hidden_width = expand.shape[1]
    pixels = height * breadth
    copies = fetch(
        (expand, project, patch, wide_taps, wide_gain, cotangent, residual),
        (expand_here, project_here, patch_here, wide_taps_here, wide_gain_here, cotangent_here, residual_here),
        semaphores,
    )
    fill_frame(frame, (center, top, bottom, left, right))
    convolve(frame, taps, False, image)
    at_normed = slice(hidden_width, hidden_width + channels)
    at_patches = slice(hidden_width + channels, hidden_width + 2 * channels)

    @over_rows(height, breadth)
    def _(y, rows):
        unit, inverse = normalize(image[y])
        unit_mixed[rows] = unit
        inverse_mixed[rows] = inverse
        early[rows, at_normed] = (unit * gain[...]).astype(BF)

    copies[0].wait()

    def chunk(index, carry):
        lanes = pl.ds(pl.multiple_of(index * CHUNK, CHUNK), CHUNK)
        upward[...] = dot(early[:, at_normed], expand_here[:, lanes])
        for start in range(0, pixels, 64):
            rows = slice(start, start + 64)
            value = upward[rows]
            cumulative = 0.5 + 0.5 * lax.erf(value * (1.0 / math.sqrt(2.0)))
            density = jnp.exp(-0.5 * value * value) * (1.0 / math.sqrt(2.0 * math.pi))
            early[rows, lanes] = (value * cumulative).astype(BF)
            slope[rows, lanes] = (cumulative + value * density).astype(BF)
        return carry

    lax.fori_loop(0, hidden_width // CHUNK, chunk, 0)
    copies[1].wait()
    branch[...] = dot(early[:, :hidden_width], project_here[...])

    @over_rows(height, breadth)
    def _(y, rows):
        summed = center[y].astype(F32) + layer_scale[...] * branch[rows]
        unit, inverse = normalize(summed)
        unit_summed[rows] = unit
        inverse_summed[rows] = inverse
        merged = unit * merge_gain[...]
        for k in range(channels // 128):
            pairs[k, y] = merged[:, k * 128 : (k + 1) * 128]

    quarter = pixels // 4
    for dy in range(2):
        for dx in range(2):
            j = 2 * dy + dx
            for y in range(height // 2):
                start = j * quarter + y * (breadth // 2)
                for k in range(channels // 128):
                    piece = pairs[k, 2 * y + dy, pl.ds(dx, breadth // 2, stride=2), :]
                    lane = hidden_width + channels + k * 128
                    early[start : start + breadth // 2, lane : lane + 128] = piece.astype(BF)
    copies[2].wait()
    total = dot(early[:quarter, at_patches], patch_here[:channels])
    for j in range(1, 4):
        total = total + dot(
            early[j * quarter : (j + 1) * quarter, at_patches],
            patch_here[j * channels : (j + 1) * channels],
        )
    total = total.reshape(section.shape)
    section[...] = total.astype(BF)
    first[...] = total[:3].astype(BF)
    last[...] = total[height // 2 - 3 :].astype(BF)
    for copy in copies[3:]:
        copy.wait()


def mixer_kernel(
    center, top, bottom, left, right, taps, gain, cotangent,
    grad, grad_half, first, last, gain_part,
    frame, image,
):
    height, breadth, channels = center.shape
    fill_frame(frame, (center, top, bottom, left, right))
    convolve(frame, taps, False, image)
    part = jnp.zeros((1, channels), F32)
    for y in range(height):
        unit, inverse = normalize(image[y])
        cot = cotangent[y].astype(F32)
        part = part + jnp.sum(cot * unit, axis=0, keepdims=True)
        value = normalize_back(cot * gain[...], unit, inverse)
        grad[y] = value
        narrow = value.astype(BF)
        grad_half[y] = narrow
        if y < 3:
            first[y] = narrow
        if y >= height - 3:
            last[y - (height - 3)] = narrow
    gain_part[...] = part


def weight_kernel(scale, center, top, bottom, left, right, grads, out, frame):
    fill_frame(frame, (center, top, bottom, left, right))
    weight_sums(frame, grads, scale, out)


def split_halves(values, start, keep, send):
    half = values.shape[1] // 2
    rows = slice(start, start + values.shape[0])
    core = lax.axis_index("col") % 2
    for i in range(2):

        @pl.when(core == i)
        def _():
            keep[rows] = values[:, i * half : (i + 1) * half]
            send[rows] = values[:, (1 - i) * half : (2 - i) * half]


def weight_pack_kernel(
    scale, center, top, bottom, left, right, grads, gain_part,
    keep, send, frame, wide_grads, packed,
):
    fill_frame(frame, (center, top, bottom, left, right))
    wide_grads[...] = grads[...].astype(F32)
    packed[...] = jnp.zeros(packed.shape, F32)
    weight_sums(frame, wide_grads, scale, packed)
    packed[49:50] = scale * gain_part[...]
    split_halves(packed[...].astype(BF), 0, keep, send)


def section_kernel(
    center, top, bottom, left, right, taps, residual,
    flat, keep, send,
    frame, image,
):
    height, breadth, channels = center.shape
    fill_frame(frame, (center, top, bottom, left, right))
    convolve(frame, taps, True, image)
    value = (image[...] + residual[...].astype(F32)).reshape(flat.shape).astype(BF)
    flat[...] = value
    blocks, _, width = keep.shape
    core = lax.axis_index("col") % 2
    for i in range(2):

        @pl.when(core == i)
        def _():
            for m in range(blocks):
                mine, other = (2 * m + i) * width, (2 * m + 1 - i) * width
                keep[m] = value[:, mine : mine + width]
                send[m] = value[:, other : other + width]


def merge_kernel(
    scale, scale_wide,
    flat, patch, unit_summed, inverse_summed, merge_gain, branch, layer_scale, wide_part, wide_gain,
    grad_summed, grad_branch, keep, send,
    pairs, packed, sums,
):
    tiles, height, breadth, _ = pairs.shape
    channels = 128 * tiles
    value = flat[...]
    for dy in range(2):
        for dx in range(2):
            j = 2 * dy + dx
            part = dot_last(value, patch[j * channels : (j + 1) * channels])
            part = part.reshape(height // 2, breadth // 2, channels)
            for y in range(height // 2):
                for k in range(tiles):
                    piece = part[y, :, k * 128 : (k + 1) * 128]
                    pairs[k, 2 * y + dy, pl.ds(dx, breadth // 2, stride=2), :] = piece
    sums[...] = jnp.zeros(sums.shape, F32)

    @over_rows(height, breadth)
    def _(y, rows):
        merged = jnp.concatenate([pairs[k, y] for k in range(tiles)], axis=1)
        unit = unit_summed[rows]
        sums[0:1] += jnp.sum(merged * unit, axis=0, keepdims=True)
        grad = normalize_back(merged * merge_gain[...], unit, inverse_summed[rows])
        grad_summed[rows] = grad
        sums[1:2] += jnp.sum(grad * branch[rows], axis=0, keepdims=True)
        grad_branch[rows] = (layer_scale[...] * grad).astype(BF)

    split_halves(grad_branch[...], 0, keep, send)
    packed[...] = jnp.zeros(packed.shape, F32)
    for i in range(2):
        columns = slice(i * channels, (i + 1) * channels)
        packed[49 * i : 49 + 49 * i] = wide_part[:, columns]
        packed[98 + i : 99 + i] = scale_wide * wide_gain[:, columns]
        packed[100 + i : 101 + i] = scale * sums[i : i + 1]
    split_halves(packed[...].astype(BF), grad_branch.shape[0], keep, send)


def back_kernel(
    grad_branch, project, slope, expand, unit_mixed, inverse_mixed, gain,
    keep, send, grad_mixed, first, last, gain_part,
    hidden, upward, normed,
):
    height, breadth, channels = grad_mixed.shape
    pixels, hidden_width = slope.shape

    def chunk(index, carry):
        span = pl.ds(pl.multiple_of(index * CHUNK, CHUNK), CHUNK)
        hidden[...] = dot_last(grad_branch[...], project[span])
        for start in range(0, pixels, 64):
            rows = slice(start, start + 64)
            upward[rows, span] = (hidden[rows] * slope[rows, span].astype(F32)).astype(BF)
        return carry

    lax.fori_loop(0, hidden_width // CHUNK, chunk, 0)
    normed[...] = dot_last(upward[...], expand[...])
    split_halves(upward[...], 0, keep, send)
    part = jnp.zeros((1, channels), F32)
    for y in range(height):
        rows = slice(y * breadth, (y + 1) * breadth)
        value = normed[rows]
        unit = unit_mixed[rows]
        part = part + jnp.sum(value * unit, axis=0, keepdims=True)
        narrow = normalize_back(value * gain[...], unit, inverse_mixed[rows]).astype(BF)
        grad_mixed[y] = narrow
        if y < 3:
            first[y] = narrow
        if y >= height - 3:
            last[y - (height - 3)] = narrow
    gain_part[...] = part


def patch_product_kernel(factor, slices, channels, early, early_other, own, other, *outs):
    upper_keep, upper_send, lower_keep, lower_send = outs
    blocks, quarter, _ = own.shape
    part = 4 * channels // slices // 2
    at_patches = early.shape[1] - channels
    lateral = (lax.axis_index("col") // 2) % 2
    vertical = lax.axis_index("row") % 2
    per = channels // (2 * part)
    for j in range(4):
        span = slice(j * quarter, (j + 1) * quarter)
        left = jnp.concatenate([early[span, at_patches:], early_other[span, at_patches:]], axis=0)
        for m in range(blocks):
            right = jnp.concatenate([own[m], other[m]], axis=0)
            value = (factor * dot_first(left, right)).astype(BF)
            for i in range(2):

                @pl.when(lateral == i)
                def _():
                    target = upper_keep if m % 2 == i else upper_send
                    for k in range(per):
                        at = (m // 2 * slices + j * per + k) * part
                        target[at : at + part] = value[2 * k * part : (2 * k + 1) * part]

                @pl.when(vertical == i)
                def _():
                    for k in range(per):
                        r = j * per + k
                        target = lower_keep if r % 2 == i else lower_send
                        at = (m * (slices // 2) + r // 2) * part
                        target[at : at + part] = value[(2 * k + 1) * part : (2 * k + 2) * part]


def store_slices(position, value, begin, offset, rows, pitch, keep, send):
    bit = (lax.axis_index("row") >> position) % 2
    low = (1 << position) - 1
    for i in range(2):

        @pl.when(bit == i)
        def _():
            for k in range(value.shape[0] // rows):
                r = begin + k
                target = keep if (r >> position) & 1 == i else send
                at = ((r >> (position + 1)) << position | (r & low)) * pitch + offset
                target[at : at + rows] = value[k * rows : (k + 1) * rows]


def project_product_kernel(factor, slices, early, early_other, own, other, keep, send):
    width = keep.shape[1]
    hidden_width = early.shape[1] - 4 * width
    pixels = early.shape[0]
    deep = hidden_width // slices
    right = jnp.concatenate([own[:pixels], other[:pixels]], axis=0)
    step = max(CHUNK, deep)
    for start in range(0, hidden_width, step):
        columns = slice(start, start + step)
        left = jnp.concatenate([early[:, columns], early_other[:, columns]], axis=0)
        value = (factor * dot_first(left, right)).astype(BF)
        store_slices(1, value, start // deep, 0, deep, deep, keep, send)
    tail = (own[pixels:].astype(F32) + other[pixels:].astype(F32)).astype(BF)
    at = slices // 2 * deep
    keep[at:] = tail
    send[at:] = tail


def expand_product_kernel(factor, slices, early, early_other, own, other, keep, send):
    width = keep.shape[1]
    channels = 2 * width
    hidden_width = early.shape[1] - 2 * channels
    shallow = channels // slices
    blocks = own.shape[1] // width
    columns = slice(hidden_width, hidden_width + channels)
    left = jnp.concatenate([early[:, columns], early_other[:, columns]], axis=0)
    for k in range(blocks):
        columns = slice(k * width, (k + 1) * width)
        right = jnp.concatenate([own[:, columns], other[:, columns]], axis=0)
        value = (factor * dot_first(left, right)).astype(BF)
        store_slices(0, value, 0, k * shallow, shallow, blocks * shallow, keep, send)


def finish_patch_kernel(own, other, out):
    blocks, _, width = own.shape
    core = lax.axis_index("col") % 2
    for i in range(2):

        @pl.when(core == i)
        def _():
            for m in range(blocks):
                a, b = (2 * m + i) * width, (2 * m + 1 - i) * width
                out[:, a : a + width] = own[m].astype(F32)
                out[:, b : b + width] = other[m].astype(F32)


def join_halves(own, other, start, out):
    half = own.shape[1]
    rows = slice(start, start + out.shape[0])
    core = lax.axis_index("col") % 2
    for i in range(2):

        @pl.when(core == i)
        def _():
            out[:, i * half : (i + 1) * half] = own[rows].astype(F32)
            out[:, (1 - i) * half : (2 - i) * half] = other[rows].astype(F32)


def finish_project_kernel(own, other, project, wide_taps, wide_gain, merge, layer, small):
    deep, channels = project.shape
    join_halves(own, other, 0, project)
    join_halves(own, other, deep, small)
    for i in range(2):
        columns = slice(i * channels, (i + 1) * channels)
        for p in range(7):
            start = 49 * i + 7 * p
            wide_taps[p, :, columns] = small[start : start + 7]
        wide_gain[:, columns] = small[98 + i : 99 + i]
    merge[...] = small[100:101]
    layer[...] = small[101:102]


def finish_expand_kernel(own, other, expand, taps, gain, small):
    shallow, hidden_width = expand.shape
    width = own.shape[1]
    blocks = hidden_width // (2 * width)
    core = lax.axis_index("col") % 2
    for i in range(2):

        @pl.when(core == i)
        def _():
            for k in range(blocks):
                rows = slice(k * shallow, (k + 1) * shallow)
                a, b = (i * blocks + k) * width, ((1 - i) * blocks + k) * width
                expand[:, a : a + width] = own[rows].astype(F32)
                expand[:, b : b + width] = other[rows].astype(F32)

    join_halves(own, other, blocks * shallow, small)
    for p in range(7):
        taps[p] = small[7 * p : 7 * p + 7]
    gain[...] = small[49:50]


def input_kernel(center, top, bottom, left, right, taps, grad_summed, out, frame, image):
    fill_frame(frame, (center, top, bottom, left, right))
    convolve(frame, taps, True, image)
    out[...] = (image[...] + grad_summed[...].reshape(image.shape)).astype(BF)


def body(
    block_input,
    kernel_three,
    gain_three,
    expand_weight,
    project_weight,
    layer_scale,
    merge_gain,
    patch_weight,
    kernel_four,
    gain_four,
    normed_cotangent,
    residual_cotangent,
):
    _, height, breadth, channels = block_input.shape
    hidden_width = expand_weight.shape[1]
    wide = patch_weight.shape[1]
    pixels = height * breadth
    quarter = pixels // 4
    rows4, cols4 = height // 2, breadth // 2
    row_count = lax.axis_size("row")
    col_count = lax.axis_size("col")
    scale_three = 1.0 / math.sqrt(pixels * row_count * col_count)
    scale_four = 1.0 / math.sqrt(quarter * row_count * col_count)
    center = block_input[0]
    gain_three, layer_scale, merge_gain, gain_four = (
        v[None] for v in (gain_three, layer_scale, merge_gain, gain_four)
    )
    dma = pltpu.SemaphoreType.DMA
    half = channels // 2
    hbm = pltpu.HBM

    def like(array):
        return shape_of(*array.shape, dtype=array.dtype)

    edge = shape_of(3, breadth, channels, dtype=BF)
    rows_input = neighbours(center[:3], center[height - 3 :], "row")
    inputs = (center, kernel_three, gain_three, layer_scale, merge_gain)
    center, taps_three, gain_three, layer_scale, merge_gain = run(
        load_kernel,
        "load",
        inputs,
        tuple(map(like, inputs)),
        scratch=(dma((5,)),),
        spaces=dict.fromkeys(range(5), hbm),
        after=rows_input[:1],
        limit=4,
        us=2,
    )
    framed = halo(center, rows_input, "strips_input")
    inputs = (
        expand_weight, project_weight, patch_weight, kernel_four, gain_four,
        normed_cotangent[0], residual_cotangent[0],
    )
    edge_four = shape_of(3, cols4, wide, dtype=BF)
    (
        early, unit_mixed, inverse_mixed, slope, branch, unit_summed, inverse_summed,
        section, first, last,
        expand_weight, project_weight, patch_weight, taps_four, gain_four, cotangent, residual,
    ) = run(
        front_kernel,
        "front",
        (*framed, taps_three, gain_three, layer_scale, merge_gain, *inputs),
        (
            shape_of(pixels, hidden_width + 2 * channels, dtype=BF),
            shape_of(pixels, channels),
            shape_of(pixels, 1),
            shape_of(pixels, hidden_width, dtype=BF),
            shape_of(pixels, channels),
            shape_of(pixels, channels),
            shape_of(pixels, 1),
            shape_of(rows4, cols4, wide, dtype=BF),
            edge_four,
            edge_four,
            *map(like, inputs),
        ),
        scratch=(
            frame_scratch(center),
            pltpu.VMEM((height, breadth, channels), F32),
            pltpu.VMEM((channels // 128, height, breadth, 128), F32),
            pltpu.VMEM((pixels, CHUNK), F32),
            dma((7,)),
        ),
        spaces=dict.fromkeys(range(9, 16), hbm),
        limit=28,
        us=12,
    )

    framed_four = halo(section, neighbours(first, last, "row"), "strips_section")
    mixer_image = pltpu.VMEM((rows4, cols4, wide), F32)
    grad_four, grad_four_half, first, last, gain_four_part = run(
        mixer_kernel,
        "mixer",
        (*framed_four, taps_four, gain_four, cotangent),
        (
            shape_of(rows4, cols4, wide),
            shape_of(rows4, cols4, wide, dtype=BF),
            edge_four,
            edge_four,
            shape_of(1, wide),
        ),
        scratch=(frame_scratch(section), mixer_image),
        limit=12,
        us=3,
    )
    rows_grad = neighbours(first, last, "row")
    (kernel_four_part,) = run(
        functools.partial(weight_kernel, scale_four),
        "mixer_weights",
        (*framed_four, grad_four),
        (shape_of(49, wide),),
        scratch=(frame_scratch(section),),
        after=rows_grad[:1],
        limit=12,
        us=3,
    )
    framed_grad = halo(grad_four_half, rows_grad, "strips_mixer", after=(kernel_four_part,))
    block_count = col_count // 2
    block = wide // col_count
    blocked = shape_of(block_count, quarter, block, dtype=BF)
    flat, flat_keep, flat_send, early = hold(
        section_kernel,
        "section_grad",
        (*framed_grad, taps_four, residual),
        (shape_of(quarter, wide, dtype=BF), blocked, blocked),
        early,
        scratch=(frame_scratch(section), mixer_image),
        limit=12,
        us=3,
    )

    flat_other = swap(flat_send, "col", 1)
    early_other = swap(early, "col", 1)
    split = shape_of(pixels + 112, half, dtype=BF)
    grad_summed, grad_branch, branch_keep, branch_send = run(
        functools.partial(merge_kernel, scale_three, scale_four),
        "merge_back",
        (
            flat, patch_weight, unit_summed, inverse_summed, merge_gain, branch, layer_scale,
            kernel_four_part, gain_four_part,
        ),
        (shape_of(pixels, channels), shape_of(pixels, channels, dtype=BF), split, split),
        scratch=(
            pltpu.VMEM((channels // 128, height, breadth, 128), F32),
            pltpu.VMEM((112, channels), F32),
            pltpu.VMEM((8, channels), F32),
        ),
        limit=16,
        us=0.8,
    )
    branch_other = swap(branch_send, "col", 1)
    patch_part = shape_of(block_count // 2 * 2 * channels, block, dtype=BF)
    upper_keep, upper_send, lower_keep, lower_send = run(
        functools.partial(patch_product_kernel, scale_four, row_count, channels),
        "patch_product",
        (early, early_other, flat_keep, flat_other),
        (patch_part,) * 4,
        limit=16,
        us=1,
    )
    deep, shallow = hidden_width // row_count, channels // row_count
    groups = hidden_width // channels
    project_half = shape_of(row_count // 2 * deep + 112, half, dtype=BF)
    upward_half = shape_of(pixels, hidden_width // 2, dtype=BF)
    upward_keep, upward_send, grad_mixed, first, last, gain_part = run(
        back_kernel,
        "mlp_back",
        (grad_branch, project_weight, slope, expand_weight, unit_mixed, inverse_mixed, gain_three),
        (
            upward_half,
            upward_half,
            shape_of(height, breadth, channels, dtype=BF),
            edge,
            edge,
            shape_of(1, channels),
        ),
        scratch=(
            pltpu.VMEM((pixels, CHUNK), F32),
            pltpu.VMEM((pixels, hidden_width), BF),
            pltpu.VMEM((pixels, channels), F32),
        ),
        after=(upper_send,),
        limit=16,
        us=1.2,
    )
    rows_back = neighbours(first, last, "row")
    upward_other = swap(upward_send, "col", 1)
    project_keep, project_send = run(
        functools.partial(project_product_kernel, scale_three, row_count),
        "project_product",
        (early, early_other, branch_keep, branch_other),
        (project_half, project_half),
        after=(upward_send,),
        limit=16,
        us=0.9,
    )
    expand_half = shape_of(row_count // 2 * groups * shallow, half, dtype=BF)
    expand_keep, expand_send = run(
        functools.partial(expand_product_kernel, scale_three, row_count),
        "expand_product",
        (early, early_other, upward_keep, upward_other),
        (expand_half, expand_half),
        after=(project_send, rows_back[0]),
        limit=16,
        us=0.6,
    )
    framed_back = halo(grad_mixed, rows_back, "strips_back", after=(expand_send,))
    small_half = shape_of(64, half, dtype=BF)
    small_keep, small_send = run(
        functools.partial(weight_pack_kernel, scale_three),
        "block_weights",
        (*framed, grad_mixed, gain_part),
        (small_half, small_half),
        scratch=(
            frame_scratch(center),
            pltpu.VMEM((height, breadth, channels), F32),
            pltpu.VMEM((64, channels), F32),
        ),
        after=(expand_send,),
        limit=12,
        us=1.8,
    )
    def finish_input(sent):
        return run(
            input_kernel,
            "input_grad",
            (*framed_back, taps_three, grad_summed),
            (shape_of(height, breadth, channels, dtype=BF),),
            scratch=(frame_scratch(center), pltpu.VMEM((height, breadth, channels), F32)),
            after=(small_keep, sent),
            limit=12,
            us=2,
        )

    row_bits, col_bits = axis_bits("row"), axis_bits("col")
    outer = len(row_bits)
    low_first = [("row", bit, 0) for bit in row_bits]
    lateral = [("col", bit, outer) for bit in col_bits[1:]]
    upper_order = lateral + low_first
    lower_order = low_first[:1] + [("col", bit, outer - 1) for bit in col_bits[1:]] + low_first[1:]
    part_rows = 2 * channels // row_count
    patch_sum = jnp.concatenate(
        [
            chain(upper_keep, upper_send, upper_order, block_count * row_count, part_rows),
            chain(lower_keep, lower_send, lower_order, block_count * row_count, part_rows),
        ]
    )
    patch_sum = gather(patch_sum, "col", col_bits[1:])
    (patch_grad,) = run(
        finish_patch_kernel,
        "finish_patch",
        (patch_sum, swap(patch_sum, "col", 1)),
        (shape_of(4 * channels // row_count, wide),),
        limit=8,
    )

    def share(total):
        for bit in col_bits[1:]:
            total = total + swap(total, "col", bit)
        return total, swap(total, "col", 1)

    project_order = [("row", row_bits[1], 1), low_first[0], *low_first[2:]]
    vector, wide_vector = shape_of(1, channels), shape_of(1, wide)
    project_grad, wide_taps, wide_gain, merge_sum, layer_sum = run(
        finish_project_kernel,
        "finish_project",
        share(chain(project_keep, project_send, project_order, row_count, deep)),
        (shape_of(deep, channels), shape_of(7, 7, wide), wide_vector, vector, vector),
        scratch=(pltpu.VMEM((112, channels), F32),),
        limit=8,
    )
    small = small_keep + swap(small_send, "col", 1)
    pair = (small, swap(small, "row", 1))
    input_grad = []

    def between(sent):
        input_grad.extend(finish_input(sent))
        return input_grad

    expand_sum = chain(expand_keep, expand_send, low_first, row_count, groups * shallow, pair, between)
    expand_grad, taps_sum, gain_sum = run(
        finish_expand_kernel,
        "finish_expand",
        share(expand_sum),
        (shape_of(shallow, hidden_width), shape_of(7, 7, channels), vector),
        scratch=(pltpu.VMEM((64, channels), F32),),
        limit=8,
    )
    return (
        input_grad[0][None],
        taps_sum,
        gain_sum[0],
        expand_grad,
        project_grad,
        layer_sum[0],
        merge_sum[0],
        patch_grad,
        wide_taps,
        wide_gain[0],
    )


def solution(mesh):
    pixels = P(None, "row", "col", None)
    return jax.shard_map(
        body,
        mesh=mesh,
        in_specs=(pixels,) + (P(),) * 9 + (pixels, pixels),
        out_specs=(pixels, P(), P(), P("row", None), P("row", None), P(), P(), P("row", None), P(), P()),
        check_vma=False,
    )
```

```python
import functools
import math

import jax
import jax.numpy as jnp
from jax import lax
from jax.experimental import pallas as pl
from jax.experimental.pallas import tpu as pltpu
from jax.sharding import PartitionSpec as P

EPSILON = 1e-06
BF = jnp.bfloat16
F32 = jnp.float32
MIB = 1 << 20
PAD = 8
CHUNK = 256


def shape_of(*dims, dtype=F32):
    return jax.ShapeDtypeStruct(dims, dtype)


def run(kernel, name, args, outs, scratch=(), spaces=None, after=(), aliases=None, limit=24, us=0.0):
    spaces = spaces or {}
    count, extra = len(args), len(after)

    def spec(place):
        return pl.BlockSpec(memory_space=spaces.get(place, pltpu.VMEM))

    def inner(*refs):
        kernel(*refs[:count], *refs[count + extra :])

    return pl.pallas_call(
        inner,
        name=name,
        out_shape=outs,
        in_specs=[spec(i) for i in range(count)] + [pl.BlockSpec(memory_space=pl.ANY)] * extra,
        out_specs=[spec(("out", i)) for i in range(len(outs))],
        scratch_shapes=list(scratch),
        input_output_aliases=aliases or {},
        compiler_params=pltpu.CompilerParams(vmem_limit_bytes=limit * MIB),
        cost_estimate=pl.CostEstimate(flops=int(us * 1.1e9) + 1000, bytes_accessed=1000, transcendentals=0),
    )(*args, *after)


def swap(values, axis, bit):
    return lax.ppermute(values, axis, [(i, i ^ bit) for i in range(lax.axis_size(axis))])


def axis_bits(axis):
    return [1 << k for k in range((lax.axis_size(axis) - 1).bit_length())]


def own_bit(axis, bit):
    return (lax.axis_index(axis) // bit) % 2


def chain(keep, send, order, count, rows, extra=(), between=None):
    for place, (axis, bit, _) in enumerate(order):
        received = swap(send, axis, bit)
        if place + 1 == len(order):
            return keep + received
        axis, bit, position = order[place + 1]
        grown = extra if place == 0 else ()
        count //= 2
        tail = keep.shape[0] - count * rows + (grown[0].shape[0] if grown else 0)
        out = shape_of(count // 2 * rows + tail, keep.shape[1], dtype=BF)
        keep, send = run(
            functools.partial(step_kernel, axis, bit, position, count, rows),
            "sum_step",
            (keep, received, *grown),
            (out, out),
            after=between(send) if between and place == 1 else (),
            limit=8,
            us=0.2,
        )


def step_kernel(axis, bit, position, count, rows, keep, received, *refs):
    *grown, next_keep, next_send = refs
    mine = (lax.axis_index(axis) // bit) % 2
    low = (1 << position) - 1
    for i in range(2):

        @pl.when(mine == i)
        def _():
            for s in range(count):
                span = slice(s * rows, (s + 1) * rows)
                at = ((s >> (position + 1)) << position | (s & low)) * rows
                target = next_keep if (s >> position) & 1 == i else next_send
                target[at : at + rows] = (keep[span].astype(F32) + received[span].astype(F32)).astype(BF)

    tails = []
    if keep.shape[0] > count * rows:
        tails.append(keep[count * rows :].astype(F32) + received[count * rows :].astype(F32))
    if grown:
        tails.append(sum(g[...].astype(F32) for g in grown))
    at = count // 2 * rows
    for tail in tails:
        for target in (next_keep, next_send):
            target[at : at + tail.shape[0]] = tail.astype(BF)
        at += tail.shape[0]


def gather(values, axis, bits):
    values = values[None]
    for bit in reversed(bits):
        other = swap(values, axis, bit)
        mine = own_bit(axis, bit)
        low = jnp.where(mine == 0, values, other)
        high = jnp.where(mine == 0, other, values)
        values = jnp.stack([low, high], axis=1).reshape(-1, *values.shape[1:])
    return values


def neighbours(first, last, axis):
    count = lax.axis_size(axis)
    forward = [(i, i + 1) for i in range(count - 1)]
    backward = [(i + 1, i) for i in range(count - 1)]
    return lax.ppermute(last, axis, forward), lax.ppermute(first, axis, backward)


def strip_kernel(center, top, bottom, first, last):
    height, breadth = center.shape[:2]
    for source, start in ((top, 0), (center, 3), (bottom, 3 + height)):
        values = source[...].astype(F32)
        rows = slice(start, start + source.shape[0])
        first[rows] = values[:, :PAD].astype(BF)
        last[rows] = values[:, breadth - PAD :].astype(BF)


def halo(center, rows, name, after=()):
    height, _, channels = center.shape
    top, bottom = rows
    strip = shape_of(height + 6, PAD, channels, dtype=BF)
    first, last = run(strip_kernel, name, (center, top, bottom), (strip, strip), after=after, limit=8)
    left, right = neighbours(first, last, "col")
    return center, top, bottom, left, right


def hold(kernel, name, args, outs, carried, **options):
    count = len(args)

    def inner(*refs):
        kernel(*refs[:count], *refs[count + 1 : count + 1 + len(outs)], *refs[count + 2 + len(outs) :])

    return run(
        inner,
        name,
        (*args, carried),
        (*outs, shape_of(*carried.shape, dtype=carried.dtype)),
        spaces={count: pl.ANY, ("out", len(outs)): pl.ANY},
        aliases={count: len(outs)},
        **options,
    )


def fill_frame(frame, parts):
    center, top, bottom, left, right = parts
    height, breadth = center.shape[:2]
    middle = slice(PAD, PAD + breadth)
    frame[0:3, middle] = top[...].astype(F32)
    frame[3 : 3 + height, middle] = center[...].astype(F32)
    frame[3 + height :, middle] = bottom[...].astype(F32)
    frame[:, :PAD] = left[...].astype(F32)
    frame[:, PAD + breadth :] = right[...].astype(F32)


def frame_scratch(center):
    height, breadth, channels = center.shape
    return pltpu.VMEM((height + 6, breadth + 2 * PAD, channels), F32)


def lane_tiles(channels):
    def over(step):
        def wrapped(index, carry):
            step(pl.ds(pl.multiple_of(index * 128, 128), 128))
            return carry

        lax.fori_loop(0, channels // 128, wrapped, 0)

    return over


def convolve(frame, taps, flip, out):
    height, breadth, channels = out.shape

    @lane_tiles(channels)
    def _(lanes):
        for column in range(0, breadth, 8):
            total = jnp.zeros((height, 8, 128), F32)
            for q in range(7):
                rows = frame[:, pl.ds(column + PAD - 3 + q, 8), lanes]
                for p in range(7):
                    a, b = (6 - p, 6 - q) if flip else (p, q)
                    total = total + rows[p : p + height] * taps[a, pl.ds(b, 1), lanes]
            out[:, pl.ds(column, 8), lanes] = total


def weight_sums(frame, grads, scale, out):
    height, breadth, channels = grads.shape

    @lane_tiles(channels)
    def _(lanes):
        for q in range(7):
            totals = [jnp.zeros((8, 128), F32)] * 7
            for column in range(0, breadth, 8):
                rows = frame[:, pl.ds(column + PAD - 3 + q, 8), lanes]
                grad = grads[:, pl.ds(column, 8), lanes]
                for p in range(7):
                    totals[p] = totals[p] + jnp.sum(rows[p : p + height] * grad, axis=0)
            for p in range(7):
                out[pl.ds(7 * p + q, 1), lanes] = scale * jnp.sum(totals[p], axis=0, keepdims=True)


def mean(values):
    return jnp.mean(values, axis=-1, keepdims=True)


def normalize(values):
    level = mean(values)
    inverse = lax.rsqrt(mean(values * values) - level * level + EPSILON)
    return (values - level) * inverse, inverse


def normalize_back(grads, unit_values, inverse):
    return (grads - mean(grads) - unit_values * mean(grads * unit_values)) * inverse


def dot(left, right):
    return jnp.dot(left, right, preferred_element_type=F32)


def dot_last(left, right):
    return lax.dot_general(left, right, (((1,), (1,)), ((), ())), preferred_element_type=F32)


def dot_first(left, right):
    return lax.dot_general(left, right, (((0,), (0,)), ((), ())), preferred_element_type=F32)


def over_rows(count, size):
    def over(step):
        def wrapped(index, carry):
            step(index, pl.ds(pl.multiple_of(index * size, size), size))
            return carry

        lax.fori_loop(0, count, wrapped, 0)

    return over


def fetch(sources, targets, semaphores):
    copies = [
        pltpu.make_async_copy(source, target, semaphores.at[i])
        for i, (source, target) in enumerate(zip(sources, targets))
    ]
    for copy in copies:
        copy.start()
    return copies


def load_kernel(*refs):
    *arrays, semaphores = refs
    count = len(arrays) // 2
    for copy in fetch(arrays[:count], arrays[count:], semaphores):
        copy.wait()


def front_kernel(
    center, top, bottom, left, right, taps, gain, layer_scale, merge_gain,
    expand, project, patch, wide_taps, wide_gain, cotangent, residual,
    early, unit_mixed, inverse_mixed, slope, branch, unit_summed, inverse_summed, section, first, last,
    expand_here, project_here, patch_here, wide_taps_here, wide_gain_here, cotangent_here, residual_here,
    frame, image, pairs, upward, semaphores,
):
    height, breadth, channels = center.shape
    hidden_width = expand.shape[1]
    pixels = height * breadth
    copies = fetch(
        (expand, project, patch, wide_taps, wide_gain, cotangent, residual),
        (expand_here, project_here, patch_here, wide_taps_here, wide_gain_here, cotangent_here, residual_here),
        semaphores,
    )
    fill_frame(frame, (center, top, bottom, left, right))
    convolve(frame, taps, False, image)
    at_normed = slice(hidden_width, hidden_width + channels)
    at_patches = slice(hidden_width + channels, hidden_width + 2 * channels)

    @over_rows(height, breadth)
    def _(y, rows):
        unit, inverse = normalize(image[y])
        unit_mixed[rows] = unit
        inverse_mixed[rows] = inverse
        early[rows, at_normed] = (unit * gain[...]).astype(BF)

    copies[0].wait()

    def chunk(index, carry):
        lanes = pl.ds(pl.multiple_of(index * CHUNK, CHUNK), CHUNK)
        upward[...] = dot(early[:, at_normed], expand_here[:, lanes])
        for start in range(0, pixels, 64):
            rows = slice(start, start + 64)
            value = upward[rows]
            cumulative = 0.5 + 0.5 * lax.erf(value * (1.0 / math.sqrt(2.0)))
            density = jnp.exp(-0.5 * value * value) * (1.0 / math.sqrt(2.0 * math.pi))
            early[rows, lanes] = (value * cumulative).astype(BF)
            slope[rows, lanes] = (cumulative + value * density).astype(BF)
        return carry

    lax.fori_loop(0, hidden_width // CHUNK, chunk, 0)
    copies[1].wait()
    branch[...] = dot(early[:, :hidden_width], project_here[...])

    @over_rows(height, breadth)
    def _(y, rows):
        summed = center[y].astype(F32) + layer_scale[...] * branch[rows]
        unit, inverse = normalize(summed)
        unit_summed[rows] = unit
        inverse_summed[rows] = inverse
        merged = unit * merge_gain[...]
        for k in range(channels // 128):
            pairs[k, y] = merged[:, k * 128 : (k + 1) * 128]

    quarter = pixels // 4
    for dy in range(2):
        for dx in range(2):
            j = 2 * dy + dx
            for y in range(height // 2):
                start = j * quarter + y * (breadth // 2)
                for k in range(channels // 128):
                    piece = pairs[k, 2 * y + dy, pl.ds(dx, breadth // 2, stride=2), :]
                    lane = hidden_width + channels + k * 128
                    early[start : start + breadth // 2, lane : lane + 128] = piece.astype(BF)
    copies[2].wait()
    total = dot(early[:quarter, at_patches], patch_here[:channels])
    for j in range(1, 4):
        total = total + dot(
            early[j * quarter : (j + 1) * quarter, at_patches],
            patch_here[j * channels : (j + 1) * channels],
        )
    total = total.reshape(section.shape)
    section[...] = total.astype(BF)
    first[...] = total[:3].astype(BF)
    last[...] = total[height // 2 - 3 :].astype(BF)
    for copy in copies[3:]:
        copy.wait()


def mixer_kernel(
    center, top, bottom, left, right, taps, gain, cotangent,
    grad, grad_half, first, last, gain_part,
    frame, image,
):
    height, breadth, channels = center.shape
    fill_frame(frame, (center, top, bottom, left, right))
    convolve(frame, taps, False, image)
    part = jnp.zeros((1, channels), F32)
    for y in range(height):
        unit, inverse = normalize(image[y])
        cot = cotangent[y].astype(F32)
        part = part + jnp.sum(cot * unit, axis=0, keepdims=True)
        value = normalize_back(cot * gain[...], unit, inverse)
        grad[y] = value
        narrow = value.astype(BF)
        grad_half[y] = narrow
        if y < 3:
            first[y] = narrow
        if y >= height - 3:
            last[y - (height - 3)] = narrow
    gain_part[...] = part


def weight_kernel(scale, center, top, bottom, left, right, grads, out, frame):
    fill_frame(frame, (center, top, bottom, left, right))
    weight_sums(frame, grads, scale, out)


def split_halves(values, start, keep, send):
    half = values.shape[1] // 2
    rows = slice(start, start + values.shape[0])
    core = lax.axis_index("col") % 2
    for i in range(2):

        @pl.when(core == i)
        def _():
            keep[rows] = values[:, i * half : (i + 1) * half]
            send[rows] = values[:, (1 - i) * half : (2 - i) * half]


def weight_pack_kernel(
    scale, center, top, bottom, left, right, grads, gain_part,
    keep, send, frame, wide_grads, packed,
):
    fill_frame(frame, (center, top, bottom, left, right))
    wide_grads[...] = grads[...].astype(F32)
    packed[...] = jnp.zeros(packed.shape, F32)
    weight_sums(frame, wide_grads, scale, packed)
    packed[49:50] = scale * gain_part[...]
    split_halves(packed[...].astype(BF), 0, keep, send)


def section_kernel(
    center, top, bottom, left, right, taps, residual,
    flat, keep, send,
    frame, image,
):
    height, breadth, channels = center.shape
    fill_frame(frame, (center, top, bottom, left, right))
    convolve(frame, taps, True, image)
    value = (image[...] + residual[...].astype(F32)).reshape(flat.shape).astype(BF)
    flat[...] = value
    blocks, _, width = keep.shape
    core = lax.axis_index("col") % 2
    for i in range(2):

        @pl.when(core == i)
        def _():
            for m in range(blocks):
                mine, other = (2 * m + i) * width, (2 * m + 1 - i) * width
                keep[m] = value[:, mine : mine + width]
                send[m] = value[:, other : other + width]


def merge_kernel(
    scale, scale_wide,
    flat, patch, unit_summed, inverse_summed, merge_gain, branch, layer_scale, wide_part, wide_gain,
    grad_summed, grad_branch, keep, send,
    pairs, packed, sums,
):
    tiles, height, breadth, _ = pairs.shape
    channels = 128 * tiles
    value = flat[...]
    for dy in range(2):
        for dx in range(2):
            j = 2 * dy + dx
            part = dot_last(value, patch[j * channels : (j + 1) * channels])
            part = part.reshape(height // 2, breadth // 2, channels)
            for y in range(height // 2):
                for k in range(tiles):
                    piece = part[y, :, k * 128 : (k + 1) * 128]
                    pairs[k, 2 * y + dy, pl.ds(dx, breadth // 2, stride=2), :] = piece
    sums[...] = jnp.zeros(sums.shape, F32)

    @over_rows(height, breadth)
    def _(y, rows):
        merged = jnp.concatenate([pairs[k, y] for k in range(tiles)], axis=1)
        unit = unit_summed[rows]
        sums[0:1] += jnp.sum(merged * unit, axis=0, keepdims=True)
        grad = normalize_back(merged * merge_gain[...], unit, inverse_summed[rows])
        grad_summed[rows] = grad
        sums[1:2] += jnp.sum(grad * branch[rows], axis=0, keepdims=True)
        grad_branch[rows] = (layer_scale[...] * grad).astype(BF)

    split_halves(grad_branch[...], 0, keep, send)
    packed[...] = jnp.zeros(packed.shape, F32)
    for i in range(2):
        columns = slice(i * channels, (i + 1) * channels)
        packed[49 * i : 49 + 49 * i] = wide_part[:, columns]
        packed[98 + i : 99 + i] = scale_wide * wide_gain[:, columns]
        packed[100 + i : 101 + i] = scale * sums[i : i + 1]
    split_halves(packed[...].astype(BF), grad_branch.shape[0], keep, send)


def back_kernel(
    grad_branch, project, slope, expand, unit_mixed, inverse_mixed, gain,
    keep, send, grad_mixed, first, last, gain_part,
    hidden, upward, normed,
):
    height, breadth, channels = grad_mixed.shape
    pixels, hidden_width = slope.shape

    def chunk(index, carry):
        span = pl.ds(pl.multiple_of(index * CHUNK, CHUNK), CHUNK)
        hidden[...] = dot_last(grad_branch[...], project[span])
        for start in range(0, pixels, 64):
            rows = slice(start, start + 64)
            upward[rows, span] = (hidden[rows] * slope[rows, span].astype(F32)).astype(BF)
        return carry

    lax.fori_loop(0, hidden_width // CHUNK, chunk, 0)
    normed[...] = dot_last(upward[...], expand[...])
    split_halves(upward[...], 0, keep, send)
    part = jnp.zeros((1, channels), F32)
    for y in range(height):
        rows = slice(y * breadth, (y + 1) * breadth)
        value = normed[rows]
        unit = unit_mixed[rows]
        part = part + jnp.sum(value * unit, axis=0, keepdims=True)
        narrow = normalize_back(value * gain[...], unit, inverse_mixed[rows]).astype(BF)
        grad_mixed[y] = narrow
        if y < 3:
            first[y] = narrow
        if y >= height - 3:
            last[y - (height - 3)] = narrow
    gain_part[...] = part


def patch_product_kernel(factor, early, early_other, own, other, keep, send):
    blocks, quarter, _ = own.shape
    rows = keep.shape[0] // max(blocks // 2, 1)
    channels = rows // 4
    at_patches = early.shape[1] - channels
    bit = (lax.axis_index("col") // 2) % 2
    for j in range(4):
        span = slice(j * quarter, (j + 1) * quarter)
        left = jnp.concatenate([early[span, at_patches:], early_other[span, at_patches:]], axis=0)
        for m in range(blocks):
            right = jnp.concatenate([own[m], other[m]], axis=0)
            value = (factor * dot_first(left, right)).astype(BF)
            at = m // 2 * rows + j * channels
            for i in range(2):

                @pl.when(bit == i)
                def _():
                    target = keep if m % 2 == i else send
                    target[at : at + channels] = value


def store_slices(position, value, begin, offset, rows, pitch, keep, send):
    bit = (lax.axis_index("row") >> position) % 2
    low = (1 << position) - 1
    for i in range(2):

        @pl.when(bit == i)
        def _():
            for k in range(value.shape[0] // rows):
                r = begin + k
                target = keep if (r >> position) & 1 == i else send
                at = ((r >> (position + 1)) << position | (r & low)) * pitch + offset
                target[at : at + rows] = value[k * rows : (k + 1) * rows]


def project_product_kernel(factor, slices, early, early_other, own, other, keep, send):
    width = keep.shape[1]
    hidden_width = early.shape[1] - 4 * width
    pixels = early.shape[0]
    deep = hidden_width // slices
    right = jnp.concatenate([own[:pixels], other[:pixels]], axis=0)
    step = max(CHUNK, deep)
    for start in range(0, hidden_width, step):
        columns = slice(start, start + step)
        left = jnp.concatenate([early[:, columns], early_other[:, columns]], axis=0)
        value = (factor * dot_first(left, right)).astype(BF)
        store_slices(1, value, start // deep, 0, deep, deep, keep, send)
    tail = (own[pixels:].astype(F32) + other[pixels:].astype(F32)).astype(BF)
    at = slices // 2 * deep
    keep[at:] = tail
    send[at:] = tail


def expand_product_kernel(factor, slices, early, early_other, own, other, keep, send):
    width = keep.shape[1]
    channels = 2 * width
    hidden_width = early.shape[1] - 2 * channels
    shallow = channels // slices
    blocks = own.shape[1] // width
    columns = slice(hidden_width, hidden_width + channels)
    left = jnp.concatenate([early[:, columns], early_other[:, columns]], axis=0)
    for k in range(blocks):
        columns = slice(k * width, (k + 1) * width)
        right = jnp.concatenate([own[:, columns], other[:, columns]], axis=0)
        value = (factor * dot_first(left, right)).astype(BF)
        store_slices(0, value, 0, k * shallow, shallow, blocks * shallow, keep, send)


def finish_patch_kernel(own, other, out):
    blocks, _, width = own.shape
    core = lax.axis_index("col") % 2
    for i in range(2):

        @pl.when(core == i)
        def _():
            for m in range(blocks):
                a, b = (2 * m + i) * width, (2 * m + 1 - i) * width
                out[:, a : a + width] = own[m].astype(F32)
                out[:, b : b + width] = other[m].astype(F32)


def join_halves(own, other, start, out):
    half = own.shape[1]
    rows = slice(start, start + out.shape[0])
    core = lax.axis_index("col") % 2
    for i in range(2):

        @pl.when(core == i)
        def _():
            out[:, i * half : (i + 1) * half] = own[rows].astype(F32)
            out[:, (1 - i) * half : (2 - i) * half] = other[rows].astype(F32)


def finish_project_kernel(own, other, project, wide_taps, wide_gain, merge, layer, small):
    deep, channels = project.shape
    join_halves(own, other, 0, project)
    join_halves(own, other, deep, small)
    for i in range(2):
        columns = slice(i * channels, (i + 1) * channels)
        for p in range(7):
            start = 49 * i + 7 * p
            wide_taps[p, :, columns] = small[start : start + 7]
        wide_gain[:, columns] = small[98 + i : 99 + i]
    merge[...] = small[100:101]
    layer[...] = small[101:102]


def finish_expand_kernel(own, other, expand, taps, gain, small):
    shallow, hidden_width = expand.shape
    width = own.shape[1]
    blocks = hidden_width // (2 * width)
    core = lax.axis_index("col") % 2
    for i in range(2):

        @pl.when(core == i)
        def _():
            for k in range(blocks):
                rows = slice(k * shallow, (k + 1) * shallow)
                a, b = (i * blocks + k) * width, ((1 - i) * blocks + k) * width
                expand[:, a : a + width] = own[rows].astype(F32)
                expand[:, b : b + width] = other[rows].astype(F32)

    join_halves(own, other, blocks * shallow, small)
    for p in range(7):
        taps[p] = small[7 * p : 7 * p + 7]
    gain[...] = small[49:50]


def input_kernel(center, top, bottom, left, right, taps, grad_summed, out, frame, image):
    fill_frame(frame, (center, top, bottom, left, right))
    convolve(frame, taps, True, image)
    out[...] = (image[...] + grad_summed[...].reshape(image.shape)).astype(BF)


def body(
    block_input,
    kernel_three,
    gain_three,
    expand_weight,
    project_weight,
    layer_scale,
    merge_gain,
    patch_weight,
    kernel_four,
    gain_four,
    normed_cotangent,
    residual_cotangent,
):
    _, height, breadth, channels = block_input.shape
    hidden_width = expand_weight.shape[1]
    wide = patch_weight.shape[1]
    pixels = height * breadth
    quarter = pixels // 4
    rows4, cols4 = height // 2, breadth // 2
    row_count = lax.axis_size("row")
    col_count = lax.axis_size("col")
    scale_three = 1.0 / math.sqrt(pixels * row_count * col_count)
    scale_four = 1.0 / math.sqrt(quarter * row_count * col_count)
    center = block_input[0]
    gain_three, layer_scale, merge_gain, gain_four = (
        v[None] for v in (gain_three, layer_scale, merge_gain, gain_four)
    )
    dma = pltpu.SemaphoreType.DMA
    half = channels // 2
    hbm = pltpu.HBM

    def like(array):
        return shape_of(*array.shape, dtype=array.dtype)

    edge = shape_of(3, breadth, channels, dtype=BF)
    rows_input = neighbours(center[:3], center[height - 3 :], "row")
    inputs = (center, kernel_three, gain_three, layer_scale, merge_gain)
    center, taps_three, gain_three, layer_scale, merge_gain = run(
        load_kernel,
        "load",
        inputs,
        tuple(map(like, inputs)),
        scratch=(dma((5,)),),
        spaces=dict.fromkeys(range(5), hbm),
        after=rows_input[:1],
        limit=4,
        us=2,
    )
    framed = halo(center, rows_input, "strips_input")
    inputs = (
        expand_weight, project_weight, patch_weight, kernel_four, gain_four,
        normed_cotangent[0], residual_cotangent[0],
    )
    edge_four = shape_of(3, cols4, wide, dtype=BF)
    (
        early, unit_mixed, inverse_mixed, slope, branch, unit_summed, inverse_summed,
        section, first, last,
        expand_weight, project_weight, patch_weight, taps_four, gain_four, cotangent, residual,
    ) = run(
        front_kernel,
        "front",
        (*framed, taps_three, gain_three, layer_scale, merge_gain, *inputs),
        (
            shape_of(pixels, hidden_width + 2 * channels, dtype=BF),
            shape_of(pixels, channels),
            shape_of(pixels, 1),
            shape_of(pixels, hidden_width, dtype=BF),
            shape_of(pixels, channels),
            shape_of(pixels, channels),
            shape_of(pixels, 1),
            shape_of(rows4, cols4, wide, dtype=BF),
            edge_four,
            edge_four,
            *map(like, inputs),
        ),
        scratch=(
            frame_scratch(center),
            pltpu.VMEM((height, breadth, channels), F32),
            pltpu.VMEM((channels // 128, height, breadth, 128), F32),
            pltpu.VMEM((pixels, CHUNK), F32),
            dma((7,)),
        ),
        spaces=dict.fromkeys(range(9, 16), hbm),
        limit=28,
        us=12,
    )

    framed_four = halo(section, neighbours(first, last, "row"), "strips_section")
    mixer_image = pltpu.VMEM((rows4, cols4, wide), F32)
    grad_four, grad_four_half, first, last, gain_four_part = run(
        mixer_kernel,
        "mixer",
        (*framed_four, taps_four, gain_four, cotangent),
        (
            shape_of(rows4, cols4, wide),
            shape_of(rows4, cols4, wide, dtype=BF),
            edge_four,
            edge_four,
            shape_of(1, wide),
        ),
        scratch=(frame_scratch(section), mixer_image),
        limit=12,
        us=3,
    )
    rows_grad = neighbours(first, last, "row")
    (kernel_four_part,) = run(
        functools.partial(weight_kernel, scale_four),
        "mixer_weights",
        (*framed_four, grad_four),
        (shape_of(49, wide),),
        scratch=(frame_scratch(section),),
        after=rows_grad[:1],
        limit=12,
        us=3,
    )
    framed_grad = halo(grad_four_half, rows_grad, "strips_mixer", after=(kernel_four_part,))
    block_count = col_count // 2
    block = wide // col_count
    blocked = shape_of(block_count, quarter, block, dtype=BF)
    flat, flat_keep, flat_send, early = hold(
        section_kernel,
        "section_grad",
        (*framed_grad, taps_four, residual),
        (shape_of(quarter, wide, dtype=BF), blocked, blocked),
        early,
        scratch=(frame_scratch(section), mixer_image),
        limit=12,
        us=3,
    )

    flat_other = swap(flat_send, "col", 1)
    early_other = swap(early, "col", 1)
    split = shape_of(pixels + 112, half, dtype=BF)
    grad_summed, grad_branch, branch_keep, branch_send = run(
        functools.partial(merge_kernel, scale_three, scale_four),
        "merge_back",
        (
            flat, patch_weight, unit_summed, inverse_summed, merge_gain, branch, layer_scale,
            kernel_four_part, gain_four_part,
        ),
        (shape_of(pixels, channels), shape_of(pixels, channels, dtype=BF), split, split),
        scratch=(
            pltpu.VMEM((channels // 128, height, breadth, 128), F32),
            pltpu.VMEM((112, channels), F32),
            pltpu.VMEM((8, channels), F32),
        ),
        limit=16,
        us=0.8,
    )
    branch_other = swap(branch_send, "col", 1)
    deep, shallow = hidden_width // row_count, channels // row_count
    groups = hidden_width // channels
    upward_half = shape_of(pixels, hidden_width // 2, dtype=BF)
    upward_keep, upward_send, grad_mixed, first, last, gain_part = run(
        back_kernel,
        "mlp_back",
        (grad_branch, project_weight, slope, expand_weight, unit_mixed, inverse_mixed, gain_three),
        (
            upward_half,
            upward_half,
            shape_of(height, breadth, channels, dtype=BF),
            edge,
            edge,
            shape_of(1, channels),
        ),
        scratch=(
            pltpu.VMEM((pixels, CHUNK), F32),
            pltpu.VMEM((pixels, hidden_width), BF),
            pltpu.VMEM((pixels, channels), F32),
        ),
        limit=16,
        us=1.2,
    )
    rows_back = neighbours(first, last, "row")
    upward_other = swap(upward_send, "col", 1)
    patch_half = shape_of(block_count // 2 * 4 * channels, block, dtype=BF)
    patch_keep, patch_send = run(
        functools.partial(patch_product_kernel, scale_four),
        "patch_product",
        (early, early_other, flat_keep, flat_other),
        (patch_half, patch_half),
        after=(upward_send,),
        limit=16,
        us=0.9,
    )
    expand_half = shape_of(row_count // 2 * groups * shallow, half, dtype=BF)
    expand_keep, expand_send = run(
        functools.partial(expand_product_kernel, scale_three, row_count),
        "expand_product",
        (early, early_other, upward_keep, upward_other),
        (expand_half, expand_half),
        after=(patch_send,),
        limit=16,
        us=0.6,
    )
    project_half = shape_of(row_count // 2 * deep + 112, half, dtype=BF)
    project_keep, project_send = run(
        functools.partial(project_product_kernel, scale_three, row_count),
        "project_product",
        (early, early_other, branch_keep, branch_other),
        (project_half, project_half),
        after=(expand_send,),
        limit=16,
        us=0.9,
    )
    framed_back = halo(grad_mixed, rows_back, "strips_back", after=(project_send,))
    small_half = shape_of(64, half, dtype=BF)
    small_keep, small_send = run(
        functools.partial(weight_pack_kernel, scale_three),
        "block_weights",
        (*framed, grad_mixed, gain_part),
        (small_half, small_half),
        scratch=(
            frame_scratch(center),
            pltpu.VMEM((height, breadth, channels), F32),
            pltpu.VMEM((64, channels), F32),
        ),
        after=(project_send,),
        limit=12,
        us=1.8,
    )
    def finish_input(sent):
        return run(
            input_kernel,
            "input_grad",
            (*framed_back, taps_three, grad_summed),
            (shape_of(height, breadth, channels, dtype=BF),),
            scratch=(frame_scratch(center), pltpu.VMEM((height, breadth, channels), F32)),
            after=(small_keep, sent),
            limit=12,
            us=2,
        )

    row_bits, col_bits = axis_bits("row"), axis_bits("col")
    outer = len(row_bits)
    low_first = [("row", bit, 0) for bit in row_bits]
    patch_order = [("col", bit, outer) for bit in col_bits[1:]] + low_first
    patch_sum = chain(
        patch_keep, patch_send, patch_order, block_count * row_count, 4 * channels // row_count
    )
    patch_sum = gather(patch_sum, "col", col_bits[1:])
    (patch_grad,) = run(
        finish_patch_kernel,
        "finish_patch",
        (patch_sum, swap(patch_sum, "col", 1)),
        (shape_of(4 * channels // row_count, wide),),
        limit=8,
    )

    def share(total):
        for bit in col_bits[1:]:
            total = total + swap(total, "col", bit)
        return total, swap(total, "col", 1)

    project_order = [("row", row_bits[1], 1), low_first[0], *low_first[2:]]
    vector, wide_vector = shape_of(1, channels), shape_of(1, wide)
    project_grad, wide_taps, wide_gain, merge_sum, layer_sum = run(
        finish_project_kernel,
        "finish_project",
        share(chain(project_keep, project_send, project_order, row_count, deep)),
        (shape_of(deep, channels), shape_of(7, 7, wide), wide_vector, vector, vector),
        scratch=(pltpu.VMEM((112, channels), F32),),
        limit=8,
    )
    small = small_keep + swap(small_send, "col", 1)
    pair = (small, swap(small, "row", 1))
    input_grad = []

    def between(sent):
        input_grad.extend(finish_input(sent))
        return input_grad

    expand_sum = chain(expand_keep, expand_send, low_first, row_count, groups * shallow, pair, between)
    expand_grad, taps_sum, gain_sum = run(
        finish_expand_kernel,
        "finish_expand",
        share(expand_sum),
        (shape_of(shallow, hidden_width), shape_of(7, 7, channels), vector),
        scratch=(pltpu.VMEM((64, channels), F32),),
        limit=8,
    )
    return (
        input_grad[0][None],
        taps_sum,
        gain_sum[0],
        expand_grad,
        project_grad,
        layer_sum[0],
        merge_sum[0],
        patch_grad,
        wide_taps,
        wide_gain[0],
    )


def solution(mesh):
    pixels = P(None, "row", "col", None)
    return jax.shard_map(
        body,
        mesh=mesh,
        in_specs=(pixels,) + (P(),) * 9 + (pixels, pixels),
        out_specs=(pixels, P(), P(), P("row", None), P("row", None), P(), P(), P("row", None), P(), P()),
        check_vma=False,
    )
```

```python
import functools
import math

import jax
import jax.numpy as jnp
from jax import lax
from jax.experimental import pallas as pl
from jax.experimental.pallas import tpu as pltpu
from jax.sharding import PartitionSpec as P

EPSILON = 1e-06
BF = jnp.bfloat16
F32 = jnp.float32
MIB = 1 << 20
PAD = 8
CHUNK = 256


def shape_of(*dims, dtype=F32):
    return jax.ShapeDtypeStruct(dims, dtype)


def run(kernel, name, args, outs, scratch=(), spaces=None, after=(), aliases=None, limit=24, us=0.0):
    spaces = spaces or {}
    count, extra = len(args), len(after)

    def spec(place):
        return pl.BlockSpec(memory_space=spaces.get(place, pltpu.VMEM))

    def inner(*refs):
        kernel(*refs[:count], *refs[count + extra :])

    return pl.pallas_call(
        inner,
        name=name,
        out_shape=outs,
        in_specs=[spec(i) for i in range(count)] + [pl.BlockSpec(memory_space=pl.ANY)] * extra,
        out_specs=[spec(("out", i)) for i in range(len(outs))],
        scratch_shapes=list(scratch),
        input_output_aliases=aliases or {},
        compiler_params=pltpu.CompilerParams(vmem_limit_bytes=limit * MIB),
        cost_estimate=pl.CostEstimate(flops=int(us * 1.1e9) + 1000, bytes_accessed=1000, transcendentals=0),
    )(*args, *after)


def swap(values, axis, bit):
    return lax.ppermute(values, axis, [(i, i ^ bit) for i in range(lax.axis_size(axis))])


def axis_bits(axis):
    return [1 << k for k in range((lax.axis_size(axis) - 1).bit_length())]


def own_bit(axis, bit):
    return (lax.axis_index(axis) // bit) % 2


class Chain:
    def __init__(self, keep, send, order, count, rows):
        self.keep, self.send, self.order = keep, send, list(order)
        self.count, self.rows = count, rows

    def advance(self, after=(), extra=()):
        axis, bit, _ = self.order.pop(0)
        keep, received = self.keep, swap(self.send, axis, bit)
        if not self.order:
            self.keep = keep + received
            return ()
        axis, bit, position = self.order[0]
        self.count //= 2
        tail = keep.shape[0] - self.count * self.rows + (extra[0].shape[0] if extra else 0)
        out = shape_of(self.count // 2 * self.rows + tail, keep.shape[1], dtype=BF)
        self.keep, self.send = run(
            functools.partial(step_kernel, axis, bit, position, self.count, self.rows),
            "sum_step",
            (keep, received, *extra),
            (out, out),
            after=after,
            limit=8,
            us=0.2,
        )
        return (self.send,)

    def finish(self):
        while self.order:
            self.advance()
        return self.keep


def step_kernel(axis, bit, position, count, rows, keep, received, *refs):
    *grown, next_keep, next_send = refs
    mine = (lax.axis_index(axis) // bit) % 2
    low = (1 << position) - 1
    for i in range(2):

        @pl.when(mine == i)
        def _():
            for s in range(count):
                span = slice(s * rows, (s + 1) * rows)
                at = ((s >> (position + 1)) << position | (s & low)) * rows
                target = next_keep if (s >> position) & 1 == i else next_send
                target[at : at + rows] = (keep[span].astype(F32) + received[span].astype(F32)).astype(BF)

    tails = []
    if keep.shape[0] > count * rows:
        tails.append(keep[count * rows :].astype(F32) + received[count * rows :].astype(F32))
    if grown:
        tails.append(sum(g[...].astype(F32) for g in grown))
    at = count // 2 * rows
    for tail in tails:
        for target in (next_keep, next_send):
            target[at : at + tail.shape[0]] = tail.astype(BF)
        at += tail.shape[0]


def gather(values, axis, bits):
    values = values[None]
    for bit in reversed(bits):
        other = swap(values, axis, bit)
        mine = own_bit(axis, bit)
        low = jnp.where(mine == 0, values, other)
        high = jnp.where(mine == 0, other, values)
        values = jnp.stack([low, high], axis=1).reshape(-1, *values.shape[1:])
    return values


def neighbours(first, last, axis):
    count = lax.axis_size(axis)
    forward = [(i, i + 1) for i in range(count - 1)]
    backward = [(i + 1, i) for i in range(count - 1)]
    return lax.ppermute(last, axis, forward), lax.ppermute(first, axis, backward)


def strip_kernel(center, top, bottom, first, last):
    height, breadth = center.shape[:2]
    for source, start in ((top, 0), (center, 3), (bottom, 3 + height)):
        values = source[...].astype(F32)
        rows = slice(start, start + source.shape[0])
        first[rows] = values[:, :PAD].astype(BF)
        last[rows] = values[:, breadth - PAD :].astype(BF)


def halo(center, rows, name, after=()):
    height, _, channels = center.shape
    top, bottom = rows
    strip = shape_of(height + 6, PAD, channels, dtype=BF)
    first, last = run(strip_kernel, name, (center, top, bottom), (strip, strip), after=after, limit=8)
    left, right = neighbours(first, last, "col")
    return center, top, bottom, left, right


def hold(kernel, name, args, outs, carried, **options):
    count = len(args)

    def inner(*refs):
        kernel(*refs[:count], *refs[count + 1 : count + 1 + len(outs)], *refs[count + 2 + len(outs) :])

    return run(
        inner,
        name,
        (*args, carried),
        (*outs, shape_of(*carried.shape, dtype=carried.dtype)),
        spaces={count: pl.ANY, ("out", len(outs)): pl.ANY},
        aliases={count: len(outs)},
        **options,
    )


def fill_frame(frame, parts):
    center, top, bottom, left, right = parts
    height, breadth = center.shape[:2]
    middle = slice(PAD, PAD + breadth)
    frame[0:3, middle] = top[...].astype(F32)
    frame[3 : 3 + height, middle] = center[...].astype(F32)
    frame[3 + height :, middle] = bottom[...].astype(F32)
    frame[:, :PAD] = left[...].astype(F32)
    frame[:, PAD + breadth :] = right[...].astype(F32)


def frame_scratch(center):
    height, breadth, channels = center.shape
    return pltpu.VMEM((height + 6, breadth + 2 * PAD, channels), F32)


def lane_tiles(channels):
    def over(step):
        def wrapped(index, carry):
            step(pl.ds(pl.multiple_of(index * 128, 128), 128))
            return carry

        lax.fori_loop(0, channels // 128, wrapped, 0)

    return over


def convolve(frame, taps, flip, out):
    height, breadth, channels = out.shape

    @lane_tiles(channels)
    def _(lanes):
        for column in range(0, breadth, 8):
            total = jnp.zeros((height, 8, 128), F32)
            for q in range(7):
                rows = frame[:, pl.ds(column + PAD - 3 + q, 8), lanes]
                for p in range(7):
                    a, b = (6 - p, 6 - q) if flip else (p, q)
                    total = total + rows[p : p + height] * taps[a, pl.ds(b, 1), lanes]
            out[:, pl.ds(column, 8), lanes] = total


def weight_sums(frame, grads, scale, out):
    height, breadth, channels = grads.shape

    @lane_tiles(channels)
    def _(lanes):
        for q in range(7):
            totals = [jnp.zeros((8, 128), F32)] * 7
            for column in range(0, breadth, 8):
                rows = frame[:, pl.ds(column + PAD - 3 + q, 8), lanes]
                grad = grads[:, pl.ds(column, 8), lanes]
                for p in range(7):
                    totals[p] = totals[p] + jnp.sum(rows[p : p + height] * grad, axis=0)
            for p in range(7):
                out[pl.ds(7 * p + q, 1), lanes] = scale * jnp.sum(totals[p], axis=0, keepdims=True)


def mean(values):
    return jnp.mean(values, axis=-1, keepdims=True)


def normalize(values):
    level = mean(values)
    inverse = lax.rsqrt(mean(values * values) - level * level + EPSILON)
    return (values - level) * inverse, inverse


def normalize_back(grads, unit_values, inverse):
    return (grads - mean(grads) - unit_values * mean(grads * unit_values)) * inverse


def dot(left, right):
    return jnp.dot(left, right, preferred_element_type=F32)


def dot_last(left, right):
    return lax.dot_general(left, right, (((1,), (1,)), ((), ())), preferred_element_type=F32)


def dot_first(left, right):
    return lax.dot_general(left, right, (((0,), (0,)), ((), ())), preferred_element_type=F32)


def over_rows(count, size):
    def over(step):
        def wrapped(index, carry):
            step(index, pl.ds(pl.multiple_of(index * size, size), size))
            return carry

        lax.fori_loop(0, count, wrapped, 0)

    return over


def fetch(sources, targets, semaphores):
    copies = [
        pltpu.make_async_copy(source, target, semaphores.at[i])
        for i, (source, target) in enumerate(zip(sources, targets))
    ]
    for copy in copies:
        copy.start()
    return copies


def load_kernel(*refs):
    *arrays, semaphores = refs
    count = len(arrays) // 2
    for copy in fetch(arrays[:count], arrays[count:], semaphores):
        copy.wait()


def front_kernel(
    center, top, bottom, left, right, taps, gain, layer_scale, merge_gain,
    expand, project, patch, wide_taps, wide_gain, cotangent, residual,
    early, unit_mixed, inverse_mixed, slope, branch, unit_summed, inverse_summed, section, first, last,
    expand_here, project_here, patch_here, wide_taps_here, wide_gain_here, cotangent_here, residual_here,
    frame, image, pairs, upward, semaphores,
):
    height, breadth, channels = center.shape
    hidden_width = expand.shape[1]
    pixels = height * breadth
    copies = fetch(
        (expand, project, patch, wide_taps, wide_gain, cotangent, residual),
        (expand_here, project_here, patch_here, wide_taps_here, wide_gain_here, cotangent_here, residual_here),
        semaphores,
    )
    fill_frame(frame, (center, top, bottom, left, right))
    convolve(frame, taps, False, image)
    at_normed = slice(hidden_width, hidden_width + channels)
    at_patches = slice(hidden_width + channels, hidden_width + 2 * channels)

    @over_rows(height, breadth)
    def _(y, rows):
        unit, inverse = normalize(image[y])
        unit_mixed[rows] = unit
        inverse_mixed[rows] = inverse
        early[rows, at_normed] = (unit * gain[...]).astype(BF)

    copies[0].wait()

    def chunk(index, carry):
        lanes = pl.ds(pl.multiple_of(index * CHUNK, CHUNK), CHUNK)
        upward[...] = dot(early[:, at_normed], expand_here[:, lanes])
        for start in range(0, pixels, 64):
            rows = slice(start, start + 64)
            value = upward[rows]
            cumulative = 0.5 + 0.5 * lax.erf(value * (1.0 / math.sqrt(2.0)))
            density = jnp.exp(-0.5 * value * value) * (1.0 / math.sqrt(2.0 * math.pi))
            early[rows, lanes] = (value * cumulative).astype(BF)
            slope[rows, lanes] = (cumulative + value * density).astype(BF)
        return carry

    lax.fori_loop(0, hidden_width // CHUNK, chunk, 0)
    copies[1].wait()
    branch[...] = dot(early[:, :hidden_width], project_here[...])

    @over_rows(height, breadth)
    def _(y, rows):
        summed = center[y].astype(F32) + layer_scale[...] * branch[rows]
        unit, inverse = normalize(summed)
        unit_summed[rows] = unit
        inverse_summed[rows] = inverse
        merged = unit * merge_gain[...]
        for k in range(channels // 128):
            pairs[k, y] = merged[:, k * 128 : (k + 1) * 128]

    quarter = pixels // 4
    for dy in range(2):
        for dx in range(2):
            j = 2 * dy + dx
            for y in range(height // 2):
                start = j * quarter + y * (breadth // 2)
                for k in range(channels // 128):
                    piece = pairs[k, 2 * y + dy, pl.ds(dx, breadth // 2, stride=2), :]
                    lane = hidden_width + channels + k * 128
                    early[start : start + breadth // 2, lane : lane + 128] = piece.astype(BF)
    copies[2].wait()
    total = dot(early[:quarter, at_patches], patch_here[:channels])
    for j in range(1, 4):
        total = total + dot(
            early[j * quarter : (j + 1) * quarter, at_patches],
            patch_here[j * channels : (j + 1) * channels],
        )
    total = total.reshape(section.shape)
    section[...] = total.astype(BF)
    first[...] = total[:3].astype(BF)
    last[...] = total[height // 2 - 3 :].astype(BF)
    for copy in copies[3:]:
        copy.wait()


def mixer_kernel(
    center, top, bottom, left, right, taps, gain, cotangent,
    grad, grad_half, first, last, gain_part,
    frame, image,
):
    height, breadth, channels = center.shape
    fill_frame(frame, (center, top, bottom, left, right))
    convolve(frame, taps, False, image)
    part = jnp.zeros((1, channels), F32)
    for y in range(height):
        unit, inverse = normalize(image[y])
        cot = cotangent[y].astype(F32)
        part = part + jnp.sum(cot * unit, axis=0, keepdims=True)
        value = normalize_back(cot * gain[...], unit, inverse)
        grad[y] = value
        narrow = value.astype(BF)
        grad_half[y] = narrow
        if y < 3:
            first[y] = narrow
        if y >= height - 3:
            last[y - (height - 3)] = narrow
    gain_part[...] = part


def weight_kernel(scale, center, top, bottom, left, right, grads, out, frame):
    fill_frame(frame, (center, top, bottom, left, right))
    weight_sums(frame, grads, scale, out)


def split_halves(values, start, keep, send):
    half = values.shape[1] // 2
    rows = slice(start, start + values.shape[0])
    core = lax.axis_index("col") % 2
    for i in range(2):

        @pl.when(core == i)
        def _():
            keep[rows] = values[:, i * half : (i + 1) * half]
            send[rows] = values[:, (1 - i) * half : (2 - i) * half]


def weight_pack_kernel(
    scale, center, top, bottom, left, right, grads, gain_part,
    keep, send, frame, wide_grads, packed,
):
    fill_frame(frame, (center, top, bottom, left, right))
    wide_grads[...] = grads[...].astype(F32)
    packed[...] = jnp.zeros(packed.shape, F32)
    weight_sums(frame, wide_grads, scale, packed)
    packed[49:50] = scale * gain_part[...]
    split_halves(packed[...].astype(BF), 0, keep, send)


def section_kernel(
    center, top, bottom, left, right, taps, residual,
    flat, keep, send,
    frame, image,
):
    height, breadth, channels = center.shape
    fill_frame(frame, (center, top, bottom, left, right))
    convolve(frame, taps, True, image)
    value = (image[...] + residual[...].astype(F32)).reshape(flat.shape).astype(BF)
    flat[...] = value
    blocks, _, width = keep.shape
    core = lax.axis_index("col") % 2
    for i in range(2):

        @pl.when(core == i)
        def _():
            for m in range(blocks):
                mine, other = (2 * m + i) * width, (2 * m + 1 - i) * width
                keep[m] = value[:, mine : mine + width]
                send[m] = value[:, other : other + width]


def merge_kernel(
    scale, scale_wide,
    flat, patch, unit_summed, inverse_summed, merge_gain, branch, layer_scale, wide_part, wide_gain,
    grad_summed, grad_branch, keep, send,
    pairs, packed, sums,
):
    tiles, height, breadth, _ = pairs.shape
    channels = 128 * tiles
    value = flat[...]
    for dy in range(2):
        for dx in range(2):
            j = 2 * dy + dx
            part = dot_last(value, patch[j * channels : (j + 1) * channels])
            part = part.reshape(height // 2, breadth // 2, channels)
            for y in range(height // 2):
                for k in range(tiles):
                    piece = part[y, :, k * 128 : (k + 1) * 128]
                    pairs[k, 2 * y + dy, pl.ds(dx, breadth // 2, stride=2), :] = piece
    sums[...] = jnp.zeros(sums.shape, F32)

    @over_rows(height, breadth)
    def _(y, rows):
        merged = jnp.concatenate([pairs[k, y] for k in range(tiles)], axis=1)
        unit = unit_summed[rows]
        sums[0:1] += jnp.sum(merged * unit, axis=0, keepdims=True)
        grad = normalize_back(merged * merge_gain[...], unit, inverse_summed[rows])
        grad_summed[rows] = grad
        sums[1:2] += jnp.sum(grad * branch[rows], axis=0, keepdims=True)
        grad_branch[rows] = (layer_scale[...] * grad).astype(BF)

    split_halves(grad_branch[...], 0, keep, send)
    packed[...] = jnp.zeros(packed.shape, F32)
    for i in range(2):
        columns = slice(i * channels, (i + 1) * channels)
        packed[49 * i : 49 + 49 * i] = wide_part[:, columns]
        packed[98 + i : 99 + i] = scale_wide * wide_gain[:, columns]
        packed[100 + i : 101 + i] = scale * sums[i : i + 1]
    split_halves(packed[...].astype(BF), grad_branch.shape[0], keep, send)


def back_kernel(
    grad_branch, project, slope, expand, unit_mixed, inverse_mixed, gain,
    keep, send, grad_mixed, first, last, gain_part,
    hidden, upward, normed,
):
    height, breadth, channels = grad_mixed.shape
    pixels, hidden_width = slope.shape

    def chunk(index, carry):
        span = pl.ds(pl.multiple_of(index * CHUNK, CHUNK), CHUNK)
        hidden[...] = dot_last(grad_branch[...], project[span])
        for start in range(0, pixels, 64):
            rows = slice(start, start + 64)
            upward[rows, span] = (hidden[rows] * slope[rows, span].astype(F32)).astype(BF)
        return carry

    lax.fori_loop(0, hidden_width // CHUNK, chunk, 0)
    normed[...] = dot_last(upward[...], expand[...])
    split_halves(upward[...], 0, keep, send)
    part = jnp.zeros((1, channels), F32)
    for y in range(height):
        rows = slice(y * breadth, (y + 1) * breadth)
        value = normed[rows]
        unit = unit_mixed[rows]
        part = part + jnp.sum(value * unit, axis=0, keepdims=True)
        narrow = normalize_back(value * gain[...], unit, inverse_mixed[rows]).astype(BF)
        grad_mixed[y] = narrow
        if y < 3:
            first[y] = narrow
        if y >= height - 3:
            last[y - (height - 3)] = narrow
    gain_part[...] = part


def patch_product_kernel(factor, early, early_other, own, other, keep, send):
    blocks, quarter, _ = own.shape
    rows = keep.shape[0] // max(blocks // 2, 1)
    channels = rows // 4
    at_patches = early.shape[1] - channels
    bit = (lax.axis_index("col") // 2) % 2
    for j in range(4):
        span = slice(j * quarter, (j + 1) * quarter)
        left = jnp.concatenate([early[span, at_patches:], early_other[span, at_patches:]], axis=0)
        for m in range(blocks):
            right = jnp.concatenate([own[m], other[m]], axis=0)
            value = (factor * dot_first(left, right)).astype(BF)
            at = m // 2 * rows + j * channels
            for i in range(2):

                @pl.when(bit == i)
                def _():
                    target = keep if m % 2 == i else send
                    target[at : at + channels] = value


def store_slices(position, value, begin, offset, rows, pitch, keep, send):
    bit = (lax.axis_index("row") >> position) % 2
    low = (1 << position) - 1
    for i in range(2):

        @pl.when(bit == i)
        def _():
            for k in range(value.shape[0] // rows):
                r = begin + k
                target = keep if (r >> position) & 1 == i else send
                at = ((r >> (position + 1)) << position | (r & low)) * pitch + offset
                target[at : at + rows] = value[k * rows : (k + 1) * rows]


def project_product_kernel(factor, slices, early, early_other, own, other, keep, send):
    width = keep.shape[1]
    hidden_width = early.shape[1] - 4 * width
    pixels = early.shape[0]
    deep = hidden_width // slices
    right = jnp.concatenate([own[:pixels], other[:pixels]], axis=0)
    step = max(CHUNK, deep)
    for start in range(0, hidden_width, step):
        columns = slice(start, start + step)
        left = jnp.concatenate([early[:, columns], early_other[:, columns]], axis=0)
        value = (factor * dot_first(left, right)).astype(BF)
        store_slices(1, value, start // deep, 0, deep, deep, keep, send)
    tail = (own[pixels:].astype(F32) + other[pixels:].astype(F32)).astype(BF)
    at = slices // 2 * deep
    keep[at:] = tail
    send[at:] = tail


def expand_product_kernel(factor, slices, early, early_other, own, other, keep, send):
    width = keep.shape[1]
    channels = 2 * width
    hidden_width = early.shape[1] - 2 * channels
    shallow = channels // slices
    blocks = own.shape[1] // width
    columns = slice(hidden_width, hidden_width + channels)
    left = jnp.concatenate([early[:, columns], early_other[:, columns]], axis=0)
    for k in range(blocks):
        columns = slice(k * width, (k + 1) * width)
        right = jnp.concatenate([own[:, columns], other[:, columns]], axis=0)
        value = (factor * dot_first(left, right)).astype(BF)
        store_slices(0, value, 0, k * shallow, shallow, blocks * shallow, keep, send)


def finish_patch_kernel(own, other, out):
    blocks, _, width = own.shape
    core = lax.axis_index("col") % 2
    for i in range(2):

        @pl.when(core == i)
        def _():
            for m in range(blocks):
                a, b = (2 * m + i) * width, (2 * m + 1 - i) * width
                out[:, a : a + width] = own[m].astype(F32)
                out[:, b : b + width] = other[m].astype(F32)


def join_halves(own, other, start, out):
    half = own.shape[1]
    rows = slice(start, start + out.shape[0])
    core = lax.axis_index("col") % 2
    for i in range(2):

        @pl.when(core == i)
        def _():
            out[:, i * half : (i + 1) * half] = own[rows].astype(F32)
            out[:, (1 - i) * half : (2 - i) * half] = other[rows].astype(F32)


def finish_project_kernel(own, other, project, wide_taps, wide_gain, merge, layer, small):
    deep, channels = project.shape
    join_halves(own, other, 0, project)
    join_halves(own, other, deep, small)
    for i in range(2):
        columns = slice(i * channels, (i + 1) * channels)
        for p in range(7):
            start = 49 * i + 7 * p
            wide_taps[p, :, columns] = small[start : start + 7]
        wide_gain[:, columns] = small[98 + i : 99 + i]
    merge[...] = small[100:101]
    layer[...] = small[101:102]


def finish_expand_kernel(own, other, expand, taps, gain, small):
    shallow, hidden_width = expand.shape
    width = own.shape[1]
    blocks = hidden_width // (2 * width)
    core = lax.axis_index("col") % 2
    for i in range(2):

        @pl.when(core == i)
        def _():
            for k in range(blocks):
                rows = slice(k * shallow, (k + 1) * shallow)
                a, b = (i * blocks + k) * width, ((1 - i) * blocks + k) * width
                expand[:, a : a + width] = own[rows].astype(F32)
                expand[:, b : b + width] = other[rows].astype(F32)

    join_halves(own, other, blocks * shallow, small)
    for p in range(7):
        taps[p] = small[7 * p : 7 * p + 7]
    gain[...] = small[49:50]


def input_kernel(center, top, bottom, left, right, taps, grad_summed, out, frame, image):
    fill_frame(frame, (center, top, bottom, left, right))
    convolve(frame, taps, True, image)
    out[...] = (image[...] + grad_summed[...].reshape(image.shape)).astype(BF)


def body(
    block_input,
    kernel_three,
    gain_three,
    expand_weight,
    project_weight,
    layer_scale,
    merge_gain,
    patch_weight,
    kernel_four,
    gain_four,
    normed_cotangent,
    residual_cotangent,
):
    _, height, breadth, channels = block_input.shape
    hidden_width = expand_weight.shape[1]
    wide = patch_weight.shape[1]
    pixels = height * breadth
    quarter = pixels // 4
    rows4, cols4 = height // 2, breadth // 2
    row_count = lax.axis_size("row")
    col_count = lax.axis_size("col")
    scale_three = 1.0 / math.sqrt(pixels * row_count * col_count)
    scale_four = 1.0 / math.sqrt(quarter * row_count * col_count)
    center = block_input[0]
    gain_three, layer_scale, merge_gain, gain_four = (
        v[None] for v in (gain_three, layer_scale, merge_gain, gain_four)
    )
    dma = pltpu.SemaphoreType.DMA
    half = channels // 2
    hbm = pltpu.HBM

    def like(array):
        return shape_of(*array.shape, dtype=array.dtype)

    edge = shape_of(3, breadth, channels, dtype=BF)
    rows_input = neighbours(center[:3], center[height - 3 :], "row")
    inputs = (center, kernel_three, gain_three, layer_scale, merge_gain)
    center, taps_three, gain_three, layer_scale, merge_gain = run(
        load_kernel,
        "load",
        inputs,
        tuple(map(like, inputs)),
        scratch=(dma((5,)),),
        spaces=dict.fromkeys(range(5), hbm),
        after=rows_input[:1],
        limit=4,
        us=2,
    )
    framed = halo(center, rows_input, "strips_input")
    inputs = (
        expand_weight, project_weight, patch_weight, kernel_four, gain_four,
        normed_cotangent[0], residual_cotangent[0],
    )
    edge_four = shape_of(3, cols4, wide, dtype=BF)
    (
        early, unit_mixed, inverse_mixed, slope, branch, unit_summed, inverse_summed,
        section, first, last,
        expand_weight, project_weight, patch_weight, taps_four, gain_four, cotangent, residual,
    ) = run(
        front_kernel,
        "front",
        (*framed, taps_three, gain_three, layer_scale, merge_gain, *inputs),
        (
            shape_of(pixels, hidden_width + 2 * channels, dtype=BF),
            shape_of(pixels, channels),
            shape_of(pixels, 1),
            shape_of(pixels, hidden_width, dtype=BF),
            shape_of(pixels, channels),
            shape_of(pixels, channels),
            shape_of(pixels, 1),
            shape_of(rows4, cols4, wide, dtype=BF),
            edge_four,
            edge_four,
            *map(like, inputs),
        ),
        scratch=(
            frame_scratch(center),
            pltpu.VMEM((height, breadth, channels), F32),
            pltpu.VMEM((channels // 128, height, breadth, 128), F32),
            pltpu.VMEM((pixels, CHUNK), F32),
            dma((7,)),
        ),
        spaces=dict.fromkeys(range(9, 16), hbm),
        limit=28,
        us=12,
    )

    framed_four = halo(section, neighbours(first, last, "row"), "strips_section")
    mixer_image = pltpu.VMEM((rows4, cols4, wide), F32)
    grad_four, grad_four_half, first, last, gain_four_part = run(
        mixer_kernel,
        "mixer",
        (*framed_four, taps_four, gain_four, cotangent),
        (
            shape_of(rows4, cols4, wide),
            shape_of(rows4, cols4, wide, dtype=BF),
            edge_four,
            edge_four,
            shape_of(1, wide),
        ),
        scratch=(frame_scratch(section), mixer_image),
        limit=12,
        us=3,
    )
    rows_grad = neighbours(first, last, "row")
    (kernel_four_part,) = run(
        functools.partial(weight_kernel, scale_four),
        "mixer_weights",
        (*framed_four, grad_four),
        (shape_of(49, wide),),
        scratch=(frame_scratch(section),),
        after=rows_grad[:1],
        limit=12,
        us=3,
    )
    framed_grad = halo(grad_four_half, rows_grad, "strips_mixer", after=(kernel_four_part,))
    block_count = col_count // 2
    block = wide // col_count
    blocked = shape_of(block_count, quarter, block, dtype=BF)
    flat, flat_keep, flat_send, early = hold(
        section_kernel,
        "section_grad",
        (*framed_grad, taps_four, residual),
        (shape_of(quarter, wide, dtype=BF), blocked, blocked),
        early,
        scratch=(frame_scratch(section), mixer_image),
        limit=12,
        us=3,
    )

    flat_other = swap(flat_send, "col", 1)
    early_other = swap(early, "col", 1)
    split = shape_of(pixels + 112, half, dtype=BF)
    grad_summed, grad_branch, branch_keep, branch_send = run(
        functools.partial(merge_kernel, scale_three, scale_four),
        "merge_back",
        (
            flat, patch_weight, unit_summed, inverse_summed, merge_gain, branch, layer_scale,
            kernel_four_part, gain_four_part,
        ),
        (shape_of(pixels, channels), shape_of(pixels, channels, dtype=BF), split, split),
        scratch=(
            pltpu.VMEM((channels // 128, height, breadth, 128), F32),
            pltpu.VMEM((112, channels), F32),
            pltpu.VMEM((8, channels), F32),
        ),
        limit=16,
        us=0.8,
    )
    branch_other = swap(branch_send, "col", 1)
    deep, shallow = hidden_width // row_count, channels // row_count
    groups = hidden_width // channels
    upward_half = shape_of(pixels, hidden_width // 2, dtype=BF)
    upward_keep, upward_send, grad_mixed, first, last, gain_part = run(
        back_kernel,
        "mlp_back",
        (grad_branch, project_weight, slope, expand_weight, unit_mixed, inverse_mixed, gain_three),
        (
            upward_half,
            upward_half,
            shape_of(height, breadth, channels, dtype=BF),
            edge,
            edge,
            shape_of(1, channels),
        ),
        scratch=(
            pltpu.VMEM((pixels, CHUNK), F32),
            pltpu.VMEM((pixels, hidden_width), BF),
            pltpu.VMEM((pixels, channels), F32),
        ),
        limit=16,
        us=1.2,
    )
    rows_back = neighbours(first, last, "row")
    upward_other = swap(upward_send, "col", 1)
    patch_half = shape_of(block_count // 2 * 4 * channels, block, dtype=BF)
    patch_keep, patch_send = run(
        functools.partial(patch_product_kernel, scale_four),
        "patch_product",
        (early, early_other, flat_keep, flat_other),
        (patch_half, patch_half),
        after=(upward_send,),
        limit=16,
        us=0.9,
    )
    expand_half = shape_of(row_count // 2 * groups * shallow, half, dtype=BF)
    expand_keep, expand_send = run(
        functools.partial(expand_product_kernel, scale_three, row_count),
        "expand_product",
        (early, early_other, upward_keep, upward_other),
        (expand_half, expand_half),
        after=(patch_send, rows_back[0]),
        limit=16,
        us=0.6,
    )
    project_half = shape_of(row_count // 2 * deep + 112, half, dtype=BF)
    project_keep, project_send = run(
        functools.partial(project_product_kernel, scale_three, row_count),
        "project_product",
        (early, early_other, branch_keep, branch_other),
        (project_half, project_half),
        after=(expand_send,),
        limit=16,
        us=0.9,
    )
    framed_back = halo(grad_mixed, rows_back, "strips_back", after=(project_send,))
    small_half = shape_of(64, half, dtype=BF)
    small_keep, small_send = run(
        functools.partial(weight_pack_kernel, scale_three),
        "block_weights",
        (*framed, grad_mixed, gain_part),
        (small_half, small_half),
        scratch=(
            frame_scratch(center),
            pltpu.VMEM((height, breadth, channels), F32),
            pltpu.VMEM((64, channels), F32),
        ),
        after=(project_send,),
        limit=12,
        us=1.8,
    )
    row_bits, col_bits = axis_bits("row"), axis_bits("col")
    outer = len(row_bits)
    low_first = [("row", bit, 0) for bit in row_bits]
    patch_order = [("col", bit, outer) for bit in col_bits[1:]] + low_first
    project_order = [("row", row_bits[1], 1), low_first[0], *low_first[2:]]
    patch_chain = Chain(patch_keep, patch_send, patch_order, block_count * row_count, 4 * channels // row_count)
    project_chain = Chain(project_keep, project_send, project_order, row_count, deep)
    expand_chain = Chain(expand_keep, expand_send, low_first, row_count, groups * shallow)
    small = small_keep + swap(small_send, "col", 1)
    sent = expand_chain.advance(extra=(small, swap(small, "row", 1)))
    sent = project_chain.advance(sent)
    sent = patch_chain.advance(sent)
    (input_grad,) = run(
        input_kernel,
        "input_grad",
        (*framed_back, taps_three, grad_summed),
        (shape_of(height, breadth, channels, dtype=BF),),
        scratch=(frame_scratch(center), pltpu.VMEM((height, breadth, channels), F32)),
        after=sent,
        limit=12,
        us=2,
    )
    sent = expand_chain.advance((input_grad,))
    sent = project_chain.advance(sent)
    patch_chain.advance(sent)
    patch_sum = patch_chain.finish()
    patch_sum = gather(patch_sum, "col", col_bits[1:])
    (patch_grad,) = run(
        finish_patch_kernel,
        "finish_patch",
        (patch_sum, swap(patch_sum, "col", 1)),
        (shape_of(4 * channels // row_count, wide),),
        limit=8,
    )

    def share(total):
        for bit in col_bits[1:]:
            total = total + swap(total, "col", bit)
        return total, swap(total, "col", 1)

    vector, wide_vector = shape_of(1, channels), shape_of(1, wide)
    project_grad, wide_taps, wide_gain, merge_sum, layer_sum = run(
        finish_project_kernel,
        "finish_project",
        share(project_chain.finish()),
        (shape_of(deep, channels), shape_of(7, 7, wide), wide_vector, vector, vector),
        scratch=(pltpu.VMEM((112, channels), F32),),
        limit=8,
    )
    expand_grad, taps_sum, gain_sum = run(
        finish_expand_kernel,
        "finish_expand",
        share(expand_chain.finish()),
        (shape_of(shallow, hidden_width), shape_of(7, 7, channels), vector),
        scratch=(pltpu.VMEM((64, channels), F32),),
        limit=8,
    )
    return (
        input_grad[None],
        taps_sum,
        gain_sum[0],
        expand_grad,
        project_grad,
        layer_sum[0],
        merge_sum[0],
        patch_grad,
        wide_taps,
        wide_gain[0],
    )


def solution(mesh):
    pixels = P(None, "row", "col", None)
    return jax.shard_map(
        body,
        mesh=mesh,
        in_specs=(pixels,) + (P(),) * 9 + (pixels, pixels),
        out_specs=(pixels, P(), P(), P("row", None), P("row", None), P(), P(), P("row", None), P(), P()),
        check_vma=False,
    )
```

```python
import functools
import math

import jax
import jax.numpy as jnp
from jax import lax
from jax.experimental import pallas as pl
from jax.experimental.pallas import tpu as pltpu
from jax.sharding import PartitionSpec as P

EPSILON = 1e-06
BF = jnp.bfloat16
F32 = jnp.float32
MIB = 1 << 20
PAD = 8
CHUNK = 256


def shape_of(*dims, dtype=F32):
    return jax.ShapeDtypeStruct(dims, dtype)


def run(kernel, name, args, outs, scratch=(), spaces=None, after=(), aliases=None, limit=24, us=0.0):
    spaces = spaces or {}
    count, extra = len(args), len(after)

    def spec(place):
        return pl.BlockSpec(memory_space=spaces.get(place, pltpu.VMEM))

    def inner(*refs):
        kernel(*refs[:count], *refs[count + extra :])

    return pl.pallas_call(
        inner,
        name=name,
        out_shape=outs,
        in_specs=[spec(i) for i in range(count)] + [pl.BlockSpec(memory_space=pl.ANY)] * extra,
        out_specs=[spec(("out", i)) for i in range(len(outs))],
        scratch_shapes=list(scratch),
        input_output_aliases=aliases or {},
        compiler_params=pltpu.CompilerParams(vmem_limit_bytes=limit * MIB),
        cost_estimate=pl.CostEstimate(flops=int(us * 1.1e9) + 1000, bytes_accessed=1000, transcendentals=0),
    )(*args, *after)


def swap(values, axis, bit):
    return lax.ppermute(values, axis, [(i, i ^ bit) for i in range(lax.axis_size(axis))])


def axis_bits(axis):
    return [1 << k for k in range((lax.axis_size(axis) - 1).bit_length())]


def own_bit(axis, bit):
    return (lax.axis_index(axis) // bit) % 2


class Chain:
    def __init__(self, keep, send, order, count, rows):
        self.keep, self.send, self.order = keep, send, list(order)
        self.count, self.rows = count, rows

    def advance(self, after=(), extra=()):
        axis, bit, _ = self.order.pop(0)
        keep, received = self.keep, swap(self.send, axis, bit)
        if not self.order:
            self.keep = keep + received
            return ()
        axis, bit, position = self.order[0]
        self.count //= 2
        tail = keep.shape[0] - self.count * self.rows + (extra[0].shape[0] if extra else 0)
        out = shape_of(self.count // 2 * self.rows + tail, keep.shape[1], dtype=BF)
        self.keep, self.send = run(
            functools.partial(step_kernel, axis, bit, position, self.count, self.rows),
            "sum_step",
            (keep, received, *extra),
            (out, out),
            after=after,
            limit=8,
            us=0.2,
        )
        return (self.send,)

    def finish(self):
        while self.order:
            self.advance()
        return self.keep


def step_kernel(axis, bit, position, count, rows, keep, received, *refs):
    *grown, next_keep, next_send = refs
    mine = (lax.axis_index(axis) // bit) % 2
    low = (1 << position) - 1
    for i in range(2):

        @pl.when(mine == i)
        def _():
            for s in range(count):
                span = slice(s * rows, (s + 1) * rows)
                at = ((s >> (position + 1)) << position | (s & low)) * rows
                target = next_keep if (s >> position) & 1 == i else next_send
                target[at : at + rows] = (keep[span].astype(F32) + received[span].astype(F32)).astype(BF)

    tails = []
    if keep.shape[0] > count * rows:
        tails.append(keep[count * rows :].astype(F32) + received[count * rows :].astype(F32))
    if grown:
        tails.append(sum(g[...].astype(F32) for g in grown))
    at = count // 2 * rows
    for tail in tails:
        for target in (next_keep, next_send):
            target[at : at + tail.shape[0]] = tail.astype(BF)
        at += tail.shape[0]


def gather(values, axis, bits):
    values = values[None]
    for bit in reversed(bits):
        other = swap(values, axis, bit)
        mine = own_bit(axis, bit)
        low = jnp.where(mine == 0, values, other)
        high = jnp.where(mine == 0, other, values)
        values = jnp.stack([low, high], axis=1).reshape(-1, *values.shape[1:])
    return values


def neighbours(first, last, axis):
    count = lax.axis_size(axis)
    forward = [(i, i + 1) for i in range(count - 1)]
    backward = [(i + 1, i) for i in range(count - 1)]
    return lax.ppermute(last, axis, forward), lax.ppermute(first, axis, backward)


def strip_kernel(center, top, bottom, first, last):
    height, breadth = center.shape[:2]
    for source, start in ((top, 0), (center, 3), (bottom, 3 + height)):
        values = source[...].astype(F32)
        rows = slice(start, start + source.shape[0])
        first[rows] = values[:, :PAD].astype(BF)
        last[rows] = values[:, breadth - PAD :].astype(BF)


def halo(center, rows, name, after=()):
    height, _, channels = center.shape
    top, bottom = rows
    strip = shape_of(height + 6, PAD, channels, dtype=BF)
    first, last = run(strip_kernel, name, (center, top, bottom), (strip, strip), after=after, limit=8)
    left, right = neighbours(first, last, "col")
    return center, top, bottom, left, right


def hold(kernel, name, args, outs, carried, **options):
    count = len(args)

    def inner(*refs):
        kernel(*refs[:count], *refs[count + 1 : count + 1 + len(outs)], *refs[count + 2 + len(outs) :])

    return run(
        inner,
        name,
        (*args, carried),
        (*outs, shape_of(*carried.shape, dtype=carried.dtype)),
        spaces={count: pl.ANY, ("out", len(outs)): pl.ANY},
        aliases={count: len(outs)},
        **options,
    )


def fill_frame(frame, parts):
    center, top, bottom, left, right = parts
    height, breadth = center.shape[:2]
    middle = slice(PAD, PAD + breadth)
    frame[0:3, middle] = top[...].astype(F32)
    frame[3 : 3 + height, middle] = center[...].astype(F32)
    frame[3 + height :, middle] = bottom[...].astype(F32)
    frame[:, :PAD] = left[...].astype(F32)
    frame[:, PAD + breadth :] = right[...].astype(F32)


def frame_scratch(center):
    height, breadth, channels = center.shape
    return pltpu.VMEM((height + 6, breadth + 2 * PAD, channels), F32)


def lane_tiles(channels):
    def over(step):
        def wrapped(index, carry):
            step(pl.ds(pl.multiple_of(index * 128, 128), 128))
            return carry

        lax.fori_loop(0, channels // 128, wrapped, 0)

    return over


def convolve(frame, taps, flip, out):
    height, breadth, channels = out.shape

    @lane_tiles(channels)
    def _(lanes):
        for column in range(0, breadth, 8):
            total = jnp.zeros((height, 8, 128), F32)
            for q in range(7):
                rows = frame[:, pl.ds(column + PAD - 3 + q, 8), lanes]
                for p in range(7):
                    a, b = (6 - p, 6 - q) if flip else (p, q)
                    total = total + rows[p : p + height] * taps[a, pl.ds(b, 1), lanes]
            out[:, pl.ds(column, 8), lanes] = total


def weight_sums(frame, grads, scale, out):
    height, breadth, channels = grads.shape

    @lane_tiles(channels)
    def _(lanes):
        for q in range(7):
            totals = [jnp.zeros((8, 128), F32)] * 7
            for column in range(0, breadth, 8):
                rows = frame[:, pl.ds(column + PAD - 3 + q, 8), lanes]
                grad = grads[:, pl.ds(column, 8), lanes]
                for p in range(7):
                    totals[p] = totals[p] + jnp.sum(rows[p : p + height] * grad, axis=0)
            for p in range(7):
                out[pl.ds(7 * p + q, 1), lanes] = scale * jnp.sum(totals[p], axis=0, keepdims=True)


def mean(values):
    return jnp.mean(values, axis=-1, keepdims=True)


def normalize(values):
    level = mean(values)
    inverse = lax.rsqrt(mean(values * values) - level * level + EPSILON)
    return (values - level) * inverse, inverse


def normalize_back(grads, unit_values, inverse):
    return (grads - mean(grads) - unit_values * mean(grads * unit_values)) * inverse


def dot(left, right):
    return jnp.dot(left, right, preferred_element_type=F32)


def dot_last(left, right):
    return lax.dot_general(left, right, (((1,), (1,)), ((), ())), preferred_element_type=F32)


def dot_first(left, right):
    return lax.dot_general(left, right, (((0,), (0,)), ((), ())), preferred_element_type=F32)


def over_rows(count, size):
    def over(step):
        def wrapped(index, carry):
            step(index, pl.ds(pl.multiple_of(index * size, size), size))
            return carry

        lax.fori_loop(0, count, wrapped, 0)

    return over


def fetch(sources, targets, semaphores):
    copies = [
        pltpu.make_async_copy(source, target, semaphores.at[i])
        for i, (source, target) in enumerate(zip(sources, targets))
    ]
    for copy in copies:
        copy.start()
    return copies


def load_kernel(*refs):
    *arrays, semaphores = refs
    count = len(arrays) // 2
    for copy in fetch(arrays[:count], arrays[count:], semaphores):
        copy.wait()


def front_kernel(
    center, top, bottom, left, right, taps, gain, layer_scale, merge_gain,
    expand, project, patch, wide_taps, wide_gain, cotangent, residual,
    early, unit_mixed, inverse_mixed, slope, branch, unit_summed, inverse_summed, section, first, last,
    expand_here, project_here, patch_here, wide_taps_here, wide_gain_here, cotangent_here, residual_here,
    frame, image, pairs, upward, semaphores,
):
    height, breadth, channels = center.shape
    hidden_width = expand.shape[1]
    pixels = height * breadth
    copies = fetch(
        (expand, project, patch, wide_taps, wide_gain, cotangent, residual),
        (expand_here, project_here, patch_here, wide_taps_here, wide_gain_here, cotangent_here, residual_here),
        semaphores,
    )
    fill_frame(frame, (center, top, bottom, left, right))
    convolve(frame, taps, False, image)
    at_normed = slice(hidden_width, hidden_width + channels)
    at_patches = slice(hidden_width + channels, hidden_width + 2 * channels)

    @over_rows(height, breadth)
    def _(y, rows):
        unit, inverse = normalize(image[y])
        unit_mixed[rows] = unit
        inverse_mixed[rows] = inverse
        early[rows, at_normed] = (unit * gain[...]).astype(BF)

    copies[0].wait()

    def chunk(index, carry):
        lanes = pl.ds(pl.multiple_of(index * CHUNK, CHUNK), CHUNK)
        upward[...] = dot(early[:, at_normed], expand_here[:, lanes])
        for start in range(0, pixels, 64):
            rows = slice(start, start + 64)
            value = upward[rows]
            cumulative = 0.5 + 0.5 * lax.erf(value * (1.0 / math.sqrt(2.0)))
            density = jnp.exp(-0.5 * value * value) * (1.0 / math.sqrt(2.0 * math.pi))
            early[rows, lanes] = (value * cumulative).astype(BF)
            slope[rows, lanes] = (cumulative + value * density).astype(BF)
        return carry

    lax.fori_loop(0, hidden_width // CHUNK, chunk, 0)
    copies[1].wait()
    branch[...] = dot(early[:, :hidden_width], project_here[...])

    @over_rows(height, breadth)
    def _(y, rows):
        summed = center[y].astype(F32) + layer_scale[...] * branch[rows]
        unit, inverse = normalize(summed)
        unit_summed[rows] = unit
        inverse_summed[rows] = inverse
        merged = unit * merge_gain[...]
        for k in range(channels // 128):
            pairs[k, y] = merged[:, k * 128 : (k + 1) * 128]

    quarter = pixels // 4
    for dy in range(2):
        for dx in range(2):
            j = 2 * dy + dx
            for y in range(height // 2):
                start = j * quarter + y * (breadth // 2)
                for k in range(channels // 128):
                    piece = pairs[k, 2 * y + dy, pl.ds(dx, breadth // 2, stride=2), :]
                    lane = hidden_width + channels + k * 128
                    early[start : start + breadth // 2, lane : lane + 128] = piece.astype(BF)
    copies[2].wait()
    total = dot(early[:quarter, at_patches], patch_here[:channels])
    for j in range(1, 4):
        total = total + dot(
            early[j * quarter : (j + 1) * quarter, at_patches],
            patch_here[j * channels : (j + 1) * channels],
        )
    total = total.reshape(section.shape)
    section[...] = total.astype(BF)
    first[...] = total[:3].astype(BF)
    last[...] = total[height // 2 - 3 :].astype(BF)
    for copy in copies[3:]:
        copy.wait()


def mixer_kernel(
    center, top, bottom, left, right, taps, gain, cotangent,
    grad, grad_half, first, last, gain_part,
    frame, image,
):
    height, breadth, channels = center.shape
    fill_frame(frame, (center, top, bottom, left, right))
    convolve(frame, taps, False, image)
    part = jnp.zeros((1, channels), F32)
    for y in range(height):
        unit, inverse = normalize(image[y])
        cot = cotangent[y].astype(F32)
        part = part + jnp.sum(cot * unit, axis=0, keepdims=True)
        value = normalize_back(cot * gain[...], unit, inverse)
        grad[y] = value
        narrow = value.astype(BF)
        grad_half[y] = narrow
        if y < 3:
            first[y] = narrow
        if y >= height - 3:
            last[y - (height - 3)] = narrow
    gain_part[...] = part


def weight_kernel(scale, center, top, bottom, left, right, grads, out, frame):
    fill_frame(frame, (center, top, bottom, left, right))
    weight_sums(frame, grads, scale, out)


def split_halves(values, start, keep, send):
    half = values.shape[1] // 2
    rows = slice(start, start + values.shape[0])
    core = lax.axis_index("col") % 2
    for i in range(2):

        @pl.when(core == i)
        def _():
            keep[rows] = values[:, i * half : (i + 1) * half]
            send[rows] = values[:, (1 - i) * half : (2 - i) * half]


def weight_pack_kernel(
    scale, center, top, bottom, left, right, grads, gain_part,
    keep, send, frame, wide_grads, packed,
):
    fill_frame(frame, (center, top, bottom, left, right))
    wide_grads[...] = grads[...].astype(F32)
    packed[...] = jnp.zeros(packed.shape, F32)
    weight_sums(frame, wide_grads, scale, packed)
    packed[49:50] = scale * gain_part[...]
    split_halves(packed[...].astype(BF), 0, keep, send)


def section_kernel(
    center, top, bottom, left, right, taps, residual,
    flat, keep, send,
    frame, image,
):
    height, breadth, channels = center.shape
    fill_frame(frame, (center, top, bottom, left, right))
    convolve(frame, taps, True, image)
    value = (image[...] + residual[...].astype(F32)).reshape(flat.shape).astype(BF)
    flat[...] = value
    blocks, _, width = keep.shape
    core = lax.axis_index("col") % 2
    for i in range(2):

        @pl.when(core == i)
        def _():
            for m in range(blocks):
                mine, other = (2 * m + i) * width, (2 * m + 1 - i) * width
                keep[m] = value[:, mine : mine + width]
                send[m] = value[:, other : other + width]


def merge_kernel(
    scale, scale_wide,
    flat, patch, unit_summed, inverse_summed, merge_gain, branch, layer_scale, wide_part, wide_gain,
    grad_summed, grad_branch, keep, send,
    pairs, packed, sums,
):
    tiles, height, breadth, _ = pairs.shape
    channels = 128 * tiles
    value = flat[...]
    for dy in range(2):
        for dx in range(2):
            j = 2 * dy + dx
            part = dot_last(value, patch[j * channels : (j + 1) * channels])
            part = part.reshape(height // 2, breadth // 2, channels)
            for y in range(height // 2):
                for k in range(tiles):
                    piece = part[y, :, k * 128 : (k + 1) * 128]
                    pairs[k, 2 * y + dy, pl.ds(dx, breadth // 2, stride=2), :] = piece
    sums[...] = jnp.zeros(sums.shape, F32)

    @over_rows(height, breadth)
    def _(y, rows):
        merged = jnp.concatenate([pairs[k, y] for k in range(tiles)], axis=1)
        unit = unit_summed[rows]
        sums[0:1] += jnp.sum(merged * unit, axis=0, keepdims=True)
        grad = normalize_back(merged * merge_gain[...], unit, inverse_summed[rows])
        grad_summed[rows] = grad
        sums[1:2] += jnp.sum(grad * branch[rows], axis=0, keepdims=True)
        grad_branch[rows] = (layer_scale[...] * grad).astype(BF)

    split_halves(grad_branch[...], 0, keep, send)
    packed[...] = jnp.zeros(packed.shape, F32)
    for i in range(2):
        columns = slice(i * channels, (i + 1) * channels)
        packed[49 * i : 49 + 49 * i] = wide_part[:, columns]
        packed[98 + i : 99 + i] = scale_wide * wide_gain[:, columns]
        packed[100 + i : 101 + i] = scale * sums[i : i + 1]
    split_halves(packed[...].astype(BF), grad_branch.shape[0], keep, send)


def back_kernel(
    grad_branch, project, slope, expand, unit_mixed, inverse_mixed, gain,
    keep, send, grad_mixed, first, last, gain_part,
    hidden, upward, normed,
):
    height, breadth, channels = grad_mixed.shape
    pixels, hidden_width = slope.shape

    def chunk(index, carry):
        span = pl.ds(pl.multiple_of(index * CHUNK, CHUNK), CHUNK)
        hidden[...] = dot_last(grad_branch[...], project[span])
        for start in range(0, pixels, 64):
            rows = slice(start, start + 64)
            upward[rows, span] = (hidden[rows] * slope[rows, span].astype(F32)).astype(BF)
        return carry

    lax.fori_loop(0, hidden_width // CHUNK, chunk, 0)
    normed[...] = dot_last(upward[...], expand[...])
    split_halves(upward[...], 0, keep, send)
    part = jnp.zeros((1, channels), F32)
    for y in range(height):
        rows = slice(y * breadth, (y + 1) * breadth)
        value = normed[rows]
        unit = unit_mixed[rows]
        part = part + jnp.sum(value * unit, axis=0, keepdims=True)
        narrow = normalize_back(value * gain[...], unit, inverse_mixed[rows]).astype(BF)
        grad_mixed[y] = narrow
        if y < 3:
            first[y] = narrow
        if y >= height - 3:
            last[y - (height - 3)] = narrow
    gain_part[...] = part


def patch_product_kernel(factor, early, early_other, own, other, keep, send):
    blocks, quarter, _ = own.shape
    rows = keep.shape[0] // max(blocks // 2, 1)
    channels = rows // 4
    at_patches = early.shape[1] - channels
    bit = (lax.axis_index("col") // 2) % 2
    for j in range(4):
        span = slice(j * quarter, (j + 1) * quarter)
        left = jnp.concatenate([early[span, at_patches:], early_other[span, at_patches:]], axis=0)
        for m in range(blocks):
            right = jnp.concatenate([own[m], other[m]], axis=0)
            value = (factor * dot_first(left, right)).astype(BF)
            at = m // 2 * rows + j * channels
            for i in range(2):

                @pl.when(bit == i)
                def _():
                    target = keep if m % 2 == i else send
                    target[at : at + channels] = value


def store_slices(position, value, begin, offset, rows, pitch, keep, send):
    bit = (lax.axis_index("row") >> position) % 2
    low = (1 << position) - 1
    for i in range(2):

        @pl.when(bit == i)
        def _():
            for k in range(value.shape[0] // rows):
                r = begin + k
                target = keep if (r >> position) & 1 == i else send
                at = ((r >> (position + 1)) << position | (r & low)) * pitch + offset
                target[at : at + rows] = value[k * rows : (k + 1) * rows]


def project_product_kernel(factor, slices, early, early_other, own, other, keep, send):
    width = keep.shape[1]
    hidden_width = early.shape[1] - 4 * width
    pixels = early.shape[0]
    deep = hidden_width // slices
    right = jnp.concatenate([own[:pixels], other[:pixels]], axis=0)
    step = max(CHUNK, deep)
    for start in range(0, hidden_width, step):
        columns = slice(start, start + step)
        left = jnp.concatenate([early[:, columns], early_other[:, columns]], axis=0)
        value = (factor * dot_first(left, right)).astype(BF)
        store_slices(1, value, start // deep, 0, deep, deep, keep, send)
    tail = (own[pixels:].astype(F32) + other[pixels:].astype(F32)).astype(BF)
    at = slices // 2 * deep
    keep[at:] = tail
    send[at:] = tail


def expand_product_kernel(factor, slices, early, early_other, own, other, keep, send):
    width = keep.shape[1]
    channels = 2 * width
    hidden_width = early.shape[1] - 2 * channels
    shallow = channels // slices
    blocks = own.shape[1] // width
    columns = slice(hidden_width, hidden_width + channels)
    left = jnp.concatenate([early[:, columns], early_other[:, columns]], axis=0)
    for k in range(blocks):
        columns = slice(k * width, (k + 1) * width)
        right = jnp.concatenate([own[:, columns], other[:, columns]], axis=0)
        value = (factor * dot_first(left, right)).astype(BF)
        store_slices(0, value, 0, k * shallow, shallow, blocks * shallow, keep, send)


def finish_patch_kernel(own, other, out):
    blocks, _, width = own.shape
    core = lax.axis_index("col") % 2
    for i in range(2):

        @pl.when(core == i)
        def _():
            for m in range(blocks):
                a, b = (2 * m + i) * width, (2 * m + 1 - i) * width
                out[:, a : a + width] = own[m].astype(F32)
                out[:, b : b + width] = other[m].astype(F32)


def join_halves(own, other, start, out):
    half = own.shape[1]
    rows = slice(start, start + out.shape[0])
    core = lax.axis_index("col") % 2
    for i in range(2):

        @pl.when(core == i)
        def _():
            out[:, i * half : (i + 1) * half] = own[rows].astype(F32)
            out[:, (1 - i) * half : (2 - i) * half] = other[rows].astype(F32)


def finish_project_kernel(own, other, project, wide_taps, wide_gain, merge, layer, small):
    deep, channels = project.shape
    join_halves(own, other, 0, project)
    join_halves(own, other, deep, small)
    for i in range(2):
        columns = slice(i * channels, (i + 1) * channels)
        for p in range(7):
            start = 49 * i + 7 * p
            wide_taps[p, :, columns] = small[start : start + 7]
        wide_gain[:, columns] = small[98 + i : 99 + i]
    merge[...] = small[100:101]
    layer[...] = small[101:102]


def finish_expand_kernel(own, other, expand, taps, gain, small):
    shallow, hidden_width = expand.shape
    width = own.shape[1]
    blocks = hidden_width // (2 * width)
    core = lax.axis_index("col") % 2
    for i in range(2):

        @pl.when(core == i)
        def _():
            for k in range(blocks):
                rows = slice(k * shallow, (k + 1) * shallow)
                a, b = (i * blocks + k) * width, ((1 - i) * blocks + k) * width
                expand[:, a : a + width] = own[rows].astype(F32)
                expand[:, b : b + width] = other[rows].astype(F32)

    join_halves(own, other, blocks * shallow, small)
    for p in range(7):
        taps[p] = small[7 * p : 7 * p + 7]
    gain[...] = small[49:50]


def input_kernel(center, top, bottom, left, right, taps, grad_summed, out, frame, image):
    fill_frame(frame, (center, top, bottom, left, right))
    convolve(frame, taps, True, image)
    out[...] = (image[...] + grad_summed[...].reshape(image.shape)).astype(BF)


def body(
    block_input,
    kernel_three,
    gain_three,
    expand_weight,
    project_weight,
    layer_scale,
    merge_gain,
    patch_weight,
    kernel_four,
    gain_four,
    normed_cotangent,
    residual_cotangent,
):
    _, height, breadth, channels = block_input.shape
    hidden_width = expand_weight.shape[1]
    wide = patch_weight.shape[1]
    pixels = height * breadth
    quarter = pixels // 4
    rows4, cols4 = height // 2, breadth // 2
    row_count = lax.axis_size("row")
    col_count = lax.axis_size("col")
    scale_three = 1.0 / math.sqrt(pixels * row_count * col_count)
    scale_four = 1.0 / math.sqrt(quarter * row_count * col_count)
    center = block_input[0]
    gain_three, layer_scale, merge_gain, gain_four = (
        v[None] for v in (gain_three, layer_scale, merge_gain, gain_four)
    )
    dma = pltpu.SemaphoreType.DMA
    half = channels // 2
    hbm = pltpu.HBM

    def like(array):
        return shape_of(*array.shape, dtype=array.dtype)

    edge = shape_of(3, breadth, channels, dtype=BF)
    rows_input = neighbours(center[:3], center[height - 3 :], "row")
    inputs = (center, kernel_three, gain_three, layer_scale, merge_gain)
    center, taps_three, gain_three, layer_scale, merge_gain = run(
        load_kernel,
        "load",
        inputs,
        tuple(map(like, inputs)),
        scratch=(dma((5,)),),
        spaces=dict.fromkeys(range(5), hbm),
        after=rows_input[:1],
        limit=4,
        us=2,
    )
    framed = halo(center, rows_input, "strips_input")
    inputs = (
        expand_weight, project_weight, patch_weight, kernel_four, gain_four,
        normed_cotangent[0], residual_cotangent[0],
    )
    edge_four = shape_of(3, cols4, wide, dtype=BF)
    (
        early, unit_mixed, inverse_mixed, slope, branch, unit_summed, inverse_summed,
        section, first, last,
        expand_weight, project_weight, patch_weight, taps_four, gain_four, cotangent, residual,
    ) = run(
        front_kernel,
        "front",
        (*framed, taps_three, gain_three, layer_scale, merge_gain, *inputs),
        (
            shape_of(pixels, hidden_width + 2 * channels, dtype=BF),
            shape_of(pixels, channels),
            shape_of(pixels, 1),
            shape_of(pixels, hidden_width, dtype=BF),
            shape_of(pixels, channels),
            shape_of(pixels, channels),
            shape_of(pixels, 1),
            shape_of(rows4, cols4, wide, dtype=BF),
            edge_four,
            edge_four,
            *map(like, inputs),
        ),
        scratch=(
            frame_scratch(center),
            pltpu.VMEM((height, breadth, channels), F32),
            pltpu.VMEM((channels // 128, height, breadth, 128), F32),
            pltpu.VMEM((pixels, CHUNK), F32),
            dma((7,)),
        ),
        spaces=dict.fromkeys(range(9, 16), hbm),
        limit=28,
        us=12,
    )

    framed_four = halo(section, neighbours(first, last, "row"), "strips_section")
    mixer_image = pltpu.VMEM((rows4, cols4, wide), F32)
    grad_four, grad_four_half, first, last, gain_four_part = run(
        mixer_kernel,
        "mixer",
        (*framed_four, taps_four, gain_four, cotangent),
        (
            shape_of(rows4, cols4, wide),
            shape_of(rows4, cols4, wide, dtype=BF),
            edge_four,
            edge_four,
            shape_of(1, wide),
        ),
        scratch=(frame_scratch(section), mixer_image),
        limit=12,
        us=3,
    )
    rows_grad = neighbours(first, last, "row")
    (kernel_four_part,) = run(
        functools.partial(weight_kernel, scale_four),
        "mixer_weights",
        (*framed_four, grad_four),
        (shape_of(49, wide),),
        scratch=(frame_scratch(section),),
        after=rows_grad[:1],
        limit=12,
        us=3,
    )
    framed_grad = halo(grad_four_half, rows_grad, "strips_mixer", after=(kernel_four_part,))
    block_count = col_count // 2
    block = wide // col_count
    blocked = shape_of(block_count, quarter, block, dtype=BF)
    flat, flat_keep, flat_send, early = hold(
        section_kernel,
        "section_grad",
        (*framed_grad, taps_four, residual),
        (shape_of(quarter, wide, dtype=BF), blocked, blocked),
        early,
        scratch=(frame_scratch(section), mixer_image),
        limit=12,
        us=3,
    )

    flat_other = swap(flat_send, "col", 1)
    early_other = swap(early, "col", 1)
    split = shape_of(pixels + 112, half, dtype=BF)
    grad_summed, grad_branch, branch_keep, branch_send = run(
        functools.partial(merge_kernel, scale_three, scale_four),
        "merge_back",
        (
            flat, patch_weight, unit_summed, inverse_summed, merge_gain, branch, layer_scale,
            kernel_four_part, gain_four_part,
        ),
        (shape_of(pixels, channels), shape_of(pixels, channels, dtype=BF), split, split),
        scratch=(
            pltpu.VMEM((channels // 128, height, breadth, 128), F32),
            pltpu.VMEM((112, channels), F32),
            pltpu.VMEM((8, channels), F32),
        ),
        limit=16,
        us=0.8,
    )
    branch_other = swap(branch_send, "col", 1)
    deep, shallow = hidden_width // row_count, channels // row_count
    groups = hidden_width // channels
    upward_half = shape_of(pixels, hidden_width // 2, dtype=BF)
    upward_keep, upward_send, grad_mixed, first, last, gain_part = run(
        back_kernel,
        "mlp_back",
        (grad_branch, project_weight, slope, expand_weight, unit_mixed, inverse_mixed, gain_three),
        (
            upward_half,
            upward_half,
            shape_of(height, breadth, channels, dtype=BF),
            edge,
            edge,
            shape_of(1, channels),
        ),
        scratch=(
            pltpu.VMEM((pixels, CHUNK), F32),
            pltpu.VMEM((pixels, hidden_width), BF),
            pltpu.VMEM((pixels, channels), F32),
        ),
        limit=16,
        us=1.2,
    )
    rows_back = neighbours(first, last, "row")
    upward_other = swap(upward_send, "col", 1)
    patch_half = shape_of(block_count // 2 * 4 * channels, block, dtype=BF)
    patch_keep, patch_send = run(
        functools.partial(patch_product_kernel, scale_four),
        "patch_product",
        (early, early_other, flat_keep, flat_other),
        (patch_half, patch_half),
        after=(upward_send,),
        limit=16,
        us=0.9,
    )
    expand_half = shape_of(row_count // 2 * groups * shallow, half, dtype=BF)
    expand_keep, expand_send = run(
        functools.partial(expand_product_kernel, scale_three, row_count),
        "expand_product",
        (early, early_other, upward_keep, upward_other),
        (expand_half, expand_half),
        after=(patch_send, *rows_back),
        limit=16,
        us=0.6,
    )
    project_half = shape_of(row_count // 2 * deep + 112, half, dtype=BF)
    project_keep, project_send = run(
        functools.partial(project_product_kernel, scale_three, row_count),
        "project_product",
        (early, early_other, branch_keep, branch_other),
        (project_half, project_half),
        after=(expand_send,),
        limit=16,
        us=0.9,
    )
    framed_back = halo(grad_mixed, rows_back, "strips_back", after=(project_send,))
    small_half = shape_of(64, half, dtype=BF)
    small_keep, small_send = run(
        functools.partial(weight_pack_kernel, scale_three),
        "block_weights",
        (*framed, grad_mixed, gain_part),
        (small_half, small_half),
        scratch=(
            frame_scratch(center),
            pltpu.VMEM((height, breadth, channels), F32),
            pltpu.VMEM((64, channels), F32),
        ),
        after=(project_send,),
        limit=12,
        us=1.8,
    )
    row_bits, col_bits = axis_bits("row"), axis_bits("col")
    outer = len(row_bits)
    low_first = [("row", bit, 0) for bit in row_bits]
    patch_order = [("col", bit, outer) for bit in col_bits[1:]] + low_first
    project_order = [("row", row_bits[1], 1), low_first[0], *low_first[2:]]
    patch_chain = Chain(patch_keep, patch_send, patch_order, block_count * row_count, 4 * channels // row_count)
    project_chain = Chain(project_keep, project_send, project_order, row_count, deep)
    expand_chain = Chain(expand_keep, expand_send, low_first, row_count, groups * shallow)
    small = small_keep + swap(small_send, "col", 1)
    sent = expand_chain.advance(extra=(small, swap(small, "row", 1)))
    sent = project_chain.advance(sent)
    sent = patch_chain.advance((*sent, *framed_back[3:]))
    (input_grad,) = run(
        input_kernel,
        "input_grad",
        (*framed_back, taps_three, grad_summed),
        (shape_of(height, breadth, channels, dtype=BF),),
        scratch=(frame_scratch(center), pltpu.VMEM((height, breadth, channels), F32)),
        after=sent,
        limit=12,
        us=2,
    )
    sent = expand_chain.advance((input_grad,))
    sent = project_chain.advance(sent)
    patch_chain.advance(sent)
    patch_sum = patch_chain.finish()
    patch_sum = gather(patch_sum, "col", col_bits[1:])
    (patch_grad,) = run(
        finish_patch_kernel,
        "finish_patch",
        (patch_sum, swap(patch_sum, "col", 1)),
        (shape_of(4 * channels // row_count, wide),),
        limit=8,
    )

    def share(total):
        for bit in col_bits[1:]:
            total = total + swap(total, "col", bit)
        return total, swap(total, "col", 1)

    vector, wide_vector = shape_of(1, channels), shape_of(1, wide)
    project_grad, wide_taps, wide_gain, merge_sum, layer_sum = run(
        finish_project_kernel,
        "finish_project",
        share(project_chain.finish()),
        (shape_of(deep, channels), shape_of(7, 7, wide), wide_vector, vector, vector),
        scratch=(pltpu.VMEM((112, channels), F32),),
        limit=8,
    )
    expand_grad, taps_sum, gain_sum = run(
        finish_expand_kernel,
        "finish_expand",
        share(expand_chain.finish()),
        (shape_of(shallow, hidden_width), shape_of(7, 7, channels), vector),
        scratch=(pltpu.VMEM((64, channels), F32),),
        limit=8,
    )
    return (
        input_grad[None],
        taps_sum,
        gain_sum[0],
        expand_grad,
        project_grad,
        layer_sum[0],
        merge_sum[0],
        patch_grad,
        wide_taps,
        wide_gain[0],
    )


def solution(mesh):
    pixels = P(None, "row", "col", None)
    return jax.shard_map(
        body,
        mesh=mesh,
        in_specs=(pixels,) + (P(),) * 9 + (pixels, pixels),
        out_specs=(pixels, P(), P(), P("row", None), P("row", None), P(), P(), P("row", None), P(), P()),
        check_vma=False,
    )
```

```python
import functools
import math

import jax
import jax.numpy as jnp
from jax import lax
from jax.experimental import pallas as pl
from jax.experimental.pallas import tpu as pltpu
from jax.sharding import PartitionSpec as P

EPSILON = 1e-06
BF = jnp.bfloat16
F32 = jnp.float32
MIB = 1 << 20
PAD = 8
CHUNK = 256


def shape_of(*dims, dtype=F32):
    return jax.ShapeDtypeStruct(dims, dtype)


def run(kernel, name, args, outs, scratch=(), spaces=None, after=(), aliases=None, limit=24, us=0.0):
    spaces = spaces or {}
    count, extra = len(args), len(after)

    def spec(place):
        return pl.BlockSpec(memory_space=spaces.get(place, pltpu.VMEM))

    def inner(*refs):
        kernel(*refs[:count], *refs[count + extra :])

    return pl.pallas_call(
        inner,
        name=name,
        out_shape=outs,
        in_specs=[spec(i) for i in range(count)] + [pl.BlockSpec(memory_space=pl.ANY)] * extra,
        out_specs=[spec(("out", i)) for i in range(len(outs))],
        scratch_shapes=list(scratch),
        input_output_aliases=aliases or {},
        compiler_params=pltpu.CompilerParams(vmem_limit_bytes=limit * MIB),
        cost_estimate=pl.CostEstimate(flops=int(us * 1.1e9) + 1000, bytes_accessed=1000, transcendentals=0),
    )(*args, *after)


def swap(values, axis, bit):
    return lax.ppermute(values, axis, [(i, i ^ bit) for i in range(lax.axis_size(axis))])


def axis_bits(axis):
    return [1 << k for k in range((lax.axis_size(axis) - 1).bit_length())]


def own_bit(axis, bit):
    return (lax.axis_index(axis) // bit) % 2


def chain(keep, send, order, count, rows, extra=(), after=()):
    for place, (axis, bit, _) in enumerate(order):
        received = swap(send, axis, bit)
        if place + 1 == len(order):
            return keep + received
        axis, bit, position = order[place + 1]
        grown = extra if place == 0 else ()
        count //= 2
        tail = keep.shape[0] - count * rows + (grown[0].shape[0] if grown else 0)
        out = shape_of(count // 2 * rows + tail, keep.shape[1], dtype=BF)
        keep, send = run(
            functools.partial(step_kernel, axis, bit, position, count, rows),
            "sum_step",
            (keep, received, *grown),
            (out, out),
            after=after if place == 0 else (),
            limit=8,
            us=0.2,
        )


def step_kernel(axis, bit, position, count, rows, keep, received, *refs):
    *grown, next_keep, next_send = refs
    mine = (lax.axis_index(axis) // bit) % 2
    low = (1 << position) - 1
    for i in range(2):

        @pl.when(mine == i)
        def _():
            for s in range(count):
                span = slice(s * rows, (s + 1) * rows)
                at = ((s >> (position + 1)) << position | (s & low)) * rows
                target = next_keep if (s >> position) & 1 == i else next_send
                target[at : at + rows] = (keep[span].astype(F32) + received[span].astype(F32)).astype(BF)

    tails = []
    if keep.shape[0] > count * rows:
        tails.append(keep[count * rows :].astype(F32) + received[count * rows :].astype(F32))
    if grown:
        tails.append(sum(g[...].astype(F32) for g in grown))
    at = count // 2 * rows
    for tail in tails:
        for target in (next_keep, next_send):
            target[at : at + tail.shape[0]] = tail.astype(BF)
        at += tail.shape[0]


def gather(values, axis, bits):
    values = values[None]
    for bit in reversed(bits):
        other = swap(values, axis, bit)
        mine = own_bit(axis, bit)
        low = jnp.where(mine == 0, values, other)
        high = jnp.where(mine == 0, other, values)
        values = jnp.stack([low, high], axis=1).reshape(-1, *values.shape[1:])
    return values


def neighbours(first, last, axis):
    count = lax.axis_size(axis)
    forward = [(i, i + 1) for i in range(count - 1)]
    backward = [(i + 1, i) for i in range(count - 1)]
    return lax.ppermute(last, axis, forward), lax.ppermute(first, axis, backward)


def strip_kernel(center, top, bottom, first, last):
    height, breadth = center.shape[:2]
    for source, start in ((top, 0), (center, 3), (bottom, 3 + height)):
        values = source[...].astype(F32)
        rows = slice(start, start + source.shape[0])
        first[rows] = values[:, :PAD].astype(BF)
        last[rows] = values[:, breadth - PAD :].astype(BF)


def halo(center, rows, name, after=()):
    height, _, channels = center.shape
    top, bottom = rows
    strip = shape_of(height + 6, PAD, channels, dtype=BF)
    first, last = run(strip_kernel, name, (center, top, bottom), (strip, strip), after=after, limit=8)
    left, right = neighbours(first, last, "col")
    return center, top, bottom, left, right


def hold(kernel, name, args, outs, carried, **options):
    count = len(args)

    def inner(*refs):
        kernel(*refs[:count], *refs[count + 1 : count + 1 + len(outs)], *refs[count + 2 + len(outs) :])

    return run(
        inner,
        name,
        (*args, carried),
        (*outs, shape_of(*carried.shape, dtype=carried.dtype)),
        spaces={count: pl.ANY, ("out", len(outs)): pl.ANY},
        aliases={count: len(outs)},
        **options,
    )


def fill_frame(frame, parts):
    center, top, bottom, left, right = parts
    height, breadth = center.shape[:2]
    middle = slice(PAD, PAD + breadth)
    frame[0:3, middle] = top[...].astype(F32)
    frame[3 : 3 + height, middle] = center[...].astype(F32)
    frame[3 + height :, middle] = bottom[...].astype(F32)
    frame[:, :PAD] = left[...].astype(F32)
    frame[:, PAD + breadth :] = right[...].astype(F32)


def frame_scratch(center):
    height, breadth, channels = center.shape
    return pltpu.VMEM((height + 6, breadth + 2 * PAD, channels), F32)


def lane_tiles(channels):
    def over(step):
        def wrapped(index, carry):
            step(pl.ds(pl.multiple_of(index * 128, 128), 128))
            return carry

        lax.fori_loop(0, channels // 128, wrapped, 0)

    return over


def convolve(frame, taps, flip, out):
    height, breadth, channels = out.shape

    @lane_tiles(channels)
    def _(lanes):
        for column in range(0, breadth, 8):
            total = jnp.zeros((height, 8, 128), F32)
            for q in range(7):
                rows = frame[:, pl.ds(column + PAD - 3 + q, 8), lanes]
                for p in range(7):
                    a, b = (6 - p, 6 - q) if flip else (p, q)
                    total = total + rows[p : p + height] * taps[a, pl.ds(b, 1), lanes]
            out[:, pl.ds(column, 8), lanes] = total


def weight_sums(frame, grads, scale, out):
    height, breadth, channels = grads.shape

    @lane_tiles(channels)
    def _(lanes):
        for q in range(7):
            totals = [jnp.zeros((8, 128), F32)] * 7
            for column in range(0, breadth, 8):
                rows = frame[:, pl.ds(column + PAD - 3 + q, 8), lanes]
                grad = grads[:, pl.ds(column, 8), lanes]
                for p in range(7):
                    totals[p] = totals[p] + jnp.sum(rows[p : p + height] * grad, axis=0)
            for p in range(7):
                out[pl.ds(7 * p + q, 1), lanes] = scale * jnp.sum(totals[p], axis=0, keepdims=True)


def mean(values):
    return jnp.mean(values, axis=-1, keepdims=True)


def normalize(values):
    level = mean(values)
    inverse = lax.rsqrt(mean(values * values) - level * level + EPSILON)
    return (values - level) * inverse, inverse


def normalize_back(grads, unit_values, inverse):
    return (grads - mean(grads) - unit_values * mean(grads * unit_values)) * inverse


def dot(left, right):
    return jnp.dot(left, right, preferred_element_type=F32)


def dot_last(left, right):
    return lax.dot_general(left, right, (((1,), (1,)), ((), ())), preferred_element_type=F32)


def dot_first(left, right):
    return lax.dot_general(left, right, (((0,), (0,)), ((), ())), preferred_element_type=F32)


def over_rows(count, size):
    def over(step):
        def wrapped(index, carry):
            step(index, pl.ds(pl.multiple_of(index * size, size), size))
            return carry

        lax.fori_loop(0, count, wrapped, 0)

    return over


def fetch(sources, targets, semaphores):
    copies = [
        pltpu.make_async_copy(source, target, semaphores.at[i])
        for i, (source, target) in enumerate(zip(sources, targets))
    ]
    for copy in copies:
        copy.start()
    return copies


def load_kernel(*refs):
    *arrays, semaphores = refs
    count = len(arrays) // 2
    for copy in fetch(arrays[:count], arrays[count:], semaphores):
        copy.wait()


def front_kernel(
    center, top, bottom, left, right, taps, gain, layer_scale, merge_gain,
    expand, project, patch, wide_taps, wide_gain, cotangent, residual,
    early, unit_mixed, inverse_mixed, slope, branch, unit_summed, inverse_summed, section, first, last,
    expand_here, project_here, patch_here, wide_taps_here, wide_gain_here, cotangent_here, residual_here,
    frame, image, pairs, upward, semaphores,
):
    height, breadth, channels = center.shape
    hidden_width = expand.shape[1]
    pixels = height * breadth
    copies = fetch(
        (expand, project, patch, wide_taps, wide_gain, cotangent, residual),
        (expand_here, project_here, patch_here, wide_taps_here, wide_gain_here, cotangent_here, residual_here),
        semaphores,
    )
    fill_frame(frame, (center, top, bottom, left, right))
    convolve(frame, taps, False, image)
    at_normed = slice(hidden_width, hidden_width + channels)
    at_patches = slice(hidden_width + channels, hidden_width + 2 * channels)

    @over_rows(height, breadth)
    def _(y, rows):
        unit, inverse = normalize(image[y])
        unit_mixed[rows] = unit
        inverse_mixed[rows] = inverse
        early[rows, at_normed] = (unit * gain[...]).astype(BF)

    copies[0].wait()

    def chunk(index, carry):
        lanes = pl.ds(pl.multiple_of(index * CHUNK, CHUNK), CHUNK)
        upward[...] = dot(early[:, at_normed], expand_here[:, lanes])
        for start in range(0, pixels, 64):
            rows = slice(start, start + 64)
            value = upward[rows]
            cumulative = 0.5 + 0.5 * lax.erf(value * (1.0 / math.sqrt(2.0)))
            density = jnp.exp(-0.5 * value * value) * (1.0 / math.sqrt(2.0 * math.pi))
            early[rows, lanes] = (value * cumulative).astype(BF)
            slope[rows, lanes] = (cumulative + value * density).astype(BF)
        return carry

    lax.fori_loop(0, hidden_width // CHUNK, chunk, 0)
    copies[1].wait()
    branch[...] = dot(early[:, :hidden_width], project_here[...])

    @over_rows(height, breadth)
    def _(y, rows):
        summed = center[y].astype(F32) + layer_scale[...] * branch[rows]
        unit, inverse = normalize(summed)
        unit_summed[rows] = unit
        inverse_summed[rows] = inverse
        merged = unit * merge_gain[...]
        for k in range(channels // 128):
            pairs[k, y] = merged[:, k * 128 : (k + 1) * 128]

    quarter = pixels // 4
    for dy in range(2):
        for dx in range(2):
            j = 2 * dy + dx
            for y in range(height // 2):
                start = j * quarter + y * (breadth // 2)
                for k in range(channels // 128):
                    piece = pairs[k, 2 * y + dy, pl.ds(dx, breadth // 2, stride=2), :]
                    lane = hidden_width + channels + k * 128
                    early[start : start + breadth // 2, lane : lane + 128] = piece.astype(BF)
    copies[2].wait()
    total = dot(early[:quarter, at_patches], patch_here[:channels])
    for j in range(1, 4):
        total = total + dot(
            early[j * quarter : (j + 1) * quarter, at_patches],
            patch_here[j * channels : (j + 1) * channels],
        )
    total = total.reshape(section.shape)
    section[...] = total.astype(BF)
    first[...] = total[:3].astype(BF)
    last[...] = total[height // 2 - 3 :].astype(BF)
    for copy in copies[3:]:
        copy.wait()


def mixer_kernel(
    center, top, bottom, left, right, taps, gain, cotangent,
    grad, grad_half, first, last, gain_part,
    frame, image,
):
    height, breadth, channels = center.shape
    fill_frame(frame, (center, top, bottom, left, right))
    convolve(frame, taps, False, image)
    part = jnp.zeros((1, channels), F32)
    for y in range(height):
        unit, inverse = normalize(image[y])
        cot = cotangent[y].astype(F32)
        part = part + jnp.sum(cot * unit, axis=0, keepdims=True)
        value = normalize_back(cot * gain[...], unit, inverse)
        grad[y] = value
        narrow = value.astype(BF)
        grad_half[y] = narrow
        if y < 3:
            first[y] = narrow
        if y >= height - 3:
            last[y - (height - 3)] = narrow
    gain_part[...] = part


def weight_kernel(scale, center, top, bottom, left, right, grads, out, frame):
    fill_frame(frame, (center, top, bottom, left, right))
    weight_sums(frame, grads, scale, out)


def split_halves(values, start, keep, send):
    half = values.shape[1] // 2
    rows = slice(start, start + values.shape[0])
    core = lax.axis_index("col") % 2
    for i in range(2):

        @pl.when(core == i)
        def _():
            keep[rows] = values[:, i * half : (i + 1) * half]
            send[rows] = values[:, (1 - i) * half : (2 - i) * half]


def weight_pack_kernel(
    scale, center, top, bottom, left, right, grads, gain_part,
    keep, send, frame, wide_grads, packed,
):
    fill_frame(frame, (center, top, bottom, left, right))
    wide_grads[...] = grads[...].astype(F32)
    packed[...] = jnp.zeros(packed.shape, F32)
    weight_sums(frame, wide_grads, scale, packed)
    packed[49:50] = scale * gain_part[...]
    split_halves(packed[...].astype(BF), 0, keep, send)


def section_kernel(
    center, top, bottom, left, right, taps, residual,
    flat, keep, send,
    frame, image,
):
    height, breadth, channels = center.shape
    fill_frame(frame, (center, top, bottom, left, right))
    convolve(frame, taps, True, image)
    value = (image[...] + residual[...].astype(F32)).reshape(flat.shape).astype(BF)
    flat[...] = value
    blocks, _, width = keep.shape
    core = lax.axis_index("col") % 2
    for i in range(2):

        @pl.when(core == i)
        def _():
            for m in range(blocks):
                mine, other = (2 * m + i) * width, (2 * m + 1 - i) * width
                keep[m] = value[:, mine : mine + width]
                send[m] = value[:, other : other + width]


def merge_kernel(
    scale, scale_wide,
    flat, patch, unit_summed, inverse_summed, merge_gain, branch, layer_scale, wide_part, wide_gain,
    grad_summed, grad_branch, keep, send,
    pairs, packed, sums,
):
    tiles, height, breadth, _ = pairs.shape
    channels = 128 * tiles
    value = flat[...]
    for dy in range(2):
        for dx in range(2):
            j = 2 * dy + dx
            part = dot_last(value, patch[j * channels : (j + 1) * channels])
            part = part.reshape(height // 2, breadth // 2, channels)
            for y in range(height // 2):
                for k in range(tiles):
                    piece = part[y, :, k * 128 : (k + 1) * 128]
                    pairs[k, 2 * y + dy, pl.ds(dx, breadth // 2, stride=2), :] = piece
    sums[...] = jnp.zeros(sums.shape, F32)

    @over_rows(height, breadth)
    def _(y, rows):
        merged = jnp.concatenate([pairs[k, y] for k in range(tiles)], axis=1)
        unit = unit_summed[rows]
        sums[0:1] += jnp.sum(merged * unit, axis=0, keepdims=True)
        grad = normalize_back(merged * merge_gain[...], unit, inverse_summed[rows])
        grad_summed[rows] = grad
        sums[1:2] += jnp.sum(grad * branch[rows], axis=0, keepdims=True)
        grad_branch[rows] = (layer_scale[...] * grad).astype(BF)

    split_halves(grad_branch[...], 0, keep, send)
    packed[...] = jnp.zeros(packed.shape, F32)
    for i in range(2):
        columns = slice(i * channels, (i + 1) * channels)
        packed[49 * i : 49 + 49 * i] = wide_part[:, columns]
        packed[98 + i : 99 + i] = scale_wide * wide_gain[:, columns]
        packed[100 + i : 101 + i] = scale * sums[i : i + 1]
    split_halves(packed[...].astype(BF), grad_branch.shape[0], keep, send)


def back_kernel(
    grad_branch, project, slope, expand, unit_mixed, inverse_mixed, gain,
    keep, send, grad_mixed, first, last, gain_part,
    hidden, upward, normed,
):
    height, breadth, channels = grad_mixed.shape
    pixels, hidden_width = slope.shape

    def chunk(index, carry):
        span = pl.ds(pl.multiple_of(index * CHUNK, CHUNK), CHUNK)
        hidden[...] = dot_last(grad_branch[...], project[span])
        for start in range(0, pixels, 64):
            rows = slice(start, start + 64)
            upward[rows, span] = (hidden[rows] * slope[rows, span].astype(F32)).astype(BF)
        return carry

    lax.fori_loop(0, hidden_width // CHUNK, chunk, 0)
    normed[...] = dot_last(upward[...], expand[...])
    split_halves(upward[...], 0, keep, send)
    part = jnp.zeros((1, channels), F32)
    for y in range(height):
        rows = slice(y * breadth, (y + 1) * breadth)
        value = normed[rows]
        unit = unit_mixed[rows]
        part = part + jnp.sum(value * unit, axis=0, keepdims=True)
        narrow = normalize_back(value * gain[...], unit, inverse_mixed[rows]).astype(BF)
        grad_mixed[y] = narrow
        if y < 3:
            first[y] = narrow
        if y >= height - 3:
            last[y - (height - 3)] = narrow
    gain_part[...] = part


def patch_product_kernel(factor, early, early_other, own, other, keep, send):
    blocks, quarter, _ = own.shape
    rows = keep.shape[0] // max(blocks // 2, 1)
    channels = rows // 4
    at_patches = early.shape[1] - channels
    bit = (lax.axis_index("col") // 2) % 2
    for j in range(4):
        span = slice(j * quarter, (j + 1) * quarter)
        left = jnp.concatenate([early[span, at_patches:], early_other[span, at_patches:]], axis=0)
        for m in range(blocks):
            right = jnp.concatenate([own[m], other[m]], axis=0)
            value = (factor * dot_first(left, right)).astype(BF)
            at = m // 2 * rows + j * channels
            for i in range(2):

                @pl.when(bit == i)
                def _():
                    target = keep if m % 2 == i else send
                    target[at : at + channels] = value


def store_slices(position, value, begin, offset, rows, pitch, keep, send):
    bit = (lax.axis_index("row") >> position) % 2
    low = (1 << position) - 1
    for i in range(2):

        @pl.when(bit == i)
        def _():
            for k in range(value.shape[0] // rows):
                r = begin + k
                target = keep if (r >> position) & 1 == i else send
                at = ((r >> (position + 1)) << position | (r & low)) * pitch + offset
                target[at : at + rows] = value[k * rows : (k + 1) * rows]


def project_product_kernel(factor, slices, early, early_other, own, other, keep, send):
    width = keep.shape[1]
    hidden_width = early.shape[1] - 4 * width
    pixels = early.shape[0]
    deep = hidden_width // slices
    right = jnp.concatenate([own[:pixels], other[:pixels]], axis=0)
    step = max(CHUNK, deep)
    for start in range(0, hidden_width, step):
        columns = slice(start, start + step)
        left = jnp.concatenate([early[:, columns], early_other[:, columns]], axis=0)
        value = (factor * dot_first(left, right)).astype(BF)
        store_slices(1, value, start // deep, 0, deep, deep, keep, send)
    tail = (own[pixels:].astype(F32) + other[pixels:].astype(F32)).astype(BF)
    at = slices // 2 * deep
    keep[at:] = tail
    send[at:] = tail


def expand_product_kernel(factor, slices, early, early_other, own, other, keep, send):
    width = keep.shape[1]
    channels = 2 * width
    hidden_width = early.shape[1] - 2 * channels
    shallow = channels // slices
    blocks = own.shape[1] // width
    columns = slice(hidden_width, hidden_width + channels)
    left = jnp.concatenate([early[:, columns], early_other[:, columns]], axis=0)
    for k in range(blocks):
        columns = slice(k * width, (k + 1) * width)
        right = jnp.concatenate([own[:, columns], other[:, columns]], axis=0)
        value = (factor * dot_first(left, right)).astype(BF)
        store_slices(0, value, 0, k * shallow, shallow, blocks * shallow, keep, send)


def finish_patch_kernel(own, other, out):
    blocks, _, width = own.shape
    core = lax.axis_index("col") % 2
    for i in range(2):

        @pl.when(core == i)
        def _():
            for m in range(blocks):
                a, b = (2 * m + i) * width, (2 * m + 1 - i) * width
                out[:, a : a + width] = own[m].astype(F32)
                out[:, b : b + width] = other[m].astype(F32)


def join_halves(own, other, start, out):
    half = own.shape[1]
    rows = slice(start, start + out.shape[0])
    core = lax.axis_index("col") % 2
    for i in range(2):

        @pl.when(core == i)
        def _():
            out[:, i * half : (i + 1) * half] = own[rows].astype(F32)
            out[:, (1 - i) * half : (2 - i) * half] = other[rows].astype(F32)


def finish_project_kernel(own, other, project, wide_taps, wide_gain, merge, layer, small):
    deep, channels = project.shape
    join_halves(own, other, 0, project)
    join_halves(own, other, deep, small)
    for i in range(2):
        columns = slice(i * channels, (i + 1) * channels)
        for p in range(7):
            start = 49 * i + 7 * p
            wide_taps[p, :, columns] = small[start : start + 7]
        wide_gain[:, columns] = small[98 + i : 99 + i]
    merge[...] = small[100:101]
    layer[...] = small[101:102]


def finish_expand_kernel(own, other, expand, taps, gain, small):
    shallow, hidden_width = expand.shape
    width = own.shape[1]
    blocks = hidden_width // (2 * width)
    core = lax.axis_index("col") % 2
    for i in range(2):

        @pl.when(core == i)
        def _():
            for k in range(blocks):
                rows = slice(k * shallow, (k + 1) * shallow)
                a, b = (i * blocks + k) * width, ((1 - i) * blocks + k) * width
                expand[:, a : a + width] = own[rows].astype(F32)
                expand[:, b : b + width] = other[rows].astype(F32)

    join_halves(own, other, blocks * shallow, small)
    for p in range(7):
        taps[p] = small[7 * p : 7 * p + 7]
    gain[...] = small[49:50]


def input_kernel(center, top, bottom, left, right, taps, grad_summed, out, frame, image):
    fill_frame(frame, (center, top, bottom, left, right))
    convolve(frame, taps, True, image)
    out[...] = (image[...] + grad_summed[...].reshape(image.shape)).astype(BF)


def body(
    block_input,
    kernel_three,
    gain_three,
    expand_weight,
    project_weight,
    layer_scale,
    merge_gain,
    patch_weight,
    kernel_four,
    gain_four,
    normed_cotangent,
    residual_cotangent,
):
    _, height, breadth, channels = block_input.shape
    hidden_width = expand_weight.shape[1]
    wide = patch_weight.shape[1]
    pixels = height * breadth
    quarter = pixels // 4
    rows4, cols4 = height // 2, breadth // 2
    row_count = lax.axis_size("row")
    col_count = lax.axis_size("col")
    scale_three = 1.0 / math.sqrt(pixels * row_count * col_count)
    scale_four = 1.0 / math.sqrt(quarter * row_count * col_count)
    center = block_input[0]
    gain_three, layer_scale, merge_gain, gain_four = (
        v[None] for v in (gain_three, layer_scale, merge_gain, gain_four)
    )
    dma = pltpu.SemaphoreType.DMA
    half = channels // 2
    hbm = pltpu.HBM

    def like(array):
        return shape_of(*array.shape, dtype=array.dtype)

    edge = shape_of(3, breadth, channels, dtype=BF)
    rows_input = neighbours(center[:3], center[height - 3 :], "row")
    inputs = (center, kernel_three, gain_three, layer_scale, merge_gain)
    center, taps_three, gain_three, layer_scale, merge_gain = run(
        load_kernel,
        "load",
        inputs,
        tuple(map(like, inputs)),
        scratch=(dma((5,)),),
        spaces=dict.fromkeys(range(5), hbm),
        after=rows_input[:1],
        limit=4,
        us=2,
    )
    framed = halo(center, rows_input, "strips_input")
    inputs = (
        expand_weight, project_weight, patch_weight, kernel_four, gain_four,
        normed_cotangent[0], residual_cotangent[0],
    )
    edge_four = shape_of(3, cols4, wide, dtype=BF)
    (
        early, unit_mixed, inverse_mixed, slope, branch, unit_summed, inverse_summed,
        section, first, last,
        expand_weight, project_weight, patch_weight, taps_four, gain_four, cotangent, residual,
    ) = run(
        front_kernel,
        "front",
        (*framed, taps_three, gain_three, layer_scale, merge_gain, *inputs),
        (
            shape_of(pixels, hidden_width + 2 * channels, dtype=BF),
            shape_of(pixels, channels),
            shape_of(pixels, 1),
            shape_of(pixels, hidden_width, dtype=BF),
            shape_of(pixels, channels),
            shape_of(pixels, channels),
            shape_of(pixels, 1),
            shape_of(rows4, cols4, wide, dtype=BF),
            edge_four,
            edge_four,
            *map(like, inputs),
        ),
        scratch=(
            frame_scratch(center),
            pltpu.VMEM((height, breadth, channels), F32),
            pltpu.VMEM((channels // 128, height, breadth, 128), F32),
            pltpu.VMEM((pixels, CHUNK), F32),
            dma((7,)),
        ),
        spaces=dict.fromkeys(range(9, 16), hbm),
        limit=28,
        us=12,
    )

    framed_four = halo(section, neighbours(first, last, "row"), "strips_section")
    mixer_image = pltpu.VMEM((rows4, cols4, wide), F32)
    grad_four, grad_four_half, first, last, gain_four_part = run(
        mixer_kernel,
        "mixer",
        (*framed_four, taps_four, gain_four, cotangent),
        (
            shape_of(rows4, cols4, wide),
            shape_of(rows4, cols4, wide, dtype=BF),
            edge_four,
            edge_four,
            shape_of(1, wide),
        ),
        scratch=(frame_scratch(section), mixer_image),
        limit=12,
        us=3,
    )
    rows_grad = neighbours(first, last, "row")
    (kernel_four_part,) = run(
        functools.partial(weight_kernel, scale_four),
        "mixer_weights",
        (*framed_four, grad_four),
        (shape_of(49, wide),),
        scratch=(frame_scratch(section),),
        after=rows_grad[:1],
        limit=12,
        us=3,
    )
    framed_grad = halo(grad_four_half, rows_grad, "strips_mixer", after=(kernel_four_part,))
    block_count = col_count // 2
    block = wide // col_count
    blocked = shape_of(block_count, quarter, block, dtype=BF)
    flat, flat_keep, flat_send, early = hold(
        section_kernel,
        "section_grad",
        (*framed_grad, taps_four, residual),
        (shape_of(quarter, wide, dtype=BF), blocked, blocked),
        early,
        scratch=(frame_scratch(section), mixer_image),
        limit=12,
        us=3,
    )

    flat_other = swap(flat_send, "col", 1)
    early_other = swap(early, "col", 1)
    split = shape_of(pixels + 112, half, dtype=BF)
    grad_summed, grad_branch, branch_keep, branch_send = run(
        functools.partial(merge_kernel, scale_three, scale_four),
        "merge_back",
        (
            flat, patch_weight, unit_summed, inverse_summed, merge_gain, branch, layer_scale,
            kernel_four_part, gain_four_part,
        ),
        (shape_of(pixels, channels), shape_of(pixels, channels, dtype=BF), split, split),
        scratch=(
            pltpu.VMEM((channels // 128, height, breadth, 128), F32),
            pltpu.VMEM((112, channels), F32),
            pltpu.VMEM((8, channels), F32),
        ),
        limit=16,
        us=0.8,
    )
    branch_other = swap(branch_send, "col", 1)
    patch_half = shape_of(block_count // 2 * 4 * channels, block, dtype=BF)
    patch_keep, patch_send = run(
        functools.partial(patch_product_kernel, scale_four),
        "patch_product",
        (early, early_other, flat_keep, flat_other),
        (patch_half, patch_half),
        limit=16,
        us=0.9,
    )
    deep, shallow = hidden_width // row_count, channels // row_count
    groups = hidden_width // channels
    project_half = shape_of(row_count // 2 * deep + 112, half, dtype=BF)
    upward_half = shape_of(pixels, hidden_width // 2, dtype=BF)
    upward_keep, upward_send, grad_mixed, first, last, gain_part = run(
        back_kernel,
        "mlp_back",
        (grad_branch, project_weight, slope, expand_weight, unit_mixed, inverse_mixed, gain_three),
        (
            upward_half,
            upward_half,
            shape_of(height, breadth, channels, dtype=BF),
            edge,
            edge,
            shape_of(1, channels),
        ),
        scratch=(
            pltpu.VMEM((pixels, CHUNK), F32),
            pltpu.VMEM((pixels, hidden_width), BF),
            pltpu.VMEM((pixels, channels), F32),
        ),
        after=(patch_send,),
        limit=16,
        us=1.2,
    )
    rows_back = neighbours(first, last, "row")
    upward_other = swap(upward_send, "col", 1)
    project_keep, project_send = run(
        functools.partial(project_product_kernel, scale_three, row_count),
        "project_product",
        (early, early_other, branch_keep, branch_other),
        (project_half, project_half),
        after=(upward_send,),
        limit=16,
        us=0.9,
    )
    expand_half = shape_of(row_count // 2 * groups * shallow, half, dtype=BF)
    expand_keep, expand_send = run(
        functools.partial(expand_product_kernel, scale_three, row_count),
        "expand_product",
        (early, early_other, upward_keep, upward_other),
        (expand_half, expand_half),
        after=(project_send, *rows_back),
        limit=16,
        us=0.6,
    )
    framed_back = halo(grad_mixed, rows_back, "strips_back", after=(expand_send,))
    small_half = shape_of(64, half, dtype=BF)
    small_keep, small_send = run(
        functools.partial(weight_pack_kernel, scale_three),
        "block_weights",
        (*framed, grad_mixed, gain_part),
        (small_half, small_half),
        scratch=(
            frame_scratch(center),
            pltpu.VMEM((height, breadth, channels), F32),
            pltpu.VMEM((64, channels), F32),
        ),
        after=(*framed_back[1:3], expand_send),
        limit=12,
        us=1.8,
    )
    (input_grad,) = run(
        input_kernel,
        "input_grad",
        (*framed_back, taps_three, grad_summed),
        (shape_of(height, breadth, channels, dtype=BF),),
        scratch=(frame_scratch(center), pltpu.VMEM((height, breadth, channels), F32)),
        after=(small_keep,),
        limit=12,
        us=2,
    )

    row_bits, col_bits = axis_bits("row"), axis_bits("col")
    outer = len(row_bits)
    low_first = [("row", bit, 0) for bit in row_bits]
    patch_order = [("col", bit, outer) for bit in col_bits[1:]] + low_first
    patch_sum = chain(
        patch_keep, patch_send, patch_order, block_count * row_count, 4 * channels // row_count,
        after=(small_keep,),
    )
    patch_sum = gather(patch_sum, "col", col_bits[1:])
    (patch_grad,) = run(
        finish_patch_kernel,
        "finish_patch",
        (patch_sum, swap(patch_sum, "col", 1)),
        (shape_of(4 * channels // row_count, wide),),
        limit=8,
    )

    def share(keep, send, order, rows, extra=(), after=()):
        total = chain(keep, send, order, row_count, rows, extra, after)
        for bit in col_bits[1:]:
            total = total + swap(total, "col", bit)
        return total, swap(total, "col", 1)

    project_order = [("row", bit, 1) for bit in row_bits[1:]] + low_first[:1]
    vector, wide_vector = shape_of(1, channels), shape_of(1, wide)
    project_grad, wide_taps, wide_gain, merge_sum, layer_sum = run(
        finish_project_kernel,
        "finish_project",
        share(project_keep, project_send, project_order, deep, after=(small_keep,)),
        (shape_of(deep, channels), shape_of(7, 7, wide), wide_vector, vector, vector),
        scratch=(pltpu.VMEM((112, channels), F32),),
        limit=8,
    )
    small = small_keep + swap(small_send, "col", 1)
    expand_grad, taps_sum, gain_sum = run(
        finish_expand_kernel,
        "finish_expand",
        share(expand_keep, expand_send, low_first, groups * shallow, (small, swap(small, "row", 1)), (input_grad,)),
        (shape_of(shallow, hidden_width), shape_of(7, 7, channels), vector),
        scratch=(pltpu.VMEM((64, channels), F32),),
        limit=8,
    )
    return (
        input_grad[None],
        taps_sum,
        gain_sum[0],
        expand_grad,
        project_grad,
        layer_sum[0],
        merge_sum[0],
        patch_grad,
        wide_taps,
        wide_gain[0],
    )


def solution(mesh):
    pixels = P(None, "row", "col", None)
    return jax.shard_map(
        body,
        mesh=mesh,
        in_specs=(pixels,) + (P(),) * 9 + (pixels, pixels),
        out_specs=(pixels, P(), P(), P("row", None), P("row", None), P(), P(), P("row", None), P(), P()),
        check_vma=False,
    )
```

```python
import functools
import math

import jax
import jax.numpy as jnp
from jax import lax
from jax.experimental import pallas as pl
from jax.experimental.pallas import tpu as pltpu
from jax.sharding import PartitionSpec as P

EPSILON = 1e-06
BF = jnp.bfloat16
F32 = jnp.float32
MIB = 1 << 20
PAD = 8
CHUNK = 256


def shape_of(*dims, dtype=F32):
    return jax.ShapeDtypeStruct(dims, dtype)


def run(kernel, name, args, outs, scratch=(), spaces=None, after=(), aliases=None, limit=24, us=0.0):
    spaces = spaces or {}
    count, extra = len(args), len(after)

    def spec(place):
        return pl.BlockSpec(memory_space=spaces.get(place, pltpu.VMEM))

    def inner(*refs):
        kernel(*refs[:count], *refs[count + extra :])

    return pl.pallas_call(
        inner,
        name=name,
        out_shape=outs,
        in_specs=[spec(i) for i in range(count)] + [pl.BlockSpec(memory_space=pl.ANY)] * extra,
        out_specs=[spec(("out", i)) for i in range(len(outs))],
        scratch_shapes=list(scratch),
        input_output_aliases=aliases or {},
        compiler_params=pltpu.CompilerParams(vmem_limit_bytes=limit * MIB),
        cost_estimate=pl.CostEstimate(flops=int(us * 1.1e9) + 1000, bytes_accessed=1000, transcendentals=0),
    )(*args, *after)


def swap(values, axis, bit):
    return lax.ppermute(values, axis, [(i, i ^ bit) for i in range(lax.axis_size(axis))])


def axis_bits(axis):
    return [1 << k for k in range((lax.axis_size(axis) - 1).bit_length())]


def own_bit(axis, bit):
    return (lax.axis_index(axis) // bit) % 2


class Chain:
    def __init__(self, keep, send, order, count, rows):
        self.keep, self.send, self.order = keep, send, list(order)
        self.count, self.rows = count, rows

    def advance(self, after=(), extra=()):
        axis, bit, _ = self.order.pop(0)
        keep, received = self.keep, swap(self.send, axis, bit)
        if not self.order:
            self.keep = keep + received
            return ()
        axis, bit, position = self.order[0]
        self.count //= 2
        tail = keep.shape[0] - self.count * self.rows + (extra[0].shape[0] if extra else 0)
        out = shape_of(self.count // 2 * self.rows + tail, keep.shape[1], dtype=BF)
        self.keep, self.send = run(
            functools.partial(step_kernel, axis, bit, position, self.count, self.rows),
            "sum_step",
            (keep, received, *extra),
            (out, out),
            after=after,
            limit=8,
            us=0.1,
        )
        return (self.send,)

    def finish(self):
        while self.order:
            self.advance()
        return self.keep


def step_kernel(axis, bit, position, count, rows, keep, received, *refs):
    *grown, next_keep, next_send = refs
    mine = (lax.axis_index(axis) // bit) % 2
    low = (1 << position) - 1
    for i in range(2):

        @pl.when(mine == i)
        def _():
            for s in range(count):
                span = slice(s * rows, (s + 1) * rows)
                at = ((s >> (position + 1)) << position | (s & low)) * rows
                target = next_keep if (s >> position) & 1 == i else next_send
                target[at : at + rows] = (keep[span].astype(F32) + received[span].astype(F32)).astype(BF)

    tails = []
    if keep.shape[0] > count * rows:
        tails.append(keep[count * rows :].astype(F32) + received[count * rows :].astype(F32))
    if grown:
        tails.append(sum(g[...].astype(F32) for g in grown))
    at = count // 2 * rows
    for tail in tails:
        for target in (next_keep, next_send):
            target[at : at + tail.shape[0]] = tail.astype(BF)
        at += tail.shape[0]


def gather(values, axis, bits):
    values = values[None]
    for bit in reversed(bits):
        other = swap(values, axis, bit)
        mine = own_bit(axis, bit)
        low = jnp.where(mine == 0, values, other)
        high = jnp.where(mine == 0, other, values)
        values = jnp.stack([low, high], axis=1).reshape(-1, *values.shape[1:])
    return values


def neighbours(first, last, axis):
    count = lax.axis_size(axis)
    forward = [(i, i + 1) for i in range(count - 1)]
    backward = [(i + 1, i) for i in range(count - 1)]
    return lax.ppermute(last, axis, forward), lax.ppermute(first, axis, backward)


def strip_kernel(center, top, bottom, first, last):
    height, breadth = center.shape[:2]
    for source, start in ((top, 0), (center, 3), (bottom, 3 + height)):
        values = source[...].astype(F32)
        rows = slice(start, start + source.shape[0])
        first[rows] = values[:, :PAD].astype(BF)
        last[rows] = values[:, breadth - PAD :].astype(BF)


def halo(center, rows, name, after=()):
    height, _, channels = center.shape
    top, bottom = rows
    strip = shape_of(height + 6, PAD, channels, dtype=BF)
    first, last = run(strip_kernel, name, (center, top, bottom), (strip, strip), after=after, limit=8)
    left, right = neighbours(first, last, "col")
    return center, top, bottom, left, right


def hold(kernel, name, args, outs, carried, **options):
    count = len(args)

    def inner(*refs):
        kernel(*refs[:count], *refs[count + 1 : count + 1 + len(outs)], *refs[count + 2 + len(outs) :])

    return run(
        inner,
        name,
        (*args, carried),
        (*outs, shape_of(*carried.shape, dtype=carried.dtype)),
        spaces={count: pl.ANY, ("out", len(outs)): pl.ANY},
        aliases={count: len(outs)},
        **options,
    )


def fill_frame(frame, parts):
    center, top, bottom, left, right = parts
    height, breadth = center.shape[:2]
    middle = slice(PAD, PAD + breadth)
    frame[0:3, middle] = top[...].astype(F32)
    frame[3 : 3 + height, middle] = center[...].astype(F32)
    frame[3 + height :, middle] = bottom[...].astype(F32)
    frame[:, :PAD] = left[...].astype(F32)
    frame[:, PAD + breadth :] = right[...].astype(F32)


def frame_scratch(center):
    height, breadth, channels = center.shape
    return pltpu.VMEM((height + 6, breadth + 2 * PAD, channels), F32)


def lane_tiles(channels):
    def over(step):
        def wrapped(index, carry):
            step(pl.ds(pl.multiple_of(index * 128, 128), 128))
            return carry

        lax.fori_loop(0, channels // 128, wrapped, 0)

    return over


def convolve(frame, taps, flip, out):
    height, breadth, channels = out.shape

    @lane_tiles(channels)
    def _(lanes):
        for column in range(0, breadth, 8):
            total = jnp.zeros((height, 8, 128), F32)
            for q in range(7):
                rows = frame[:, pl.ds(column + PAD - 3 + q, 8), lanes]
                for p in range(7):
                    a, b = (6 - p, 6 - q) if flip else (p, q)
                    total = total + rows[p : p + height] * taps[a, pl.ds(b, 1), lanes]
            out[:, pl.ds(column, 8), lanes] = total


def weight_sums(frame, grads, scale, out):
    height, breadth, channels = grads.shape

    @lane_tiles(channels)
    def _(lanes):
        for q in range(7):
            totals = [jnp.zeros((8, 128), F32)] * 7
            for column in range(0, breadth, 8):
                rows = frame[:, pl.ds(column + PAD - 3 + q, 8), lanes]
                grad = grads[:, pl.ds(column, 8), lanes]
                for p in range(7):
                    totals[p] = totals[p] + jnp.sum(rows[p : p + height] * grad, axis=0)
            for p in range(7):
                out[pl.ds(7 * p + q, 1), lanes] = scale * jnp.sum(totals[p], axis=0, keepdims=True)


def mean(values):
    return jnp.mean(values, axis=-1, keepdims=True)


def normalize(values):
    level = mean(values)
    inverse = lax.rsqrt(mean(values * values) - level * level + EPSILON)
    return (values - level) * inverse, inverse


def normalize_back(grads, unit_values, inverse):
    return (grads - mean(grads) - unit_values * mean(grads * unit_values)) * inverse


def dot(left, right):
    return jnp.dot(left, right, preferred_element_type=F32)


def dot_last(left, right):
    return lax.dot_general(left, right, (((1,), (1,)), ((), ())), preferred_element_type=F32)


def dot_first(left, right):
    return lax.dot_general(left, right, (((0,), (0,)), ((), ())), preferred_element_type=F32)


def over_rows(count, size):
    def over(step):
        def wrapped(index, carry):
            step(index, pl.ds(pl.multiple_of(index * size, size), size))
            return carry

        lax.fori_loop(0, count, wrapped, 0)

    return over


def fetch(sources, targets, semaphores):
    copies = [
        pltpu.make_async_copy(source, target, semaphores.at[i])
        for i, (source, target) in enumerate(zip(sources, targets))
    ]
    for copy in copies:
        copy.start()
    return copies


def load_kernel(*refs):
    *arrays, semaphores = refs
    count = len(arrays) // 2
    for copy in fetch(arrays[:count], arrays[count:], semaphores):
        copy.wait()


def front_kernel(
    center, top, bottom, left, right, taps, gain, layer_scale, merge_gain,
    expand, project, patch, wide_taps, wide_gain, cotangent, residual,
    early, unit_mixed, inverse_mixed, slope, branch, unit_summed, inverse_summed, section, first, last,
    expand_here, project_here, patch_here, wide_taps_here, wide_gain_here, cotangent_here, residual_here,
    frame, image, pairs, upward, semaphores,
):
    height, breadth, channels = center.shape
    hidden_width = expand.shape[1]
    pixels = height * breadth
    copies = fetch(
        (expand, project, patch, wide_taps, wide_gain, cotangent, residual),
        (expand_here, project_here, patch_here, wide_taps_here, wide_gain_here, cotangent_here, residual_here),
        semaphores,
    )
    fill_frame(frame, (center, top, bottom, left, right))
    convolve(frame, taps, False, image)
    at_normed = slice(hidden_width, hidden_width + channels)
    at_patches = slice(hidden_width + channels, hidden_width + 2 * channels)

    @over_rows(height, breadth)
    def _(y, rows):
        unit, inverse = normalize(image[y])
        unit_mixed[rows] = unit
        inverse_mixed[rows] = inverse
        early[rows, at_normed] = (unit * gain[...]).astype(BF)

    copies[0].wait()

    def chunk(index, carry):
        lanes = pl.ds(pl.multiple_of(index * CHUNK, CHUNK), CHUNK)
        upward[...] = dot(early[:, at_normed], expand_here[:, lanes])
        for start in range(0, pixels, 64):
            rows = slice(start, start + 64)
            value = upward[rows]
            cumulative = 0.5 + 0.5 * lax.erf(value * (1.0 / math.sqrt(2.0)))
            density = jnp.exp(-0.5 * value * value) * (1.0 / math.sqrt(2.0 * math.pi))
            early[rows, lanes] = (value * cumulative).astype(BF)
            slope[rows, lanes] = (cumulative + value * density).astype(BF)
        return carry

    lax.fori_loop(0, hidden_width // CHUNK, chunk, 0)
    copies[1].wait()
    branch[...] = dot(early[:, :hidden_width], project_here[...])

    @over_rows(height, breadth)
    def _(y, rows):
        summed = center[y].astype(F32) + layer_scale[...] * branch[rows]
        unit, inverse = normalize(summed)
        unit_summed[rows] = unit
        inverse_summed[rows] = inverse
        merged = unit * merge_gain[...]
        for k in range(channels // 128):
            pairs[k, y] = merged[:, k * 128 : (k + 1) * 128]

    quarter = pixels // 4
    for dy in range(2):
        for dx in range(2):
            j = 2 * dy + dx
            for y in range(height // 2):
                start = j * quarter + y * (breadth // 2)
                for k in range(channels // 128):
                    piece = pairs[k, 2 * y + dy, pl.ds(dx, breadth // 2, stride=2), :]
                    lane = hidden_width + channels + k * 128
                    early[start : start + breadth // 2, lane : lane + 128] = piece.astype(BF)
    copies[2].wait()
    total = dot(early[:quarter, at_patches], patch_here[:channels])
    for j in range(1, 4):
        total = total + dot(
            early[j * quarter : (j + 1) * quarter, at_patches],
            patch_here[j * channels : (j + 1) * channels],
        )
    total = total.reshape(section.shape)
    section[...] = total.astype(BF)
    first[...] = total[:3].astype(BF)
    last[...] = total[height // 2 - 3 :].astype(BF)
    for copy in copies[3:]:
        copy.wait()


def mixer_kernel(
    center, top, bottom, left, right, taps, gain, cotangent,
    grad, grad_half, first, last, gain_part,
    frame, image,
):
    height, breadth, channels = center.shape
    fill_frame(frame, (center, top, bottom, left, right))
    convolve(frame, taps, False, image)
    part = jnp.zeros((1, channels), F32)
    for y in range(height):
        unit, inverse = normalize(image[y])
        cot = cotangent[y].astype(F32)
        part = part + jnp.sum(cot * unit, axis=0, keepdims=True)
        value = normalize_back(cot * gain[...], unit, inverse)
        grad[y] = value
        narrow = value.astype(BF)
        grad_half[y] = narrow
        if y < 3:
            first[y] = narrow
        if y >= height - 3:
            last[y - (height - 3)] = narrow
    gain_part[...] = part


def weight_kernel(scale, center, top, bottom, left, right, grads, out, frame):
    fill_frame(frame, (center, top, bottom, left, right))
    weight_sums(frame, grads, scale, out)


def split_halves(values, start, keep, send):
    half = values.shape[1] // 2
    rows = slice(start, start + values.shape[0])
    core = lax.axis_index("col") % 2
    for i in range(2):

        @pl.when(core == i)
        def _():
            keep[rows] = values[:, i * half : (i + 1) * half]
            send[rows] = values[:, (1 - i) * half : (2 - i) * half]


def weight_pack_kernel(
    scale, center, top, bottom, left, right, grads, gain_part,
    keep, send, frame, wide_grads, packed,
):
    fill_frame(frame, (center, top, bottom, left, right))
    wide_grads[...] = grads[...].astype(F32)
    packed[...] = jnp.zeros(packed.shape, F32)
    weight_sums(frame, wide_grads, scale, packed)
    packed[49:50] = scale * gain_part[...]
    split_halves(packed[...].astype(BF), 0, keep, send)


def section_kernel(
    center, top, bottom, left, right, taps, residual,
    flat, keep, send,
    frame, image,
):
    height, breadth, channels = center.shape
    fill_frame(frame, (center, top, bottom, left, right))
    convolve(frame, taps, True, image)
    value = (image[...] + residual[...].astype(F32)).reshape(flat.shape).astype(BF)
    flat[...] = value
    blocks, _, width = keep.shape
    core = lax.axis_index("col") % 2
    for i in range(2):

        @pl.when(core == i)
        def _():
            for m in range(blocks):
                mine, other = (2 * m + i) * width, (2 * m + 1 - i) * width
                keep[m] = value[:, mine : mine + width]
                send[m] = value[:, other : other + width]


def merge_kernel(
    scale, scale_wide,
    flat, patch, unit_summed, inverse_summed, merge_gain, branch, layer_scale, wide_part, wide_gain,
    grad_summed, grad_branch, keep, send,
    pairs, packed, sums,
):
    tiles, height, breadth, _ = pairs.shape
    channels = 128 * tiles
    value = flat[...]
    for dy in range(2):
        for dx in range(2):
            j = 2 * dy + dx
            part = dot_last(value, patch[j * channels : (j + 1) * channels])
            part = part.reshape(height // 2, breadth // 2, channels)
            for y in range(height // 2):
                for k in range(tiles):
                    piece = part[y, :, k * 128 : (k + 1) * 128]
                    pairs[k, 2 * y + dy, pl.ds(dx, breadth // 2, stride=2), :] = piece
    sums[...] = jnp.zeros(sums.shape, F32)

    @over_rows(height, breadth)
    def _(y, rows):
        merged = jnp.concatenate([pairs[k, y] for k in range(tiles)], axis=1)
        unit = unit_summed[rows]
        sums[0:1] += jnp.sum(merged * unit, axis=0, keepdims=True)
        grad = normalize_back(merged * merge_gain[...], unit, inverse_summed[rows])
        grad_summed[rows] = grad
        sums[1:2] += jnp.sum(grad * branch[rows], axis=0, keepdims=True)
        grad_branch[rows] = (layer_scale[...] * grad).astype(BF)

    split_halves(grad_branch[...], 0, keep, send)
    packed[...] = jnp.zeros(packed.shape, F32)
    for i in range(2):
        columns = slice(i * channels, (i + 1) * channels)
        packed[49 * i : 49 + 49 * i] = wide_part[:, columns]
        packed[98 + i : 99 + i] = scale_wide * wide_gain[:, columns]
        packed[100 + i : 101 + i] = scale * sums[i : i + 1]
    split_halves(packed[...].astype(BF), grad_branch.shape[0], keep, send)


def back_kernel(
    grad_branch, project, slope, expand, unit_mixed, inverse_mixed, gain,
    keep, send, grad_mixed, first, last, gain_part,
    hidden, upward, normed,
):
    height, breadth, channels = grad_mixed.shape
    pixels, hidden_width = slope.shape

    def chunk(index, carry):
        span = pl.ds(pl.multiple_of(index * CHUNK, CHUNK), CHUNK)
        hidden[...] = dot_last(grad_branch[...], project[span])
        for start in range(0, pixels, 64):
            rows = slice(start, start + 64)
            upward[rows, span] = (hidden[rows] * slope[rows, span].astype(F32)).astype(BF)
        return carry

    lax.fori_loop(0, hidden_width // CHUNK, chunk, 0)
    normed[...] = dot_last(upward[...], expand[...])
    split_halves(upward[...], 0, keep, send)
    part = jnp.zeros((1, channels), F32)
    for y in range(height):
        rows = slice(y * breadth, (y + 1) * breadth)
        value = normed[rows]
        unit = unit_mixed[rows]
        part = part + jnp.sum(value * unit, axis=0, keepdims=True)
        narrow = normalize_back(value * gain[...], unit, inverse_mixed[rows]).astype(BF)
        grad_mixed[y] = narrow
        if y < 3:
            first[y] = narrow
        if y >= height - 3:
            last[y - (height - 3)] = narrow
    gain_part[...] = part


def patch_product_kernel(factor, early, early_other, own, other, keep, send):
    blocks, quarter, _ = own.shape
    rows = keep.shape[0] // max(blocks // 2, 1)
    channels = rows // 4
    at_patches = early.shape[1] - channels
    bit = (lax.axis_index("col") // 2) % 2
    for j in range(4):
        span = slice(j * quarter, (j + 1) * quarter)
        left = jnp.concatenate([early[span, at_patches:], early_other[span, at_patches:]], axis=0)
        for m in range(blocks):
            right = jnp.concatenate([own[m], other[m]], axis=0)
            value = (factor * dot_first(left, right)).astype(BF)
            at = m // 2 * rows + j * channels
            for i in range(2):

                @pl.when(bit == i)
                def _():
                    target = keep if m % 2 == i else send
                    target[at : at + channels] = value


def store_slices(position, value, begin, offset, rows, pitch, keep, send):
    bit = (lax.axis_index("row") >> position) % 2
    low = (1 << position) - 1
    for i in range(2):

        @pl.when(bit == i)
        def _():
            for k in range(value.shape[0] // rows):
                r = begin + k
                target = keep if (r >> position) & 1 == i else send
                at = ((r >> (position + 1)) << position | (r & low)) * pitch + offset
                target[at : at + rows] = value[k * rows : (k + 1) * rows]


def project_product_kernel(factor, slices, early, early_other, own, other, keep, send):
    width = keep.shape[1]
    hidden_width = early.shape[1] - 4 * width
    pixels = early.shape[0]
    deep = hidden_width // slices
    right = jnp.concatenate([own[:pixels], other[:pixels]], axis=0)
    step = max(CHUNK, deep)
    for start in range(0, hidden_width, step):
        columns = slice(start, start + step)
        left = jnp.concatenate([early[:, columns], early_other[:, columns]], axis=0)
        value = (factor * dot_first(left, right)).astype(BF)
        store_slices(1, value, start // deep, 0, deep, deep, keep, send)
    tail = (own[pixels:].astype(F32) + other[pixels:].astype(F32)).astype(BF)
    at = slices // 2 * deep
    keep[at:] = tail
    send[at:] = tail


def expand_product_kernel(factor, slices, early, early_other, own, other, keep, send):
    width = keep.shape[1]
    channels = 2 * width
    hidden_width = early.shape[1] - 2 * channels
    shallow = channels // slices
    blocks = own.shape[1] // width
    columns = slice(hidden_width, hidden_width + channels)
    left = jnp.concatenate([early[:, columns], early_other[:, columns]], axis=0)
    for k in range(blocks):
        columns = slice(k * width, (k + 1) * width)
        right = jnp.concatenate([own[:, columns], other[:, columns]], axis=0)
        value = (factor * dot_first(left, right)).astype(BF)
        store_slices(0, value, 0, k * shallow, shallow, blocks * shallow, keep, send)


def finish_patch_kernel(own, other, out):
    blocks, _, width = own.shape
    core = lax.axis_index("col") % 2
    for i in range(2):

        @pl.when(core == i)
        def _():
            for m in range(blocks):
                a, b = (2 * m + i) * width, (2 * m + 1 - i) * width
                out[:, a : a + width] = own[m].astype(F32)
                out[:, b : b + width] = other[m].astype(F32)


def join_halves(own, other, start, out):
    half = own.shape[1]
    rows = slice(start, start + out.shape[0])
    core = lax.axis_index("col") % 2
    for i in range(2):

        @pl.when(core == i)
        def _():
            out[:, i * half : (i + 1) * half] = own[rows].astype(F32)
            out[:, (1 - i) * half : (2 - i) * half] = other[rows].astype(F32)


def finish_project_kernel(own, other, project, wide_taps, wide_gain, merge, layer, small):
    deep, channels = project.shape
    join_halves(own, other, 0, project)
    join_halves(own, other, deep, small)
    for i in range(2):
        columns = slice(i * channels, (i + 1) * channels)
        for p in range(7):
            start = 49 * i + 7 * p
            wide_taps[p, :, columns] = small[start : start + 7]
        wide_gain[:, columns] = small[98 + i : 99 + i]
    merge[...] = small[100:101]
    layer[...] = small[101:102]


def finish_expand_kernel(own, other, expand, taps, gain, small):
    shallow, hidden_width = expand.shape
    width = own.shape[1]
    blocks = hidden_width // (2 * width)
    core = lax.axis_index("col") % 2
    for i in range(2):

        @pl.when(core == i)
        def _():
            for k in range(blocks):
                rows = slice(k * shallow, (k + 1) * shallow)
                a, b = (i * blocks + k) * width, ((1 - i) * blocks + k) * width
                expand[:, a : a + width] = own[rows].astype(F32)
                expand[:, b : b + width] = other[rows].astype(F32)

    join_halves(own, other, blocks * shallow, small)
    for p in range(7):
        taps[p] = small[7 * p : 7 * p + 7]
    gain[...] = small[49:50]


def input_kernel(center, top, bottom, left, right, taps, grad_summed, out, frame, image):
    fill_frame(frame, (center, top, bottom, left, right))
    convolve(frame, taps, True, image)
    out[...] = (image[...] + grad_summed[...].reshape(image.shape)).astype(BF)


def body(
    block_input,
    kernel_three,
    gain_three,
    expand_weight,
    project_weight,
    layer_scale,
    merge_gain,
    patch_weight,
    kernel_four,
    gain_four,
    normed_cotangent,
    residual_cotangent,
):
    _, height, breadth, channels = block_input.shape
    hidden_width = expand_weight.shape[1]
    wide = patch_weight.shape[1]
    pixels = height * breadth
    quarter = pixels // 4
    rows4, cols4 = height // 2, breadth // 2
    row_count = lax.axis_size("row")
    col_count = lax.axis_size("col")
    scale_three = 1.0 / math.sqrt(pixels * row_count * col_count)
    scale_four = 1.0 / math.sqrt(quarter * row_count * col_count)
    center = block_input[0]
    gain_three, layer_scale, merge_gain, gain_four = (
        v[None] for v in (gain_three, layer_scale, merge_gain, gain_four)
    )
    dma = pltpu.SemaphoreType.DMA
    half = channels // 2
    hbm = pltpu.HBM

    def like(array):
        return shape_of(*array.shape, dtype=array.dtype)

    edge = shape_of(3, breadth, channels, dtype=BF)
    rows_input = neighbours(center[:3], center[height - 3 :], "row")
    inputs = (center, kernel_three, gain_three, layer_scale, merge_gain)
    center, taps_three, gain_three, layer_scale, merge_gain = run(
        load_kernel,
        "load",
        inputs,
        tuple(map(like, inputs)),
        scratch=(dma((5,)),),
        spaces=dict.fromkeys(range(5), hbm),
        after=rows_input[:1],
        limit=4,
        us=2,
    )
    framed = halo(center, rows_input, "strips_input")
    inputs = (
        expand_weight, project_weight, patch_weight, kernel_four, gain_four,
        normed_cotangent[0], residual_cotangent[0],
    )
    edge_four = shape_of(3, cols4, wide, dtype=BF)
    (
        early, unit_mixed, inverse_mixed, slope, branch, unit_summed, inverse_summed,
        section, first, last,
        expand_weight, project_weight, patch_weight, taps_four, gain_four, cotangent, residual,
    ) = run(
        front_kernel,
        "front",
        (*framed, taps_three, gain_three, layer_scale, merge_gain, *inputs),
        (
            shape_of(pixels, hidden_width + 2 * channels, dtype=BF),
            shape_of(pixels, channels),
            shape_of(pixels, 1),
            shape_of(pixels, hidden_width, dtype=BF),
            shape_of(pixels, channels),
            shape_of(pixels, channels),
            shape_of(pixels, 1),
            shape_of(rows4, cols4, wide, dtype=BF),
            edge_four,
            edge_four,
            *map(like, inputs),
        ),
        scratch=(
            frame_scratch(center),
            pltpu.VMEM((height, breadth, channels), F32),
            pltpu.VMEM((channels // 128, height, breadth, 128), F32),
            pltpu.VMEM((pixels, CHUNK), F32),
            dma((7,)),
        ),
        spaces=dict.fromkeys(range(9, 16), hbm),
        limit=28,
        us=12,
    )

    framed_four = halo(section, neighbours(first, last, "row"), "strips_section")
    mixer_image = pltpu.VMEM((rows4, cols4, wide), F32)
    grad_four, grad_four_half, first, last, gain_four_part = run(
        mixer_kernel,
        "mixer",
        (*framed_four, taps_four, gain_four, cotangent),
        (
            shape_of(rows4, cols4, wide),
            shape_of(rows4, cols4, wide, dtype=BF),
            edge_four,
            edge_four,
            shape_of(1, wide),
        ),
        scratch=(frame_scratch(section), mixer_image),
        limit=12,
        us=3,
    )
    rows_grad = neighbours(first, last, "row")
    (kernel_four_part,) = run(
        functools.partial(weight_kernel, scale_four),
        "mixer_weights",
        (*framed_four, grad_four),
        (shape_of(49, wide),),
        scratch=(frame_scratch(section),),
        after=rows_grad[:1],
        limit=12,
        us=3,
    )
    framed_grad = halo(grad_four_half, rows_grad, "strips_mixer", after=(kernel_four_part,))
    block_count = col_count // 2
    block = wide // col_count
    blocked = shape_of(block_count, quarter, block, dtype=BF)
    flat, flat_keep, flat_send, early = hold(
        section_kernel,
        "section_grad",
        (*framed_grad, taps_four, residual),
        (shape_of(quarter, wide, dtype=BF), blocked, blocked),
        early,
        scratch=(frame_scratch(section), mixer_image),
        limit=12,
        us=3,
    )

    flat_other = swap(flat_send, "col", 1)
    early_other = swap(early, "col", 1)
    split = shape_of(pixels + 112, half, dtype=BF)
    grad_summed, grad_branch, branch_keep, branch_send = run(
        functools.partial(merge_kernel, scale_three, scale_four),
        "merge_back",
        (
            flat, patch_weight, unit_summed, inverse_summed, merge_gain, branch, layer_scale,
            kernel_four_part, gain_four_part,
        ),
        (shape_of(pixels, channels), shape_of(pixels, channels, dtype=BF), split, split),
        scratch=(
            pltpu.VMEM((channels // 128, height, breadth, 128), F32),
            pltpu.VMEM((112, channels), F32),
            pltpu.VMEM((8, channels), F32),
        ),
        limit=16,
        us=0.8,
    )
    branch_other = swap(branch_send, "col", 1)
    patch_half = shape_of(block_count // 2 * 4 * channels, block, dtype=BF)
    patch_keep, patch_send = run(
        functools.partial(patch_product_kernel, scale_four),
        "patch_product",
        (early, early_other, flat_keep, flat_other),
        (patch_half, patch_half),
        limit=16,
        us=0.9,
    )
    deep, shallow = hidden_width // row_count, channels // row_count
    groups = hidden_width // channels
    project_half = shape_of(row_count // 2 * deep + 112, half, dtype=BF)
    upward_half = shape_of(pixels, hidden_width // 2, dtype=BF)
    upward_keep, upward_send, grad_mixed, first, last, gain_part = run(
        back_kernel,
        "mlp_back",
        (grad_branch, project_weight, slope, expand_weight, unit_mixed, inverse_mixed, gain_three),
        (
            upward_half,
            upward_half,
            shape_of(height, breadth, channels, dtype=BF),
            edge,
            edge,
            shape_of(1, channels),
        ),
        scratch=(
            pltpu.VMEM((pixels, CHUNK), F32),
            pltpu.VMEM((pixels, hidden_width), BF),
            pltpu.VMEM((pixels, channels), F32),
        ),
        after=(patch_send,),
        limit=16,
        us=1.2,
    )
    rows_back = neighbours(first, last, "row")
    upward_other = swap(upward_send, "col", 1)
    project_keep, project_send = run(
        functools.partial(project_product_kernel, scale_three, row_count),
        "project_product",
        (early, early_other, branch_keep, branch_other),
        (project_half, project_half),
        after=(upward_send,),
        limit=16,
        us=0.9,
    )
    expand_half = shape_of(row_count // 2 * groups * shallow, half, dtype=BF)
    expand_keep, expand_send = run(
        functools.partial(expand_product_kernel, scale_three, row_count),
        "expand_product",
        (early, early_other, upward_keep, upward_other),
        (expand_half, expand_half),
        after=(project_send, *rows_back),
        limit=16,
        us=0.6,
    )
    framed_back = halo(grad_mixed, rows_back, "strips_back", after=(expand_send,))
    small_half = shape_of(64, half, dtype=BF)
    small_keep, small_send = run(
        functools.partial(weight_pack_kernel, scale_three),
        "block_weights",
        (*framed, grad_mixed, gain_part),
        (small_half, small_half),
        scratch=(
            frame_scratch(center),
            pltpu.VMEM((height, breadth, channels), F32),
            pltpu.VMEM((64, channels), F32),
        ),
        after=(*framed_back[1:3], expand_send),
        limit=12,
        us=1.8,
    )
    row_bits, col_bits = axis_bits("row"), axis_bits("col")
    outer = len(row_bits)
    low_first = [("row", bit, 0) for bit in row_bits]
    patch_order = [("col", bit, outer) for bit in col_bits[1:]] + low_first
    project_order = [("row", bit, 1) for bit in row_bits[1:]] + low_first[:1]
    patch_chain = Chain(patch_keep, patch_send, patch_order, block_count * row_count, 4 * channels // row_count)
    project_chain = Chain(project_keep, project_send, project_order, row_count, deep)
    expand_chain = Chain(expand_keep, expand_send, low_first, row_count, groups * shallow)
    sent = project_chain.advance((small_keep,))
    sent = patch_chain.advance((small_keep, *sent))
    (input_grad,) = run(
        input_kernel,
        "input_grad",
        (*framed_back, taps_three, grad_summed),
        (shape_of(height, breadth, channels, dtype=BF),),
        scratch=(frame_scratch(center), pltpu.VMEM((height, breadth, channels), F32)),
        after=(small_keep, *sent),
        limit=12,
        us=0.4,
    )
    small = small_keep + swap(small_send, "col", 1)
    expand_chain.advance((input_grad,), (small, swap(small, "row", 1)))
    patch_chain.advance((input_grad,))
    patch_sum = patch_chain.finish()
    patch_sum = gather(patch_sum, "col", col_bits[1:])
    (patch_grad,) = run(
        finish_patch_kernel,
        "finish_patch",
        (patch_sum, swap(patch_sum, "col", 1)),
        (shape_of(4 * channels // row_count, wide),),
        limit=8,
    )

    def share(total):
        for bit in col_bits[1:]:
            total = total + swap(total, "col", bit)
        return total, swap(total, "col", 1)

    vector, wide_vector = shape_of(1, channels), shape_of(1, wide)
    project_grad, wide_taps, wide_gain, merge_sum, layer_sum = run(
        finish_project_kernel,
        "finish_project",
        share(project_chain.finish()),
        (shape_of(deep, channels), shape_of(7, 7, wide), wide_vector, vector, vector),
        scratch=(pltpu.VMEM((112, channels), F32),),
        limit=8,
    )
    expand_grad, taps_sum, gain_sum = run(
        finish_expand_kernel,
        "finish_expand",
        share(expand_chain.finish()),
        (shape_of(shallow, hidden_width), shape_of(7, 7, channels), vector),
        scratch=(pltpu.VMEM((64, channels), F32),),
        limit=8,
    )
    return (
        input_grad[None],
        taps_sum,
        gain_sum[0],
        expand_grad,
        project_grad,
        layer_sum[0],
        merge_sum[0],
        patch_grad,
        wide_taps,
        wide_gain[0],
    )


def solution(mesh):
    pixels = P(None, "row", "col", None)
    return jax.shard_map(
        body,
        mesh=mesh,
        in_specs=(pixels,) + (P(),) * 9 + (pixels, pixels),
        out_specs=(pixels, P(), P(), P("row", None), P("row", None), P(), P(), P("row", None), P(), P()),
        check_vma=False,
    )
```

```python
import functools
import math

import jax
import jax.numpy as jnp
from jax import lax
from jax.experimental import pallas as pl
from jax.experimental.pallas import tpu as pltpu
from jax.sharding import PartitionSpec as P

EPSILON = 1e-06
BF = jnp.bfloat16
F32 = jnp.float32
MIB = 1 << 20
PAD = 8
CHUNK = 256


def shape_of(*dims, dtype=F32):
    return jax.ShapeDtypeStruct(dims, dtype)


def run(kernel, name, args, outs, scratch=(), spaces=None, after=(), aliases=None, limit=24, us=0.0):
    spaces = spaces or {}
    count, extra = len(args), len(after)

    def spec(place):
        return pl.BlockSpec(memory_space=spaces.get(place, pltpu.VMEM))

    def inner(*refs):
        kernel(*refs[:count], *refs[count + extra :])

    return pl.pallas_call(
        inner,
        name=name,
        out_shape=outs,
        in_specs=[spec(i) for i in range(count)] + [pl.BlockSpec(memory_space=pl.ANY)] * extra,
        out_specs=[spec(("out", i)) for i in range(len(outs))],
        scratch_shapes=list(scratch),
        input_output_aliases=aliases or {},
        compiler_params=pltpu.CompilerParams(vmem_limit_bytes=limit * MIB),
        cost_estimate=pl.CostEstimate(flops=int(us * 1.1e9) + 1000, bytes_accessed=1000, transcendentals=0),
    )(*args, *after)


def swap(values, axis, bit):
    return lax.ppermute(values, axis, [(i, i ^ bit) for i in range(lax.axis_size(axis))])


def axis_bits(axis):
    return [1 << k for k in range((lax.axis_size(axis) - 1).bit_length())]


def own_bit(axis, bit):
    return (lax.axis_index(axis) // bit) % 2


def chain(keep, send, order, count, rows, extra=(), after=()):
    for place, (axis, bit, _) in enumerate(order):
        received = swap(send, axis, bit)
        if place + 1 == len(order):
            return keep + received
        axis, bit, position = order[place + 1]
        grown = extra if place == 0 else ()
        count //= 2
        tail = keep.shape[0] - count * rows + (grown[0].shape[0] if grown else 0)
        out = shape_of(count // 2 * rows + tail, keep.shape[1], dtype=BF)
        keep, send = run(
            functools.partial(step_kernel, axis, bit, position, count, rows),
            "sum_step",
            (keep, received, *grown),
            (out, out),
            after=after if place == (1 if extra else 0) else (),
            limit=8,
            us=0.2,
        )


def step_kernel(axis, bit, position, count, rows, keep, received, *refs):
    *grown, next_keep, next_send = refs
    mine = (lax.axis_index(axis) // bit) % 2
    low = (1 << position) - 1
    for i in range(2):

        @pl.when(mine == i)
        def _():
            for s in range(count):
                span = slice(s * rows, (s + 1) * rows)
                at = ((s >> (position + 1)) << position | (s & low)) * rows
                target = next_keep if (s >> position) & 1 == i else next_send
                target[at : at + rows] = (keep[span].astype(F32) + received[span].astype(F32)).astype(BF)

    tails = []
    if keep.shape[0] > count * rows:
        tails.append(keep[count * rows :].astype(F32) + received[count * rows :].astype(F32))
    if grown:
        tails.append(sum(g[...].astype(F32) for g in grown))
    at = count // 2 * rows
    for tail in tails:
        for target in (next_keep, next_send):
            target[at : at + tail.shape[0]] = tail.astype(BF)
        at += tail.shape[0]


def gather(values, axis, bits):
    values = values[None]
    for bit in reversed(bits):
        other = swap(values, axis, bit)
        mine = own_bit(axis, bit)
        low = jnp.where(mine == 0, values, other)
        high = jnp.where(mine == 0, other, values)
        values = jnp.stack([low, high], axis=1).reshape(-1, *values.shape[1:])
    return values


def neighbours(first, last, axis):
    count = lax.axis_size(axis)
    forward = [(i, i + 1) for i in range(count - 1)]
    backward = [(i + 1, i) for i in range(count - 1)]
    return lax.ppermute(last, axis, forward), lax.ppermute(first, axis, backward)


def strip_kernel(center, top, bottom, first, last):
    height, breadth = center.shape[:2]
    for source, start in ((top, 0), (center, 3), (bottom, 3 + height)):
        values = source[...].astype(F32)
        rows = slice(start, start + source.shape[0])
        first[rows] = values[:, :PAD].astype(BF)
        last[rows] = values[:, breadth - PAD :].astype(BF)


def halo(center, rows, name, after=()):
    height, _, channels = center.shape
    top, bottom = rows
    strip = shape_of(height + 6, PAD, channels, dtype=BF)
    first, last = run(strip_kernel, name, (center, top, bottom), (strip, strip), after=after, limit=8)
    left, right = neighbours(first, last, "col")
    return center, top, bottom, left, right


def hold(kernel, name, args, outs, carried, **options):
    count = len(args)

    def inner(*refs):
        kernel(*refs[:count], *refs[count + 1 : count + 1 + len(outs)], *refs[count + 2 + len(outs) :])

    return run(
        inner,
        name,
        (*args, carried),
        (*outs, shape_of(*carried.shape, dtype=carried.dtype)),
        spaces={count: pl.ANY, ("out", len(outs)): pl.ANY},
        aliases={count: len(outs)},
        **options,
    )


def fill_frame(frame, parts):
    center, top, bottom, left, right = parts
    height, breadth = center.shape[:2]
    middle = slice(PAD, PAD + breadth)
    frame[0:3, middle] = top[...].astype(F32)
    frame[3 : 3 + height, middle] = center[...].astype(F32)
    frame[3 + height :, middle] = bottom[...].astype(F32)
    frame[:, :PAD] = left[...].astype(F32)
    frame[:, PAD + breadth :] = right[...].astype(F32)


def frame_scratch(center):
    height, breadth, channels = center.shape
    return pltpu.VMEM((height + 6, breadth + 2 * PAD, channels), F32)


def lane_tiles(channels):
    def over(step):
        def wrapped(index, carry):
            step(pl.ds(pl.multiple_of(index * 128, 128), 128))
            return carry

        lax.fori_loop(0, channels // 128, wrapped, 0)

    return over


def convolve(frame, taps, flip, out):
    height, breadth, channels = out.shape

    @lane_tiles(channels)
    def _(lanes):
        for column in range(0, breadth, 8):
            total = jnp.zeros((height, 8, 128), F32)
            for q in range(7):
                rows = frame[:, pl.ds(column + PAD - 3 + q, 8), lanes]
                for p in range(7):
                    a, b = (6 - p, 6 - q) if flip else (p, q)
                    total = total + rows[p : p + height] * taps[a, pl.ds(b, 1), lanes]
            out[:, pl.ds(column, 8), lanes] = total


def weight_sums(frame, grads, scale, out):
    height, breadth, channels = grads.shape

    @lane_tiles(channels)
    def _(lanes):
        for q in range(7):
            totals = [jnp.zeros((8, 128), F32)] * 7
            for column in range(0, breadth, 8):
                rows = frame[:, pl.ds(column + PAD - 3 + q, 8), lanes]
                grad = grads[:, pl.ds(column, 8), lanes]
                for p in range(7):
                    totals[p] = totals[p] + jnp.sum(rows[p : p + height] * grad, axis=0)
            for p in range(7):
                out[pl.ds(7 * p + q, 1), lanes] = scale * jnp.sum(totals[p], axis=0, keepdims=True)


def mean(values):
    return jnp.mean(values, axis=-1, keepdims=True)


def normalize(values):
    level = mean(values)
    inverse = lax.rsqrt(mean(values * values) - level * level + EPSILON)
    return (values - level) * inverse, inverse


def normalize_back(grads, unit_values, inverse):
    return (grads - mean(grads) - unit_values * mean(grads * unit_values)) * inverse


def dot(left, right):
    return jnp.dot(left, right, preferred_element_type=F32)


def dot_last(left, right):
    return lax.dot_general(left, right, (((1,), (1,)), ((), ())), preferred_element_type=F32)


def dot_first(left, right):
    return lax.dot_general(left, right, (((0,), (0,)), ((), ())), preferred_element_type=F32)


def over_rows(count, size):
    def over(step):
        def wrapped(index, carry):
            step(index, pl.ds(pl.multiple_of(index * size, size), size))
            return carry

        lax.fori_loop(0, count, wrapped, 0)

    return over


def fetch(sources, targets, semaphores):
    copies = [
        pltpu.make_async_copy(source, target, semaphores.at[i])
        for i, (source, target) in enumerate(zip(sources, targets))
    ]
    for copy in copies:
        copy.start()
    return copies


def load_kernel(*refs):
    *arrays, semaphores = refs
    count = len(arrays) // 2
    for copy in fetch(arrays[:count], arrays[count:], semaphores):
        copy.wait()


def front_kernel(
    center, top, bottom, left, right, taps, gain, layer_scale, merge_gain,
    expand, project, patch, wide_taps, wide_gain, cotangent, residual,
    early, unit_mixed, inverse_mixed, slope, branch, unit_summed, inverse_summed, section, first, last,
    expand_here, project_here, patch_here, wide_taps_here, wide_gain_here, cotangent_here, residual_here,
    frame, image, pairs, upward, semaphores,
):
    height, breadth, channels = center.shape
    hidden_width = expand.shape[1]
    pixels = height * breadth
    copies = fetch(
        (expand, project, patch, wide_taps, wide_gain, cotangent, residual),
        (expand_here, project_here, patch_here, wide_taps_here, wide_gain_here, cotangent_here, residual_here),
        semaphores,
    )
    fill_frame(frame, (center, top, bottom, left, right))
    convolve(frame, taps, False, image)
    at_normed = slice(hidden_width, hidden_width + channels)
    at_patches = slice(hidden_width + channels, hidden_width + 2 * channels)

    @over_rows(height, breadth)
    def _(y, rows):
        unit, inverse = normalize(image[y])
        unit_mixed[rows] = unit
        inverse_mixed[rows] = inverse
        early[rows, at_normed] = (unit * gain[...]).astype(BF)

    copies[0].wait()

    def chunk(index, carry):
        lanes = pl.ds(pl.multiple_of(index * CHUNK, CHUNK), CHUNK)
        upward[...] = dot(early[:, at_normed], expand_here[:, lanes])
        for start in range(0, pixels, 64):
            rows = slice(start, start + 64)
            value = upward[rows]
            cumulative = 0.5 + 0.5 * lax.erf(value * (1.0 / math.sqrt(2.0)))
            density = jnp.exp(-0.5 * value * value) * (1.0 / math.sqrt(2.0 * math.pi))
            early[rows, lanes] = (value * cumulative).astype(BF)
            slope[rows, lanes] = (cumulative + value * density).astype(BF)
        return carry

    lax.fori_loop(0, hidden_width // CHUNK, chunk, 0)
    copies[1].wait()
    branch[...] = dot(early[:, :hidden_width], project_here[...])

    @over_rows(height, breadth)
    def _(y, rows):
        summed = center[y].astype(F32) + layer_scale[...] * branch[rows]
        unit, inverse = normalize(summed)
        unit_summed[rows] = unit
        inverse_summed[rows] = inverse
        merged = unit * merge_gain[...]
        for k in range(channels // 128):
            pairs[k, y] = merged[:, k * 128 : (k + 1) * 128]

    quarter = pixels // 4
    for dy in range(2):
        for dx in range(2):
            j = 2 * dy + dx
            for y in range(height // 2):
                start = j * quarter + y * (breadth // 2)
                for k in range(channels // 128):
                    piece = pairs[k, 2 * y + dy, pl.ds(dx, breadth // 2, stride=2), :]
                    lane = hidden_width + channels + k * 128
                    early[start : start + breadth // 2, lane : lane + 128] = piece.astype(BF)
    copies[2].wait()
    total = dot(early[:quarter, at_patches], patch_here[:channels])
    for j in range(1, 4):
        total = total + dot(
            early[j * quarter : (j + 1) * quarter, at_patches],
            patch_here[j * channels : (j + 1) * channels],
        )
    total = total.reshape(section.shape)
    section[...] = total.astype(BF)
    first[...] = total[:3].astype(BF)
    last[...] = total[height // 2 - 3 :].astype(BF)
    for copy in copies[3:]:
        copy.wait()


def mixer_kernel(
    center, top, bottom, left, right, taps, gain, cotangent,
    grad, grad_half, first, last, gain_part,
    frame, image,
):
    height, breadth, channels = center.shape
    fill_frame(frame, (center, top, bottom, left, right))
    convolve(frame, taps, False, image)
    part = jnp.zeros((1, channels), F32)
    for y in range(height):
        unit, inverse = normalize(image[y])
        cot = cotangent[y].astype(F32)
        part = part + jnp.sum(cot * unit, axis=0, keepdims=True)
        value = normalize_back(cot * gain[...], unit, inverse)
        grad[y] = value
        narrow = value.astype(BF)
        grad_half[y] = narrow
        if y < 3:
            first[y] = narrow
        if y >= height - 3:
            last[y - (height - 3)] = narrow
    gain_part[...] = part


def weight_kernel(scale, center, top, bottom, left, right, grads, out, frame):
    fill_frame(frame, (center, top, bottom, left, right))
    weight_sums(frame, grads, scale, out)


def split_halves(values, start, keep, send):
    half = values.shape[1] // 2
    rows = slice(start, start + values.shape[0])
    core = lax.axis_index("col") % 2
    for i in range(2):

        @pl.when(core == i)
        def _():
            keep[rows] = values[:, i * half : (i + 1) * half]
            send[rows] = values[:, (1 - i) * half : (2 - i) * half]


def weight_pack_kernel(
    scale, center, top, bottom, left, right, grads, gain_part,
    keep, send, frame, wide_grads, packed,
):
    fill_frame(frame, (center, top, bottom, left, right))
    wide_grads[...] = grads[...].astype(F32)
    packed[...] = jnp.zeros(packed.shape, F32)
    weight_sums(frame, wide_grads, scale, packed)
    packed[49:50] = scale * gain_part[...]
    split_halves(packed[...].astype(BF), 0, keep, send)


def section_kernel(
    center, top, bottom, left, right, taps, residual,
    flat, keep, send,
    frame, image,
):
    height, breadth, channels = center.shape
    fill_frame(frame, (center, top, bottom, left, right))
    convolve(frame, taps, True, image)
    value = (image[...] + residual[...].astype(F32)).reshape(flat.shape).astype(BF)
    flat[...] = value
    blocks, _, width = keep.shape
    core = lax.axis_index("col") % 2
    for i in range(2):

        @pl.when(core == i)
        def _():
            for m in range(blocks):
                mine, other = (2 * m + i) * width, (2 * m + 1 - i) * width
                keep[m] = value[:, mine : mine + width]
                send[m] = value[:, other : other + width]


def merge_kernel(
    scale, scale_wide,
    flat, patch, unit_summed, inverse_summed, merge_gain, branch, layer_scale, wide_part, wide_gain,
    grad_summed, grad_branch, keep, send,
    pairs, packed, sums,
):
    tiles, height, breadth, _ = pairs.shape
    channels = 128 * tiles
    value = flat[...]
    for dy in range(2):
        for dx in range(2):
            j = 2 * dy + dx
            part = dot_last(value, patch[j * channels : (j + 1) * channels])
            part = part.reshape(height // 2, breadth // 2, channels)
            for y in range(height // 2):
                for k in range(tiles):
                    piece = part[y, :, k * 128 : (k + 1) * 128]
                    pairs[k, 2 * y + dy, pl.ds(dx, breadth // 2, stride=2), :] = piece
    sums[...] = jnp.zeros(sums.shape, F32)

    @over_rows(height, breadth)
    def _(y, rows):
        merged = jnp.concatenate([pairs[k, y] for k in range(tiles)], axis=1)
        unit = unit_summed[rows]
        sums[0:1] += jnp.sum(merged * unit, axis=0, keepdims=True)
        grad = normalize_back(merged * merge_gain[...], unit, inverse_summed[rows])
        grad_summed[rows] = grad
        sums[1:2] += jnp.sum(grad * branch[rows], axis=0, keepdims=True)
        grad_branch[rows] = (layer_scale[...] * grad).astype(BF)

    split_halves(grad_branch[...], 0, keep, send)
    packed[...] = jnp.zeros(packed.shape, F32)
    for i in range(2):
        columns = slice(i * channels, (i + 1) * channels)
        packed[49 * i : 49 + 49 * i] = wide_part[:, columns]
        packed[98 + i : 99 + i] = scale_wide * wide_gain[:, columns]
        packed[100 + i : 101 + i] = scale * sums[i : i + 1]
    split_halves(packed[...].astype(BF), grad_branch.shape[0], keep, send)


def back_kernel(
    grad_branch, project, slope, expand, unit_mixed, inverse_mixed, gain,
    keep, send, grad_mixed, first, last, gain_part,
    hidden, upward, normed,
):
    height, breadth, channels = grad_mixed.shape
    pixels, hidden_width = slope.shape

    def chunk(index, carry):
        span = pl.ds(pl.multiple_of(index * CHUNK, CHUNK), CHUNK)
        hidden[...] = dot_last(grad_branch[...], project[span])
        for start in range(0, pixels, 64):
            rows = slice(start, start + 64)
            upward[rows, span] = (hidden[rows] * slope[rows, span].astype(F32)).astype(BF)
        return carry

    lax.fori_loop(0, hidden_width // CHUNK, chunk, 0)
    normed[...] = dot_last(upward[...], expand[...])
    split_halves(upward[...], 0, keep, send)
    part = jnp.zeros((1, channels), F32)
    for y in range(height):
        rows = slice(y * breadth, (y + 1) * breadth)
        value = normed[rows]
        unit = unit_mixed[rows]
        part = part + jnp.sum(value * unit, axis=0, keepdims=True)
        narrow = normalize_back(value * gain[...], unit, inverse_mixed[rows]).astype(BF)
        grad_mixed[y] = narrow
        if y < 3:
            first[y] = narrow
        if y >= height - 3:
            last[y - (height - 3)] = narrow
    gain_part[...] = part


def patch_product_kernel(factor, early, early_other, own, other, keep, send):
    blocks, quarter, _ = own.shape
    rows = keep.shape[0] // max(blocks // 2, 1)
    channels = rows // 4
    at_patches = early.shape[1] - channels
    bit = (lax.axis_index("col") // 2) % 2
    for j in range(4):
        span = slice(j * quarter, (j + 1) * quarter)
        left = jnp.concatenate([early[span, at_patches:], early_other[span, at_patches:]], axis=0)
        for m in range(blocks):
            right = jnp.concatenate([own[m], other[m]], axis=0)
            value = (factor * dot_first(left, right)).astype(BF)
            at = m // 2 * rows + j * channels
            for i in range(2):

                @pl.when(bit == i)
                def _():
                    target = keep if m % 2 == i else send
                    target[at : at + channels] = value


def store_slices(position, value, begin, offset, rows, pitch, keep, send):
    bit = (lax.axis_index("row") >> position) % 2
    low = (1 << position) - 1
    for i in range(2):

        @pl.when(bit == i)
        def _():
            for k in range(value.shape[0] // rows):
                r = begin + k
                target = keep if (r >> position) & 1 == i else send
                at = ((r >> (position + 1)) << position | (r & low)) * pitch + offset
                target[at : at + rows] = value[k * rows : (k + 1) * rows]


def project_product_kernel(factor, slices, early, early_other, own, other, keep, send):
    width = keep.shape[1]
    hidden_width = early.shape[1] - 4 * width
    pixels = early.shape[0]
    deep = hidden_width // slices
    right = jnp.concatenate([own[:pixels], other[:pixels]], axis=0)
    step = max(CHUNK, deep)
    for start in range(0, hidden_width, step):
        columns = slice(start, start + step)
        left = jnp.concatenate([early[:, columns], early_other[:, columns]], axis=0)
        value = (factor * dot_first(left, right)).astype(BF)
        store_slices(1, value, start // deep, 0, deep, deep, keep, send)
    tail = (own[pixels:].astype(F32) + other[pixels:].astype(F32)).astype(BF)
    at = slices // 2 * deep
    keep[at:] = tail
    send[at:] = tail


def expand_product_kernel(factor, slices, early, early_other, own, other, keep, send):
    width = keep.shape[1]
    channels = 2 * width
    hidden_width = early.shape[1] - 2 * channels
    shallow = channels // slices
    blocks = own.shape[1] // width
    columns = slice(hidden_width, hidden_width + channels)
    left = jnp.concatenate([early[:, columns], early_other[:, columns]], axis=0)
    for k in range(blocks):
        columns = slice(k * width, (k + 1) * width)
        right = jnp.concatenate([own[:, columns], other[:, columns]], axis=0)
        value = (factor * dot_first(left, right)).astype(BF)
        store_slices(0, value, 0, k * shallow, shallow, blocks * shallow, keep, send)


def finish_patch_kernel(own, other, out):
    blocks, _, width = own.shape
    core = lax.axis_index("col") % 2
    for i in range(2):

        @pl.when(core == i)
        def _():
            for m in range(blocks):
                a, b = (2 * m + i) * width, (2 * m + 1 - i) * width
                out[:, a : a + width] = own[m].astype(F32)
                out[:, b : b + width] = other[m].astype(F32)


def join_halves(own, other, start, out):
    half = own.shape[1]
    rows = slice(start, start + out.shape[0])
    core = lax.axis_index("col") % 2
    for i in range(2):

        @pl.when(core == i)
        def _():
            out[:, i * half : (i + 1) * half] = own[rows].astype(F32)
            out[:, (1 - i) * half : (2 - i) * half] = other[rows].astype(F32)


def finish_project_kernel(own, other, project, wide_taps, wide_gain, merge, layer, small):
    deep, channels = project.shape
    join_halves(own, other, 0, project)
    join_halves(own, other, deep, small)
    for i in range(2):
        columns = slice(i * channels, (i + 1) * channels)
        for p in range(7):
            start = 49 * i + 7 * p
            wide_taps[p, :, columns] = small[start : start + 7]
        wide_gain[:, columns] = small[98 + i : 99 + i]
    merge[...] = small[100:101]
    layer[...] = small[101:102]


def finish_expand_kernel(own, other, expand, taps, gain, small):
    shallow, hidden_width = expand.shape
    width = own.shape[1]
    blocks = hidden_width // (2 * width)
    core = lax.axis_index("col") % 2
    for i in range(2):

        @pl.when(core == i)
        def _():
            for k in range(blocks):
                rows = slice(k * shallow, (k + 1) * shallow)
                a, b = (i * blocks + k) * width, ((1 - i) * blocks + k) * width
                expand[:, a : a + width] = own[rows].astype(F32)
                expand[:, b : b + width] = other[rows].astype(F32)

    join_halves(own, other, blocks * shallow, small)
    for p in range(7):
        taps[p] = small[7 * p : 7 * p + 7]
    gain[...] = small[49:50]


def input_kernel(center, top, bottom, left, right, taps, grad_summed, out, frame, image):
    fill_frame(frame, (center, top, bottom, left, right))
    convolve(frame, taps, True, image)
    out[...] = (image[...] + grad_summed[...].reshape(image.shape)).astype(BF)


def body(
    block_input,
    kernel_three,
    gain_three,
    expand_weight,
    project_weight,
    layer_scale,
    merge_gain,
    patch_weight,
    kernel_four,
    gain_four,
    normed_cotangent,
    residual_cotangent,
):
    _, height, breadth, channels = block_input.shape
    hidden_width = expand_weight.shape[1]
    wide = patch_weight.shape[1]
    pixels = height * breadth
    quarter = pixels // 4
    rows4, cols4 = height // 2, breadth // 2
    row_count = lax.axis_size("row")
    col_count = lax.axis_size("col")
    scale_three = 1.0 / math.sqrt(pixels * row_count * col_count)
    scale_four = 1.0 / math.sqrt(quarter * row_count * col_count)
    center = block_input[0]
    gain_three, layer_scale, merge_gain, gain_four = (
        v[None] for v in (gain_three, layer_scale, merge_gain, gain_four)
    )
    dma = pltpu.SemaphoreType.DMA
    half = channels // 2
    hbm = pltpu.HBM

    def like(array):
        return shape_of(*array.shape, dtype=array.dtype)

    edge = shape_of(3, breadth, channels, dtype=BF)
    rows_input = neighbours(center[:3], center[height - 3 :], "row")
    inputs = (center, kernel_three, gain_three, layer_scale, merge_gain)
    center, taps_three, gain_three, layer_scale, merge_gain = run(
        load_kernel,
        "load",
        inputs,
        tuple(map(like, inputs)),
        scratch=(dma((5,)),),
        spaces=dict.fromkeys(range(5), hbm),
        after=rows_input[:1],
        limit=4,
        us=2,
    )
    framed = halo(center, rows_input, "strips_input")
    inputs = (
        expand_weight, project_weight, patch_weight, kernel_four, gain_four,
        normed_cotangent[0], residual_cotangent[0],
    )
    edge_four = shape_of(3, cols4, wide, dtype=BF)
    (
        early, unit_mixed, inverse_mixed, slope, branch, unit_summed, inverse_summed,
        section, first, last,
        expand_weight, project_weight, patch_weight, taps_four, gain_four, cotangent, residual,
    ) = run(
        front_kernel,
        "front",
        (*framed, taps_three, gain_three, layer_scale, merge_gain, *inputs),
        (
            shape_of(pixels, hidden_width + 2 * channels, dtype=BF),
            shape_of(pixels, channels),
            shape_of(pixels, 1),
            shape_of(pixels, hidden_width, dtype=BF),
            shape_of(pixels, channels),
            shape_of(pixels, channels),
            shape_of(pixels, 1),
            shape_of(rows4, cols4, wide, dtype=BF),
            edge_four,
            edge_four,
            *map(like, inputs),
        ),
        scratch=(
            frame_scratch(center),
            pltpu.VMEM((height, breadth, channels), F32),
            pltpu.VMEM((channels // 128, height, breadth, 128), F32),
            pltpu.VMEM((pixels, CHUNK), F32),
            dma((7,)),
        ),
        spaces=dict.fromkeys(range(9, 16), hbm),
        limit=28,
        us=12,
    )

    framed_four = halo(section, neighbours(first, last, "row"), "strips_section")
    mixer_image = pltpu.VMEM((rows4, cols4, wide), F32)
    grad_four, grad_four_half, first, last, gain_four_part = run(
        mixer_kernel,
        "mixer",
        (*framed_four, taps_four, gain_four, cotangent),
        (
            shape_of(rows4, cols4, wide),
            shape_of(rows4, cols4, wide, dtype=BF),
            edge_four,
            edge_four,
            shape_of(1, wide),
        ),
        scratch=(frame_scratch(section), mixer_image),
        limit=12,
        us=3,
    )
    rows_grad = neighbours(first, last, "row")
    (kernel_four_part,) = run(
        functools.partial(weight_kernel, scale_four),
        "mixer_weights",
        (*framed_four, grad_four),
        (shape_of(49, wide),),
        scratch=(frame_scratch(section),),
        after=rows_grad[:1],
        limit=12,
        us=3,
    )
    framed_grad = halo(grad_four_half, rows_grad, "strips_mixer", after=(kernel_four_part,))
    block_count = col_count // 2
    block = wide // col_count
    blocked = shape_of(block_count, quarter, block, dtype=BF)
    flat, flat_keep, flat_send, early = hold(
        section_kernel,
        "section_grad",
        (*framed_grad, taps_four, residual),
        (shape_of(quarter, wide, dtype=BF), blocked, blocked),
        early,
        scratch=(frame_scratch(section), mixer_image),
        limit=12,
        us=3,
    )

    flat_other = swap(flat_send, "col", 1)
    early_other = swap(early, "col", 1)
    split = shape_of(pixels + 112, half, dtype=BF)
    grad_summed, grad_branch, branch_keep, branch_send = run(
        functools.partial(merge_kernel, scale_three, scale_four),
        "merge_back",
        (
            flat, patch_weight, unit_summed, inverse_summed, merge_gain, branch, layer_scale,
            kernel_four_part, gain_four_part,
        ),
        (shape_of(pixels, channels), shape_of(pixels, channels, dtype=BF), split, split),
        scratch=(
            pltpu.VMEM((channels // 128, height, breadth, 128), F32),
            pltpu.VMEM((112, channels), F32),
            pltpu.VMEM((8, channels), F32),
        ),
        limit=16,
        us=0.8,
    )
    branch_other = swap(branch_send, "col", 1)
    patch_half = shape_of(block_count // 2 * 4 * channels, block, dtype=BF)
    patch_keep, patch_send = run(
        functools.partial(patch_product_kernel, scale_four),
        "patch_product",
        (early, early_other, flat_keep, flat_other),
        (patch_half, patch_half),
        limit=16,
        us=0.9,
    )
    deep, shallow = hidden_width // row_count, channels // row_count
    groups = hidden_width // channels
    project_half = shape_of(row_count // 2 * deep + 112, half, dtype=BF)
    upward_half = shape_of(pixels, hidden_width // 2, dtype=BF)
    upward_keep, upward_send, grad_mixed, first, last, gain_part = run(
        back_kernel,
        "mlp_back",
        (grad_branch, project_weight, slope, expand_weight, unit_mixed, inverse_mixed, gain_three),
        (
            upward_half,
            upward_half,
            shape_of(height, breadth, channels, dtype=BF),
            edge,
            edge,
            shape_of(1, channels),
        ),
        scratch=(
            pltpu.VMEM((pixels, CHUNK), F32),
            pltpu.VMEM((pixels, hidden_width), BF),
            pltpu.VMEM((pixels, channels), F32),
        ),
        after=(patch_send,),
        limit=16,
        us=1.2,
    )
    rows_back = neighbours(first, last, "row")
    upward_other = swap(upward_send, "col", 1)
    project_keep, project_send = run(
        functools.partial(project_product_kernel, scale_three, row_count),
        "project_product",
        (early, early_other, branch_keep, branch_other),
        (project_half, project_half),
        after=(upward_send,),
        limit=16,
        us=0.9,
    )
    expand_half = shape_of(row_count // 2 * groups * shallow, half, dtype=BF)
    expand_keep, expand_send = run(
        functools.partial(expand_product_kernel, scale_three, row_count),
        "expand_product",
        (early, early_other, upward_keep, upward_other),
        (expand_half, expand_half),
        after=(project_send, *rows_back),
        limit=16,
        us=0.6,
    )
    framed_back = halo(grad_mixed, rows_back, "strips_back", after=(expand_send,))
    small_half = shape_of(64, half, dtype=BF)
    small_keep, small_send = run(
        functools.partial(weight_pack_kernel, scale_three),
        "block_weights",
        (*framed, grad_mixed, gain_part),
        (small_half, small_half),
        scratch=(
            frame_scratch(center),
            pltpu.VMEM((height, breadth, channels), F32),
            pltpu.VMEM((64, channels), F32),
        ),
        after=(*framed_back[1:3], expand_send),
        limit=12,
        us=1.8,
    )
    (input_grad,) = run(
        input_kernel,
        "input_grad",
        (*framed_back, taps_three, grad_summed),
        (shape_of(height, breadth, channels, dtype=BF),),
        scratch=(frame_scratch(center), pltpu.VMEM((height, breadth, channels), F32)),
        after=(small_keep,),
        limit=12,
        us=2,
    )

    row_bits, col_bits = axis_bits("row"), axis_bits("col")
    outer = len(row_bits)
    low_first = [("row", bit, 0) for bit in row_bits]
    patch_order = [("col", bit, outer) for bit in col_bits[1:]] + low_first
    patch_sum = chain(
        patch_keep, patch_send, patch_order, block_count * row_count, 4 * channels // row_count,
        after=(small_keep,),
    )
    patch_sum = gather(patch_sum, "col", col_bits[1:])
    (patch_grad,) = run(
        finish_patch_kernel,
        "finish_patch",
        (patch_sum, swap(patch_sum, "col", 1)),
        (shape_of(4 * channels // row_count, wide),),
        limit=8,
    )

    def share(keep, send, order, rows, extra=(), after=()):
        total = chain(keep, send, order, row_count, rows, extra, after)
        for bit in col_bits[1:]:
            total = total + swap(total, "col", bit)
        return total, swap(total, "col", 1)

    project_order = [("row", bit, 1) for bit in row_bits[1:]] + low_first[:1]
    vector, wide_vector = shape_of(1, channels), shape_of(1, wide)
    project_grad, wide_taps, wide_gain, merge_sum, layer_sum = run(
        finish_project_kernel,
        "finish_project",
        share(project_keep, project_send, project_order, deep, after=(small_keep,)),
        (shape_of(deep, channels), shape_of(7, 7, wide), wide_vector, vector, vector),
        scratch=(pltpu.VMEM((112, channels), F32),),
        limit=8,
    )
    small = small_keep + swap(small_send, "col", 1)
    expand_grad, taps_sum, gain_sum = run(
        finish_expand_kernel,
        "finish_expand",
        share(expand_keep, expand_send, low_first, groups * shallow, (small, swap(small, "row", 1)), (input_grad,)),
        (shape_of(shallow, hidden_width), shape_of(7, 7, channels), vector),
        scratch=(pltpu.VMEM((64, channels), F32),),
        limit=8,
    )
    return (
        input_grad[None],
        taps_sum,
        gain_sum[0],
        expand_grad,
        project_grad,
        layer_sum[0],
        merge_sum[0],
        patch_grad,
        wide_taps,
        wide_gain[0],
    )


def solution(mesh):
    pixels = P(None, "row", "col", None)
    return jax.shard_map(
        body,
        mesh=mesh,
        in_specs=(pixels,) + (P(),) * 9 + (pixels, pixels),
        out_specs=(pixels, P(), P(), P("row", None), P("row", None), P(), P(), P("row", None), P(), P()),
        check_vma=False,
    )
```
